32 devices in a mesh: dp: 8 (over y, x, core), narrow: 4 (over z).
Axes of the slice: x: 2, y: 2, z: 4, core: 2. Of those that a mesh axis runs over, the one named last changes fastest.
Arguments:
- tokens: bfloat16 [16384, 2048], P(('dp', 'narrow')), may hold values from -6 to 6
- doc_lengths: int32 [8, 4], P('dp'), may hold values from 1 to 1792, as said below
- attn_gain: float32 [2048], replicated, may hold values from 0.5 to 1.5
- w_query: bfloat16 [2048, 2048], replicated, may hold values from -0.125 to 0.125
- w_key: bfloat16 [2048, 2048], replicated, may hold values from -0.125 to 0.125
- w_value: bfloat16 [2048, 2048], replicated, may hold values from -0.125 to 0.125
- w_beta: bfloat16 [2048, 16], replicated, may hold values from -0.125 to 0.125
- conv_weight: float32 [3, 4, 2048], replicated, may hold values from -3 to 3
- out_gain: float32 [128], replicated, may hold values from 0.25 to 1.75
- w_out: bfloat16 [2048, 2048], replicated, may hold values from -0.125 to 0.125
- mlp_gain: float32 [2048], replicated, may hold values from 0.5 to 1.5
- w_gate: bfloat16 [2048, 5632], P(None, 'narrow'), may hold values from -0.125 to 0.125
- w_up: bfloat16 [2048, 5632], P(None, 'narrow'), may hold values from -0.125 to 0.125
- w_down: bfloat16 [5632, 2048], P('narrow'), may hold values from -0.078125 to 0.078125
- grad_out: bfloat16 [16384, 2048], P(('dp', 'narrow')), may hold values from -6 to 6
Outputs:
- block_out: bfloat16 [16384, 2048], P(('dp', 'narrow'))
- grad_tokens: bfloat16 [16384, 2048], P(('dp', 'narrow'))
- grad_attn_gain: float32 [2048], P(('dp', 'narrow'))
- grad_query: float32 [2048, 2048], P(('dp', 'narrow'))
- grad_key: float32 [2048, 2048], P(('dp', 'narrow'))
- grad_value: float32 [2048, 2048], P(('dp', 'narrow'))
- grad_beta: float32 [2048, 16], P(('dp', 'narrow'))
- grad_conv: float32 [3, 4, 2048], P(None, None, ('dp', 'narrow'))
- grad_out_gain: float32 [128], P(('dp', 'narrow'))
- grad_w_out: float32 [2048, 2048], P(None, ('dp', 'narrow'))
- grad_mlp_gain: float32 [2048], P(('dp', 'narrow'))
- grad_gate: float32 [2048, 5632], P('dp', 'narrow')
- grad_up: float32 [2048, 5632], P('dp', 'narrow')
- grad_down: float32 [5632, 2048], P('narrow', 'dp')
The draws below stay inside these ranges and needn't reach their ends.
Inputs may be any that keep to these rules, and one draw needn't show every extreme that they name: `doc_lengths`: each row holds the 4 document lengths of one packed sequence in order, summing to 2048; in every row the largest is exactly 1792.
All inputs are finite; a program needn't handle non-finite values.
Results may differ from the reference program's by a relative error of at most 0.017.
Values may be sent and summed in bfloat16 or wider, within the bound.
A program may use at most 512 MiB of HBM per device.

```python
import math
import jax
import jax.numpy as jnp
from jax import lax

D = 2048
H = 16
DK = 128
FF = 5632
CONV = 4
SPAN = 64
DOCS = 4
SEQ_LEN = 2048
TOK_DEV = 512
SEQS = 8
TOKENS = 16384
N_NARROW = 4


def one_row(row_key):
    short_total = TOK_DEV // 2
    key_first, key_second, key_slot = jax.random.split(row_key, 3)
    first_cut = jax.random.randint(key_first, (), 1, short_total)
    second_cut = jax.random.randint(key_second, (), 1, short_total - 1)
    second_cut = jnp.where(second_cut >= first_cut, second_cut + 1, second_cut)
    lower_cut = jnp.minimum(first_cut, second_cut)
    upper_cut = jnp.maximum(first_cut, second_cut)
    shorts = jnp.stack([lower_cut, upper_cut - lower_cut, short_total - upper_cut]).astype(jnp.int32)
    long_slot = jax.random.randint(key_slot, (), 0, DOCS)
    slot_ids = jnp.arange(DOCS, dtype=jnp.int32)
    short_pick = jnp.clip(slot_ids - (slot_ids > long_slot).astype(jnp.int32), 0, DOCS - 2)
    return jnp.where(slot_ids == long_slot, SEQ_LEN - short_total, shorts[short_pick]).astype(jnp.int32)


def draw_doc_lengths(key, part):
    key = jax.random.fold_in(key, 11)
    row_keys = jax.random.split(key, SEQS)
    return jax.vmap(one_row)(row_keys).astype(jnp.int32)


def raised(result, stream_key, source, target, shards_of, factor):
    owner, partner = [(jnp.arange(result.shape[dim]) // (result.shape[dim] // shards_of)).reshape([-1 if axis == dim else 1 for axis in range(result.ndim)]) for dim in (source, target)]
    chosen = jax.random.permutation(stream_key, shards_of)[partner]
    strong = (owner == chosen) | (owner == (partner + shards_of // 2) % shards_of)
    return jnp.where(strong, factor * result, result)


def levels(rng, dims, cuts, least, high):
    gain = 1.0
    for axis_at, shards_of in cuts:
        steps = jax.random.uniform(jax.random.fold_in(jax.random.fold_in(rng, 6), axis_at), (shards_of,), jnp.float32, least / len(cuts), high / len(cuts))
        gain = gain * jnp.repeat(jnp.exp(steps), dims[axis_at] // shards_of).reshape((-1,) + (1,) * (len(dims) - 1 - axis_at))
    return gain


def bell_draw(stream_key, extent, width, bound, shards=(), kind=jnp.bfloat16):
    level = levels(stream_key, extent, shards, -0.22, 0.18) if shards else 1.0
    values = jax.random.normal(stream_key, extent, jnp.float32) * width * level
    return jnp.minimum(jnp.maximum(values, -bound), bound).astype(kind)


def heavy_noise(own_key, dims, deviation, limit, cuts, heavy, kind=jnp.bfloat16):
    drawn = deviation * jax.random.normal(own_key, dims, jnp.float32)
    if cuts:
        drawn = drawn * levels(own_key, dims, cuts, -0.22, 0.18)
    return jnp.clip(raised(drawn, jax.random.fold_in(own_key, 3), *heavy), -limit, limit).astype(kind)


def setup_inputs(seed: int = 0) -> dict:
    key_list = jax.random.split(jax.random.key(seed), 16)
    tokens = heavy_noise(key_list[0], (TOKENS, D), 1.0, 6.0, ((0, 32),), (0, 1, 32, 2.75))
    doc_lengths = draw_doc_lengths(jax.random.fold_in(key_list[15], 71), 0)
    attn_gain = jnp.clip(1.0 + 0.1 * jax.random.normal(key_list[2], (D,), jnp.float32), 0.5, 1.5)
    w_query = bell_draw(key_list[3], (D, D), D ** -0.5, 0.125)
    w_key = bell_draw(key_list[4], (D, D), D ** -0.5, 0.125)
    w_value = bell_draw(key_list[5], (D, D), D ** -0.5, 0.125)
    w_beta = bell_draw(key_list[6], (D, H), D ** -0.5, 0.125)
    conv_weight = bell_draw(key_list[7], (3, CONV, D), 0.5, 3.0, (), jnp.float32)
    out_gain = jnp.clip(1.0 + 0.15 * jax.random.normal(key_list[8], (DK,), jnp.float32), 0.25, 1.75)
    w_out = bell_draw(key_list[9], (D, D), D ** -0.5, 0.125)
    mlp_gain = jnp.clip(1.0 + 0.1 * jax.random.normal(key_list[10], (D,), jnp.float32), 0.5, 1.5)
    w_gate = bell_draw(key_list[11], (D, FF), D ** -0.5, 0.125, ((1, 4),))
    w_up = bell_draw(key_list[12], (D, FF), D ** -0.5, 0.125, ((1, 4),))
    w_down = bell_draw(key_list[13], (FF, D), FF ** -0.5, 0.078125, ((0, 4),))
    grad_out = heavy_noise(key_list[14], (TOKENS, D), 1.0, 6.0, ((0, 32),), (0, 1, 32, 2.75))
    return {"tokens": tokens, "doc_lengths": doc_lengths, "attn_gain": attn_gain, "w_query": w_query, "w_key": w_key, "w_value": w_value, "w_beta": w_beta, "conv_weight": conv_weight, "out_gain": out_gain, "w_out": w_out, "mlp_gain": mlp_gain, "w_gate": w_gate, "w_up": w_up, "w_down": w_down, "grad_out": grad_out}


@jax.custom_vjp
def low(v):
    return lax.optimization_barrier(v.astype(jnp.bfloat16)).astype(jnp.float32)

@jax.custom_vjp
def low_back(v):
    return v

def low_keep(v):
    return (low(v), None)

def low_pass(kept, grad):
    return (grad,)

def back_keep(v):
    return (v, None)

def back_low(kept, grad):
    return (low(grad),)
low.defvjp(low_keep, low_pass)
low_back.defvjp(back_keep, back_low)
EXACT_PRECISION = lax.Precision.HIGHEST

def matmul(left, right):
    return jnp.dot(left.astype(jnp.float32), right.astype(jnp.float32), precision=EXACT_PRECISION, preferred_element_type=jnp.float32)

def rms_scale(value_in, gain_vec, epsilon):
    return value_in * lax.rsqrt(lax.optimization_barrier(jnp.mean(value_in * value_in, axis=-1, keepdims=True)) + epsilon) * gain_vec

def doc_positions(doc_lengths, seq_length):
    doc_ends = jnp.cumsum(doc_lengths, axis=1).astype(jnp.int32)
    position = jnp.arange(seq_length, dtype=jnp.int32)
    return lax.optimization_barrier(jnp.sum((position[None, :, None] >= doc_ends[:, None, :]).astype(jnp.int32), axis=2)).astype(jnp.int32)

def short_conv(projected, conv_weight, doc_index):
    summed = projected * conv_weight[:, 0, :]
    for lag_steps in range(1, CONV):
        shifted = jnp.pad(projected, ((0, 0), (lag_steps, 0), (0, 0), (0, 0)))[:, :-lag_steps]
        earlier = jnp.pad(doc_index, ((0, 0), (lag_steps, 0)), constant_values=-1)[:, :-lag_steps]
        same_doc = (earlier == doc_index)[:, :, None, None]
        summed = summed + jnp.where(same_doc, shifted, 0.0) * conv_weight[:, lag_steps, :]
    return jax.nn.silu(summed)

def span_step(carried, block_in):
    span_state, last_doc = carried
    query_vec, key_vec, value_vec, beta_gate, doc_block = block_in
    block_len = doc_block.shape[1]
    key_size = key_vec.shape[-1]
    position = jnp.arange(block_len, dtype=jnp.int32)
    same_doc = doc_block[:, :, None] == doc_block[:, None, :]
    strict = (position[:, None] > position[None, :])[None] & same_doc
    causal = (position[:, None] >= position[None, :])[None] & same_doc
    key_gram = jnp.einsum('bhid,bhjd->bhij', key_vec, key_vec, precision=EXACT_PRECISION)
    lower_terms = jnp.where(strict[:, None], key_gram * beta_gate[..., None], 0.0)
    system = lower_terms + jnp.eye(block_len, dtype=jnp.float32)
    right_side = jnp.concatenate([key_vec * beta_gate[..., None], value_vec * beta_gate[..., None]], axis=-1)
    solved = jax.scipy.linalg.solve_triangular(system, right_side, lower=True, unit_diagonal=True)
    w_rows = solved[..., :key_size]
    u_rows = solved[..., key_size:]
    keep_state = (doc_block == last_doc[:, None]).astype(jnp.float32)[:, None, :, None]
    new_values = u_rows - keep_state * jnp.einsum('bhed,bhcd->bhce', span_state, w_rows, precision=EXACT_PRECISION)
    scores = jnp.where(causal[:, None], jnp.einsum('bhid,bhjd->bhij', query_vec, key_vec, precision=EXACT_PRECISION), 0.0)
    span_out = keep_state * jnp.einsum('bhed,bhcd->bhce', span_state, query_vec, precision=EXACT_PRECISION)
    span_out = span_out + jnp.einsum('bhij,bhje->bhie', scores, new_values, precision=EXACT_PRECISION)
    last_mask = (doc_block == doc_block[:, -1:]).astype(jnp.float32)[:, None, :, None]
    state_add = jnp.einsum('bhce,bhcd->bhed', new_values * last_mask, key_vec, precision=EXACT_PRECISION)
    span_state = keep_state[:, :, -1:, :] * span_state + state_add
    return ((span_state, doc_block[:, -1]), span_out)

def delta_core(projected, beta_logit, conv_weight, out_gain, doc_index):
    seq_count, seq_length = doc_index.shape
    head_count = beta_logit.shape[2]
    key_size = out_gain.shape[0]
    mixer_in = short_conv(projected, conv_weight, doc_index)
    query_vec = mixer_in[:, :, 0].reshape(seq_count, seq_length, head_count, key_size)
    key_vec = mixer_in[:, :, 1].reshape(seq_count, seq_length, head_count, key_size)
    value_vec = mixer_in[:, :, 2].reshape(seq_count, seq_length, head_count, key_size)
    query_vec = query_vec * lax.rsqrt(lax.optimization_barrier(jnp.sum(query_vec * query_vec, axis=-1, keepdims=True)) + 1e-06) * key_size ** (-0.5)
    key_vec = key_vec * lax.rsqrt(lax.optimization_barrier(jnp.sum(key_vec * key_vec, axis=-1, keepdims=True)) + 1e-06)
    beta_gate = jax.nn.sigmoid(beta_logit)
    blocks = seq_length // SPAN

    def to_blocks(array_in):
        return array_in.reshape(seq_count, blocks, SPAN, head_count, key_size).transpose(1, 0, 3, 2, 4)
    beta_blocks = beta_gate.reshape(seq_count, blocks, SPAN, head_count).transpose(1, 0, 3, 2)
    doc_blocks = doc_index.reshape(seq_count, blocks, SPAN).transpose(1, 0, 2)
    start_carry = (jnp.zeros((seq_count, head_count, key_size, key_size), jnp.float32), jnp.full((seq_count,), -1, jnp.int32))
    final_carry, span_outs = lax.scan(jax.checkpoint(span_step), start_carry, (to_blocks(query_vec), to_blocks(key_vec), to_blocks(value_vec), beta_blocks, doc_blocks))
    core_out = span_outs.transpose(1, 0, 3, 2, 4).reshape(seq_count, seq_length, head_count, key_size)
    core_out = core_out * lax.rsqrt(lax.optimization_barrier(jnp.mean(core_out * core_out, axis=-1, keepdims=True)) + 1e-05) * out_gain
    return core_out.reshape(seq_count, seq_length, head_count * key_size)

def block_forward(inputs, doc_index, attn_gain, w_query, w_key, w_value, w_beta, conv_weight, out_gain, w_out, mlp_gain, w_gate, w_up, w_down):
    normed = low(rms_scale(inputs, attn_gain, 1e-06))
    projected = low_back(jnp.stack([matmul(normed, w_query), matmul(normed, w_key), matmul(normed, w_value)], axis=2))
    beta_logit = low_back(matmul(normed, w_beta))
    attn_mixed = low(delta_core(projected, beta_logit, conv_weight, out_gain, doc_index))
    branch = low_back(matmul(attn_mixed, w_out))
    hidden = inputs + branch
    normed_mlp = low(rms_scale(hidden, mlp_gain, 1e-06))
    piece_width = w_gate.shape[1] // N_NARROW
    summed = hidden
    for shard_index in range(N_NARROW):
        first_col = shard_index * piece_width
        copy_rows = low_back(normed_mlp)
        gate_proj = low_back(matmul(copy_rows, w_gate[:, first_col:first_col + piece_width]))
        up_proj = low_back(matmul(copy_rows, w_up[:, first_col:first_col + piece_width]))
        activation = low(jax.nn.silu(gate_proj) * up_proj)
        summed = summed + low(matmul(activation, w_down[first_col:first_col + piece_width]))
    return summed

def reference(tokens, doc_lengths, attn_gain, w_query, w_key, w_value, w_beta, conv_weight, out_gain, w_out, mlp_gain, w_gate, w_up, w_down, grad_out):
    seq_total = doc_lengths.shape[0]
    seq_length = tokens.shape[0] // seq_total
    group_seqs = math.gcd(seq_total, max(1, 4096 // seq_length))
    group_count = seq_total // group_seqs
    doc_index = doc_positions(doc_lengths, seq_length).reshape(group_count, group_seqs, seq_length)
    inputs = tokens.astype(jnp.float32).reshape(group_count, group_seqs, seq_length, D)
    cotangent = grad_out.astype(jnp.float32).reshape(group_count, group_seqs, seq_length, D)
    weights = tuple((item.astype(jnp.float32) for item in (attn_gain, w_query, w_key, w_value, w_beta, conv_weight, out_gain, w_out, mlp_gain, w_gate, w_up, w_down)))

    def group_step(grad_sums, group_in):
        group_x, group_docs, group_cot = group_in

        def forward_fn(x_value, *weight_values):
            return block_forward(x_value, group_docs, *weight_values)
        group_out, back_fn = jax.vjp(forward_fn, group_x, *weights)
        group_grads = back_fn(group_cot)
        grad_sums = tuple((old + new for old, new in zip(grad_sums, group_grads[1:])))
        return (grad_sums, (group_out.astype(jnp.bfloat16), group_grads[0].astype(jnp.bfloat16)))
    zero_grads = tuple((jnp.zeros_like(item) for item in weights))
    grad_sums, (outputs, input_grads) = lax.scan(group_step, zero_grads, (inputs, doc_index, cotangent))
    block_out = outputs.reshape(TOKENS, D)
    grad_tokens = input_grads.reshape(TOKENS, D)
    return (block_out, grad_tokens, grad_sums[0], grad_sums[1], grad_sums[2], grad_sums[3], grad_sums[4], grad_sums[5], grad_sums[6], grad_sums[7], grad_sums[8], grad_sums[9], grad_sums[10], grad_sums[11])
```

```python
import functools

import jax
import jax.numpy as jnp
from jax import lax
from jax.experimental import pallas as pl
from jax.experimental.pallas import tpu as pltpu
from jax.sharding import PartitionSpec as P

CONV = 4
BLOCK = 128
HEADS_STEP = 2
PAD = 8
MESH = pl.DeviceIdType.MESH
F32 = jnp.float32
BF16 = jnp.bfloat16
VMEM_LIMIT = 56 * 1024 * 1024


def mm(left, right, contract=(1, 0)):
    return lax.dot_general(
        left.astype(BF16),
        right.astype(BF16),
        (((contract[0],), (contract[1],)), ((), ())),
        preferred_element_type=F32,
    )


def mm_nt(left, right):
    return mm(left, right, (1, 1))


def mm_tn(left, right):
    return mm(left, right, (0, 0))


def iotas(size):
    row = lax.broadcasted_iota(jnp.int32, (size, size), 0)
    col = lax.broadcasted_iota(jnp.int32, (size, size), 1)
    return row, col


def block_masks(since):
    size = since.shape[0]
    row, col = iotas(size)
    back = row - col
    causal = (back >= 0) & (back <= since)
    strict = (back > 0) & (back <= since)
    keep = (since > row).astype(F32)
    last = since[size - 1 : size, :]
    last_mask = (row >= size - 1 - last).astype(F32)
    keep_last = (last > size - 1).astype(F32)
    return causal, strict, keep, last_mask, keep_last


def unit_lower_inverses(lowers):
    size = lowers[0].shape[0]
    row, col = iotas(size)
    width = 1
    inverses = None
    while width < size:
        join = (row // (2 * width) == col // (2 * width)) & (row // width != col // width)
        pieces = [jnp.where(join, low, 0.0) for low in lowers]
        if inverses is None:
            eye = (row == col).astype(F32)
            inverses = [eye - piece for piece in pieces]
        else:
            halves = [mm(piece, inv) for piece, inv in zip(pieces, inverses)]
            inverses = [inv - mm(inv, half) for inv, half in zip(inverses, halves)]
        width *= 2
    return inverses


def conv_front(ext, proj, halo, taps, since):
    rows = proj.shape[0]
    ext[0:PAD, :] = halo.astype(F32)
    ext[PAD : PAD + rows, :] = proj
    pre = proj * taps[0:1, :]
    for lag in range(1, CONV):
        moved = ext[PAD - lag : PAD - lag + rows, :]
        pre = pre + jnp.where(since >= lag, moved, 0.0) * taps[lag : lag + 1, :]
    gate = 1.0 / (1.0 + jnp.exp(-pre))
    return pre, gate, pre * gate


def unit_rows(value):
    inv = lax.rsqrt(jnp.sum(value * value, axis=-1, keepdims=True) + 1e-06)
    return value * inv, inv


def head_column(array, head):
    lane = lax.broadcasted_iota(jnp.int32, array.shape, 1)
    return jnp.sum(jnp.where(lane == head, array, 0.0), axis=1, keepdims=True)


def forward_kernel(
    since_ref, beta_ref, query_ref, key_ref, value_ref, halo_ref, taps_ref,
    out_add_ref, out_map_ref, new_add_ref, new_map_ref, inverse_ref, starts_ref, end_ref,
    ext,
):
    rows = since_ref.shape[0]
    blocks = rows // BLOCK
    since = since_ref[...]
    jobs = []
    for sub in range(HEADS_STEP):
        head = pl.program_id(0) * HEADS_STEP + sub
        lanes = slice(sub * BLOCK, (sub + 1) * BLOCK)
        mixed = []
        for part, ref in enumerate((query_ref, key_ref, value_ref)):
            _, _, act = conv_front(
                ext.at[sub * 3 + part], ref[:, lanes].astype(F32), halo_ref[part, :, lanes],
                taps_ref[part, :, lanes], since,
            )
            mixed.append(act)
        query = unit_rows(mixed[0])[0] * (BLOCK ** -0.5)
        key = unit_rows(mixed[1])[0]
        beta = 1.0 / (1.0 + jnp.exp(-head_column(beta_ref[...], head)))
        jobs.append((lanes, query, key, mixed[2], beta))
    lowers, scores = [], []
    for lanes, query, key, value, beta in jobs:
        for blk in range(blocks):
            span = slice(blk * BLOCK, (blk + 1) * BLOCK)
            causal, strict, _, _, _ = block_masks(since[span])
            both = mm_nt(jnp.concatenate([key[span], query[span]], axis=0), key[span])
            lowers.append(jnp.where(strict, both[:BLOCK] * beta[span], 0.0))
            scores.append(jnp.where(causal, both[BLOCK:], 0.0).astype(BF16))
    inverses = [inv.astype(BF16) for inv in unit_lower_inverses(lowers)]
    row, col = iotas(BLOCK)
    eye = (row == col).astype(F32)
    states = [jnp.concatenate([jnp.zeros((BLOCK, BLOCK), F32), eye], axis=1) for _ in jobs]
    for blk in range(blocks):
        span = slice(blk * BLOCK, (blk + 1) * BLOCK)
        _, _, keep, last_mask, keep_last = block_masks(since[span])
        for sub, (lanes, query, key, value, beta) in enumerate(jobs):
            at = sub * blocks + blk
            inverse_ref[sub, blk] = inverses[at]
            state = states[sub].astype(BF16)
            starts_ref[sub, blk] = state
            stacked = jnp.concatenate([key[span] * keep, query[span] * keep], axis=0)
            seen = mm(stacked, state)
            rest = jnp.concatenate([value[span], jnp.zeros((BLOCK, BLOCK), F32)], axis=1)
            right = (rest - seen[:BLOCK]) * beta[span]
            new = mm(inverses[at], right).astype(BF16)
            out = seen[BLOCK:] + mm(scores[at], new)
            out_add_ref[span, lanes] = out[:, :BLOCK].astype(BF16)
            out_map_ref[span, lanes] = out[:, BLOCK:].astype(BF16)
            new_add_ref[span, lanes] = new[:, :BLOCK]
            new_map_ref[span, lanes] = new[:, BLOCK:]
            keep_both = jnp.concatenate([keep_last, keep_last], axis=1)
            states[sub] = states[sub] * keep_both + mm_tn(key[span] * last_mask, new)
    for sub in range(len(jobs)):
        end_ref[sub] = states[sub]


def whole_spec(shape):
    return pl.BlockSpec(shape, lambda h: (0,) * len(shape))


def head_spec(rows):
    return pl.BlockSpec((rows, HEADS_STEP * BLOCK), lambda h: (0, h))


def per_head(*tail):
    return pl.BlockSpec((HEADS_STEP,) + tail, lambda h: (h,) + (0,) * len(tail))


def lanes_spec(first, second):
    return pl.BlockSpec((first, second, HEADS_STEP * BLOCK), lambda h: (0, 0, h))


def params():
    return pltpu.CompilerParams(vmem_limit_bytes=VMEM_LIMIT)


def mixer_forward(since, beta_logit, query, key, value, halo, taps):
    rows, width = query.shape
    heads = width // BLOCK
    blocks = rows // BLOCK
    wide = jax.ShapeDtypeStruct((rows, width), BF16)
    return pl.pallas_call(
        forward_kernel,
        grid=(heads // HEADS_STEP,),
        in_specs=[
            whole_spec(since.shape), whole_spec(beta_logit.shape),
            head_spec(rows), head_spec(rows), head_spec(rows),
            lanes_spec(3, PAD), lanes_spec(3, CONV),
        ],
        out_specs=[
            head_spec(rows), head_spec(rows), head_spec(rows), head_spec(rows),
            per_head(blocks, BLOCK, BLOCK), per_head(blocks, BLOCK, 2 * BLOCK),
            per_head(BLOCK, 2 * BLOCK),
        ],
        out_shape=[
            wide, wide, wide, wide,
            jax.ShapeDtypeStruct((heads, blocks, BLOCK, BLOCK), BF16),
            jax.ShapeDtypeStruct((heads, blocks, BLOCK, 2 * BLOCK), BF16),
            jax.ShapeDtypeStruct((heads, BLOCK, 2 * BLOCK), F32),
        ],
        scratch_shapes=[pltpu.VMEM((3 * HEADS_STEP, PAD + rows, BLOCK), F32)],
        compiler_params=params(),
        name="mixer_forward",
    )(since, beta_logit, query, key, value, halo, taps)


def join_kernel(out_add_ref, out_map_ref, entry_ref, gain_ref, mixed_ref):
    for sub in range(HEADS_STEP):
        lanes = slice(sub * BLOCK, (sub + 1) * BLOCK)
        core = out_add_ref[:, lanes].astype(F32) + mm(out_map_ref[:, lanes], entry_ref[sub])
        scale = lax.rsqrt(jnp.mean(core * core, axis=-1, keepdims=True) + 1e-05)
        mixed_ref[:, lanes] = (core * scale * gain_ref[...]).astype(BF16)


def mixer_join(out_add, out_map, entry, gain):
    rows, width = out_add.shape
    heads = width // BLOCK
    return pl.pallas_call(
        join_kernel,
        grid=(heads // HEADS_STEP,),
        in_specs=[head_spec(rows), head_spec(rows), per_head(BLOCK, BLOCK), whole_spec((1, BLOCK))],
        out_specs=head_spec(rows),
        out_shape=jax.ShapeDtypeStruct((rows, width), BF16),
        compiler_params=params(),
        name="mixer_join",
    )(out_add, out_map, entry, gain)


def core_back_kernel(out_add_ref, out_map_ref, entry_ref, gain_ref, up_ref, d_core_ref, start_ref, gain_out_ref):
    @pl.when(pl.program_id(0) == 0)
    def _():
        gain_out_ref[...] = jnp.zeros_like(gain_out_ref)

    for sub in range(HEADS_STEP):
        lanes = slice(sub * BLOCK, (sub + 1) * BLOCK)
        out_map = out_map_ref[:, lanes]
        core = out_add_ref[:, lanes].astype(F32) + mm(out_map, entry_ref[sub])
        scale = lax.rsqrt(jnp.mean(core * core, axis=-1, keepdims=True) + 1e-05)
        unit = core * scale
        up = up_ref[:, lanes].astype(F32)
        gain_out_ref[...] += jnp.sum(up * unit, axis=0, keepdims=True)
        scaled = up * gain_ref[...]
        d_core = scale * (scaled - unit * jnp.mean(scaled * unit, axis=-1, keepdims=True))
        d_core = d_core.astype(BF16)
        d_core_ref[:, lanes] = d_core
        start_ref[sub] = mm_tn(out_map, d_core)


def mixer_core_back(out_add, out_map, entry, gain, up):
    rows, width = out_add.shape
    heads = width // BLOCK
    return pl.pallas_call(
        core_back_kernel,
        grid=(heads // HEADS_STEP,),
        in_specs=[
            head_spec(rows), head_spec(rows), per_head(BLOCK, BLOCK), whole_spec((1, BLOCK)), head_spec(rows),
        ],
        out_specs=[head_spec(rows), per_head(BLOCK, BLOCK), whole_spec((1, BLOCK))],
        out_shape=[
            jax.ShapeDtypeStruct((rows, width), BF16),
            jax.ShapeDtypeStruct((heads, BLOCK, BLOCK), F32),
            jax.ShapeDtypeStruct((1, BLOCK), F32),
        ],
        compiler_params=params(),
        name="mixer_core_back",
    )(out_add, out_map, entry, gain, up)


def backward_kernel(
    since_ref, beta_ref, query_ref, key_ref, value_ref, halo_ref, taps_ref,
    new_add_ref, new_map_ref, inverse_ref, starts_ref, entry_ref, exit_ref, d_core_ref,
    d_query_ref, d_key_ref, d_value_ref, d_halo_ref, d_taps_ref, d_beta_ref,
    ext, back,
):
    rows = since_ref.shape[0]
    blocks = rows // BLOCK
    since = since_ref[...]
    jobs = []
    for sub in range(HEADS_STEP):
        head = pl.program_id(0) * HEADS_STEP + sub
        lanes = slice(sub * BLOCK, (sub + 1) * BLOCK)
        fronts = []
        for part, ref in enumerate((query_ref, key_ref, value_ref)):
            fronts.append(
                conv_front(
                    ext.at[sub * 3 + part], ref[:, lanes].astype(F32), halo_ref[part, :, lanes],
                    taps_ref[part, :, lanes], since,
                )
            )
        query_unit, query_inv = unit_rows(fronts[0][2])
        key, key_inv = unit_rows(fronts[1][2])
        query = query_unit * (BLOCK ** -0.5)
        beta = 1.0 / (1.0 + jnp.exp(-head_column(beta_ref[...], head)))
        jobs.append((head, lanes, fronts, query, query_unit, query_inv, key, key_inv, beta))

    saved = {}
    for sub, (head, lanes, fronts, query, query_unit, query_inv, key, key_inv, beta) in enumerate(jobs):
        entry = entry_ref[sub].astype(BF16)
        for blk in range(blocks):
            span = slice(blk * BLOCK, (blk + 1) * BLOCK)
            causal, _, keep, last_mask, _ = block_masks(since[span])
            start = starts_ref[sub, blk]
            state = (start[:, :BLOCK].astype(F32) + mm(start[:, BLOCK:], entry)).astype(BF16)
            new = (new_add_ref[span, lanes].astype(F32) + mm(new_map_ref[span, lanes], entry)).astype(BF16)
            scores = jnp.where(causal, mm_nt(query[span], key[span]), 0.0).astype(BF16)
            d_out = d_core_ref[span, lanes]
            d_new = mm_tn(scores, d_out)
            d_state = mm_tn(query[span] * keep, d_out)
            saved[sub, blk] = (state, new, d_out, d_new, d_state)

    carried = [exit_ref[sub].astype(F32) for sub in range(HEADS_STEP)]
    chain = {}
    for blk in reversed(range(blocks)):
        span = slice(blk * BLOCK, (blk + 1) * BLOCK)
        _, _, keep, last_mask, keep_last = block_masks(since[span])
        for sub, (head, lanes, fronts, query, query_unit, query_inv, key, key_inv, beta) in enumerate(jobs):
            state, new, d_out, d_new, d_state = saved[sub, blk]
            after = carried[sub].astype(BF16)
            d_new = d_new + mm(key[span] * last_mask, after)
            d_right = mm_tn(inverse_ref[sub, blk], d_new)
            d_rest = d_right * beta[span]
            carried[sub] = carried[sub] * keep_last + d_state - mm_tn(key[span] * keep, d_rest)
            chain[sub, blk] = (after, d_right, d_rest)

    lane = lax.broadcasted_iota(jnp.int32, (rows, beta_ref.shape[1]), 1)
    d_beta_all = jnp.zeros((rows, beta_ref.shape[1]), F32)
    for sub, (head, lanes, fronts, query, query_unit, query_inv, key, key_inv, beta) in enumerate(jobs):
        d_queries, d_keys, d_values, d_betas = [], [], [], []
        for blk in range(blocks):
            span = slice(blk * BLOCK, (blk + 1) * BLOCK)
            causal, strict, keep, last_mask, _ = block_masks(since[span])
            state, new, d_out, _, _ = saved[sub, blk]
            after, d_right, d_rest = chain[sub, blk]
            both = mm_nt(jnp.concatenate([d_out, d_right.astype(BF16)], axis=0), new)
            d_scores = jnp.where(causal, both[:BLOCK], 0.0).astype(BF16)
            d_gram = (jnp.where(strict, both[BLOCK:], 0.0) * (-beta[span])).astype(BF16)
            key_b = key[span].astype(BF16)
            from_state = mm_nt(jnp.concatenate([d_out, d_rest.astype(BF16)], axis=0), state)
            left = mm(jnp.concatenate([d_scores, d_gram], axis=0), key_b)
            d_queries.append(from_state[:BLOCK] * keep + left[:BLOCK])
            d_key = left[BLOCK:] + mm_tn(
                jnp.concatenate([d_scores, d_gram], axis=0),
                jnp.concatenate([query[span].astype(BF16), key_b], axis=0),
            )
            d_key = d_key + mm_nt(new, after) * last_mask - from_state[BLOCK:] * keep
            d_keys.append(d_key)
            d_values.append(d_rest)
            d_betas.append(
                jnp.sum(d_right * new.astype(F32), axis=1, keepdims=True) * (1.0 - beta[span])
            )
        d_query = jnp.concatenate(d_queries, axis=0) * (BLOCK ** -0.5)
        d_key = jnp.concatenate(d_keys, axis=0)
        d_query = query_inv * (
            d_query - query_unit * jnp.sum(d_query * query_unit, axis=-1, keepdims=True)
        )
        d_key = key_inv * (d_key - key * jnp.sum(d_key * key, axis=-1, keepdims=True))
        d_value = jnp.concatenate(d_values, axis=0)
        d_beta_all = d_beta_all + jnp.where(lane == head, jnp.concatenate(d_betas, axis=0), 0.0)
        outs = (d_query_ref, d_key_ref, d_value_ref)
        for part, d_act in enumerate((d_query, d_key, d_value)):
            pre, gate, _ = fronts[part]
            taps = taps_ref[part, :, lanes]
            source = ext.at[sub * 3 + part]
            d_pre = d_act * gate * (1.0 + pre * (1.0 - gate))
            room = back.at[sub * 3 + part]
            total = None
            d_taps = []
            for lag in range(CONV):
                masked = d_pre if lag == 0 else jnp.where(since >= lag, d_pre, 0.0)
                moved = source[PAD - lag : PAD - lag + rows, :]
                d_taps.append(jnp.sum(masked * moved, axis=0, keepdims=True))
                room[lag, 0:PAD, :] = jnp.zeros((PAD, BLOCK), F32)
                room[lag, PAD : PAD + rows, :] = masked * taps[lag : lag + 1, :]
                room[lag, PAD + rows : PAD + rows + PAD, :] = jnp.zeros((PAD, BLOCK), F32)
                term = room[lag, lag : lag + PAD + rows, :]
                total = term if total is None else total + term
            d_taps_ref[part, :, lanes] = jnp.concatenate(d_taps, axis=0)
            d_halo_ref[part, :, lanes] = total[:PAD].astype(d_halo_ref.dtype)
            outs[part][:, lanes] = total[PAD:].astype(BF16)

    @pl.when(pl.program_id(0) == 0)
    def _():
        d_beta_ref[...] = d_beta_all

    @pl.when(pl.program_id(0) > 0)
    def _():
        d_beta_ref[...] += d_beta_all


def mixer_backward(
    since, beta_logit, query, key, value, halo, taps, new_add, new_map, inverse, starts, entry, exit_grad, d_core
):
    rows, width = query.shape
    heads = width // BLOCK
    blocks = rows // BLOCK
    wide = jax.ShapeDtypeStruct((rows, width), BF16)
    return pl.pallas_call(
        backward_kernel,
        grid=(heads // HEADS_STEP,),
        in_specs=[
            whole_spec(since.shape), whole_spec(beta_logit.shape),
            head_spec(rows), head_spec(rows), head_spec(rows),
            lanes_spec(3, PAD), lanes_spec(3, CONV),
            head_spec(rows), head_spec(rows),
            per_head(blocks, BLOCK, BLOCK), per_head(blocks, BLOCK, 2 * BLOCK),
            per_head(BLOCK, BLOCK), per_head(BLOCK, BLOCK), head_spec(rows),
        ],
        out_specs=[
            head_spec(rows), head_spec(rows), head_spec(rows),
            lanes_spec(3, PAD), lanes_spec(3, CONV), whole_spec(beta_logit.shape),
        ],
        out_shape=[
            wide, wide, wide,
            jax.ShapeDtypeStruct((3, PAD, width), F32),
            jax.ShapeDtypeStruct((3, CONV, width), F32),
            jax.ShapeDtypeStruct(beta_logit.shape, F32),
        ],
        scratch_shapes=[
            pltpu.VMEM((3 * HEADS_STEP, PAD + rows, BLOCK), F32),
            pltpu.VMEM((3 * HEADS_STEP, CONV, PAD + rows + PAD, BLOCK), F32),
        ],
        compiler_params=params(),
        name="mixer_backward",
    )(
        since, beta_logit, query, key, value, halo, taps, new_add, new_map, inverse, starts, entry, exit_grad, d_core
    )


GROUPS = 4


def chain_kernel(axis, forward, map_ref, add_ref, out_ref, sent, landed, send_sem, recv_sem):
    count = lax.axis_size(axis)
    me = lax.axis_index(axis)
    heads = add_ref.shape[0]
    step = heads // GROUPS
    up, down = (me + 1, me - 1) if forward else (me - 1, me + 1)
    first, last = (0, count - 1) if forward else (count - 1, 0)
    barrier = pltpu.get_barrier_semaphore()

    @pl.when(me != first)
    def _():
        pl.semaphore_signal(barrier, inc=1, device_id={axis: down}, device_id_type=MESH)

    @pl.when(me != last)
    def _():
        pl.semaphore_wait(barrier, 1)

    def copy(group, target):
        return pltpu.make_async_remote_copy(
            src_ref=sent.at[group],
            dst_ref=landed.at[group],
            send_sem=send_sem.at[group],
            recv_sem=recv_sem.at[group],
            device_id={axis: target},
            device_id_type=MESH,
        )

    for group in range(GROUPS):
        @pl.when(me != first)
        def _():
            copy(group, up).wait_recv()
            for sub in range(step):
                head = group * step + sub
                out_ref[head] = landed[group, sub].astype(F32)

        @pl.when(me == first)
        def _():
            out_ref[group * step : (group + 1) * step] = jnp.zeros((step,) + out_ref.shape[1:], F32)

        @pl.when(me != last)
        def _():
            for sub in range(step):
                head = group * step + sub
                if forward:
                    moved = mm(map_ref[head], out_ref[head])
                else:
                    moved = mm_tn(map_ref[head], out_ref[head])
                sent[group, sub] = (moved + add_ref[head]).astype(BF16)
            copy(group, up).start()

    @pl.when(me != last)
    def _():
        for group in range(GROUPS):
            copy(group, up).wait_send()


def carry_chain(map_part, add_part, axis, forward):
    heads = add_part.shape[0]
    part = (GROUPS, heads // GROUPS, BLOCK, BLOCK)
    return pl.pallas_call(
        functools.partial(chain_kernel, axis, forward),
        in_specs=[pl.BlockSpec(memory_space=pltpu.VMEM)] * 2,
        out_specs=pl.BlockSpec(memory_space=pltpu.VMEM),
        out_shape=jax.ShapeDtypeStruct(add_part.shape, F32),
        scratch_shapes=[
            pltpu.VMEM(part, BF16),
            pltpu.VMEM(part, BF16),
            pltpu.SemaphoreType.DMA((GROUPS,)),
            pltpu.SemaphoreType.DMA((GROUPS,)),
        ],
        compiler_params=pltpu.CompilerParams(
            collective_id=1 if forward else 2, has_side_effects=True, vmem_limit_bytes=VMEM_LIMIT // 2
        ),
        name="carry_forward" if forward else "carry_backward",
    )(map_part, add_part)


def shifted(value, axis, steps):
    count = lax.axis_size(axis)
    first, last = (max(0, -steps), min(count, count - steps))
    return lax.ppermute(value, axis, [(source, source + steps) for source in range(first, last)])


def matmul(left, right):
    return jnp.dot(left, right, preferred_element_type=F32)


def dot_tn(left, right):
    return jnp.einsum("rd,re->de", left, right, preferred_element_type=F32)


def dot_nt(left, right):
    return jnp.einsum("re,de->rd", left, right, preferred_element_type=F32)


def rms_scale(value_in, gain_vec, epsilon):
    return value_in * lax.rsqrt(jnp.mean(value_in * value_in, axis=-1, keepdims=True) + epsilon) * gain_vec


def norm_back(value_in, gain_vec, upstream, epsilon):
    inv_scale = lax.rsqrt(jnp.mean(value_in * value_in, axis=-1, keepdims=True) + epsilon)
    scaled_up = upstream * gain_vec
    gain_term = jnp.sum(upstream * value_in * inv_scale, axis=0)
    cubed = inv_scale * inv_scale * inv_scale
    back_value = inv_scale * scaled_up - value_in * cubed * jnp.mean(
        scaled_up * value_in, axis=-1, keepdims=True
    )
    return (back_value, gain_term)


def since_start(doc_lengths, offset, rows):
    ends = jnp.cumsum(doc_lengths[0])
    position = offset + jnp.arange(rows, dtype=jnp.int32)
    starts = jnp.max(jnp.where(position[:, None] >= ends[None, :], ends[None, :], 0), axis=1)
    return jnp.broadcast_to((position - starts)[:, None], (rows, BLOCK)).astype(jnp.int32)


def scatter_all(value, dim):
    part = lax.psum_scatter(value, "dp", scatter_dimension=dim, tiled=True)
    return lax.psum_scatter(part, "narrow", scatter_dimension=dim, tiled=True)


def local(
    tokens,
    doc_lengths,
    attn_gain,
    w_query,
    w_key,
    w_value,
    w_beta,
    conv_weight,
    out_gain,
    w_out,
    mlp_gain,
    w_gate,
    w_up,
    w_down,
    grad_out,
):
    tok_rows, model_width = tokens.shape
    edge = CONV - 1
    offset = lax.axis_index("narrow") * tok_rows
    cot_rows = lax.all_gather(grad_out, "narrow", axis=0, tiled=True)
    since = since_start(doc_lengths, offset, tok_rows)
    inputs = tokens.astype(F32)
    normed = rms_scale(inputs, attn_gain, 1e-06).astype(BF16)
    query, key, value = (matmul(normed, w) for w in (w_query, w_key, w_value))
    beta_logit = matmul(normed, w_beta)
    halo = shifted(
        jnp.stack([part[tok_rows - PAD :].astype(BF16) for part in (query, key, value)]), "narrow", 1
    )
    out_add, out_map, new_add, new_map, inverse, starts, end = mixer_forward(
        since, beta_logit, query, key, value, halo, conv_weight
    )
    transfer = end[:, :, BLOCK:].astype(BF16)
    entry = carry_chain(transfer, end[:, :, :BLOCK], "narrow", True)
    gain_row = out_gain[None, :]
    attn_mixed = mixer_join(out_add, out_map, entry, gain_row)
    hidden = inputs + matmul(attn_mixed, w_out)
    normed_mlp = rms_scale(hidden, mlp_gain, 1e-06).astype(BF16)
    gathered = lax.all_gather(normed_mlp, "narrow", axis=0, tiled=True)
    gate_proj = matmul(gathered, w_gate)
    up_proj = matmul(gathered, w_up)
    gate_sigmoid = jax.nn.sigmoid(gate_proj)
    silu_gate = gate_proj * gate_sigmoid
    activation = (silu_gate * up_proj).astype(BF16)
    d_act = jnp.einsum("rd,fd->rf", cot_rows, w_down, preferred_element_type=F32)
    d_gate = (d_act * up_proj * gate_sigmoid * (1.0 + gate_proj * (1.0 - gate_sigmoid))).astype(BF16)
    d_up = (d_act * silu_gate).astype(BF16)
    from_gate = jnp.einsum("rf,df->rd", d_gate, w_gate, preferred_element_type=F32)
    d_normed_mlp = lax.psum_scatter(
        (from_gate + jnp.einsum("rf,df->rd", d_up, w_up, preferred_element_type=F32)).astype(BF16),
        "narrow",
        scatter_dimension=0,
        tiled=True,
    ).astype(F32)
    ffn_sum = lax.psum_scatter(
        matmul(activation, w_down).astype(BF16), "narrow", scatter_dimension=0, tiled=True
    ).astype(F32)
    block_out = (hidden + ffn_sum).astype(BF16)
    down_term_grad = dot_tn(activation, cot_rows)
    gate_term_grad = dot_tn(gathered, d_gate)
    up_term_grad = dot_tn(gathered, d_up)
    grad_gate, grad_up, grad_down = (
        lax.psum_scatter(gate_term_grad.astype(BF16), "dp", scatter_dimension=0, tiled=True).astype(F32),
        lax.psum_scatter(up_term_grad.astype(BF16), "dp", scatter_dimension=0, tiled=True).astype(F32),
        lax.psum_scatter(down_term_grad.astype(BF16), "dp", scatter_dimension=1, tiled=True).astype(F32),
    )
    d_hidden_norm, mlp_gain_term = norm_back(hidden, mlp_gain, d_normed_mlp, 1e-06)
    d_hidden = grad_out.astype(F32) + d_hidden_norm
    d_branch = d_hidden.astype(BF16)
    w_out_term = dot_tn(attn_mixed, d_branch)
    d_mixed = dot_nt(d_branch, w_out)
    d_core, start_grad, out_gain_term = mixer_core_back(out_add, out_map, entry, gain_row, d_mixed)
    exit_grad = carry_chain(transfer, start_grad, "narrow", False)
    d_query, d_key, d_value, d_halo, conv_term, d_beta = mixer_backward(
        since, beta_logit, query, key, value, halo, conv_weight,
        new_add, new_map, inverse, starts, entry, exit_grad, d_core,
    )
    after = shifted(d_halo.astype(BF16), "narrow", -1)
    d_query, d_key, d_value = (
        part.at[tok_rows - PAD :].add(after[place])
        for place, part in enumerate((d_query, d_key, d_value))
    )
    d_beta_low = d_beta.astype(BF16)
    query_term = dot_tn(normed, d_query)
    key_term = dot_tn(normed, d_key)
    value_term = dot_tn(normed, d_value)
    beta_term = jnp.einsum("rd,rh->dh", normed, d_beta_low, preferred_element_type=F32)
    d_normed = dot_nt(d_query, w_query) + dot_nt(d_key, w_key) + dot_nt(d_value, w_value)
    d_normed = d_normed + jnp.einsum("rh,dh->rd", d_beta_low, w_beta, preferred_element_type=F32)
    d_input_norm, attn_gain_term = norm_back(inputs, attn_gain, d_normed, 1e-06)
    grad_tokens = (d_hidden + d_input_norm).astype(BF16)
    both = ("dp", "narrow")
    grad_query, grad_key, grad_value = (
        scatter_all(term.astype(BF16), 0).astype(F32) for term in (query_term, key_term, value_term)
    )
    grad_w_out = scatter_all(w_out_term.astype(BF16), 1).astype(F32)
    grad_beta, grad_conv, grad_attn_gain, grad_out_gain, grad_mlp_gain = (
        lax.psum_scatter(beta_term, both, scatter_dimension=0, tiled=True),
        lax.psum_scatter(conv_term, both, scatter_dimension=2, tiled=True),
        lax.psum_scatter(attn_gain_term, both, scatter_dimension=0, tiled=True),
        lax.psum_scatter(out_gain_term[0], both, scatter_dimension=0, tiled=True),
        lax.psum_scatter(mlp_gain_term, both, scatter_dimension=0, tiled=True),
    )
    return (
        block_out,
        grad_tokens,
        grad_attn_gain,
        grad_query,
        grad_key,
        grad_value,
        grad_beta,
        grad_conv,
        grad_out_gain,
        grad_w_out,
        grad_mlp_gain,
        grad_gate,
        grad_up,
        grad_down,
    )


def solution(mesh):
    placed = (
        P(("dp", "narrow"), None),
        P("dp", None),
        P(),
        P(),
        P(),
        P(),
        P(),
        P(),
        P(),
        P(),
        P(),
        P(None, "narrow"),
        P(None, "narrow"),
        P("narrow", None),
        P(("dp", "narrow"), None),
    )
    return jax.shard_map(
        local,
        mesh=mesh,
        in_specs=placed,
        out_specs=(
            P(("dp", "narrow"), None),
            P(("dp", "narrow"), None),
            P(("dp", "narrow")),
            P(("dp", "narrow"), None),
            P(("dp", "narrow"), None),
            P(("dp", "narrow"), None),
            P(("dp", "narrow"), None),
            P(None, None, ("dp", "narrow")),
            P(("dp", "narrow")),
            P(None, ("dp", "narrow")),
            P(("dp", "narrow")),
            P("dp", "narrow"),
            P("dp", "narrow"),
            P("narrow", "dp"),
        ),
        check_vma=False,
    )
```

```python
import functools

import jax
import jax.numpy as jnp
from jax import lax
from jax.experimental import pallas as pl
from jax.experimental.pallas import tpu as pltpu
from jax.sharding import PartitionSpec as P

CONV = 4
BLOCK = 128
HEADS_STEP = 2
PAD = 8
MESH = pl.DeviceIdType.MESH
F32 = jnp.float32
BF16 = jnp.bfloat16
VMEM_LIMIT = 56 * 1024 * 1024


def mm(left, right, contract=(1, 0)):
    return lax.dot_general(
        left.astype(BF16),
        right.astype(BF16),
        (((contract[0],), (contract[1],)), ((), ())),
        preferred_element_type=F32,
    )


def mm_nt(left, right):
    return mm(left, right, (1, 1))


def mm_tn(left, right):
    return mm(left, right, (0, 0))


def iotas(size):
    row = lax.broadcasted_iota(jnp.int32, (size, size), 0)
    col = lax.broadcasted_iota(jnp.int32, (size, size), 1)
    return row, col


def block_masks(since):
    size = since.shape[0]
    row, col = iotas(size)
    back = row - col
    causal = (back >= 0) & (back <= since)
    strict = (back > 0) & (back <= since)
    keep = (since > row).astype(F32)
    last = since[size - 1 : size, :]
    last_mask = (row >= size - 1 - last).astype(F32)
    keep_last = (last > size - 1).astype(F32)
    return causal, strict, keep, last_mask, keep_last


def unit_lower_inverses(lowers):
    size = lowers[0].shape[0]
    row, col = iotas(size)
    width = 1
    inverses = None
    while width < size:
        join = (row // (2 * width) == col // (2 * width)) & (row // width != col // width)
        pieces = [jnp.where(join, low, 0.0) for low in lowers]
        if inverses is None:
            eye = (row == col).astype(F32)
            inverses = [eye - piece for piece in pieces]
        else:
            halves = [mm(piece, inv) for piece, inv in zip(pieces, inverses)]
            inverses = [inv - mm(inv, half) for inv, half in zip(inverses, halves)]
        width *= 2
    return inverses


def conv_front(ext, proj, halo, taps, since):
    rows = proj.shape[0]
    ext[0:PAD, :] = halo.astype(F32)
    ext[PAD : PAD + rows, :] = proj
    pre = proj * taps[0:1, :]
    for lag in range(1, CONV):
        moved = ext[PAD - lag : PAD - lag + rows, :]
        pre = pre + jnp.where(since >= lag, moved, 0.0) * taps[lag : lag + 1, :]
    gate = 1.0 / (1.0 + jnp.exp(-pre))
    return pre, gate, pre * gate


def unit_rows(value):
    inv = lax.rsqrt(jnp.sum(value * value, axis=-1, keepdims=True) + 1e-06)
    return value * inv, inv


def head_column(array, head):
    lane = lax.broadcasted_iota(jnp.int32, array.shape, 1)
    return jnp.sum(jnp.where(lane == head, array, 0.0), axis=1, keepdims=True)


def forward_kernel(
    since_ref, beta_ref, query_ref, key_ref, value_ref, halo_ref, taps_ref,
    out_add_ref, out_map_ref, new_add_ref, new_map_ref, inverse_ref, starts_ref, end_ref,
    ext,
):
    rows = since_ref.shape[0]
    blocks = rows // BLOCK
    since = since_ref[...]
    jobs = []
    for sub in range(HEADS_STEP):
        head = pl.program_id(0) * HEADS_STEP + sub
        lanes = slice(sub * BLOCK, (sub + 1) * BLOCK)
        mixed = []
        for part, ref in enumerate((query_ref, key_ref, value_ref)):
            _, _, act = conv_front(
                ext.at[sub * 3 + part], ref[:, lanes].astype(F32), halo_ref[part, :, lanes],
                taps_ref[part, :, lanes], since,
            )
            mixed.append(act)
        query = unit_rows(mixed[0])[0] * (BLOCK ** -0.5)
        key = unit_rows(mixed[1])[0]
        beta = 1.0 / (1.0 + jnp.exp(-head_column(beta_ref[...], head)))
        jobs.append((lanes, query, key, mixed[2], beta))
    lowers, scores = [], []
    for lanes, query, key, value, beta in jobs:
        for blk in range(blocks):
            span = slice(blk * BLOCK, (blk + 1) * BLOCK)
            causal, strict, _, _, _ = block_masks(since[span])
            both = mm_nt(jnp.concatenate([key[span], query[span]], axis=0), key[span])
            lowers.append(jnp.where(strict, both[:BLOCK] * beta[span], 0.0))
            scores.append(jnp.where(causal, both[BLOCK:], 0.0).astype(BF16))
    inverses = [inv.astype(BF16) for inv in unit_lower_inverses(lowers)]
    row, col = iotas(BLOCK)
    eye = (row == col).astype(F32)
    states = [jnp.concatenate([jnp.zeros((BLOCK, BLOCK), F32), eye], axis=1) for _ in jobs]
    for blk in range(blocks):
        span = slice(blk * BLOCK, (blk + 1) * BLOCK)
        _, _, keep, last_mask, keep_last = block_masks(since[span])
        for sub, (lanes, query, key, value, beta) in enumerate(jobs):
            at = sub * blocks + blk
            inverse_ref[sub, blk] = inverses[at]
            state = states[sub].astype(BF16)
            starts_ref[sub, blk] = state
            stacked = jnp.concatenate([key[span] * keep, query[span] * keep], axis=0)
            seen = mm(stacked, state)
            rest = jnp.concatenate([value[span], jnp.zeros((BLOCK, BLOCK), F32)], axis=1)
            right = (rest - seen[:BLOCK]) * beta[span]
            new = mm(inverses[at], right).astype(BF16)
            out = seen[BLOCK:] + mm(scores[at], new)
            out_add_ref[span, lanes] = out[:, :BLOCK].astype(BF16)
            out_map_ref[span, lanes] = out[:, BLOCK:].astype(BF16)
            new_add_ref[span, lanes] = new[:, :BLOCK]
            new_map_ref[span, lanes] = new[:, BLOCK:]
            keep_both = jnp.concatenate([keep_last, keep_last], axis=1)
            states[sub] = states[sub] * keep_both + mm_tn(key[span] * last_mask, new)
    for sub in range(len(jobs)):
        end_ref[sub] = states[sub]


def whole_spec(shape):
    return pl.BlockSpec(shape, lambda h: (0,) * len(shape))


def head_spec(rows):
    return pl.BlockSpec((rows, HEADS_STEP * BLOCK), lambda h: (0, h))


def per_head(*tail):
    return pl.BlockSpec((HEADS_STEP,) + tail, lambda h: (h,) + (0,) * len(tail))


def lanes_spec(first, second):
    return pl.BlockSpec((first, second, HEADS_STEP * BLOCK), lambda h: (0, 0, h))


def params():
    return pltpu.CompilerParams(vmem_limit_bytes=VMEM_LIMIT)


def mixer_forward(since, beta_logit, query, key, value, halo, taps):
    rows, width = query.shape
    heads = width // BLOCK
    blocks = rows // BLOCK
    wide = jax.ShapeDtypeStruct((rows, width), BF16)
    return pl.pallas_call(
        forward_kernel,
        grid=(heads // HEADS_STEP,),
        in_specs=[
            whole_spec(since.shape), whole_spec(beta_logit.shape),
            head_spec(rows), head_spec(rows), head_spec(rows),
            lanes_spec(3, PAD), lanes_spec(3, CONV),
        ],
        out_specs=[
            head_spec(rows), head_spec(rows), head_spec(rows), head_spec(rows),
            per_head(blocks, BLOCK, BLOCK), per_head(blocks, BLOCK, 2 * BLOCK),
            per_head(BLOCK, 2 * BLOCK),
        ],
        out_shape=[
            wide, wide, wide, wide,
            jax.ShapeDtypeStruct((heads, blocks, BLOCK, BLOCK), BF16),
            jax.ShapeDtypeStruct((heads, blocks, BLOCK, 2 * BLOCK), BF16),
            jax.ShapeDtypeStruct((heads, BLOCK, 2 * BLOCK), F32),
        ],
        scratch_shapes=[pltpu.VMEM((3 * HEADS_STEP, PAD + rows, BLOCK), F32)],
        compiler_params=params(),
        name="mixer_forward",
    )(since, beta_logit, query, key, value, halo, taps)


def join_kernel(out_add_ref, out_map_ref, entry_ref, gain_ref, mixed_ref):
    for sub in range(HEADS_STEP):
        lanes = slice(sub * BLOCK, (sub + 1) * BLOCK)
        core = out_add_ref[:, lanes].astype(F32) + mm(out_map_ref[:, lanes], entry_ref[sub])
        scale = lax.rsqrt(jnp.mean(core * core, axis=-1, keepdims=True) + 1e-05)
        mixed_ref[:, lanes] = (core * scale * gain_ref[...]).astype(BF16)


def mixer_join(out_add, out_map, entry, gain):
    rows, width = out_add.shape
    heads = width // BLOCK
    return pl.pallas_call(
        join_kernel,
        grid=(heads // HEADS_STEP,),
        in_specs=[head_spec(rows), head_spec(rows), per_head(BLOCK, BLOCK), whole_spec((1, BLOCK))],
        out_specs=head_spec(rows),
        out_shape=jax.ShapeDtypeStruct((rows, width), BF16),
        compiler_params=params(),
        name="mixer_join",
    )(out_add, out_map, entry, gain)


def core_back_kernel(out_add_ref, out_map_ref, entry_ref, gain_ref, up_ref, d_core_ref, start_ref, gain_out_ref):
    @pl.when(pl.program_id(0) == 0)
    def _():
        gain_out_ref[...] = jnp.zeros_like(gain_out_ref)

    for sub in range(HEADS_STEP):
        lanes = slice(sub * BLOCK, (sub + 1) * BLOCK)
        out_map = out_map_ref[:, lanes]
        core = out_add_ref[:, lanes].astype(F32) + mm(out_map, entry_ref[sub])
        scale = lax.rsqrt(jnp.mean(core * core, axis=-1, keepdims=True) + 1e-05)
        unit = core * scale
        up = up_ref[:, lanes].astype(F32)
        gain_out_ref[...] += jnp.sum(up * unit, axis=0, keepdims=True)
        scaled = up * gain_ref[...]
        d_core = scale * (scaled - unit * jnp.mean(scaled * unit, axis=-1, keepdims=True))
        d_core = d_core.astype(BF16)
        d_core_ref[:, lanes] = d_core
        start_ref[sub] = mm_tn(out_map, d_core)


def mixer_core_back(out_add, out_map, entry, gain, up):
    rows, width = out_add.shape
    heads = width // BLOCK
    return pl.pallas_call(
        core_back_kernel,
        grid=(heads // HEADS_STEP,),
        in_specs=[
            head_spec(rows), head_spec(rows), per_head(BLOCK, BLOCK), whole_spec((1, BLOCK)), head_spec(rows),
        ],
        out_specs=[head_spec(rows), per_head(BLOCK, BLOCK), whole_spec((1, BLOCK))],
        out_shape=[
            jax.ShapeDtypeStruct((rows, width), BF16),
            jax.ShapeDtypeStruct((heads, BLOCK, BLOCK), F32),
            jax.ShapeDtypeStruct((1, BLOCK), F32),
        ],
        compiler_params=params(),
        name="mixer_core_back",
    )(out_add, out_map, entry, gain, up)


def backward_kernel(
    since_ref, beta_ref, query_ref, key_ref, value_ref, halo_ref, taps_ref,
    new_add_ref, new_map_ref, inverse_ref, starts_ref, entry_ref, exit_ref, d_core_ref,
    d_query_ref, d_key_ref, d_value_ref, d_halo_ref, d_taps_ref, d_beta_ref,
    ext, back,
):
    rows = since_ref.shape[0]
    blocks = rows // BLOCK
    since = since_ref[...]
    jobs = []
    for sub in range(HEADS_STEP):
        head = pl.program_id(0) * HEADS_STEP + sub
        lanes = slice(sub * BLOCK, (sub + 1) * BLOCK)
        fronts = []
        for part, ref in enumerate((query_ref, key_ref, value_ref)):
            fronts.append(
                conv_front(
                    ext.at[sub * 3 + part], ref[:, lanes].astype(F32), halo_ref[part, :, lanes],
                    taps_ref[part, :, lanes], since,
                )
            )
        query_unit, query_inv = unit_rows(fronts[0][2])
        key, key_inv = unit_rows(fronts[1][2])
        query = query_unit * (BLOCK ** -0.5)
        beta = 1.0 / (1.0 + jnp.exp(-head_column(beta_ref[...], head)))
        jobs.append((head, lanes, fronts, query, query_unit, query_inv, key, key_inv, beta))

    saved = {}
    for sub, (head, lanes, fronts, query, query_unit, query_inv, key, key_inv, beta) in enumerate(jobs):
        entry = entry_ref[sub].astype(BF16)
        for blk in range(blocks):
            span = slice(blk * BLOCK, (blk + 1) * BLOCK)
            causal, _, keep, last_mask, _ = block_masks(since[span])
            start = starts_ref[sub, blk]
            state = (start[:, :BLOCK].astype(F32) + mm(start[:, BLOCK:], entry)).astype(BF16)
            new = (new_add_ref[span, lanes].astype(F32) + mm(new_map_ref[span, lanes], entry)).astype(BF16)
            scores = jnp.where(causal, mm_nt(query[span], key[span]), 0.0).astype(BF16)
            d_out = d_core_ref[span, lanes]
            d_new = mm_tn(scores, d_out)
            d_state = mm_tn(query[span] * keep, d_out)
            saved[sub, blk] = (state, new, d_out, d_new, d_state)

    carried = [exit_ref[sub].astype(F32) for sub in range(HEADS_STEP)]
    chain = {}
    for blk in reversed(range(blocks)):
        span = slice(blk * BLOCK, (blk + 1) * BLOCK)
        _, _, keep, last_mask, keep_last = block_masks(since[span])
        for sub, (head, lanes, fronts, query, query_unit, query_inv, key, key_inv, beta) in enumerate(jobs):
            state, new, d_out, d_new, d_state = saved[sub, blk]
            after = carried[sub].astype(BF16)
            d_new = d_new + mm(key[span] * last_mask, after)
            d_right = mm_tn(inverse_ref[sub, blk], d_new)
            d_rest = d_right * beta[span]
            carried[sub] = carried[sub] * keep_last + d_state - mm_tn(key[span] * keep, d_rest)
            chain[sub, blk] = (after, d_right, d_rest)

    lane = lax.broadcasted_iota(jnp.int32, (rows, beta_ref.shape[1]), 1)
    d_beta_all = jnp.zeros((rows, beta_ref.shape[1]), F32)
    for sub, (head, lanes, fronts, query, query_unit, query_inv, key, key_inv, beta) in enumerate(jobs):
        d_queries, d_keys, d_values, d_betas = [], [], [], []
        for blk in range(blocks):
            span = slice(blk * BLOCK, (blk + 1) * BLOCK)
            causal, strict, keep, last_mask, _ = block_masks(since[span])
            state, new, d_out, _, _ = saved[sub, blk]
            after, d_right, d_rest = chain[sub, blk]
            both = mm_nt(jnp.concatenate([d_out, d_right.astype(BF16)], axis=0), new)
            d_scores = jnp.where(causal, both[:BLOCK], 0.0).astype(BF16)
            d_gram = (jnp.where(strict, both[BLOCK:], 0.0) * (-beta[span])).astype(BF16)
            key_b = key[span].astype(BF16)
            from_state = mm_nt(jnp.concatenate([d_out, d_rest.astype(BF16)], axis=0), state)
            left = mm(jnp.concatenate([d_scores, d_gram], axis=0), key_b)
            d_queries.append(from_state[:BLOCK] * keep + left[:BLOCK])
            d_key = left[BLOCK:] + mm_tn(
                jnp.concatenate([d_scores, d_gram], axis=0),
                jnp.concatenate([query[span].astype(BF16), key_b], axis=0),
            )
            d_key = d_key + mm_nt(new, after) * last_mask - from_state[BLOCK:] * keep
            d_keys.append(d_key)
            d_values.append(d_rest)
            d_betas.append(
                jnp.sum(d_right * new.astype(F32), axis=1, keepdims=True) * (1.0 - beta[span])
            )
        d_query = jnp.concatenate(d_queries, axis=0) * (BLOCK ** -0.5)
        d_key = jnp.concatenate(d_keys, axis=0)
        d_query = query_inv * (
            d_query - query_unit * jnp.sum(d_query * query_unit, axis=-1, keepdims=True)
        )
        d_key = key_inv * (d_key - key * jnp.sum(d_key * key, axis=-1, keepdims=True))
        d_value = jnp.concatenate(d_values, axis=0)
        d_beta_all = d_beta_all + jnp.where(lane == head, jnp.concatenate(d_betas, axis=0), 0.0)
        outs = (d_query_ref, d_key_ref, d_value_ref)
        for part, d_act in enumerate((d_query, d_key, d_value)):
            pre, gate, _ = fronts[part]
            taps = taps_ref[part, :, lanes]
            source = ext.at[sub * 3 + part]
            d_pre = d_act * gate * (1.0 + pre * (1.0 - gate))
            room = back.at[sub * 3 + part]
            total = None
            d_taps = []
            for lag in range(CONV):
                masked = d_pre if lag == 0 else jnp.where(since >= lag, d_pre, 0.0)
                moved = source[PAD - lag : PAD - lag + rows, :]
                d_taps.append(jnp.sum(masked * moved, axis=0, keepdims=True))
                room[lag, 0:PAD, :] = jnp.zeros((PAD, BLOCK), F32)
                room[lag, PAD : PAD + rows, :] = masked * taps[lag : lag + 1, :]
                room[lag, PAD + rows : PAD + rows + PAD, :] = jnp.zeros((PAD, BLOCK), F32)
                term = room[lag, lag : lag + PAD + rows, :]
                total = term if total is None else total + term
            d_taps_ref[part, :, lanes] = jnp.concatenate(d_taps, axis=0)
            d_halo_ref[part, :, lanes] = total[:PAD].astype(d_halo_ref.dtype)
            outs[part][:, lanes] = total[PAD:].astype(BF16)

    @pl.when(pl.program_id(0) == 0)
    def _():
        d_beta_ref[...] = d_beta_all

    @pl.when(pl.program_id(0) > 0)
    def _():
        d_beta_ref[...] += d_beta_all


def mixer_backward(
    since, beta_logit, query, key, value, halo, taps, new_add, new_map, inverse, starts, entry, exit_grad, d_core
):
    rows, width = query.shape
    heads = width // BLOCK
    blocks = rows // BLOCK
    wide = jax.ShapeDtypeStruct((rows, width), BF16)
    return pl.pallas_call(
        backward_kernel,
        grid=(heads // HEADS_STEP,),
        in_specs=[
            whole_spec(since.shape), whole_spec(beta_logit.shape),
            head_spec(rows), head_spec(rows), head_spec(rows),
            lanes_spec(3, PAD), lanes_spec(3, CONV),
            head_spec(rows), head_spec(rows),
            per_head(blocks, BLOCK, BLOCK), per_head(blocks, BLOCK, 2 * BLOCK),
            per_head(BLOCK, BLOCK), per_head(BLOCK, BLOCK), head_spec(rows),
        ],
        out_specs=[
            head_spec(rows), head_spec(rows), head_spec(rows),
            lanes_spec(3, PAD), lanes_spec(3, CONV), whole_spec(beta_logit.shape),
        ],
        out_shape=[
            wide, wide, wide,
            jax.ShapeDtypeStruct((3, PAD, width), F32),
            jax.ShapeDtypeStruct((3, CONV, width), F32),
            jax.ShapeDtypeStruct(beta_logit.shape, F32),
        ],
        scratch_shapes=[
            pltpu.VMEM((3 * HEADS_STEP, PAD + rows, BLOCK), F32),
            pltpu.VMEM((3 * HEADS_STEP, CONV, PAD + rows + PAD, BLOCK), F32),
        ],
        compiler_params=params(),
        name="mixer_backward",
    )(
        since, beta_logit, query, key, value, halo, taps, new_add, new_map, inverse, starts, entry, exit_grad, d_core
    )


GROUPS = 4
HALVES = 2


def chain_kernel(axis, forward, map_ref, add_ref, out_ref, sent, landed, send_sem, recv_sem):
    count = lax.axis_size(axis)
    me = lax.axis_index(axis)
    heads = add_ref.shape[0]
    step = heads // GROUPS
    up, down = (me + 1, me - 1) if forward else (me - 1, me + 1)
    first, last = (0, count - 1) if forward else (count - 1, 0)
    barrier = pltpu.get_barrier_semaphore()

    @pl.when(me != first)
    def _():
        pl.semaphore_signal(barrier, inc=1, device_id={axis: down}, device_id_type=MESH)

    @pl.when(me != last)
    def _():
        pl.semaphore_wait(barrier, 1)

    def copy(group, target):
        return pltpu.make_async_remote_copy(
            src_ref=sent.at[group],
            dst_ref=landed.at[group],
            send_sem=send_sem.at[group],
            recv_sem=recv_sem.at[group],
            device_id={axis: target},
            device_id_type=MESH,
        )

    for group in range(GROUPS):
        @pl.when(me != first)
        def _():
            copy(group, up).wait_recv()
            for sub in range(step):
                head = group * step + sub
                out_ref[head] = landed[group, sub].astype(F32)

        @pl.when(me == first)
        def _():
            out_ref[group * step : (group + 1) * step] = jnp.zeros((step,) + out_ref.shape[1:], F32)

        @pl.when(me != last)
        def _():
            for sub in range(step):
                head = group * step + sub
                if forward:
                    moved = mm(map_ref[head], out_ref[head])
                else:
                    moved = mm_tn(map_ref[head], out_ref[head])
                sent[group, sub] = (moved + add_ref[head]).astype(BF16)
            copy(group, up).start()

    @pl.when(me != last)
    def _():
        for group in range(GROUPS):
            copy(group, up).wait_send()


def carry_chain(map_part, add_part, axis, forward):
    heads = add_part.shape[0]
    part = (GROUPS, heads // GROUPS, BLOCK, BLOCK)
    return pl.pallas_call(
        functools.partial(chain_kernel, axis, forward),
        in_specs=[pl.BlockSpec(memory_space=pltpu.VMEM)] * 2,
        out_specs=pl.BlockSpec(memory_space=pltpu.VMEM),
        out_shape=jax.ShapeDtypeStruct(add_part.shape, F32),
        scratch_shapes=[
            pltpu.VMEM(part, BF16),
            pltpu.VMEM(part, BF16),
            pltpu.SemaphoreType.DMA((GROUPS,)),
            pltpu.SemaphoreType.DMA((GROUPS,)),
        ],
        compiler_params=pltpu.CompilerParams(
            collective_id=1 if forward else 2, has_side_effects=True, vmem_limit_bytes=VMEM_LIMIT // 2
        ),
        name="carry_forward" if forward else "carry_backward",
    )(map_part, add_part)


def shifted(value, axis, steps):
    count = lax.axis_size(axis)
    first, last = (max(0, -steps), min(count, count - steps))
    return lax.ppermute(value, axis, [(source, source + steps) for source in range(first, last)])


def matmul(left, right):
    return jnp.dot(left, right, preferred_element_type=F32)


def dot_tn(left, right):
    return jnp.einsum("rd,re->de", left, right, preferred_element_type=F32)


def dot_nt(left, right):
    return jnp.einsum("re,de->rd", left, right, preferred_element_type=F32)


def rms_scale(value_in, gain_vec, epsilon):
    return value_in * lax.rsqrt(jnp.mean(value_in * value_in, axis=-1, keepdims=True) + epsilon) * gain_vec


def norm_back(value_in, gain_vec, upstream, epsilon):
    inv_scale = lax.rsqrt(jnp.mean(value_in * value_in, axis=-1, keepdims=True) + epsilon)
    scaled_up = upstream * gain_vec
    gain_term = jnp.sum(upstream * value_in * inv_scale, axis=0)
    cubed = inv_scale * inv_scale * inv_scale
    back_value = inv_scale * scaled_up - value_in * cubed * jnp.mean(
        scaled_up * value_in, axis=-1, keepdims=True
    )
    return (back_value, gain_term)


def since_start(doc_lengths, offset, rows):
    ends = jnp.cumsum(doc_lengths[0])
    position = offset + jnp.arange(rows, dtype=jnp.int32)
    starts = jnp.max(jnp.where(position[:, None] >= ends[None, :], ends[None, :], 0), axis=1)
    return jnp.broadcast_to((position - starts)[:, None], (rows, BLOCK)).astype(jnp.int32)


def scatter_all(value, dim):
    part = lax.psum_scatter(value, "dp", scatter_dimension=dim, tiled=True)
    return lax.psum_scatter(part, "narrow", scatter_dimension=dim, tiled=True)


def local(
    tokens,
    doc_lengths,
    attn_gain,
    w_query,
    w_key,
    w_value,
    w_beta,
    conv_weight,
    out_gain,
    w_out,
    mlp_gain,
    w_gate,
    w_up,
    w_down,
    grad_out,
):
    tok_rows, model_width = tokens.shape
    offset = lax.axis_index("narrow") * tok_rows
    half = tok_rows // HALVES
    parts = [slice(at * half, (at + 1) * half) for at in range(HALVES)]

    def gather(rows):
        return lax.all_gather(rows, "narrow", axis=0, tiled=True)

    def scatter(rows):
        return lax.psum_scatter(rows, "narrow", scatter_dimension=0, tiled=True)

    cot = []
    for part in parts:
        cot.append(gather(grad_out[part]))
    since = since_start(doc_lengths, offset, tok_rows)
    inputs = tokens.astype(F32)
    normed = rms_scale(inputs, attn_gain, 1e-06).astype(BF16)
    query, key, value = (matmul(normed, w) for w in (w_query, w_key, w_value))
    beta_logit = matmul(normed, w_beta)
    halo = shifted(
        jnp.stack([part[tok_rows - PAD :].astype(BF16) for part in (query, key, value)]), "narrow", 1
    )
    out_add, out_map, new_add, new_map, inverse, starts, end = mixer_forward(
        since, beta_logit, query, key, value, halo, conv_weight
    )
    transfer = end[:, :, BLOCK:].astype(BF16)
    entry = carry_chain(transfer, end[:, :, :BLOCK], "narrow", True)
    gain_row = out_gain[None, :]
    attn_mixed = mixer_join(out_add, out_map, entry, gain_row)
    hidden = inputs + matmul(attn_mixed, w_out)
    normed_mlp = rms_scale(hidden, mlp_gain, 1e-06).astype(BF16)
    normed_mlp, *cot = lax.optimization_barrier((normed_mlp, *cot))
    gathered = [gather(normed_mlp[part]) for part in parts]
    activation, d_gate, d_up, d_normed_parts = [], [], [], []
    for at in range(HALVES):
        gate_proj = matmul(gathered[at], w_gate)
        up_proj = matmul(gathered[at], w_up)
        gate_sigmoid = jax.nn.sigmoid(gate_proj)
        silu_gate = gate_proj * gate_sigmoid
        activation.append((silu_gate * up_proj).astype(BF16))
        d_act = jnp.einsum("rd,fd->rf", cot[at], w_down, preferred_element_type=F32)
        d_gate.append(
            (d_act * up_proj * gate_sigmoid * (1.0 + gate_proj * (1.0 - gate_sigmoid))).astype(BF16)
        )
        d_up.append((d_act * silu_gate).astype(BF16))
        d_normed_parts.append(scatter((dot_nt(d_gate[at], w_gate) + dot_nt(d_up[at], w_up)).astype(BF16)))
    out_parts = [matmul(act, w_down).astype(BF16) for act in activation]
    down_term_grad = sum(dot_tn(a, c) for a, c in zip(activation, cot)).astype(BF16)
    gate_term_grad = sum(dot_tn(a, c) for a, c in zip(gathered, d_gate)).astype(BF16)
    up_term_grad = sum(dot_tn(a, c) for a, c in zip(gathered, d_up)).astype(BF16)
    (d_normed_parts, out_parts, down_term_grad, gate_term_grad, up_term_grad) = lax.optimization_barrier(
        (d_normed_parts, out_parts, down_term_grad, gate_term_grad, up_term_grad)
    )
    d_normed_mlp = jnp.concatenate(d_normed_parts, axis=0).astype(F32)
    ffn_parts = [scatter(part) for part in out_parts]
    grad_gate, grad_up, grad_down = (
        lax.psum_scatter(gate_term_grad, "dp", scatter_dimension=0, tiled=True).astype(F32),
        lax.psum_scatter(up_term_grad, "dp", scatter_dimension=0, tiled=True).astype(F32),
        lax.psum_scatter(down_term_grad, "dp", scatter_dimension=1, tiled=True).astype(F32),
    )
    d_hidden_norm, mlp_gain_term = norm_back(hidden, mlp_gain, d_normed_mlp, 1e-06)
    d_hidden = grad_out.astype(F32) + d_hidden_norm
    d_branch = d_hidden.astype(BF16)
    w_out_term = dot_tn(d_branch, attn_mixed)
    d_mixed = dot_nt(d_branch, w_out)
    d_core, start_grad, out_gain_term = mixer_core_back(out_add, out_map, entry, gain_row, d_mixed)
    exit_grad = carry_chain(transfer, start_grad, "narrow", False)
    d_query, d_key, d_value, d_halo, conv_term, d_beta = mixer_backward(
        since, beta_logit, query, key, value, halo, conv_weight,
        new_add, new_map, inverse, starts, entry, exit_grad, d_core,
    )
    ffn_parts, d_halo = lax.optimization_barrier((ffn_parts, d_halo))
    block_out = (hidden + jnp.concatenate(ffn_parts, axis=0).astype(F32)).astype(BF16)
    after = shifted(d_halo.astype(BF16), "narrow", -1)
    d_query, d_key, d_value = (
        part.at[tok_rows - PAD :].add(after[place])
        for place, part in enumerate((d_query, d_key, d_value))
    )
    d_beta_low = d_beta.astype(BF16)
    query_term = dot_tn(normed, d_query)
    key_term = dot_tn(normed, d_key)
    value_term = dot_tn(normed, d_value)
    beta_term = jnp.einsum("rd,rh->dh", normed, d_beta_low, preferred_element_type=F32)
    d_normed = dot_nt(d_query, w_query) + dot_nt(d_key, w_key) + dot_nt(d_value, w_value)
    d_normed = d_normed + jnp.einsum("rh,dh->rd", d_beta_low, w_beta, preferred_element_type=F32)
    d_input_norm, attn_gain_term = norm_back(inputs, attn_gain, d_normed, 1e-06)
    grad_tokens = (d_hidden + d_input_norm).astype(BF16)
    devices = lax.axis_size("dp") * lax.axis_size("narrow")
    heads = w_beta.shape[1]
    taps = 3 * CONV
    gain_share = BLOCK // devices
    gain_column = jnp.pad(
        out_gain_term.reshape(devices, gain_share), ((0, 0), (0, model_width // devices - gain_share))
    ).reshape(model_width, 1)
    small = jnp.concatenate(
        [
            beta_term,
            conv_term.reshape(taps, model_width).T,
            attn_gain_term[:, None],
            mlp_gain_term[:, None],
            gain_column,
        ],
        axis=1,
    )
    small = jnp.pad(small, ((0, 0), (0, BLOCK - small.shape[1])))
    small = lax.psum_scatter(small, ("dp", "narrow"), scatter_dimension=0, tiled=True)
    grad_beta = small[:, :heads]
    grad_conv = small[:, heads : heads + taps].T.reshape(3, CONV, -1)
    grad_attn_gain = small[:, heads + taps]
    grad_mlp_gain = small[:, heads + taps + 1]
    grad_out_gain = small[:gain_share, heads + taps + 2]
    grad_query, grad_key, grad_value, grad_w_out = (
        scatter_all(term.astype(BF16), 0).astype(F32)
        for term in (query_term, key_term, value_term, w_out_term)
    )
    grad_w_out = grad_w_out.T
    return (
        block_out,
        grad_tokens,
        grad_attn_gain,
        grad_query,
        grad_key,
        grad_value,
        grad_beta,
        grad_conv,
        grad_out_gain,
        grad_w_out,
        grad_mlp_gain,
        grad_gate,
        grad_up,
        grad_down,
    )


def solution(mesh):
    placed = (
        P(("dp", "narrow"), None),
        P("dp", None),
        P(),
        P(),
        P(),
        P(),
        P(),
        P(),
        P(),
        P(),
        P(),
        P(None, "narrow"),
        P(None, "narrow"),
        P("narrow", None),
        P(("dp", "narrow"), None),
    )
    return jax.shard_map(
        local,
        mesh=mesh,
        in_specs=placed,
        out_specs=(
            P(("dp", "narrow"), None),
            P(("dp", "narrow"), None),
            P(("dp", "narrow")),
            P(("dp", "narrow"), None),
            P(("dp", "narrow"), None),
            P(("dp", "narrow"), None),
            P(("dp", "narrow"), None),
            P(None, None, ("dp", "narrow")),
            P(("dp", "narrow")),
            P(None, ("dp", "narrow")),
            P(("dp", "narrow")),
            P("dp", "narrow"),
            P("dp", "narrow"),
            P("narrow", "dp"),
        ),
        check_vma=False,
    )
```

```python
import functools

import jax
import jax.numpy as jnp
from jax import lax
from jax.experimental import pallas as pl
from jax.experimental.pallas import tpu as pltpu
from jax.sharding import PartitionSpec as P

CONV = 4
BLOCK = 128
HEADS_STEP = 2
PAD = 8
MESH = pl.DeviceIdType.MESH
F32 = jnp.float32
BF16 = jnp.bfloat16
VMEM_LIMIT = 56 * 1024 * 1024


def mm(left, right, contract=(1, 0)):
    return lax.dot_general(
        left.astype(BF16),
        right.astype(BF16),
        (((contract[0],), (contract[1],)), ((), ())),
        preferred_element_type=F32,
    )


def mm_nt(left, right):
    return mm(left, right, (1, 1))


def mm_tn(left, right):
    return mm(left, right, (0, 0))


def iotas(size):
    row = lax.broadcasted_iota(jnp.int32, (size, size), 0)
    col = lax.broadcasted_iota(jnp.int32, (size, size), 1)
    return row, col


def block_masks(since):
    size = since.shape[0]
    row, col = iotas(size)
    back = row - col
    causal = (back >= 0) & (back <= since)
    strict = (back > 0) & (back <= since)
    keep = (since > row).astype(F32)
    last = since[size - 1 : size, :]
    last_mask = (row >= size - 1 - last).astype(F32)
    keep_last = (last > size - 1).astype(F32)
    return causal, strict, keep, last_mask, keep_last


def unit_lower_inverses(lowers):
    size = lowers[0].shape[0]
    row, col = iotas(size)
    width = 1
    inverses = None
    while width < size:
        join = (row // (2 * width) == col // (2 * width)) & (row // width != col // width)
        pieces = [jnp.where(join, low, 0.0) for low in lowers]
        if inverses is None:
            eye = (row == col).astype(F32)
            inverses = [eye - piece for piece in pieces]
        else:
            halves = [mm(piece, inv) for piece, inv in zip(pieces, inverses)]
            inverses = [inv - mm(inv, half) for inv, half in zip(inverses, halves)]
        width *= 2
    return inverses


def conv_front(ext, proj, halo, taps, since):
    rows = proj.shape[0]
    ext[0:PAD, :] = halo.astype(F32)
    ext[PAD : PAD + rows, :] = proj
    pre = proj * taps[0:1, :]
    for lag in range(1, CONV):
        moved = ext[PAD - lag : PAD - lag + rows, :]
        pre = pre + jnp.where(since >= lag, moved, 0.0) * taps[lag : lag + 1, :]
    gate = 1.0 / (1.0 + jnp.exp(-pre))
    return pre, gate, pre * gate


def unit_rows(value):
    inv = lax.rsqrt(jnp.sum(value * value, axis=-1, keepdims=True) + 1e-06)
    return value * inv, inv


def head_column(array, head):
    lane = lax.broadcasted_iota(jnp.int32, array.shape, 1)
    return jnp.sum(jnp.where(lane == head, array, 0.0), axis=1, keepdims=True)


def forward_kernel(
    since_ref, beta_ref, query_ref, key_ref, value_ref, halo_ref, taps_ref,
    out_add_ref, out_map_ref, new_add_ref, new_map_ref, inverse_ref, starts_ref, end_ref,
    ext,
):
    rows = since_ref.shape[0]
    blocks = rows // BLOCK
    since = since_ref[...]
    jobs = []
    for sub in range(HEADS_STEP):
        head = pl.program_id(0) * HEADS_STEP + sub
        lanes = slice(sub * BLOCK, (sub + 1) * BLOCK)
        mixed = []
        for part, ref in enumerate((query_ref, key_ref, value_ref)):
            _, _, act = conv_front(
                ext.at[sub * 3 + part], ref[:, lanes].astype(F32), halo_ref[part, :, lanes],
                taps_ref[part, :, lanes], since,
            )
            mixed.append(act)
        query = unit_rows(mixed[0])[0] * (BLOCK ** -0.5)
        key = unit_rows(mixed[1])[0]
        beta = 1.0 / (1.0 + jnp.exp(-head_column(beta_ref[...], head)))
        jobs.append((lanes, query, key, mixed[2], beta))
    lowers, scores = [], []
    for lanes, query, key, value, beta in jobs:
        for blk in range(blocks):
            span = slice(blk * BLOCK, (blk + 1) * BLOCK)
            causal, strict, _, _, _ = block_masks(since[span])
            both = mm_nt(jnp.concatenate([key[span], query[span]], axis=0), key[span])
            lowers.append(jnp.where(strict, both[:BLOCK] * beta[span], 0.0))
            scores.append(jnp.where(causal, both[BLOCK:], 0.0).astype(BF16))
    inverses = [inv.astype(BF16) for inv in unit_lower_inverses(lowers)]
    row, col = iotas(BLOCK)
    eye = (row == col).astype(F32)
    states = [jnp.concatenate([jnp.zeros((BLOCK, BLOCK), F32), eye], axis=1) for _ in jobs]
    for blk in range(blocks):
        span = slice(blk * BLOCK, (blk + 1) * BLOCK)
        _, _, keep, last_mask, keep_last = block_masks(since[span])
        for sub, (lanes, query, key, value, beta) in enumerate(jobs):
            at = sub * blocks + blk
            inverse_ref[sub, blk] = inverses[at]
            state = states[sub].astype(BF16)
            starts_ref[sub, blk] = state
            stacked = jnp.concatenate([key[span] * keep, query[span] * keep], axis=0)
            seen = mm(stacked, state)
            rest = jnp.concatenate([value[span], jnp.zeros((BLOCK, BLOCK), F32)], axis=1)
            right = (rest - seen[:BLOCK]) * beta[span]
            new = mm(inverses[at], right).astype(BF16)
            out = seen[BLOCK:] + mm(scores[at], new)
            out_add_ref[span, lanes] = out[:, :BLOCK].astype(BF16)
            out_map_ref[span, lanes] = out[:, BLOCK:].astype(BF16)
            new_add_ref[span, lanes] = new[:, :BLOCK]
            new_map_ref[span, lanes] = new[:, BLOCK:]
            keep_both = jnp.concatenate([keep_last, keep_last], axis=1)
            states[sub] = states[sub] * keep_both + mm_tn(key[span] * last_mask, new)
    for sub in range(len(jobs)):
        end_ref[sub] = states[sub]


def whole_spec(shape):
    return pl.BlockSpec(shape, lambda h: (0,) * len(shape))


def head_spec(rows):
    return pl.BlockSpec((rows, HEADS_STEP * BLOCK), lambda h: (0, h))


def per_head(*tail):
    return pl.BlockSpec((HEADS_STEP,) + tail, lambda h: (h,) + (0,) * len(tail))


def lanes_spec(first, second):
    return pl.BlockSpec((first, second, HEADS_STEP * BLOCK), lambda h: (0, 0, h))


def params():
    return pltpu.CompilerParams(vmem_limit_bytes=VMEM_LIMIT)


def mixer_forward(since, beta_logit, query, key, value, halo, taps):
    rows, width = query.shape
    heads = width // BLOCK
    blocks = rows // BLOCK
    wide = jax.ShapeDtypeStruct((rows, width), BF16)
    return pl.pallas_call(
        forward_kernel,
        grid=(heads // HEADS_STEP,),
        in_specs=[
            whole_spec(since.shape), whole_spec(beta_logit.shape),
            head_spec(rows), head_spec(rows), head_spec(rows),
            lanes_spec(3, PAD), lanes_spec(3, CONV),
        ],
        out_specs=[
            head_spec(rows), head_spec(rows), head_spec(rows), head_spec(rows),
            per_head(blocks, BLOCK, BLOCK), per_head(blocks, BLOCK, 2 * BLOCK),
            per_head(BLOCK, 2 * BLOCK),
        ],
        out_shape=[
            wide, wide, wide, wide,
            jax.ShapeDtypeStruct((heads, blocks, BLOCK, BLOCK), BF16),
            jax.ShapeDtypeStruct((heads, blocks, BLOCK, 2 * BLOCK), BF16),
            jax.ShapeDtypeStruct((heads, BLOCK, 2 * BLOCK), F32),
        ],
        scratch_shapes=[pltpu.VMEM((3 * HEADS_STEP, PAD + rows, BLOCK), F32)],
        compiler_params=params(),
        name="mixer_forward",
    )(since, beta_logit, query, key, value, halo, taps)


def join_kernel(out_add_ref, out_map_ref, entry_ref, gain_ref, mixed_ref):
    for sub in range(HEADS_STEP):
        lanes = slice(sub * BLOCK, (sub + 1) * BLOCK)
        core = out_add_ref[:, lanes].astype(F32) + mm(out_map_ref[:, lanes], entry_ref[sub])
        scale = lax.rsqrt(jnp.mean(core * core, axis=-1, keepdims=True) + 1e-05)
        mixed_ref[:, lanes] = (core * scale * gain_ref[...]).astype(BF16)


def mixer_join(out_add, out_map, entry, gain):
    rows, width = out_add.shape
    heads = width // BLOCK
    return pl.pallas_call(
        join_kernel,
        grid=(heads // HEADS_STEP,),
        in_specs=[head_spec(rows), head_spec(rows), per_head(BLOCK, BLOCK), whole_spec((1, BLOCK))],
        out_specs=head_spec(rows),
        out_shape=jax.ShapeDtypeStruct((rows, width), BF16),
        compiler_params=params(),
        name="mixer_join",
    )(out_add, out_map, entry, gain)


def core_back_kernel(out_add_ref, out_map_ref, entry_ref, gain_ref, up_ref, d_core_ref, start_ref, gain_out_ref):
    @pl.when(pl.program_id(0) == 0)
    def _():
        gain_out_ref[...] = jnp.zeros_like(gain_out_ref)

    for sub in range(HEADS_STEP):
        lanes = slice(sub * BLOCK, (sub + 1) * BLOCK)
        out_map = out_map_ref[:, lanes]
        core = out_add_ref[:, lanes].astype(F32) + mm(out_map, entry_ref[sub])
        scale = lax.rsqrt(jnp.mean(core * core, axis=-1, keepdims=True) + 1e-05)
        unit = core * scale
        up = up_ref[:, lanes].astype(F32)
        gain_out_ref[...] += jnp.sum(up * unit, axis=0, keepdims=True)
        scaled = up * gain_ref[...]
        d_core = scale * (scaled - unit * jnp.mean(scaled * unit, axis=-1, keepdims=True))
        d_core = d_core.astype(BF16)
        d_core_ref[:, lanes] = d_core
        start_ref[sub] = mm_tn(out_map, d_core)


def mixer_core_back(out_add, out_map, entry, gain, up):
    rows, width = out_add.shape
    heads = width // BLOCK
    return pl.pallas_call(
        core_back_kernel,
        grid=(heads // HEADS_STEP,),
        in_specs=[
            head_spec(rows), head_spec(rows), per_head(BLOCK, BLOCK), whole_spec((1, BLOCK)), head_spec(rows),
        ],
        out_specs=[head_spec(rows), per_head(BLOCK, BLOCK), whole_spec((1, BLOCK))],
        out_shape=[
            jax.ShapeDtypeStruct((rows, width), BF16),
            jax.ShapeDtypeStruct((heads, BLOCK, BLOCK), F32),
            jax.ShapeDtypeStruct((1, BLOCK), F32),
        ],
        compiler_params=params(),
        name="mixer_core_back",
    )(out_add, out_map, entry, gain, up)


def backward_kernel(
    since_ref, beta_ref, query_ref, key_ref, value_ref, halo_ref, taps_ref,
    new_add_ref, new_map_ref, inverse_ref, starts_ref, entry_ref, exit_ref, d_core_ref,
    d_proj_ref, d_halo_ref, d_taps_ref, d_beta_ref,
    ext, back,
):
    rows = since_ref.shape[0]
    blocks = rows // BLOCK
    since = since_ref[...]
    jobs = []
    for sub in range(HEADS_STEP):
        head = pl.program_id(0) * HEADS_STEP + sub
        lanes = slice(sub * BLOCK, (sub + 1) * BLOCK)
        fronts = []
        for part, ref in enumerate((query_ref, key_ref, value_ref)):
            fronts.append(
                conv_front(
                    ext.at[sub * 3 + part], ref[:, lanes].astype(F32), halo_ref[part, :, lanes],
                    taps_ref[part, :, lanes], since,
                )
            )
        query_unit, query_inv = unit_rows(fronts[0][2])
        key, key_inv = unit_rows(fronts[1][2])
        query = query_unit * (BLOCK ** -0.5)
        beta = 1.0 / (1.0 + jnp.exp(-head_column(beta_ref[...], head)))
        jobs.append((head, lanes, fronts, query, query_unit, query_inv, key, key_inv, beta))

    saved = {}
    for sub, (head, lanes, fronts, query, query_unit, query_inv, key, key_inv, beta) in enumerate(jobs):
        entry = entry_ref[sub].astype(BF16)
        for blk in range(blocks):
            span = slice(blk * BLOCK, (blk + 1) * BLOCK)
            causal, _, keep, last_mask, _ = block_masks(since[span])
            start = starts_ref[sub, blk]
            state = (start[:, :BLOCK].astype(F32) + mm(start[:, BLOCK:], entry)).astype(BF16)
            new = (new_add_ref[span, lanes].astype(F32) + mm(new_map_ref[span, lanes], entry)).astype(BF16)
            scores = jnp.where(causal, mm_nt(query[span], key[span]), 0.0).astype(BF16)
            d_out = d_core_ref[span, lanes]
            d_new = mm_tn(scores, d_out)
            d_state = mm_tn(query[span] * keep, d_out)
            saved[sub, blk] = (state, new, d_out, d_new, d_state)

    carried = [exit_ref[sub].astype(F32) for sub in range(HEADS_STEP)]
    chain = {}
    for blk in reversed(range(blocks)):
        span = slice(blk * BLOCK, (blk + 1) * BLOCK)
        _, _, keep, last_mask, keep_last = block_masks(since[span])
        for sub, (head, lanes, fronts, query, query_unit, query_inv, key, key_inv, beta) in enumerate(jobs):
            state, new, d_out, d_new, d_state = saved[sub, blk]
            after = carried[sub].astype(BF16)
            d_new = d_new + mm(key[span] * last_mask, after)
            d_right = mm_tn(inverse_ref[sub, blk], d_new)
            d_rest = d_right * beta[span]
            carried[sub] = carried[sub] * keep_last + d_state - mm_tn(key[span] * keep, d_rest)
            chain[sub, blk] = (after, d_right, d_rest)

    lane = lax.broadcasted_iota(jnp.int32, (rows, beta_ref.shape[1]), 1)
    d_beta_all = jnp.zeros((rows, beta_ref.shape[1]), F32)
    for sub, (head, lanes, fronts, query, query_unit, query_inv, key, key_inv, beta) in enumerate(jobs):
        d_queries, d_keys, d_values, d_betas = [], [], [], []
        for blk in range(blocks):
            span = slice(blk * BLOCK, (blk + 1) * BLOCK)
            causal, strict, keep, last_mask, _ = block_masks(since[span])
            state, new, d_out, _, _ = saved[sub, blk]
            after, d_right, d_rest = chain[sub, blk]
            both = mm_nt(jnp.concatenate([d_out, d_right.astype(BF16)], axis=0), new)
            d_scores = jnp.where(causal, both[:BLOCK], 0.0).astype(BF16)
            d_gram = (jnp.where(strict, both[BLOCK:], 0.0) * (-beta[span])).astype(BF16)
            key_b = key[span].astype(BF16)
            from_state = mm_nt(jnp.concatenate([d_out, d_rest.astype(BF16)], axis=0), state)
            left = mm(jnp.concatenate([d_scores, d_gram], axis=0), key_b)
            d_queries.append(from_state[:BLOCK] * keep + left[:BLOCK])
            d_key = left[BLOCK:] + mm_tn(
                jnp.concatenate([d_scores, d_gram], axis=0),
                jnp.concatenate([query[span].astype(BF16), key_b], axis=0),
            )
            d_key = d_key + mm_nt(new, after) * last_mask - from_state[BLOCK:] * keep
            d_keys.append(d_key)
            d_values.append(d_rest)
            d_betas.append(
                jnp.sum(d_right * new.astype(F32), axis=1, keepdims=True) * (1.0 - beta[span])
            )
        d_query = jnp.concatenate(d_queries, axis=0) * (BLOCK ** -0.5)
        d_key = jnp.concatenate(d_keys, axis=0)
        d_query = query_inv * (
            d_query - query_unit * jnp.sum(d_query * query_unit, axis=-1, keepdims=True)
        )
        d_key = key_inv * (d_key - key * jnp.sum(d_key * key, axis=-1, keepdims=True))
        d_value = jnp.concatenate(d_values, axis=0)
        d_beta_all = d_beta_all + jnp.where(lane == head, jnp.concatenate(d_betas, axis=0), 0.0)
        for part, d_act in enumerate((d_query, d_key, d_value)):
            pre, gate, _ = fronts[part]
            taps = taps_ref[part, :, lanes]
            source = ext.at[sub * 3 + part]
            d_pre = d_act * gate * (1.0 + pre * (1.0 - gate))
            room = back.at[sub * 3 + part]
            total = None
            d_taps = []
            for lag in range(CONV):
                masked = d_pre if lag == 0 else jnp.where(since >= lag, d_pre, 0.0)
                moved = source[PAD - lag : PAD - lag + rows, :]
                d_taps.append(jnp.sum(masked * moved, axis=0, keepdims=True))
                room[lag, 0:PAD, :] = jnp.zeros((PAD, BLOCK), F32)
                room[lag, PAD : PAD + rows, :] = masked * taps[lag : lag + 1, :]
                room[lag, PAD + rows : PAD + rows + PAD, :] = jnp.zeros((PAD, BLOCK), F32)
                term = room[lag, lag : lag + PAD + rows, :]
                total = term if total is None else total + term
            d_taps_ref[part, :, lanes] = jnp.concatenate(d_taps, axis=0)
            d_halo_ref[part, :, lanes] = total[:PAD].astype(d_halo_ref.dtype)
            d_proj_ref[part, :, lanes] = total[PAD:].astype(BF16)

    @pl.when(pl.program_id(0) == 0)
    def _():
        d_beta_ref[...] = d_beta_all

    @pl.when(pl.program_id(0) > 0)
    def _():
        d_beta_ref[...] += d_beta_all


def mixer_backward(
    since, beta_logit, query, key, value, halo, taps, new_add, new_map, inverse, starts, entry, exit_grad, d_core
):
    rows, width = query.shape
    heads = width // BLOCK
    blocks = rows // BLOCK
    return pl.pallas_call(
        backward_kernel,
        grid=(heads // HEADS_STEP,),
        in_specs=[
            whole_spec(since.shape), whole_spec(beta_logit.shape),
            head_spec(rows), head_spec(rows), head_spec(rows),
            lanes_spec(3, PAD), lanes_spec(3, CONV),
            head_spec(rows), head_spec(rows),
            per_head(blocks, BLOCK, BLOCK), per_head(blocks, BLOCK, 2 * BLOCK),
            per_head(BLOCK, BLOCK), per_head(BLOCK, BLOCK), head_spec(rows),
        ],
        out_specs=[
            lanes_spec(3, rows), lanes_spec(3, PAD), lanes_spec(3, CONV), whole_spec(beta_logit.shape),
        ],
        out_shape=[
            jax.ShapeDtypeStruct((3, rows, width), BF16),
            jax.ShapeDtypeStruct((3, PAD, width), F32),
            jax.ShapeDtypeStruct((3, CONV, width), F32),
            jax.ShapeDtypeStruct(beta_logit.shape, F32),
        ],
        scratch_shapes=[
            pltpu.VMEM((3 * HEADS_STEP, PAD + rows, BLOCK), F32),
            pltpu.VMEM((3 * HEADS_STEP, CONV, PAD + rows + PAD, BLOCK), F32),
        ],
        compiler_params=params(),
        name="mixer_backward",
    )(
        since, beta_logit, query, key, value, halo, taps, new_add, new_map, inverse, starts, entry, exit_grad, d_core
    )


GROUPS = 4
HALVES = 2


def chain_kernel(axis, forward, map_ref, add_ref, out_ref, sent, landed, send_sem, recv_sem):
    count = lax.axis_size(axis)
    me = lax.axis_index(axis)
    heads = add_ref.shape[0]
    step = heads // GROUPS
    up, down = (me + 1, me - 1) if forward else (me - 1, me + 1)
    first, last = (0, count - 1) if forward else (count - 1, 0)
    barrier = pltpu.get_barrier_semaphore()

    @pl.when(me != first)
    def _():
        pl.semaphore_signal(barrier, inc=1, device_id={axis: down}, device_id_type=MESH)

    @pl.when(me != last)
    def _():
        pl.semaphore_wait(barrier, 1)

    def copy(group, target):
        return pltpu.make_async_remote_copy(
            src_ref=sent.at[group],
            dst_ref=landed.at[group],
            send_sem=send_sem.at[group],
            recv_sem=recv_sem.at[group],
            device_id={axis: target},
            device_id_type=MESH,
        )

    for group in range(GROUPS):
        @pl.when(me != first)
        def _():
            copy(group, up).wait_recv()
            for sub in range(step):
                head = group * step + sub
                out_ref[head] = landed[group, sub].astype(F32)

        @pl.when(me == first)
        def _():
            out_ref[group * step : (group + 1) * step] = jnp.zeros((step,) + out_ref.shape[1:], F32)

        @pl.when(me != last)
        def _():
            for sub in range(step):
                head = group * step + sub
                if forward:
                    moved = mm(map_ref[head], out_ref[head])
                else:
                    moved = mm_tn(map_ref[head], out_ref[head])
                sent[group, sub] = (moved + add_ref[head]).astype(BF16)
            copy(group, up).start()

    @pl.when(me != last)
    def _():
        for group in range(GROUPS):
            copy(group, up).wait_send()


def carry_chain(map_part, add_part, axis, forward):
    heads = add_part.shape[0]
    part = (GROUPS, heads // GROUPS, BLOCK, BLOCK)
    return pl.pallas_call(
        functools.partial(chain_kernel, axis, forward),
        in_specs=[pl.BlockSpec(memory_space=pltpu.VMEM)] * 2,
        out_specs=pl.BlockSpec(memory_space=pltpu.VMEM),
        out_shape=jax.ShapeDtypeStruct(add_part.shape, F32),
        scratch_shapes=[
            pltpu.VMEM(part, BF16),
            pltpu.VMEM(part, BF16),
            pltpu.SemaphoreType.DMA((GROUPS,)),
            pltpu.SemaphoreType.DMA((GROUPS,)),
        ],
        compiler_params=pltpu.CompilerParams(
            collective_id=1 if forward else 2, has_side_effects=True, vmem_limit_bytes=VMEM_LIMIT // 2
        ),
        name="carry_forward" if forward else "carry_backward",
    )(map_part, add_part)


WINDOW = 4
LAG = 2
SPLIT = 4


def reduce_kernel(
    left_ref, right_ref, small_ref, out_ref, small_out_ref,
    left_own, left_away, left_sib, right_sib, small_sib, total, total_small, got2, got2_small, got3, got3_small, gotz, gotz_small,
    left_send, left_recv, right_send, right_recv, small_send, small_recv,
    send2, recv2, send3, recv3, sendz, recvz,
):
    dp = lax.axis_index("dp")
    z = lax.axis_index("narrow")
    core, x, y = dp % 2, (dp // 2) % 2, dp // 4
    depth = lax.axis_size("narrow")
    parts = right_ref.shape[0]
    units = SPLIT * parts
    rows = left_ref.shape[1] // 8
    cols = right_ref.shape[2] // SPLIT
    sib = dp + 1 - 2 * core
    flip_x = dp + 2 * (1 - 2 * x)
    flip_y = dp + 4 * (1 - 2 * y)

    def peer_z(step):
        return (z + step) % depth

    barrier = pltpu.get_barrier_semaphore()
    for target in (sib, flip_x, flip_y):
        pl.semaphore_signal(barrier, inc=1, device_id={"dp": target}, device_id_type=MESH)
    for step in range(1, depth):
        pl.semaphore_signal(barrier, inc=1, device_id={"narrow": peer_z(step)}, device_id_type=MESH)
    pl.semaphore_wait(barrier, 2 + depth)

    def send(src, dst, send_sem, recv_sem, target):
        return pltpu.make_async_remote_copy(
            src_ref=src, dst_ref=dst, send_sem=send_sem, recv_sem=recv_sem,
            device_id=target, device_id_type=MESH,
        )

    def stripe_rows(stripe, which):
        return pl.ds(pl.multiple_of((stripe * 2 + which) * rows, rows), rows)

    def left_copy(stripe):
        return send(
            left_away.at[stripe], left_sib.at[stripe],
            left_send.at[stripe], left_recv.at[stripe], {"dp": sib},
        )

    def small_copy(stripe):
        return send(
            small_ref.at[stripe_rows(stripe, 1 - core)], small_sib.at[stripe],
            small_send.at[stripe], small_recv.at[stripe], {"dp": sib},
        )

    def right_copy(part):
        return send(right_ref.at[part], right_sib.at[part], right_send.at[part], right_recv.at[part], {"dp": sib})

    right_copy(0).start()
    for stripe in range(4):
        small_copy(stripe).start()
    for stripe in range(4):
        turned = left_ref[:, stripe_rows(stripe, 1 - core)].astype(F32).T
        left_away[stripe] = turned.astype(BF16)
        left_copy(stripe).start()
    for part in range(1, parts):
        right_copy(part).start()
    for stripe in range(4):
        left_own[stripe] = left_ref[:, stripe_rows(stripe, core)].astype(F32).T.astype(BF16)

    def order(unit):
        e = unit % 2

        def pick(even, odd):
            return (1 - e) * even + e * odd

        def away(j):
            return pick(2 * j + 1 - x, 2 * (1 - y) + j)

        def kept(j):
            return pick(2 * j + x, 2 * y + j)

        far = pick(1 - y, 1 - x)
        near = pick(y, x)
        return away, kept, pick(flip_x, flip_y), pick(flip_y, flip_x), far, near

    def copy2(unit, j):
        away, _, target, _, _, _ = order(unit)
        return send(total.at[unit, away(j)], got2.at[unit, j], send2.at[unit, j], recv2.at[unit, j], {"dp": target})

    def copy2_small(j):
        away, _, target, _, _, _ = order(0)
        return send(
            total_small.at[away(j)], got2_small.at[j], send2.at[units, j], recv2.at[units, j], {"dp": target}
        )

    def copy3(unit):
        _, kept, _, target, far, _ = order(unit)
        return send(total.at[unit, kept(far)], got3.at[unit], send3.at[unit], recv3.at[unit], {"dp": target})

    def copy3_small():
        _, kept, _, target, far, _ = order(0)
        return send(total_small.at[kept(far)], got3_small, send3.at[units], recv3.at[units], {"dp": target})

    share = rows // depth

    def share_rows(at):
        return pl.ds(pl.multiple_of(at * share, share), share)

    def copyz(unit, step):
        _, kept, _, _, _, near = order(unit)
        to = peer_z(step)
        return send(
            total.at[unit, kept(near), share_rows(to)], gotz.at[unit, step - 1],
            sendz.at[unit, step - 1], recvz.at[unit, step - 1], {"narrow": to},
        )

    def copyz_small(step):
        _, kept, _, _, _, near = order(0)
        to = peer_z(step)
        return send(
            total_small.at[kept(near), share_rows(to)], gotz_small.at[step - 1],
            sendz.at[units, step - 1], recvz.at[units, step - 1], {"narrow": to},
        )

    def add_to(dst, src):
        step = 32

        def one(at, _):
            at = pl.ds(pl.multiple_of(at * step, step), step)
            dst[at, :] = (dst[at, :].astype(F32) + src[at, :].astype(F32)).astype(dst.dtype)
            return 0

        lax.fori_loop(0, rows // step, one, 0)

    for stripe in range(4):
        small_copy(stripe).wait()
        total_small[stripe] = small_ref[stripe_rows(stripe, core)] + small_sib[stripe]
    for j in range(2):
        copy2_small(j).start()
    for stripe in range(4):
        left_copy(stripe).wait()

    tile = 512

    def products(unit, _):
        away, kept, _, _, _, _ = order(unit)
        part = unit // SPLIT

        @pl.when(unit % SPLIT == 0)
        def _():
            right_copy(part).wait()

        def one(k, _):
            j = k % 2
            stripe = (k // 2) * kept(j) + (1 - k // 2) * away(j)
            mine = left_own[stripe]
            other = left_sib[stripe]
            for at in range(cols // tile):
                lanes = pl.ds(pl.multiple_of((unit % SPLIT) * cols + at * tile, tile), tile)
                value = jnp.dot(mine, right_ref[part, :, lanes], preferred_element_type=F32)
                value = value + jnp.dot(other, right_sib[part, :, lanes], preferred_element_type=F32)
                total[unit, stripe, :, at * tile : (at + 1) * tile] = value.astype(BF16)

            @pl.when((k < 2) & (unit < WINDOW))
            def _():
                copy2(unit, j).start()

            return 0

        lax.fori_loop(0, 4, one, 0)
        return 0

    lax.fori_loop(0, units, products, 0)

    def second(unit):
        _, kept, _, _, far, near = order(unit)
        for j in range(2):
            copy2(unit, j).wait()

        @pl.when(unit + WINDOW < units)
        def _():
            for j in range(2):
                copy2(unit + WINDOW, j).start()

        add_to(total.at[unit, kept(far)], got2.at[unit, far])
        copy3(unit).start()
        add_to(total.at[unit, kept(near)], got2.at[unit, near])

    def third(unit):
        _, kept, _, _, _, near = order(unit)
        copy3(unit).wait()
        add_to(total.at[unit, kept(near)], got3.at[unit])
        for step in range(1, depth):
            copyz(unit, step).start()

    def fourth(unit):
        _, kept, _, _, _, near = order(unit)
        for step in range(1, depth):
            copyz(unit, step).wait()
        value = total[unit, kept(near), share_rows(z), :].astype(F32)
        for step in range(1, depth):
            value = value + gotz[unit, step - 1].astype(F32)
        out_ref[unit // SPLIT, :, pl.ds(pl.multiple_of((unit % SPLIT) * cols, cols), cols)] = value

    _, kept, _, _, far, near = order(0)
    for j in range(2):
        copy2_small(j).wait()
    add_to(total_small.at[kept(far)], got2_small.at[far])
    copy3_small().start()
    add_to(total_small.at[kept(near)], got2_small.at[near])

    def stages(at, _):
        @pl.when(at < units)
        def _():
            second(at)

        @pl.when((at >= LAG) & (at < units + LAG))
        def _():
            third(at - LAG)

        @pl.when(at >= 2 * LAG)
        def _():
            fourth(at - 2 * LAG)

        return 0

    lax.fori_loop(0, units, stages, 0)
    copy3_small().wait()
    add_to(total_small.at[kept(near)], got3_small)
    for step in range(1, depth):
        copyz_small(step).start()
    lax.fori_loop(units, units + 2 * LAG, stages, 0)
    for step in range(1, depth):
        copyz_small(step).wait()
    value = total_small[kept(near), share_rows(z), :]
    for step in range(1, depth):
        value = value + gotz_small[step - 1]
    small_out_ref[...] = value


def reduce_products(left, right, small):
    tokens, height = left.shape
    parts, _, width = right.shape
    depth = lax.axis_size("narrow")
    units = SPLIT * parts
    rows, cols = height // 8, width // SPLIT
    share = rows // depth
    lanes = small.shape[1]
    dma = pltpu.SemaphoreType.DMA
    return pl.pallas_call(
        reduce_kernel,
        in_specs=[pl.BlockSpec(memory_space=pltpu.VMEM)] * 3,
        out_specs=[pl.BlockSpec(memory_space=pltpu.VMEM)] * 2,
        out_shape=[
            jax.ShapeDtypeStruct((parts, share, width), F32),
            jax.ShapeDtypeStruct((share, lanes), F32),
        ],
        scratch_shapes=[
            pltpu.VMEM((4, rows, tokens), BF16),
            pltpu.VMEM((4, rows, tokens), BF16),
            pltpu.VMEM((4, rows, tokens), BF16),
            pltpu.VMEM(right.shape, BF16),
            pltpu.VMEM((4, rows, lanes), F32),
            pltpu.VMEM((units, 4, rows, cols), BF16),
            pltpu.VMEM((4, rows, lanes), F32),
            pltpu.VMEM((units, 2, rows, cols), BF16),
            pltpu.VMEM((2, rows, lanes), F32),
            pltpu.VMEM((units, rows, cols), BF16),
            pltpu.VMEM((rows, lanes), F32),
            pltpu.VMEM((units, depth - 1, share, cols), BF16),
            pltpu.VMEM((depth - 1, share, lanes), F32),
            dma((4,)), dma((4,)), dma((parts,)), dma((parts,)), dma((4,)), dma((4,)),
            dma((units + 1, 2)), dma((units + 1, 2)), dma((units + 1,)), dma((units + 1,)),
            dma((units + 1, depth - 1)), dma((units + 1, depth - 1)),
        ],
        compiler_params=pltpu.CompilerParams(
            collective_id=3, has_side_effects=True, vmem_limit_bytes=VMEM_LIMIT
        ),
        name="reduce_products",
    )(left, right, small)


def shifted(value, axis, steps):
    count = lax.axis_size(axis)
    first, last = (max(0, -steps), min(count, count - steps))
    return lax.ppermute(value, axis, [(source, source + steps) for source in range(first, last)])


def matmul(left, right):
    return jnp.dot(left, right, preferred_element_type=F32)


def dot_tn(left, right):
    return jnp.einsum("rd,re->de", left, right, preferred_element_type=F32)


def dot_nt(left, right):
    return jnp.einsum("re,de->rd", left, right, preferred_element_type=F32)


def rms_scale(value_in, gain_vec, epsilon):
    return value_in * lax.rsqrt(jnp.mean(value_in * value_in, axis=-1, keepdims=True) + epsilon) * gain_vec


def norm_back(value_in, gain_vec, upstream, epsilon):
    inv_scale = lax.rsqrt(jnp.mean(value_in * value_in, axis=-1, keepdims=True) + epsilon)
    scaled_up = upstream * gain_vec
    gain_term = jnp.sum(upstream * value_in * inv_scale, axis=0)
    cubed = inv_scale * inv_scale * inv_scale
    back_value = inv_scale * scaled_up - value_in * cubed * jnp.mean(
        scaled_up * value_in, axis=-1, keepdims=True
    )
    return (back_value, gain_term)


def since_start(doc_lengths, offset, rows):
    ends = jnp.cumsum(doc_lengths[0])
    position = offset + jnp.arange(rows, dtype=jnp.int32)
    starts = jnp.max(jnp.where(position[:, None] >= ends[None, :], ends[None, :], 0), axis=1)
    return jnp.broadcast_to((position - starts)[:, None], (rows, BLOCK)).astype(jnp.int32)


def scatter_all(value, dim):
    part = lax.psum_scatter(value, "dp", scatter_dimension=dim, tiled=True)
    return lax.psum_scatter(part, "narrow", scatter_dimension=dim, tiled=True)


def local(
    tokens,
    doc_lengths,
    attn_gain,
    w_query,
    w_key,
    w_value,
    w_beta,
    conv_weight,
    out_gain,
    w_out,
    mlp_gain,
    w_gate,
    w_up,
    w_down,
    grad_out,
):
    tok_rows, model_width = tokens.shape
    offset = lax.axis_index("narrow") * tok_rows
    half = tok_rows // HALVES
    parts = [slice(at * half, (at + 1) * half) for at in range(HALVES)]

    def gather(rows):
        return lax.all_gather(rows, "narrow", axis=0, tiled=True)

    def scatter(rows):
        return lax.psum_scatter(rows, "narrow", scatter_dimension=0, tiled=True)

    cot = []
    for part in parts:
        cot.append(gather(grad_out[part]))
    since = since_start(doc_lengths, offset, tok_rows)
    inputs = tokens.astype(F32)
    normed = rms_scale(inputs, attn_gain, 1e-06).astype(BF16)
    query, key, value = (matmul(normed, w) for w in (w_query, w_key, w_value))
    beta_logit = matmul(normed, w_beta)
    halo = shifted(
        jnp.stack([part[tok_rows - PAD :].astype(BF16) for part in (query, key, value)]), "narrow", 1
    )
    out_add, out_map, new_add, new_map, inverse, starts, end = mixer_forward(
        since, beta_logit, query, key, value, halo, conv_weight
    )
    transfer = end[:, :, BLOCK:].astype(BF16)
    entry = carry_chain(transfer, end[:, :, :BLOCK], "narrow", True)
    gain_row = out_gain[None, :]
    attn_mixed = mixer_join(out_add, out_map, entry, gain_row)
    hidden = inputs + matmul(attn_mixed, w_out)
    normed_mlp = rms_scale(hidden, mlp_gain, 1e-06).astype(BF16)
    normed_mlp, *cot = lax.optimization_barrier((normed_mlp, *cot))
    gathered = [gather(normed_mlp[part]) for part in parts]
    activation, d_gate, d_up, d_normed_parts = [], [], [], []
    for at in range(HALVES):
        gate_proj = matmul(gathered[at], w_gate)
        up_proj = matmul(gathered[at], w_up)
        gate_sigmoid = jax.nn.sigmoid(gate_proj)
        silu_gate = gate_proj * gate_sigmoid
        activation.append((silu_gate * up_proj).astype(BF16))
        d_act = jnp.einsum("rd,fd->rf", cot[at], w_down, preferred_element_type=F32)
        d_gate.append(
            (d_act * up_proj * gate_sigmoid * (1.0 + gate_proj * (1.0 - gate_sigmoid))).astype(BF16)
        )
        d_up.append((d_act * silu_gate).astype(BF16))
        d_normed_parts.append(scatter((dot_nt(d_gate[at], w_gate) + dot_nt(d_up[at], w_up)).astype(BF16)))
    out_parts = [matmul(act, w_down).astype(BF16) for act in activation]
    down_term_grad = sum(dot_tn(a, c) for a, c in zip(activation, cot)).astype(BF16)
    gate_term_grad = sum(dot_tn(a, c) for a, c in zip(gathered, d_gate)).astype(BF16)
    up_term_grad = sum(dot_tn(a, c) for a, c in zip(gathered, d_up)).astype(BF16)
    (d_normed_parts, out_parts, down_term_grad, gate_term_grad, up_term_grad) = lax.optimization_barrier(
        (d_normed_parts, out_parts, down_term_grad, gate_term_grad, up_term_grad)
    )
    d_normed_mlp = jnp.concatenate(d_normed_parts, axis=0).astype(F32)
    grad_gate, grad_up, grad_down = (
        lax.psum_scatter(gate_term_grad, "dp", scatter_dimension=0, tiled=True).astype(F32),
        lax.psum_scatter(up_term_grad, "dp", scatter_dimension=0, tiled=True).astype(F32),
        lax.psum_scatter(down_term_grad, "dp", scatter_dimension=1, tiled=True).astype(F32),
    )
    d_hidden_norm, mlp_gain_term = norm_back(hidden, mlp_gain, d_normed_mlp, 1e-06)
    d_hidden = grad_out.astype(F32) + d_hidden_norm
    d_branch = d_hidden.astype(BF16)
    w_out_term = dot_tn(d_branch, attn_mixed).astype(BF16)
    d_mixed = dot_nt(d_branch, w_out)
    d_core, start_grad, out_gain_term = mixer_core_back(out_add, out_map, entry, gain_row, d_mixed)
    exit_grad = carry_chain(transfer, start_grad, "narrow", False)
    exit_grad, out_parts = lax.optimization_barrier((exit_grad, out_parts))
    w_out_term = scatter_all(w_out_term, 0)
    ffn_parts = [scatter(part) for part in out_parts]
    d_proj, d_halo, conv_term, d_beta = mixer_backward(
        since, beta_logit, query, key, value, halo, conv_weight,
        new_add, new_map, inverse, starts, entry, exit_grad, d_core,
    )
    after = shifted(d_halo.astype(BF16), "narrow", -1)
    d_proj = d_proj.at[:, tok_rows - PAD :].add(after)
    d_query, d_key, d_value = d_proj[0], d_proj[1], d_proj[2]
    d_beta_low = d_beta.astype(BF16)
    beta_term = jnp.einsum("rd,rh->dh", normed, d_beta_low, preferred_element_type=F32)
    d_normed = dot_nt(d_query, w_query) + dot_nt(d_key, w_key) + dot_nt(d_value, w_value)
    d_normed = d_normed + jnp.einsum("rh,dh->rd", d_beta_low, w_beta, preferred_element_type=F32)
    d_input_norm, attn_gain_term = norm_back(inputs, attn_gain, d_normed, 1e-06)
    grad_tokens = (d_hidden + d_input_norm).astype(BF16)
    devices = lax.axis_size("dp") * lax.axis_size("narrow")
    heads = w_beta.shape[1]
    taps = 3 * CONV
    gain_share = BLOCK // devices
    gain_column = jnp.pad(
        out_gain_term.reshape(devices, gain_share), ((0, 0), (0, model_width // devices - gain_share))
    ).reshape(model_width, 1)
    small = jnp.concatenate(
        [
            beta_term,
            conv_term.reshape(taps, model_width).T,
            attn_gain_term[:, None],
            mlp_gain_term[:, None],
            gain_column,
        ],
        axis=1,
    )
    small = jnp.pad(small, ((0, 0), (0, BLOCK - small.shape[1])))
    if lax.axis_size("dp") == 8:
        grads, small = reduce_products(normed, d_proj, small)
    else:
        grads = [scatter_all(dot_tn(normed, part).astype(BF16), 0).astype(F32) for part in (d_query, d_key, d_value)]
        small = lax.psum_scatter(small, ("dp", "narrow"), scatter_dimension=0, tiled=True)
    grad_beta = small[:, :heads]
    grad_conv = small[:, heads : heads + taps].T.reshape(3, CONV, -1)
    grad_attn_gain = small[:, heads + taps]
    grad_mlp_gain = small[:, heads + taps + 1]
    grad_out_gain = small[:gain_share, heads + taps + 2]
    ffn_parts, w_out_term, grads = lax.optimization_barrier((ffn_parts, w_out_term, grads))
    block_out = (hidden + jnp.concatenate(ffn_parts, axis=0).astype(F32)).astype(BF16)
    grad_query, grad_key, grad_value = grads[0], grads[1], grads[2]
    grad_w_out = w_out_term.astype(F32).T
    return (
        block_out,
        grad_tokens,
        grad_attn_gain,
        grad_query,
        grad_key,
        grad_value,
        grad_beta,
        grad_conv,
        grad_out_gain,
        grad_w_out,
        grad_mlp_gain,
        grad_gate,
        grad_up,
        grad_down,
    )


def solution(mesh):
    placed = (
        P(("dp", "narrow"), None),
        P("dp", None),
        P(),
        P(),
        P(),
        P(),
        P(),
        P(),
        P(),
        P(),
        P(),
        P(None, "narrow"),
        P(None, "narrow"),
        P("narrow", None),
        P(("dp", "narrow"), None),
    )
    return jax.shard_map(
        local,
        mesh=mesh,
        in_specs=placed,
        out_specs=(
            P(("dp", "narrow"), None),
            P(("dp", "narrow"), None),
            P(("dp", "narrow")),
            P(("dp", "narrow"), None),
            P(("dp", "narrow"), None),
            P(("dp", "narrow"), None),
            P(("dp", "narrow"), None),
            P(None, None, ("dp", "narrow")),
            P(("dp", "narrow")),
            P(None, ("dp", "narrow")),
            P(("dp", "narrow")),
            P("dp", "narrow"),
            P("dp", "narrow"),
            P("narrow", "dp"),
        ),
        check_vma=False,
    )
```

```python
import functools

import jax
import jax.numpy as jnp
from jax import lax
from jax.experimental import pallas as pl
from jax.experimental.pallas import tpu as pltpu
from jax.sharding import PartitionSpec as P

CONV = 4
BLOCK = 128
HEADS_STEP = 2
PAD = 8
MESH = pl.DeviceIdType.MESH
F32 = jnp.float32
BF16 = jnp.bfloat16
VMEM_LIMIT = 56 * 1024 * 1024


def mm(left, right, contract=(1, 0)):
    return lax.dot_general(
        left.astype(BF16),
        right.astype(BF16),
        (((contract[0],), (contract[1],)), ((), ())),
        preferred_element_type=F32,
    )


def mm_nt(left, right):
    return mm(left, right, (1, 1))


def mm_tn(left, right):
    return mm(left, right, (0, 0))


def iotas(size):
    row = lax.broadcasted_iota(jnp.int32, (size, size), 0)
    col = lax.broadcasted_iota(jnp.int32, (size, size), 1)
    return row, col


def block_masks(since):
    size = since.shape[0]
    row, col = iotas(size)
    back = row - col
    causal = (back >= 0) & (back <= since)
    strict = (back > 0) & (back <= since)
    keep = (since > row).astype(F32)
    last = since[size - 1 : size, :]
    last_mask = (row >= size - 1 - last).astype(F32)
    keep_last = (last > size - 1).astype(F32)
    return causal, strict, keep, last_mask, keep_last


def unit_lower_inverses(lowers):
    size = lowers[0].shape[0]
    row, col = iotas(size)
    width = 1
    inverses = None
    while width < size:
        join = (row // (2 * width) == col // (2 * width)) & (row // width != col // width)
        pieces = [jnp.where(join, low, 0.0) for low in lowers]
        if inverses is None:
            eye = (row == col).astype(F32)
            inverses = [eye - piece for piece in pieces]
        else:
            halves = [mm(piece, inv) for piece, inv in zip(pieces, inverses)]
            inverses = [inv - mm(inv, half) for inv, half in zip(inverses, halves)]
        width *= 2
    return inverses


def conv_front(ext, proj, halo, taps, since):
    rows = proj.shape[0]
    ext[0:PAD, :] = halo.astype(F32)
    ext[PAD : PAD + rows, :] = proj
    pre = proj * taps[0:1, :]
    for lag in range(1, CONV):
        moved = ext[PAD - lag : PAD - lag + rows, :]
        pre = pre + jnp.where(since >= lag, moved, 0.0) * taps[lag : lag + 1, :]
    gate = 1.0 / (1.0 + jnp.exp(-pre))
    return pre, gate, pre * gate


def unit_rows(value):
    inv = lax.rsqrt(jnp.sum(value * value, axis=-1, keepdims=True) + 1e-06)
    return value * inv, inv


def head_column(array, head):
    lane = lax.broadcasted_iota(jnp.int32, array.shape, 1)
    return jnp.sum(jnp.where(lane == head, array, 0.0), axis=1, keepdims=True)


def forward_kernel(
    since_ref, beta_ref, query_ref, key_ref, value_ref, halo_ref, taps_ref,
    out_add_ref, out_map_ref, new_add_ref, new_map_ref, inverse_ref, starts_ref, end_ref,
    ext,
):
    rows = since_ref.shape[0]
    blocks = rows // BLOCK
    since = since_ref[...]
    jobs = []
    for sub in range(HEADS_STEP):
        head = pl.program_id(0) * HEADS_STEP + sub
        lanes = slice(sub * BLOCK, (sub + 1) * BLOCK)
        mixed = []
        for part, ref in enumerate((query_ref, key_ref, value_ref)):
            _, _, act = conv_front(
                ext.at[sub * 3 + part], ref[:, lanes].astype(F32), halo_ref[part, :, lanes],
                taps_ref[part, :, lanes], since,
            )
            mixed.append(act)
        query = unit_rows(mixed[0])[0] * (BLOCK ** -0.5)
        key = unit_rows(mixed[1])[0]
        beta = 1.0 / (1.0 + jnp.exp(-head_column(beta_ref[...], head)))
        jobs.append((lanes, query, key, mixed[2], beta))
    lowers, scores = [], []
    for lanes, query, key, value, beta in jobs:
        for blk in range(blocks):
            span = slice(blk * BLOCK, (blk + 1) * BLOCK)
            causal, strict, _, _, _ = block_masks(since[span])
            both = mm_nt(jnp.concatenate([key[span], query[span]], axis=0), key[span])
            lowers.append(jnp.where(strict, both[:BLOCK] * beta[span], 0.0))
            scores.append(jnp.where(causal, both[BLOCK:], 0.0).astype(BF16))
    inverses = [inv.astype(BF16) for inv in unit_lower_inverses(lowers)]
    row, col = iotas(BLOCK)
    eye = (row == col).astype(F32)
    states = [jnp.concatenate([jnp.zeros((BLOCK, BLOCK), F32), eye], axis=1) for _ in jobs]
    for blk in range(blocks):
        span = slice(blk * BLOCK, (blk + 1) * BLOCK)
        _, _, keep, last_mask, keep_last = block_masks(since[span])
        for sub, (lanes, query, key, value, beta) in enumerate(jobs):
            at = sub * blocks + blk
            inverse_ref[sub, blk] = inverses[at]
            state = states[sub].astype(BF16)
            starts_ref[sub, blk] = state
            stacked = jnp.concatenate([key[span] * keep, query[span] * keep], axis=0)
            seen = mm(stacked, state)
            rest = jnp.concatenate([value[span], jnp.zeros((BLOCK, BLOCK), F32)], axis=1)
            right = (rest - seen[:BLOCK]) * beta[span]
            new = mm(inverses[at], right).astype(BF16)
            out = seen[BLOCK:] + mm(scores[at], new)
            out_add_ref[span, lanes] = out[:, :BLOCK].astype(BF16)
            out_map_ref[span, lanes] = out[:, BLOCK:].astype(BF16)
            new_add_ref[span, lanes] = new[:, :BLOCK]
            new_map_ref[span, lanes] = new[:, BLOCK:]
            keep_both = jnp.concatenate([keep_last, keep_last], axis=1)
            states[sub] = states[sub] * keep_both + mm_tn(key[span] * last_mask, new)
    for sub in range(len(jobs)):
        end_ref[sub] = states[sub]


def whole_spec(shape):
    return pl.BlockSpec(shape, lambda h: (0,) * len(shape))


def head_spec(rows):
    return pl.BlockSpec((rows, HEADS_STEP * BLOCK), lambda h: (0, h))


def per_head(*tail):
    return pl.BlockSpec((HEADS_STEP,) + tail, lambda h: (h,) + (0,) * len(tail))


def lanes_spec(first, second):
    return pl.BlockSpec((first, second, HEADS_STEP * BLOCK), lambda h: (0, 0, h))


def params():
    return pltpu.CompilerParams(vmem_limit_bytes=VMEM_LIMIT)


def mixer_forward(since, beta_logit, query, key, value, halo, taps):
    rows, width = query.shape
    heads = width // BLOCK
    blocks = rows // BLOCK
    wide = jax.ShapeDtypeStruct((rows, width), BF16)
    return pl.pallas_call(
        forward_kernel,
        grid=(heads // HEADS_STEP,),
        in_specs=[
            whole_spec(since.shape), whole_spec(beta_logit.shape),
            head_spec(rows), head_spec(rows), head_spec(rows),
            lanes_spec(3, PAD), lanes_spec(3, CONV),
        ],
        out_specs=[
            head_spec(rows), head_spec(rows), head_spec(rows), head_spec(rows),
            per_head(blocks, BLOCK, BLOCK), per_head(blocks, BLOCK, 2 * BLOCK),
            per_head(BLOCK, 2 * BLOCK),
        ],
        out_shape=[
            wide, wide, wide, wide,
            jax.ShapeDtypeStruct((heads, blocks, BLOCK, BLOCK), BF16),
            jax.ShapeDtypeStruct((heads, blocks, BLOCK, 2 * BLOCK), BF16),
            jax.ShapeDtypeStruct((heads, BLOCK, 2 * BLOCK), F32),
        ],
        scratch_shapes=[pltpu.VMEM((3 * HEADS_STEP, PAD + rows, BLOCK), F32)],
        compiler_params=params(),
        name="mixer_forward",
    )(since, beta_logit, query, key, value, halo, taps)


def join_kernel(out_add_ref, out_map_ref, entry_ref, gain_ref, mixed_ref):
    for sub in range(HEADS_STEP):
        lanes = slice(sub * BLOCK, (sub + 1) * BLOCK)
        core = out_add_ref[:, lanes].astype(F32) + mm(out_map_ref[:, lanes], entry_ref[sub])
        scale = lax.rsqrt(jnp.mean(core * core, axis=-1, keepdims=True) + 1e-05)
        mixed_ref[:, lanes] = (core * scale * gain_ref[...]).astype(BF16)


def mixer_join(out_add, out_map, entry, gain):
    rows, width = out_add.shape
    heads = width // BLOCK
    return pl.pallas_call(
        join_kernel,
        grid=(heads // HEADS_STEP,),
        in_specs=[head_spec(rows), head_spec(rows), per_head(BLOCK, BLOCK), whole_spec((1, BLOCK))],
        out_specs=head_spec(rows),
        out_shape=jax.ShapeDtypeStruct((rows, width), BF16),
        compiler_params=params(),
        name="mixer_join",
    )(out_add, out_map, entry, gain)


def core_back_kernel(out_add_ref, out_map_ref, entry_ref, gain_ref, up_ref, d_core_ref, start_ref, gain_out_ref):
    @pl.when(pl.program_id(0) == 0)
    def _():
        gain_out_ref[...] = jnp.zeros_like(gain_out_ref)

    for sub in range(HEADS_STEP):
        lanes = slice(sub * BLOCK, (sub + 1) * BLOCK)
        out_map = out_map_ref[:, lanes]
        core = out_add_ref[:, lanes].astype(F32) + mm(out_map, entry_ref[sub])
        scale = lax.rsqrt(jnp.mean(core * core, axis=-1, keepdims=True) + 1e-05)
        unit = core * scale
        up = up_ref[:, lanes].astype(F32)
        gain_out_ref[...] += jnp.sum(up * unit, axis=0, keepdims=True)
        scaled = up * gain_ref[...]
        d_core = scale * (scaled - unit * jnp.mean(scaled * unit, axis=-1, keepdims=True))
        d_core = d_core.astype(BF16)
        d_core_ref[:, lanes] = d_core
        start_ref[sub] = mm_tn(out_map, d_core)


def mixer_core_back(out_add, out_map, entry, gain, up):
    rows, width = out_add.shape
    heads = width // BLOCK
    return pl.pallas_call(
        core_back_kernel,
        grid=(heads // HEADS_STEP,),
        in_specs=[
            head_spec(rows), head_spec(rows), per_head(BLOCK, BLOCK), whole_spec((1, BLOCK)), head_spec(rows),
        ],
        out_specs=[head_spec(rows), per_head(BLOCK, BLOCK), whole_spec((1, BLOCK))],
        out_shape=[
            jax.ShapeDtypeStruct((rows, width), BF16),
            jax.ShapeDtypeStruct((heads, BLOCK, BLOCK), F32),
            jax.ShapeDtypeStruct((1, BLOCK), F32),
        ],
        compiler_params=params(),
        name="mixer_core_back",
    )(out_add, out_map, entry, gain, up)


def backward_kernel(
    since_ref, beta_ref, query_ref, key_ref, value_ref, halo_ref, taps_ref,
    new_add_ref, new_map_ref, inverse_ref, starts_ref, entry_ref, exit_ref, d_core_ref,
    d_proj_ref, d_halo_ref, d_taps_ref, d_beta_ref,
    ext, back,
):
    rows = since_ref.shape[0]
    blocks = rows // BLOCK
    since = since_ref[...]
    jobs = []
    for sub in range(HEADS_STEP):
        head = pl.program_id(0) * HEADS_STEP + sub
        lanes = slice(sub * BLOCK, (sub + 1) * BLOCK)
        fronts = []
        for part, ref in enumerate((query_ref, key_ref, value_ref)):
            fronts.append(
                conv_front(
                    ext.at[sub * 3 + part], ref[:, lanes].astype(F32), halo_ref[part, :, lanes],
                    taps_ref[part, :, lanes], since,
                )
            )
        query_unit, query_inv = unit_rows(fronts[0][2])
        key, key_inv = unit_rows(fronts[1][2])
        query = query_unit * (BLOCK ** -0.5)
        beta = 1.0 / (1.0 + jnp.exp(-head_column(beta_ref[...], head)))
        jobs.append((head, lanes, fronts, query, query_unit, query_inv, key, key_inv, beta))

    saved = {}
    for sub, (head, lanes, fronts, query, query_unit, query_inv, key, key_inv, beta) in enumerate(jobs):
        entry = entry_ref[sub].astype(BF16)
        for blk in range(blocks):
            span = slice(blk * BLOCK, (blk + 1) * BLOCK)
            causal, _, keep, last_mask, _ = block_masks(since[span])
            start = starts_ref[sub, blk]
            state = (start[:, :BLOCK].astype(F32) + mm(start[:, BLOCK:], entry)).astype(BF16)
            new = (new_add_ref[span, lanes].astype(F32) + mm(new_map_ref[span, lanes], entry)).astype(BF16)
            scores = jnp.where(causal, mm_nt(query[span], key[span]), 0.0).astype(BF16)
            d_out = d_core_ref[span, lanes]
            d_new = mm_tn(scores, d_out)
            d_state = mm_tn(query[span] * keep, d_out)
            saved[sub, blk] = (state, new, d_out, d_new, d_state)

    carried = [exit_ref[sub].astype(F32) for sub in range(HEADS_STEP)]
    chain = {}
    for blk in reversed(range(blocks)):
        span = slice(blk * BLOCK, (blk + 1) * BLOCK)
        _, _, keep, last_mask, keep_last = block_masks(since[span])
        for sub, (head, lanes, fronts, query, query_unit, query_inv, key, key_inv, beta) in enumerate(jobs):
            state, new, d_out, d_new, d_state = saved[sub, blk]
            after = carried[sub].astype(BF16)
            d_new = d_new + mm(key[span] * last_mask, after)
            d_right = mm_tn(inverse_ref[sub, blk], d_new)
            d_rest = d_right * beta[span]
            carried[sub] = carried[sub] * keep_last + d_state - mm_tn(key[span] * keep, d_rest)
            chain[sub, blk] = (after, d_right, d_rest)

    lane = lax.broadcasted_iota(jnp.int32, (rows, beta_ref.shape[1]), 1)
    d_beta_all = jnp.zeros((rows, beta_ref.shape[1]), F32)
    for sub, (head, lanes, fronts, query, query_unit, query_inv, key, key_inv, beta) in enumerate(jobs):
        d_queries, d_keys, d_values, d_betas = [], [], [], []
        for blk in range(blocks):
            span = slice(blk * BLOCK, (blk + 1) * BLOCK)
            causal, strict, keep, last_mask, _ = block_masks(since[span])
            state, new, d_out, _, _ = saved[sub, blk]
            after, d_right, d_rest = chain[sub, blk]
            both = mm_nt(jnp.concatenate([d_out, d_right.astype(BF16)], axis=0), new)
            d_scores = jnp.where(causal, both[:BLOCK], 0.0).astype(BF16)
            d_gram = (jnp.where(strict, both[BLOCK:], 0.0) * (-beta[span])).astype(BF16)
            key_b = key[span].astype(BF16)
            from_state = mm_nt(jnp.concatenate([d_out, d_rest.astype(BF16)], axis=0), state)
            left = mm(jnp.concatenate([d_scores, d_gram], axis=0), key_b)
            d_queries.append(from_state[:BLOCK] * keep + left[:BLOCK])
            d_key = left[BLOCK:] + mm_tn(
                jnp.concatenate([d_scores, d_gram], axis=0),
                jnp.concatenate([query[span].astype(BF16), key_b], axis=0),
            )
            d_key = d_key + mm_nt(new, after) * last_mask - from_state[BLOCK:] * keep
            d_keys.append(d_key)
            d_values.append(d_rest)
            d_betas.append(
                jnp.sum(d_right * new.astype(F32), axis=1, keepdims=True) * (1.0 - beta[span])
            )
        d_query = jnp.concatenate(d_queries, axis=0) * (BLOCK ** -0.5)
        d_key = jnp.concatenate(d_keys, axis=0)
        d_query = query_inv * (
            d_query - query_unit * jnp.sum(d_query * query_unit, axis=-1, keepdims=True)
        )
        d_key = key_inv * (d_key - key * jnp.sum(d_key * key, axis=-1, keepdims=True))
        d_value = jnp.concatenate(d_values, axis=0)
        d_beta_all = d_beta_all + jnp.where(lane == head, jnp.concatenate(d_betas, axis=0), 0.0)
        for part, d_act in enumerate((d_query, d_key, d_value)):
            pre, gate, _ = fronts[part]
            taps = taps_ref[part, :, lanes]
            source = ext.at[sub * 3 + part]
            d_pre = d_act * gate * (1.0 + pre * (1.0 - gate))
            room = back.at[sub * 3 + part]
            total = None
            d_taps = []
            for lag in range(CONV):
                masked = d_pre if lag == 0 else jnp.where(since >= lag, d_pre, 0.0)
                moved = source[PAD - lag : PAD - lag + rows, :]
                d_taps.append(jnp.sum(masked * moved, axis=0, keepdims=True))
                room[lag, 0:PAD, :] = jnp.zeros((PAD, BLOCK), F32)
                room[lag, PAD : PAD + rows, :] = masked * taps[lag : lag + 1, :]
                room[lag, PAD + rows : PAD + rows + PAD, :] = jnp.zeros((PAD, BLOCK), F32)
                term = room[lag, lag : lag + PAD + rows, :]
                total = term if total is None else total + term
            d_taps_ref[part, :, lanes] = jnp.concatenate(d_taps, axis=0)
            d_halo_ref[part, :, lanes] = total[:PAD].astype(d_halo_ref.dtype)
            d_proj_ref[part, :, lanes] = total[PAD:].astype(BF16)

    @pl.when(pl.program_id(0) == 0)
    def _():
        d_beta_ref[...] = d_beta_all

    @pl.when(pl.program_id(0) > 0)
    def _():
        d_beta_ref[...] += d_beta_all


def mixer_backward(
    since, beta_logit, query, key, value, halo, taps, new_add, new_map, inverse, starts, entry, exit_grad, d_core
):
    rows, width = query.shape
    heads = width // BLOCK
    blocks = rows // BLOCK
    return pl.pallas_call(
        backward_kernel,
        grid=(heads // HEADS_STEP,),
        in_specs=[
            whole_spec(since.shape), whole_spec(beta_logit.shape),
            head_spec(rows), head_spec(rows), head_spec(rows),
            lanes_spec(3, PAD), lanes_spec(3, CONV),
            head_spec(rows), head_spec(rows),
            per_head(blocks, BLOCK, BLOCK), per_head(blocks, BLOCK, 2 * BLOCK),
            per_head(BLOCK, BLOCK), per_head(BLOCK, BLOCK), head_spec(rows),
        ],
        out_specs=[
            lanes_spec(3, rows), lanes_spec(3, PAD), lanes_spec(3, CONV), whole_spec(beta_logit.shape),
        ],
        out_shape=[
            jax.ShapeDtypeStruct((3, rows, width), BF16),
            jax.ShapeDtypeStruct((3, PAD, width), F32),
            jax.ShapeDtypeStruct((3, CONV, width), F32),
            jax.ShapeDtypeStruct(beta_logit.shape, F32),
        ],
        scratch_shapes=[
            pltpu.VMEM((3 * HEADS_STEP, PAD + rows, BLOCK), F32),
            pltpu.VMEM((3 * HEADS_STEP, CONV, PAD + rows + PAD, BLOCK), F32),
        ],
        compiler_params=params(),
        name="mixer_backward",
    )(
        since, beta_logit, query, key, value, halo, taps, new_add, new_map, inverse, starts, entry, exit_grad, d_core
    )


GROUPS = 4
HALVES = 2


def chain_kernel(axis, forward, map_ref, add_ref, out_ref, sent, landed, send_sem, recv_sem):
    count = lax.axis_size(axis)
    me = lax.axis_index(axis)
    heads = add_ref.shape[0]
    step = heads // GROUPS
    up, down = (me + 1, me - 1) if forward else (me - 1, me + 1)
    first, last = (0, count - 1) if forward else (count - 1, 0)
    barrier = pltpu.get_barrier_semaphore()

    @pl.when(me != first)
    def _():
        pl.semaphore_signal(barrier, inc=1, device_id={axis: down}, device_id_type=MESH)

    @pl.when(me != last)
    def _():
        pl.semaphore_wait(barrier, 1)

    def copy(group, target):
        return pltpu.make_async_remote_copy(
            src_ref=sent.at[group],
            dst_ref=landed.at[group],
            send_sem=send_sem.at[group],
            recv_sem=recv_sem.at[group],
            device_id={axis: target},
            device_id_type=MESH,
        )

    for group in range(GROUPS):
        @pl.when(me != first)
        def _():
            copy(group, up).wait_recv()
            for sub in range(step):
                head = group * step + sub
                out_ref[head] = landed[group, sub].astype(F32)

        @pl.when(me == first)
        def _():
            out_ref[group * step : (group + 1) * step] = jnp.zeros((step,) + out_ref.shape[1:], F32)

        @pl.when(me != last)
        def _():
            for sub in range(step):
                head = group * step + sub
                if forward:
                    moved = mm(map_ref[head], out_ref[head])
                else:
                    moved = mm_tn(map_ref[head], out_ref[head])
                sent[group, sub] = (moved + add_ref[head]).astype(BF16)
            copy(group, up).start()

    @pl.when(me != last)
    def _():
        for group in range(GROUPS):
            copy(group, up).wait_send()


def carry_chain(map_part, add_part, axis, forward):
    heads = add_part.shape[0]
    part = (GROUPS, heads // GROUPS, BLOCK, BLOCK)
    return pl.pallas_call(
        functools.partial(chain_kernel, axis, forward),
        in_specs=[pl.BlockSpec(memory_space=pltpu.VMEM)] * 2,
        out_specs=pl.BlockSpec(memory_space=pltpu.VMEM),
        out_shape=jax.ShapeDtypeStruct(add_part.shape, F32),
        scratch_shapes=[
            pltpu.VMEM(part, BF16),
            pltpu.VMEM(part, BF16),
            pltpu.SemaphoreType.DMA((GROUPS,)),
            pltpu.SemaphoreType.DMA((GROUPS,)),
        ],
        compiler_params=pltpu.CompilerParams(
            collective_id=1 if forward else 2, has_side_effects=True, vmem_limit_bytes=VMEM_LIMIT // 2
        ),
        name="carry_forward" if forward else "carry_backward",
    )(map_part, add_part)


WINDOW = 4
LAG = 2
SPLIT = 4


def reduce_kernel(
    left_ref, right_ref, small_ref, out_ref, small_out_ref,
    left_own, left_away, left_sib, right_sib, small_sib, total, total_small, got2, got2_small, got3, got3_small, gotz, gotz_small,
    left_send, left_recv, right_send, right_recv, small_send, small_recv,
    send2, recv2, send3, recv3, sendz, recvz,
):
    dp = lax.axis_index("dp")
    z = lax.axis_index("narrow")
    core, x, y = dp % 2, (dp // 2) % 2, dp // 4
    depth = lax.axis_size("narrow")
    parts = right_ref.shape[0]
    units = SPLIT * parts
    rows = left_ref.shape[1] // 8
    cols = right_ref.shape[2] // SPLIT
    sib = dp + 1 - 2 * core
    flip_x = dp + 2 * (1 - 2 * x)
    flip_y = dp + 4 * (1 - 2 * y)

    def peer_z(step):
        return (z + step) % depth

    barrier = pltpu.get_barrier_semaphore()
    for target in (sib, flip_x, flip_y):
        pl.semaphore_signal(barrier, inc=1, device_id={"dp": target}, device_id_type=MESH)
    for step in range(1, depth):
        pl.semaphore_signal(barrier, inc=1, device_id={"narrow": peer_z(step)}, device_id_type=MESH)
    pl.semaphore_wait(barrier, 2 + depth)

    def send(src, dst, send_sem, recv_sem, target):
        return pltpu.make_async_remote_copy(
            src_ref=src, dst_ref=dst, send_sem=send_sem, recv_sem=recv_sem,
            device_id=target, device_id_type=MESH,
        )

    def stripe_rows(stripe, which):
        return pl.ds(pl.multiple_of((stripe * 2 + which) * rows, rows), rows)

    def left_copy(stripe):
        return send(
            left_away.at[stripe], left_sib.at[stripe],
            left_send.at[stripe], left_recv.at[stripe], {"dp": sib},
        )

    def small_copy(stripe):
        return send(
            small_ref.at[stripe_rows(stripe, 1 - core)], small_sib.at[stripe],
            small_send.at[stripe], small_recv.at[stripe], {"dp": sib},
        )

    def right_copy(part):
        return send(right_ref.at[part], right_sib.at[part], right_send.at[part], right_recv.at[part], {"dp": sib})

    right_copy(0).start()
    for stripe in range(4):
        small_copy(stripe).start()
    for stripe in range(4):
        turned = left_ref[:, stripe_rows(stripe, 1 - core)].astype(F32).T
        left_away[stripe] = turned.astype(BF16)
        left_copy(stripe).start()
    for part in range(1, parts):
        right_copy(part).start()
    for stripe in range(4):
        left_own[stripe] = left_ref[:, stripe_rows(stripe, core)].astype(F32).T.astype(BF16)

    def order(unit):
        e = unit % 2

        def pick(even, odd):
            return (1 - e) * even + e * odd

        def away(j):
            return pick(2 * j + 1 - x, 2 * (1 - y) + j)

        def kept(j):
            return pick(2 * j + x, 2 * y + j)

        far = pick(1 - y, 1 - x)
        near = pick(y, x)
        return away, kept, pick(flip_x, flip_y), pick(flip_y, flip_x), far, near

    def copy2(unit, j):
        away, _, target, _, _, _ = order(unit)
        return send(total.at[unit, away(j)], got2.at[unit, j], send2.at[unit, j], recv2.at[unit, j], {"dp": target})

    def copy2_small(j):
        away, _, target, _, _, _ = order(0)
        return send(
            total_small.at[away(j)], got2_small.at[j], send2.at[units, j], recv2.at[units, j], {"dp": target}
        )

    def copy3(unit):
        _, kept, _, target, far, _ = order(unit)
        return send(total.at[unit, kept(far)], got3.at[unit], send3.at[unit], recv3.at[unit], {"dp": target})

    def copy3_small():
        _, kept, _, target, far, _ = order(0)
        return send(total_small.at[kept(far)], got3_small, send3.at[units], recv3.at[units], {"dp": target})

    share = rows // depth

    def share_rows(at):
        return pl.ds(pl.multiple_of(at * share, share), share)

    def copyz(unit, step):
        _, kept, _, _, _, near = order(unit)
        to = peer_z(step)
        return send(
            total.at[unit, kept(near), share_rows(to)], gotz.at[unit, step - 1],
            sendz.at[unit, step - 1], recvz.at[unit, step - 1], {"narrow": to},
        )

    def copyz_small(step):
        _, kept, _, _, _, near = order(0)
        to = peer_z(step)
        return send(
            total_small.at[kept(near), share_rows(to)], gotz_small.at[step - 1],
            sendz.at[units, step - 1], recvz.at[units, step - 1], {"narrow": to},
        )

    def add_to(dst, src):
        step = 32

        def one(at, _):
            at = pl.ds(pl.multiple_of(at * step, step), step)
            dst[at, :] = (dst[at, :].astype(F32) + src[at, :].astype(F32)).astype(dst.dtype)
            return 0

        lax.fori_loop(0, rows // step, one, 0)

    for stripe in range(4):
        small_copy(stripe).wait()
        total_small[stripe] = small_ref[stripe_rows(stripe, core)] + small_sib[stripe]
    for j in range(2):
        copy2_small(j).start()
    for stripe in range(4):
        left_copy(stripe).wait()

    tile = 512

    def products(unit, _):
        away, kept, _, _, _, _ = order(unit)
        part = unit // SPLIT

        @pl.when(unit % SPLIT == 0)
        def _():
            right_copy(part).wait()

        def one(k, _):
            j = k % 2
            stripe = (k // 2) * kept(j) + (1 - k // 2) * away(j)
            mine = left_own[stripe]
            other = left_sib[stripe]
            for at in range(cols // tile):
                lanes = pl.ds(pl.multiple_of((unit % SPLIT) * cols + at * tile, tile), tile)
                value = jnp.dot(mine, right_ref[part, :, lanes], preferred_element_type=F32)
                value = value + jnp.dot(other, right_sib[part, :, lanes], preferred_element_type=F32)
                total[unit, stripe, :, at * tile : (at + 1) * tile] = value.astype(BF16)

            @pl.when((k < 2) & (unit < WINDOW))
            def _():
                copy2(unit, j).start()

            return 0

        lax.fori_loop(0, 4, one, 0)
        return 0

    lax.fori_loop(0, units, products, 0)

    def second(unit):
        _, kept, _, _, far, near = order(unit)
        for j in range(2):
            copy2(unit, j).wait()

        @pl.when(unit + WINDOW < units)
        def _():
            for j in range(2):
                copy2(unit + WINDOW, j).start()

        add_to(total.at[unit, kept(far)], got2.at[unit, far])
        copy3(unit).start()
        add_to(total.at[unit, kept(near)], got2.at[unit, near])

    def third(unit):
        _, kept, _, _, _, near = order(unit)
        copy3(unit).wait()
        add_to(total.at[unit, kept(near)], got3.at[unit])
        for step in range(1, depth):
            copyz(unit, step).start()

    def fourth(unit):
        _, kept, _, _, _, near = order(unit)
        for step in range(1, depth):
            copyz(unit, step).wait()
        value = total[unit, kept(near), share_rows(z), :].astype(F32)
        for step in range(1, depth):
            value = value + gotz[unit, step - 1].astype(F32)
        out_ref[unit // SPLIT, :, pl.ds(pl.multiple_of((unit % SPLIT) * cols, cols), cols)] = value

    _, kept, _, _, far, near = order(0)
    for j in range(2):
        copy2_small(j).wait()
    add_to(total_small.at[kept(far)], got2_small.at[far])
    copy3_small().start()
    add_to(total_small.at[kept(near)], got2_small.at[near])

    def stages(at, _):
        @pl.when(at < units)
        def _():
            second(at)

        @pl.when((at >= LAG) & (at < units + LAG))
        def _():
            third(at - LAG)

        @pl.when(at >= 2 * LAG)
        def _():
            fourth(at - 2 * LAG)

        return 0

    lax.fori_loop(0, units, stages, 0)
    copy3_small().wait()
    add_to(total_small.at[kept(near)], got3_small)
    for step in range(1, depth):
        copyz_small(step).start()
    lax.fori_loop(units, units + 2 * LAG, stages, 0)
    for step in range(1, depth):
        copyz_small(step).wait()
    value = total_small[kept(near), share_rows(z), :]
    for step in range(1, depth):
        value = value + gotz_small[step - 1]
    small_out_ref[...] = value


def reduce_products(left, right, small):
    tokens, height = left.shape
    parts, _, width = right.shape
    depth = lax.axis_size("narrow")
    units = SPLIT * parts
    rows, cols = height // 8, width // SPLIT
    share = rows // depth
    lanes = small.shape[1]
    dma = pltpu.SemaphoreType.DMA
    return pl.pallas_call(
        reduce_kernel,
        in_specs=[pl.BlockSpec(memory_space=pltpu.VMEM)] * 3,
        out_specs=[pl.BlockSpec(memory_space=pltpu.VMEM)] * 2,
        out_shape=[
            jax.ShapeDtypeStruct((parts, share, width), F32),
            jax.ShapeDtypeStruct((share, lanes), F32),
        ],
        scratch_shapes=[
            pltpu.VMEM((4, rows, tokens), BF16),
            pltpu.VMEM((4, rows, tokens), BF16),
            pltpu.VMEM((4, rows, tokens), BF16),
            pltpu.VMEM(right.shape, BF16),
            pltpu.VMEM((4, rows, lanes), F32),
            pltpu.VMEM((units, 4, rows, cols), BF16),
            pltpu.VMEM((4, rows, lanes), F32),
            pltpu.VMEM((units, 2, rows, cols), BF16),
            pltpu.VMEM((2, rows, lanes), F32),
            pltpu.VMEM((units, rows, cols), BF16),
            pltpu.VMEM((rows, lanes), F32),
            pltpu.VMEM((units, depth - 1, share, cols), BF16),
            pltpu.VMEM((depth - 1, share, lanes), F32),
            dma((4,)), dma((4,)), dma((parts,)), dma((parts,)), dma((4,)), dma((4,)),
            dma((units + 1, 2)), dma((units + 1, 2)), dma((units + 1,)), dma((units + 1,)),
            dma((units + 1, depth - 1)), dma((units + 1, depth - 1)),
        ],
        compiler_params=pltpu.CompilerParams(
            collective_id=3, has_side_effects=True, vmem_limit_bytes=VMEM_LIMIT
        ),
        name="reduce_products",
    )(left, right, small)


def ffn_grads_kernel(*refs):
    lefts = [refs[0:HALVES], refs[0:HALVES], refs[HALVES : 2 * HALVES]]
    rights = [refs[(2 + m) * HALVES : (3 + m) * HALVES] for m in range(3)]
    (
        out_ref, left_buf, right_buf, away, landed, total, got2, got3,
        left_sem, right_sem, send1, recv1, send2, recv2, send3, recv3,
    ) = refs[5 * HALVES :]
    dp = lax.axis_index("dp")
    core, x, y = dp % 2, (dp // 2) % 2, dp // 4
    rows = total.shape[2]
    half = rows // 2
    part = left_buf.shape[1] // HALVES
    sib = dp + 1 - 2 * core
    flip_x = dp + 2 * (1 - 2 * x)
    flip_y = dp + 4 * (1 - 2 * y)
    barrier = pltpu.get_barrier_semaphore()
    for target in (sib, flip_x, flip_y):
        pl.semaphore_signal(barrier, inc=1, device_id={"dp": target}, device_id_type=MESH)

    def load_left(m, k, start):
        own = k // 4
        block = (k % 4) * 2 + own * core + (1 - own) * (1 - core)
        lanes = pl.ds(pl.multiple_of(block * rows, rows), rows)
        for at in range(HALVES):
            copy = pltpu.make_async_copy(
                lefts[m][at].at[:, lanes], left_buf.at[k % 2, at * part : (at + 1) * part], left_sem.at[k % 2, at]
            )
            if start:
                copy.start()
            else:
                copy.wait()

    def load_right(m, start):
        for at in range(HALVES):
            copy = pltpu.make_async_copy(
                rights[m][at], right_buf.at[m % 2, at * part : (at + 1) * part], right_sem.at[m % 2, at]
            )
            if start:
                copy.start()
            else:
                copy.wait()

    def send(src, dst, send_sem, recv_sem, target):
        return pltpu.make_async_remote_copy(
            src_ref=src, dst_ref=dst, send_sem=send_sem, recv_sem=recv_sem,
            device_id={"dp": target}, device_id_type=MESH,
        )

    def copy1(m, stripe):
        return send(away.at[m, stripe], landed.at[m, stripe], send1.at[m, stripe], recv1.at[m, stripe], sib)

    def band(h):
        return pl.ds(h * half, half)

    def order(h):
        if h == 0:
            return (lambda j: 2 * j + 1 - x), (lambda j: 2 * j + x), flip_x, flip_y, 1 - y, y
        return (lambda j: 2 * (1 - y) + j), (lambda j: 2 * y + j), flip_y, flip_x, 1 - x, x

    def copy2(m, h, j):
        gone, _, target, _, _, _ = order(h)
        return send(
            total.at[m, gone(j), band(h)], got2.at[m, h, j], send2.at[2 * m + h, j], recv2.at[2 * m + h, j], target
        )

    def copy3(m, h):
        _, kept, _, target, far, _ = order(h)
        return send(total.at[m, kept(far), band(h)], got3.at[m, h], send3.at[m, h], recv3.at[m, h], target)

    def add_to(dst, src):
        step = 32

        def one(at, _):
            at = pl.ds(pl.multiple_of(at * step, step), step)
            dst[at, :] = (dst[at, :].astype(F32) + src[at, :].astype(F32)).astype(dst.dtype)
            return 0

        lax.fori_loop(0, dst.shape[0] // step, one, 0)

    def compute(m):
        load_right(m, False)
        if m + 1 < 3:
            load_right(m + 1, True)

        def one(k, _):
            @pl.when(k < 7)
            def _():
                load_left(m, k + 1, True)

            if m + 1 < 3:
                @pl.when(k == 7)
                def _():
                    load_left(m + 1, 0, True)

            load_left(m, k, False)
            value = lax.dot_general(
                left_buf[k % 2], right_buf[m % 2], (((0,), (0,)), ((), ())), preferred_element_type=F32
            ).astype(BF16)

            @pl.when(k < 4)
            def _():
                away[m, k] = value
                copy1(m, k).start()

            @pl.when(k >= 4)
            def _():
                total[m, k - 4] = value

            return 0

        lax.fori_loop(0, 8, one, 0)

        def join(stripe, _):
            copy1(m, stripe).wait()
            add_to(total.at[m, stripe], landed.at[m, stripe])
            return 0

        lax.fori_loop(0, 4, join, 0)
        for h in range(2):
            for j in range(2):
                copy2(m, h, j).start()

    def second(m):
        for h in range(2):
            _, kept, _, _, far, near = order(h)
            for j in range(2):
                copy2(m, h, j).wait()
            add_to(total.at[m, kept(far), band(h)], got2.at[m, h, far])
            copy3(m, h).start()
            add_to(total.at[m, kept(near), band(h)], got2.at[m, h, near])

    def third(m):
        for h in range(2):
            _, kept, _, _, _, near = order(h)
            copy3(m, h).wait()
            step = 32

            def one(at, _):
                at = at * step
                value = total[m, kept(near), pl.ds(pl.multiple_of(h * half + at, step), step), :].astype(F32)
                value = value + got3[m, h, pl.ds(pl.multiple_of(at, step), step), :].astype(F32)
                out_ref[m, pl.ds(pl.multiple_of(h * half + at, step), step), :] = value
                return 0

            lax.fori_loop(0, half // step, one, 0)

    load_right(0, True)
    load_left(0, 0, True)
    pl.semaphore_wait(barrier, 3)
    compute(0)
    compute(1)
    second(0)
    compute(2)
    third(0)
    second(1)
    third(1)
    second(2)
    third(2)


def ffn_grads(lefts, rights):
    part, height = lefts[0][0].shape
    width = rights[0][0].shape[1]
    rows = height // 8
    half = rows // 2
    dma = pltpu.SemaphoreType.DMA
    operands = [ref for group in (*lefts, *rights) for ref in group]
    return pl.pallas_call(
        ffn_grads_kernel,
        in_specs=[pl.BlockSpec(memory_space=pl.ANY)] * len(operands),
        out_specs=pl.BlockSpec(memory_space=pltpu.VMEM),
        out_shape=jax.ShapeDtypeStruct((3, rows, width), F32),
        scratch_shapes=[
            pltpu.VMEM((2, HALVES * part, rows), BF16),
            pltpu.VMEM((2, HALVES * part, width), BF16),
            pltpu.VMEM((3, 4, rows, width), BF16),
            pltpu.VMEM((3, 4, rows, width), BF16),
            pltpu.VMEM((3, 4, rows, width), BF16),
            pltpu.VMEM((3, 2, 2, half, width), BF16),
            pltpu.VMEM((3, 2, half, width), BF16),
            dma((2, HALVES)), dma((2, HALVES)), dma((3, 4)), dma((3, 4)),
            dma((6, 2)), dma((6, 2)), dma((3, 2)), dma((3, 2)),
        ],
        compiler_params=pltpu.CompilerParams(
            collective_id=4, has_side_effects=True, vmem_limit_bytes=60 * 1024 * 1024
        ),
        name="ffn_grads",
    )(*operands)


def shifted(value, axis, steps):
    count = lax.axis_size(axis)
    first, last = (max(0, -steps), min(count, count - steps))
    return lax.ppermute(value, axis, [(source, source + steps) for source in range(first, last)])


def matmul(left, right):
    return jnp.dot(left, right, preferred_element_type=F32)


def dot_tn(left, right):
    return jnp.einsum("rd,re->de", left, right, preferred_element_type=F32)


def dot_nt(left, right):
    return jnp.einsum("re,de->rd", left, right, preferred_element_type=F32)


def rms_scale(value_in, gain_vec, epsilon):
    return value_in * lax.rsqrt(jnp.mean(value_in * value_in, axis=-1, keepdims=True) + epsilon) * gain_vec


def norm_back(value_in, gain_vec, upstream, epsilon):
    inv_scale = lax.rsqrt(jnp.mean(value_in * value_in, axis=-1, keepdims=True) + epsilon)
    scaled_up = upstream * gain_vec
    gain_term = jnp.sum(upstream * value_in * inv_scale, axis=0)
    cubed = inv_scale * inv_scale * inv_scale
    back_value = inv_scale * scaled_up - value_in * cubed * jnp.mean(
        scaled_up * value_in, axis=-1, keepdims=True
    )
    return (back_value, gain_term)


def since_start(doc_lengths, offset, rows):
    ends = jnp.cumsum(doc_lengths[0])
    position = offset + jnp.arange(rows, dtype=jnp.int32)
    starts = jnp.max(jnp.where(position[:, None] >= ends[None, :], ends[None, :], 0), axis=1)
    return jnp.broadcast_to((position - starts)[:, None], (rows, BLOCK)).astype(jnp.int32)


def scatter_all(value, dim):
    part = lax.psum_scatter(value, "dp", scatter_dimension=dim, tiled=True)
    return lax.psum_scatter(part, "narrow", scatter_dimension=dim, tiled=True)


def local(
    tokens,
    doc_lengths,
    attn_gain,
    w_query,
    w_key,
    w_value,
    w_beta,
    conv_weight,
    out_gain,
    w_out,
    mlp_gain,
    w_gate,
    w_up,
    w_down,
    grad_out,
):
    tok_rows, model_width = tokens.shape
    offset = lax.axis_index("narrow") * tok_rows
    half = tok_rows // HALVES
    parts = [slice(at * half, (at + 1) * half) for at in range(HALVES)]

    def gather(rows):
        return lax.all_gather(rows, "narrow", axis=0, tiled=True)

    def scatter(rows):
        return lax.psum_scatter(rows, "narrow", scatter_dimension=0, tiled=True)

    cot = []
    for part in parts:
        cot.append(gather(grad_out[part]))
    since = since_start(doc_lengths, offset, tok_rows)
    inputs = tokens.astype(F32)
    normed = rms_scale(inputs, attn_gain, 1e-06).astype(BF16)
    query, key, value = (matmul(normed, w) for w in (w_query, w_key, w_value))
    beta_logit = matmul(normed, w_beta)
    halo = shifted(
        jnp.stack([part[tok_rows - PAD :].astype(BF16) for part in (query, key, value)]), "narrow", 1
    )
    out_add, out_map, new_add, new_map, inverse, starts, end = mixer_forward(
        since, beta_logit, query, key, value, halo, conv_weight
    )
    transfer = end[:, :, BLOCK:].astype(BF16)
    entry = carry_chain(transfer, end[:, :, :BLOCK], "narrow", True)
    gain_row = out_gain[None, :]
    attn_mixed = mixer_join(out_add, out_map, entry, gain_row)
    hidden = inputs + matmul(attn_mixed, w_out)
    normed_mlp = rms_scale(hidden, mlp_gain, 1e-06).astype(BF16)
    normed_mlp, *cot = lax.optimization_barrier((normed_mlp, *cot))
    gathered = [gather(normed_mlp[part]) for part in parts]
    activation, d_gate, d_up, d_normed_parts = [], [], [], []
    for at in range(HALVES):
        gate_proj = matmul(gathered[at], w_gate)
        up_proj = matmul(gathered[at], w_up)
        gate_sigmoid = jax.nn.sigmoid(gate_proj)
        silu_gate = gate_proj * gate_sigmoid
        activation.append((silu_gate * up_proj).astype(BF16))
        d_act = jnp.einsum("rd,fd->rf", cot[at], w_down, preferred_element_type=F32)
        d_gate.append(
            (d_act * up_proj * gate_sigmoid * (1.0 + gate_proj * (1.0 - gate_sigmoid))).astype(BF16)
        )
        d_up.append((d_act * silu_gate).astype(BF16))
        d_normed_parts.append(scatter((dot_nt(d_gate[at], w_gate) + dot_nt(d_up[at], w_up)).astype(BF16)))
    out_parts = [matmul(act, w_down).astype(BF16) for act in activation]
    if lax.axis_size("dp") == 8:
        ffn_sums = ffn_grads((gathered, cot), (d_gate, d_up, activation))
    else:
        ffn_sums = [
            lax.psum_scatter(
                sum(dot_tn(a, c) for a, c in zip(left, right)).astype(BF16), "dp", scatter_dimension=0, tiled=True
            )
            for left, right in ((gathered, d_gate), (gathered, d_up), (cot, activation))
        ]
    d_normed_parts, out_parts, ffn_sums = lax.optimization_barrier((d_normed_parts, out_parts, ffn_sums))
    grad_gate, grad_up, grad_down = ffn_sums[0].astype(F32), ffn_sums[1].astype(F32), ffn_sums[2].astype(F32).T
    d_normed_mlp = jnp.concatenate(d_normed_parts, axis=0).astype(F32)
    d_hidden_norm, mlp_gain_term = norm_back(hidden, mlp_gain, d_normed_mlp, 1e-06)
    d_hidden = grad_out.astype(F32) + d_hidden_norm
    d_branch = d_hidden.astype(BF16)
    w_out_term = dot_tn(d_branch, attn_mixed).astype(BF16)
    d_mixed = dot_nt(d_branch, w_out)
    d_core, start_grad, out_gain_term = mixer_core_back(out_add, out_map, entry, gain_row, d_mixed)
    exit_grad = carry_chain(transfer, start_grad, "narrow", False)
    exit_grad, out_parts = lax.optimization_barrier((exit_grad, out_parts))
    w_out_term = scatter_all(w_out_term, 0)
    ffn_parts = [scatter(part) for part in out_parts]
    d_proj, d_halo, conv_term, d_beta = mixer_backward(
        since, beta_logit, query, key, value, halo, conv_weight,
        new_add, new_map, inverse, starts, entry, exit_grad, d_core,
    )
    after = shifted(d_halo.astype(BF16), "narrow", -1)
    d_proj = d_proj.at[:, tok_rows - PAD :].add(after)
    d_query, d_key, d_value = d_proj[0], d_proj[1], d_proj[2]
    d_beta_low = d_beta.astype(BF16)
    beta_term = jnp.einsum("rd,rh->dh", normed, d_beta_low, preferred_element_type=F32)
    d_normed = dot_nt(d_query, w_query) + dot_nt(d_key, w_key) + dot_nt(d_value, w_value)
    d_normed = d_normed + jnp.einsum("rh,dh->rd", d_beta_low, w_beta, preferred_element_type=F32)
    d_input_norm, attn_gain_term = norm_back(inputs, attn_gain, d_normed, 1e-06)
    grad_tokens = (d_hidden + d_input_norm).astype(BF16)
    devices = lax.axis_size("dp") * lax.axis_size("narrow")
    heads = w_beta.shape[1]
    taps = 3 * CONV
    gain_share = BLOCK // devices
    gain_column = jnp.pad(
        out_gain_term.reshape(devices, gain_share), ((0, 0), (0, model_width // devices - gain_share))
    ).reshape(model_width, 1)
    small = jnp.concatenate(
        [
            beta_term,
            conv_term.reshape(taps, model_width).T,
            attn_gain_term[:, None],
            mlp_gain_term[:, None],
            gain_column,
        ],
        axis=1,
    )
    small = jnp.pad(small, ((0, 0), (0, BLOCK - small.shape[1])))
    if lax.axis_size("dp") == 8:
        grads, small = reduce_products(normed, d_proj, small)
    else:
        grads = [scatter_all(dot_tn(normed, part).astype(BF16), 0).astype(F32) for part in (d_query, d_key, d_value)]
        small = lax.psum_scatter(small, ("dp", "narrow"), scatter_dimension=0, tiled=True)
    grad_beta = small[:, :heads]
    grad_conv = small[:, heads : heads + taps].T.reshape(3, CONV, -1)
    grad_attn_gain = small[:, heads + taps]
    grad_mlp_gain = small[:, heads + taps + 1]
    grad_out_gain = small[:gain_share, heads + taps + 2]
    ffn_parts, w_out_term, grads = lax.optimization_barrier((ffn_parts, w_out_term, grads))
    block_out = (hidden + jnp.concatenate(ffn_parts, axis=0).astype(F32)).astype(BF16)
    grad_query, grad_key, grad_value = grads[0], grads[1], grads[2]
    grad_w_out = w_out_term.astype(F32).T
    return (
        block_out,
        grad_tokens,
        grad_attn_gain,
        grad_query,
        grad_key,
        grad_value,
        grad_beta,
        grad_conv,
        grad_out_gain,
        grad_w_out,
        grad_mlp_gain,
        grad_gate,
        grad_up,
        grad_down,
    )


def solution(mesh):
    placed = (
        P(("dp", "narrow"), None),
        P("dp", None),
        P(),
        P(),
        P(),
        P(),
        P(),
        P(),
        P(),
        P(),
        P(),
        P(None, "narrow"),
        P(None, "narrow"),
        P("narrow", None),
        P(("dp", "narrow"), None),
    )
    return jax.shard_map(
        local,
        mesh=mesh,
        in_specs=placed,
        out_specs=(
            P(("dp", "narrow"), None),
            P(("dp", "narrow"), None),
            P(("dp", "narrow")),
            P(("dp", "narrow"), None),
            P(("dp", "narrow"), None),
            P(("dp", "narrow"), None),
            P(("dp", "narrow"), None),
            P(None, None, ("dp", "narrow")),
            P(("dp", "narrow")),
            P(None, ("dp", "narrow")),
            P(("dp", "narrow")),
            P("dp", "narrow"),
            P("dp", "narrow"),
            P("narrow", "dp"),
        ),
        check_vma=False,
    )
```

```python
import functools

import jax
import jax.numpy as jnp
from jax import lax
from jax.experimental import pallas as pl
from jax.experimental.pallas import tpu as pltpu
from jax.sharding import PartitionSpec as P

CONV = 4
BLOCK = 128
HEADS_STEP = 2
PAD = 8
MESH = pl.DeviceIdType.MESH
F32 = jnp.float32
BF16 = jnp.bfloat16
VMEM_LIMIT = 56 * 1024 * 1024


def mm(left, right, contract=(1, 0)):
    return lax.dot_general(
        left.astype(BF16),
        right.astype(BF16),
        (((contract[0],), (contract[1],)), ((), ())),
        preferred_element_type=F32,
    )


def mm_nt(left, right):
    return mm(left, right, (1, 1))


def mm_tn(left, right):
    return mm(left, right, (0, 0))


def iotas(size):
    row = lax.broadcasted_iota(jnp.int32, (size, size), 0)
    col = lax.broadcasted_iota(jnp.int32, (size, size), 1)
    return row, col


def block_masks(since):
    size = since.shape[0]
    row, col = iotas(size)
    back = row - col
    causal = (back >= 0) & (back <= since)
    strict = (back > 0) & (back <= since)
    keep = (since > row).astype(F32)
    last = since[size - 1 : size, :]
    last_mask = (row >= size - 1 - last).astype(F32)
    keep_last = (last > size - 1).astype(F32)
    return causal, strict, keep, last_mask, keep_last


def unit_lower_inverses(lowers):
    size = lowers[0].shape[0]
    row, col = iotas(size)
    width = 1
    inverses = None
    while width < size:
        join = (row // (2 * width) == col // (2 * width)) & (row // width != col // width)
        pieces = [jnp.where(join, low, 0.0) for low in lowers]
        if inverses is None:
            eye = (row == col).astype(F32)
            inverses = [eye - piece for piece in pieces]
        else:
            halves = [mm(piece, inv) for piece, inv in zip(pieces, inverses)]
            inverses = [inv - mm(inv, half) for inv, half in zip(inverses, halves)]
        width *= 2
    return inverses


def conv_front(ext, proj, halo, taps, since):
    rows = proj.shape[0]
    ext[0:PAD, :] = halo.astype(F32)
    ext[PAD : PAD + rows, :] = proj
    pre = proj * taps[0:1, :]
    for lag in range(1, CONV):
        moved = ext[PAD - lag : PAD - lag + rows, :]
        pre = pre + jnp.where(since >= lag, moved, 0.0) * taps[lag : lag + 1, :]
    gate = 1.0 / (1.0 + jnp.exp(-pre))
    return pre, gate, pre * gate


def unit_rows(value):
    inv = lax.rsqrt(jnp.sum(value * value, axis=-1, keepdims=True) + 1e-06)
    return value * inv, inv


def head_column(array, head):
    lane = lax.broadcasted_iota(jnp.int32, array.shape, 1)
    return jnp.sum(jnp.where(lane == head, array, 0.0), axis=1, keepdims=True)


def forward_kernel(
    since_ref, beta_ref, query_ref, key_ref, value_ref, halo_ref, taps_ref,
    out_add_ref, out_map_ref, new_add_ref, new_map_ref, inverse_ref, starts_ref, end_ref,
    ext,
):
    rows = since_ref.shape[0]
    blocks = rows // BLOCK
    since = since_ref[...]
    jobs = []
    for sub in range(HEADS_STEP):
        head = pl.program_id(0) * HEADS_STEP + sub
        lanes = slice(sub * BLOCK, (sub + 1) * BLOCK)
        mixed = []
        for part, ref in enumerate((query_ref, key_ref, value_ref)):
            _, _, act = conv_front(
                ext.at[sub * 3 + part], ref[:, lanes].astype(F32), halo_ref[part, :, lanes],
                taps_ref[part, :, lanes], since,
            )
            mixed.append(act)
        query = unit_rows(mixed[0])[0] * (BLOCK ** -0.5)
        key = unit_rows(mixed[1])[0]
        beta = 1.0 / (1.0 + jnp.exp(-head_column(beta_ref[...], head)))
        jobs.append((lanes, query, key, mixed[2], beta))
    lowers, scores = [], []
    for lanes, query, key, value, beta in jobs:
        for blk in range(blocks):
            span = slice(blk * BLOCK, (blk + 1) * BLOCK)
            causal, strict, _, _, _ = block_masks(since[span])
            both = mm_nt(jnp.concatenate([key[span], query[span]], axis=0), key[span])
            lowers.append(jnp.where(strict, both[:BLOCK] * beta[span], 0.0))
            scores.append(jnp.where(causal, both[BLOCK:], 0.0).astype(BF16))
    inverses = [inv.astype(BF16) for inv in unit_lower_inverses(lowers)]
    row, col = iotas(BLOCK)
    eye = (row == col).astype(F32)
    states = [jnp.concatenate([jnp.zeros((BLOCK, BLOCK), F32), eye], axis=1) for _ in jobs]
    for blk in range(blocks):
        span = slice(blk * BLOCK, (blk + 1) * BLOCK)
        _, _, keep, last_mask, keep_last = block_masks(since[span])
        for sub, (lanes, query, key, value, beta) in enumerate(jobs):
            at = sub * blocks + blk
            inverse_ref[sub, blk] = inverses[at]
            state = states[sub].astype(BF16)
            starts_ref[sub, blk] = state
            stacked = jnp.concatenate([key[span] * keep, query[span] * keep], axis=0)
            seen = mm(stacked, state)
            rest = jnp.concatenate([value[span], jnp.zeros((BLOCK, BLOCK), F32)], axis=1)
            right = (rest - seen[:BLOCK]) * beta[span]
            new = mm(inverses[at], right).astype(BF16)
            out = seen[BLOCK:] + mm(scores[at], new)
            out_add_ref[span, lanes] = out[:, :BLOCK].astype(BF16)
            out_map_ref[span, lanes] = out[:, BLOCK:].astype(BF16)
            new_add_ref[span, lanes] = new[:, :BLOCK]
            new_map_ref[span, lanes] = new[:, BLOCK:]
            keep_both = jnp.concatenate([keep_last, keep_last], axis=1)
            states[sub] = states[sub] * keep_both + mm_tn(key[span] * last_mask, new)
    for sub in range(len(jobs)):
        end_ref[sub] = states[sub]


def whole_spec(shape):
    return pl.BlockSpec(shape, lambda h: (0,) * len(shape))


def head_spec(rows):
    return pl.BlockSpec((rows, HEADS_STEP * BLOCK), lambda h: (0, h))


def per_head(*tail):
    return pl.BlockSpec((HEADS_STEP,) + tail, lambda h: (h,) + (0,) * len(tail))


def lanes_spec(first, second):
    return pl.BlockSpec((first, second, HEADS_STEP * BLOCK), lambda h: (0, 0, h))


def params():
    return pltpu.CompilerParams(vmem_limit_bytes=VMEM_LIMIT)


def mixer_forward(since, beta_logit, query, key, value, halo, taps):
    rows, width = query.shape
    heads = width // BLOCK
    blocks = rows // BLOCK
    wide = jax.ShapeDtypeStruct((rows, width), BF16)
    return pl.pallas_call(
        forward_kernel,
        grid=(heads // HEADS_STEP,),
        in_specs=[
            whole_spec(since.shape), whole_spec(beta_logit.shape),
            head_spec(rows), head_spec(rows), head_spec(rows),
            lanes_spec(3, PAD), lanes_spec(3, CONV),
        ],
        out_specs=[
            head_spec(rows), head_spec(rows), head_spec(rows), head_spec(rows),
            per_head(blocks, BLOCK, BLOCK), per_head(blocks, BLOCK, 2 * BLOCK),
            per_head(BLOCK, 2 * BLOCK),
        ],
        out_shape=[
            wide, wide, wide, wide,
            jax.ShapeDtypeStruct((heads, blocks, BLOCK, BLOCK), BF16),
            jax.ShapeDtypeStruct((heads, blocks, BLOCK, 2 * BLOCK), BF16),
            jax.ShapeDtypeStruct((heads, BLOCK, 2 * BLOCK), F32),
        ],
        scratch_shapes=[pltpu.VMEM((3 * HEADS_STEP, PAD + rows, BLOCK), F32)],
        compiler_params=params(),
        name="mixer_forward",
    )(since, beta_logit, query, key, value, halo, taps)


def join_kernel(out_add_ref, out_map_ref, entry_ref, gain_ref, mixed_ref):
    for sub in range(HEADS_STEP):
        lanes = slice(sub * BLOCK, (sub + 1) * BLOCK)
        core = out_add_ref[:, lanes].astype(F32) + mm(out_map_ref[:, lanes], entry_ref[sub])
        scale = lax.rsqrt(jnp.mean(core * core, axis=-1, keepdims=True) + 1e-05)
        mixed_ref[:, lanes] = (core * scale * gain_ref[...]).astype(BF16)


def mixer_join(out_add, out_map, entry, gain):
    rows, width = out_add.shape
    heads = width // BLOCK
    return pl.pallas_call(
        join_kernel,
        grid=(heads // HEADS_STEP,),
        in_specs=[head_spec(rows), head_spec(rows), per_head(BLOCK, BLOCK), whole_spec((1, BLOCK))],
        out_specs=head_spec(rows),
        out_shape=jax.ShapeDtypeStruct((rows, width), BF16),
        compiler_params=params(),
        name="mixer_join",
    )(out_add, out_map, entry, gain)


def core_back_kernel(out_add_ref, out_map_ref, entry_ref, gain_ref, up_ref, d_core_ref, start_ref, gain_out_ref):
    @pl.when(pl.program_id(0) == 0)
    def _():
        gain_out_ref[...] = jnp.zeros_like(gain_out_ref)

    for sub in range(HEADS_STEP):
        lanes = slice(sub * BLOCK, (sub + 1) * BLOCK)
        out_map = out_map_ref[:, lanes]
        core = out_add_ref[:, lanes].astype(F32) + mm(out_map, entry_ref[sub])
        scale = lax.rsqrt(jnp.mean(core * core, axis=-1, keepdims=True) + 1e-05)
        unit = core * scale
        up = up_ref[:, lanes].astype(F32)
        gain_out_ref[...] += jnp.sum(up * unit, axis=0, keepdims=True)
        scaled = up * gain_ref[...]
        d_core = scale * (scaled - unit * jnp.mean(scaled * unit, axis=-1, keepdims=True))
        d_core = d_core.astype(BF16)
        d_core_ref[:, lanes] = d_core
        start_ref[sub] = mm_tn(out_map, d_core)


def mixer_core_back(out_add, out_map, entry, gain, up):
    rows, width = out_add.shape
    heads = width // BLOCK
    return pl.pallas_call(
        core_back_kernel,
        grid=(heads // HEADS_STEP,),
        in_specs=[
            head_spec(rows), head_spec(rows), per_head(BLOCK, BLOCK), whole_spec((1, BLOCK)), head_spec(rows),
        ],
        out_specs=[head_spec(rows), per_head(BLOCK, BLOCK), whole_spec((1, BLOCK))],
        out_shape=[
            jax.ShapeDtypeStruct((rows, width), BF16),
            jax.ShapeDtypeStruct((heads, BLOCK, BLOCK), F32),
            jax.ShapeDtypeStruct((1, BLOCK), F32),
        ],
        compiler_params=params(),
        name="mixer_core_back",
    )(out_add, out_map, entry, gain, up)


def backward_heads(
    step, since_ref, beta_ref, query_ref, key_ref, value_ref, halo_ref, taps_ref,
    new_add_ref, new_map_ref, inverse_ref, starts_ref, entry_ref, exit_ref, d_core_ref,
    d_taps_ref, d_beta_ref, ext, back, emit,
):
    rows = since_ref.shape[0]
    blocks = rows // BLOCK
    since = since_ref[...]
    jobs = []
    for sub in range(HEADS_STEP):
        head = step * HEADS_STEP + sub
        lanes = slice(sub * BLOCK, (sub + 1) * BLOCK)
        fronts = []
        for part, ref in enumerate((query_ref, key_ref, value_ref)):
            fronts.append(
                conv_front(
                    ext.at[sub * 3 + part], ref[:, lanes].astype(F32), halo_ref[part, :, lanes],
                    taps_ref[part, :, lanes], since,
                )
            )
        query_unit, query_inv = unit_rows(fronts[0][2])
        key, key_inv = unit_rows(fronts[1][2])
        query = query_unit * (BLOCK ** -0.5)
        beta = 1.0 / (1.0 + jnp.exp(-head_column(beta_ref[...], head)))
        jobs.append((head, lanes, fronts, query, query_unit, query_inv, key, key_inv, beta))

    saved = {}
    for sub, (head, lanes, fronts, query, query_unit, query_inv, key, key_inv, beta) in enumerate(jobs):
        entry = entry_ref[sub].astype(BF16)
        for blk in range(blocks):
            span = slice(blk * BLOCK, (blk + 1) * BLOCK)
            causal, _, keep, last_mask, _ = block_masks(since[span])
            start = starts_ref[sub, blk]
            state = (start[:, :BLOCK].astype(F32) + mm(start[:, BLOCK:], entry)).astype(BF16)
            new = (new_add_ref[span, lanes].astype(F32) + mm(new_map_ref[span, lanes], entry)).astype(BF16)
            scores = jnp.where(causal, mm_nt(query[span], key[span]), 0.0).astype(BF16)
            d_out = d_core_ref[span, lanes]
            d_new = mm_tn(scores, d_out)
            d_state = mm_tn(query[span] * keep, d_out)
            saved[sub, blk] = (state, new, d_out, d_new, d_state)

    carried = [exit_ref[sub].astype(F32) for sub in range(HEADS_STEP)]
    chain = {}
    for blk in reversed(range(blocks)):
        span = slice(blk * BLOCK, (blk + 1) * BLOCK)
        _, _, keep, last_mask, keep_last = block_masks(since[span])
        for sub, (head, lanes, fronts, query, query_unit, query_inv, key, key_inv, beta) in enumerate(jobs):
            state, new, d_out, d_new, d_state = saved[sub, blk]
            after = carried[sub].astype(BF16)
            d_new = d_new + mm(key[span] * last_mask, after)
            d_right = mm_tn(inverse_ref[sub, blk], d_new)
            d_rest = d_right * beta[span]
            carried[sub] = carried[sub] * keep_last + d_state - mm_tn(key[span] * keep, d_rest)
            chain[sub, blk] = (after, d_right, d_rest)

    lane = lax.broadcasted_iota(jnp.int32, (rows, beta_ref.shape[1]), 1)
    d_beta_all = jnp.zeros((rows, beta_ref.shape[1]), F32)
    for sub, (head, lanes, fronts, query, query_unit, query_inv, key, key_inv, beta) in enumerate(jobs):
        d_queries, d_keys, d_values, d_betas = [], [], [], []
        for blk in range(blocks):
            span = slice(blk * BLOCK, (blk + 1) * BLOCK)
            causal, strict, keep, last_mask, _ = block_masks(since[span])
            state, new, d_out, _, _ = saved[sub, blk]
            after, d_right, d_rest = chain[sub, blk]
            both = mm_nt(jnp.concatenate([d_out, d_right.astype(BF16)], axis=0), new)
            d_scores = jnp.where(causal, both[:BLOCK], 0.0).astype(BF16)
            d_gram = (jnp.where(strict, both[BLOCK:], 0.0) * (-beta[span])).astype(BF16)
            key_b = key[span].astype(BF16)
            from_state = mm_nt(jnp.concatenate([d_out, d_rest.astype(BF16)], axis=0), state)
            left = mm(jnp.concatenate([d_scores, d_gram], axis=0), key_b)
            d_queries.append(from_state[:BLOCK] * keep + left[:BLOCK])
            d_key = left[BLOCK:] + mm_tn(
                jnp.concatenate([d_scores, d_gram], axis=0),
                jnp.concatenate([query[span].astype(BF16), key_b], axis=0),
            )
            d_key = d_key + mm_nt(new, after) * last_mask - from_state[BLOCK:] * keep
            d_keys.append(d_key)
            d_values.append(d_rest)
            d_betas.append(
                jnp.sum(d_right * new.astype(F32), axis=1, keepdims=True) * (1.0 - beta[span])
            )
        d_query = jnp.concatenate(d_queries, axis=0) * (BLOCK ** -0.5)
        d_key = jnp.concatenate(d_keys, axis=0)
        d_query = query_inv * (
            d_query - query_unit * jnp.sum(d_query * query_unit, axis=-1, keepdims=True)
        )
        d_key = key_inv * (d_key - key * jnp.sum(d_key * key, axis=-1, keepdims=True))
        d_value = jnp.concatenate(d_values, axis=0)
        d_beta_all = d_beta_all + jnp.where(lane == head, jnp.concatenate(d_betas, axis=0), 0.0)
        for part, d_act in enumerate((d_query, d_key, d_value)):
            pre, gate, _ = fronts[part]
            taps = taps_ref[part, :, lanes]
            source = ext.at[sub * 3 + part]
            d_pre = d_act * gate * (1.0 + pre * (1.0 - gate))
            room = back.at[(sub * 3 + part) % 2]
            total = None
            d_taps = []
            for lag in range(CONV):
                masked = d_pre if lag == 0 else jnp.where(since >= lag, d_pre, 0.0)
                moved = source[PAD - lag : PAD - lag + rows, :]
                d_taps.append(jnp.sum(masked * moved, axis=0, keepdims=True))
                room[lag, 0:PAD, :] = jnp.zeros((PAD, BLOCK), F32)
                room[lag, PAD : PAD + rows, :] = masked * taps[lag : lag + 1, :]
                room[lag, PAD + rows : PAD + rows + PAD, :] = jnp.zeros((PAD, BLOCK), F32)
                term = room[lag, lag : lag + PAD + rows, :]
                total = term if total is None else total + term
            d_taps_ref[part, :, lanes] = jnp.concatenate(d_taps, axis=0)
            emit(part, lanes, total)

    @pl.when(step == 0)
    def _():
        d_beta_ref[...] = d_beta_all

    @pl.when(step > 0)
    def _():
        d_beta_ref[...] += d_beta_all


def backward_kernel(*refs):
    d_proj_ref, d_halo_ref, d_taps_ref, d_beta_ref, ext, back = refs[14:]

    def emit(part, lanes, total):
        d_halo_ref[part, :, lanes] = total[:PAD]
        d_proj_ref[part, :, lanes] = total[PAD:].astype(BF16)

    backward_heads(pl.program_id(0), *refs[:14], d_taps_ref, d_beta_ref, ext, back, emit)


def mixer_backward(
    since, beta_logit, query, key, value, halo, taps, new_add, new_map, inverse, starts, entry, exit_grad, d_core
):
    rows, width = query.shape
    heads = width // BLOCK
    blocks = rows // BLOCK
    return pl.pallas_call(
        backward_kernel,
        grid=(heads // HEADS_STEP,),
        in_specs=[
            whole_spec(since.shape), whole_spec(beta_logit.shape),
            head_spec(rows), head_spec(rows), head_spec(rows),
            lanes_spec(3, PAD), lanes_spec(3, CONV),
            head_spec(rows), head_spec(rows),
            per_head(blocks, BLOCK, BLOCK), per_head(blocks, BLOCK, 2 * BLOCK),
            per_head(BLOCK, BLOCK), per_head(BLOCK, BLOCK), head_spec(rows),
        ],
        out_specs=[
            lanes_spec(3, rows), lanes_spec(3, PAD), lanes_spec(3, CONV), whole_spec(beta_logit.shape),
        ],
        out_shape=[
            jax.ShapeDtypeStruct((3, rows, width), BF16),
            jax.ShapeDtypeStruct((3, PAD, width), F32),
            jax.ShapeDtypeStruct((3, CONV, width), F32),
            jax.ShapeDtypeStruct(beta_logit.shape, F32),
        ],
        scratch_shapes=[
            pltpu.VMEM((3 * HEADS_STEP, PAD + rows, BLOCK), F32),
            pltpu.VMEM((2, CONV, PAD + rows + PAD, BLOCK), F32),
        ],
        compiler_params=params(),
        name="mixer_backward",
    )(
        since, beta_logit, query, key, value, halo, taps, new_add, new_map, inverse, starts, entry, exit_grad, d_core
    )


GROUPS = 4
HALVES = 2


def chain_kernel(axis, forward, map_ref, add_ref, out_ref, sent, landed, send_sem, recv_sem):
    count = lax.axis_size(axis)
    me = lax.axis_index(axis)
    heads = add_ref.shape[0]
    step = heads // GROUPS
    up, down = (me + 1, me - 1) if forward else (me - 1, me + 1)
    first, last = (0, count - 1) if forward else (count - 1, 0)
    barrier = pltpu.get_barrier_semaphore()

    @pl.when(me != first)
    def _():
        pl.semaphore_signal(barrier, inc=1, device_id={axis: down}, device_id_type=MESH)

    @pl.when(me != last)
    def _():
        pl.semaphore_wait(barrier, 1)

    def copy(group, target):
        return pltpu.make_async_remote_copy(
            src_ref=sent.at[group],
            dst_ref=landed.at[group],
            send_sem=send_sem.at[group],
            recv_sem=recv_sem.at[group],
            device_id={axis: target},
            device_id_type=MESH,
        )

    for group in range(GROUPS):
        @pl.when(me != first)
        def _():
            copy(group, up).wait_recv()
            for sub in range(step):
                head = group * step + sub
                out_ref[head] = landed[group, sub].astype(F32)

        @pl.when(me == first)
        def _():
            out_ref[group * step : (group + 1) * step] = jnp.zeros((step,) + out_ref.shape[1:], F32)

        @pl.when(me != last)
        def _():
            for sub in range(step):
                head = group * step + sub
                if forward:
                    moved = mm(map_ref[head], out_ref[head])
                else:
                    moved = mm_tn(map_ref[head], out_ref[head])
                sent[group, sub] = (moved + add_ref[head]).astype(BF16)
            copy(group, up).start()

    @pl.when(me != last)
    def _():
        for group in range(GROUPS):
            copy(group, up).wait_send()


def carry_chain(map_part, add_part, axis, forward):
    heads = add_part.shape[0]
    part = (GROUPS, heads // GROUPS, BLOCK, BLOCK)
    return pl.pallas_call(
        functools.partial(chain_kernel, axis, forward),
        in_specs=[pl.BlockSpec(memory_space=pltpu.VMEM)] * 2,
        out_specs=pl.BlockSpec(memory_space=pltpu.VMEM),
        out_shape=jax.ShapeDtypeStruct(add_part.shape, F32),
        scratch_shapes=[
            pltpu.VMEM(part, BF16),
            pltpu.VMEM(part, BF16),
            pltpu.SemaphoreType.DMA((GROUPS,)),
            pltpu.SemaphoreType.DMA((GROUPS,)),
        ],
        compiler_params=pltpu.CompilerParams(
            collective_id=1 if forward else 2, has_side_effects=True, vmem_limit_bytes=VMEM_LIMIT // 2
        ),
        name="carry_forward" if forward else "carry_backward",
    )(map_part, add_part)


def bits(dp):
    core, x, y = dp % 2, (dp // 2) % 2, dp // 4
    return core, x, y, dp + 1 - 2 * core, dp + 2 * (1 - 2 * x), dp + 4 * (1 - 2 * y)


def remote(src, dst, send_sem, recv_sem, target):
    return pltpu.make_async_remote_copy(
        src_ref=src, dst_ref=dst, send_sem=send_sem, recv_sem=recv_sem, device_id=target, device_id_type=MESH
    )


def meet(dp_targets, narrow_targets):
    barrier = pltpu.get_barrier_semaphore()
    for target in dp_targets:
        pl.semaphore_signal(barrier, inc=1, device_id={"dp": target}, device_id_type=MESH)
    for target in narrow_targets:
        pl.semaphore_signal(barrier, inc=1, device_id={"narrow": target}, device_id_type=MESH)
    pl.semaphore_wait(barrier, len(dp_targets) + len(narrow_targets))


def add_rows(dst, src, step):
    def one(at, _):
        at = pl.ds(pl.multiple_of(at * step, step), step)
        dst[at, :] = (dst[at, :].astype(F32) + src[at, :].astype(F32)).astype(dst.dtype)
        return 0

    lax.fori_loop(0, dst.shape[0] // step, one, 0)


def small_kernel(small_ref, out_ref, landed, total, got2, got3, gotz, send1, recv1, send2, recv2, send3, recv3, sendz, recvz):
    dp, z = lax.axis_index("dp"), lax.axis_index("narrow")
    core, x, y, sib, flip_x, flip_y = bits(dp)
    depth = lax.axis_size("narrow")
    rows = small_ref.shape[0] // 8
    share = rows // depth
    peers = [(z + step) % depth for step in range(1, depth)]
    meet((sib, flip_x, flip_y), peers)

    def stripe_rows(stripe, which):
        return pl.ds(pl.multiple_of((stripe * 2 + which) * rows, rows), rows)

    def share_rows(at):
        return pl.ds(pl.multiple_of(at * share, share), share)

    first = [
        remote(small_ref.at[stripe_rows(k, 1 - core)], landed.at[k], send1.at[k], recv1.at[k], {"dp": sib})
        for k in range(4)
    ]
    for copy in first:
        copy.start()
    for k in range(4):
        first[k].wait()
        total[k] = small_ref[stripe_rows(k, core), :] + landed[k]
    second = [
        remote(total.at[2 * j + 1 - x], got2.at[j], send2.at[j], recv2.at[j], {"dp": flip_x}) for j in range(2)
    ]
    for copy in second:
        copy.start()
    for copy in second:
        copy.wait()
    third = remote(total.at[2 * (1 - y) + x], got3, send3, recv3, {"dp": flip_y})
    total[2 * (1 - y) + x] = total[2 * (1 - y) + x] + got2[1 - y]
    third.start()
    third.wait()
    mine = 2 * y + x
    total[mine] = total[mine] + got2[y] + got3[...]
    last = [
        remote(total.at[mine, share_rows(to)], gotz.at[k], sendz.at[k], recvz.at[k], {"narrow": to})
        for k, to in enumerate(peers)
    ]
    for copy in last:
        copy.start()
    value = total[mine, share_rows(z), :]
    for k, copy in enumerate(last):
        copy.wait()
        value = value + gotz[k]
    out_ref[...] = value


def reduce_small(small):
    height, lanes = small.shape
    depth = lax.axis_size("narrow")
    rows = height // 8
    share = rows // depth
    dma = pltpu.SemaphoreType.DMA
    return pl.pallas_call(
        small_kernel,
        in_specs=[pl.BlockSpec(memory_space=pltpu.VMEM)],
        out_specs=pl.BlockSpec(memory_space=pltpu.VMEM),
        out_shape=jax.ShapeDtypeStruct((share, lanes), F32),
        scratch_shapes=[
            pltpu.VMEM((4, rows, lanes), F32),
            pltpu.VMEM((4, rows, lanes), F32),
            pltpu.VMEM((2, rows, lanes), F32),
            pltpu.VMEM((rows, lanes), F32),
            pltpu.VMEM((depth - 1, share, lanes), F32),
            dma((4,)), dma((4,)), dma((2,)), dma((2,)), dma(()), dma(()), dma((depth - 1,)), dma((depth - 1,)),
        ],
        compiler_params=pltpu.CompilerParams(
            collective_id=3, has_side_effects=True, vmem_limit_bytes=16 * 1024 * 1024
        ),
        name="reduce_small",
    )(small)


RING = 3
HELD = 6


def fused_kernel(*refs):
    heads_in = refs[:14]
    since_ref = refs[0]
    (
        w_query_ref, w_key_ref, w_value_ref, normed_hbm,
        grad_hbm, d_normed_hbm, d_taps_ref, d_beta_ref,
        ext, back, left_own, left_away, left_sib, d_proj, d_proj_sib, halo_out, halo_in,
        total, got2, got3, gotz, d_normed, grad,
        local_sem, left_send, left_recv, right_send, right_recv, halo_send, halo_recv,
        send2, recv2, send3, recv3, sendz, recvz,
    ) = refs[14:]
    step = pl.program_id(0)
    units = pl.num_programs(0) - 1
    dp, z = lax.axis_index("dp"), lax.axis_index("narrow")
    core, x, y, sib, flip_x, flip_y = bits(dp)
    depth = lax.axis_size("narrow")
    tokens = since_ref.shape[0]
    rows = left_own.shape[1]
    cols = d_proj.shape[3]
    share = rows // depth
    peers = [(z + k) % depth for k in range(1, depth)]

    def stripe_lanes(stripe, which):
        return pl.ds(pl.multiple_of((stripe * 2 + which) * rows, rows), rows)

    def left_copy(stripe):
        return remote(
            left_away.at[stripe], left_sib.at[stripe], left_send.at[stripe], left_recv.at[stripe], {"dp": sib}
        )

    def right_copy(unit):
        return remote(
            d_proj.at[unit % RING], d_proj_sib.at[unit % RING],
            right_send.at[unit % RING], right_recv.at[unit % RING], {"dp": sib},
        )

    def halo_copy(unit):
        return remote(
            halo_out.at[unit], halo_in.at[unit], halo_send.at[unit], halo_recv.at[unit], {"narrow": z - 1}
        )

    def order(unit):
        e = unit % 2

        def pick(even, odd):
            return (1 - e) * even + e * odd

        def away(j):
            return pick(2 * j + 1 - x, 2 * (1 - y) + j)

        def kept(j):
            return pick(2 * j + x, 2 * y + j)

        return away, kept, pick(flip_x, flip_y), pick(flip_y, flip_x), pick(1 - y, 1 - x), pick(y, x)

    def copy2(unit, j):
        away, _, target, _, _, _ = order(unit)
        return remote(total.at[unit % HELD, away(j)], got2.at[unit, j], send2.at[unit, j], recv2.at[unit, j], {"dp": target})

    def copy3(unit):
        _, kept, _, target, far, _ = order(unit)
        return remote(total.at[unit % HELD, kept(far)], got3.at[unit], send3.at[unit], recv3.at[unit], {"dp": target})

    def copyz(unit, part, k):
        _, kept, _, _, _, near = order(unit)
        at = pl.ds(pl.multiple_of(part * rows + peers[k] * share, share), share)
        return remote(
            total.at[unit % HELD, kept(near), at], gotz.at[unit, k, part * share : (part + 1) * share],
            sendz.at[unit, k, part], recvz.at[unit, k, part], {"narrow": peers[k]},
        )

    @pl.when(step == 0)
    def _():
        loads = [
            pltpu.make_async_copy(
                normed_hbm.at[:, stripe_lanes(k % 4, 1 - core if k < 4 else core)], d_proj.at[k // 3, k % 3], local_sem.at[k]
            )
            for k in range(8)
        ]
        for load in loads:
            load.start()
        back[:, :, 0:PAD, :] = jnp.zeros((2, CONV, PAD, BLOCK), F32)
        back[:, :, PAD + tokens :, :] = jnp.zeros((2, CONV, PAD, BLOCK), F32)
        d_normed[...] = jnp.zeros_like(d_normed)
        meet((sib, flip_x, flip_y), peers)
        for stripe in range(4):
            loads[stripe].wait()
            left_away[stripe] = d_proj[stripe // 3, stripe % 3].astype(F32).T.astype(BF16)
            left_copy(stripe).start()
        for stripe in range(4):
            loads[4 + stripe].wait()
            left_own[stripe] = d_proj[(4 + stripe) // 3, (4 + stripe) % 3].astype(F32).T.astype(BF16)

    @pl.when(step >= 1)
    def _():
        unit = step - 1

        @pl.when(z < depth - 1)
        def _():
            halo_copy(unit).wait_recv()
            for part in range(3):
                extra = jnp.concatenate([jnp.zeros((PAD, cols), F32), halo_in[unit, part]], axis=0)
                tail = slice(tokens - 2 * PAD, tokens)
                d_proj[unit % RING, part, tail, :] = (
                    d_proj[unit % RING, part, tail, :].astype(F32) + extra
                ).astype(BF16)

        @pl.when(z > 0)
        def _():
            halo_copy(unit).wait_send()

        right_copy(unit).start()

    @pl.when(step < units)
    def _():
        def emit(part, lanes, value):
            halo_out[step, part, :, lanes] = value[:PAD]
            d_proj[step % RING, part, :, lanes] = value[PAD:].astype(BF16)

        backward_heads(step, *heads_in, d_taps_ref, d_beta_ref, ext, back, emit)

        @pl.when(z > 0)
        def _():
            halo_copy(step).start()

    @pl.when(step == 1)
    def _():
        for stripe in range(4):
            left_copy(stripe).wait()

    @pl.when(step >= 1)
    def _():
        unit = step - 1
        away, kept, _, _, _, _ = order(unit)
        right_copy(unit).wait()

        def one(k, _):
            j = k % 2
            stripe = (k // 2) * kept(j) + (1 - k // 2) * away(j)
            for part in range(3):
                value = jnp.dot(left_own[stripe], d_proj[unit % RING, part], preferred_element_type=F32)
                value = value + jnp.dot(left_sib[stripe], d_proj_sib[unit % RING, part], preferred_element_type=F32)
                total[unit % HELD, stripe, part * rows : (part + 1) * rows, :] = value.astype(BF16)

            @pl.when(k < 2)
            def _():
                copy2(unit, j).start()

            return 0

        lax.fori_loop(0, 4, one, 0)

        def normed_part(at, _):
            at = pl.ds(pl.multiple_of(at * 512, 512), 512)
            value = d_normed[:, at]
            for part, ref in enumerate((w_query_ref, w_key_ref, w_value_ref)):
                value = value + lax.dot_general(
                    d_proj[unit % RING, part], ref[at, :], (((1,), (1,)), ((), ())), preferred_element_type=F32
                )
            d_normed[:, at] = value
            return 0

        lax.fori_loop(0, d_normed.shape[1] // 512, normed_part, 0)

    def second(unit):
        _, kept, _, _, far, near = order(unit)
        for j in range(2):
            copy2(unit, j).wait()
        add_rows(total.at[unit % HELD, kept(far)], got2.at[unit, far], 64)
        copy3(unit).start()
        add_rows(total.at[unit % HELD, kept(near)], got2.at[unit, near], 64)

    def third(unit):
        _, kept, _, _, _, near = order(unit)
        copy3(unit).wait()
        add_rows(total.at[unit % HELD, kept(near)], got3.at[unit], 64)
        for k in range(depth - 1):
            for part in range(3):
                copyz(unit, part, k).start()

    def fourth(unit):
        _, kept, _, _, _, near = order(unit)
        for k in range(depth - 1):
            for part in range(3):
                copyz(unit, part, k).wait()
        for part in range(3):
            at = pl.ds(pl.multiple_of(part * rows + z * share, share), share)
            value = total[unit % HELD, kept(near), at, :].astype(F32)
            for k in range(depth - 1):
                value = value + gotz[unit, k, part * share : (part + 1) * share, :].astype(F32)
            grad[part, :, pl.ds(pl.multiple_of(unit * cols, cols), cols)] = value

    def stages(at):
        @pl.when((at >= 3) & (at < units + 3))
        def _():
            second(at - 3)

        @pl.when((at >= 4) & (at < units + 4))
        def _():
            third(at - 4)

        @pl.when(at >= 5)
        def _():
            fourth(at - 5)

    stages(step)

    @pl.when(step == units)
    def _():
        save = pltpu.make_async_copy(d_normed, d_normed_hbm, local_sem.at[0])
        save.start()

        def one(at, _):
            stages(at)
            return 0

        lax.fori_loop(units + 1, units + 5, one, 0)
        save.wait()
        store = pltpu.make_async_copy(grad, grad_hbm, local_sem.at[1])
        store.start()
        store.wait()


def fused_backward(
    since, beta_logit, query, key, value, halo, taps, new_add, new_map, inverse, starts, entry, exit_grad, d_core,
    w_query, w_key, w_value, normed,
):
    tokens, width = query.shape
    heads = width // BLOCK
    blocks = tokens // BLOCK
    units = heads // HEADS_STEP
    cols = HEADS_STEP * BLOCK
    depth = lax.axis_size("narrow")
    rows = width // 8
    share = rows // depth
    dma = pltpu.SemaphoreType.DMA

    def now(step):
        return jnp.minimum(step, units - 1)

    def before(step):
        return jnp.maximum(step - 1, 0)

    def whole(shape):
        return pl.BlockSpec(shape, lambda h: (0,) * len(shape))

    wide = pl.BlockSpec((tokens, cols), lambda h: (0, now(h)))

    def lanes(first, second):
        return pl.BlockSpec((first, second, cols), lambda h: (0, 0, now(h)))

    def each(*tail):
        return pl.BlockSpec((HEADS_STEP,) + tail, lambda h: (now(h),) + (0,) * len(tail))

    weight = pl.BlockSpec((width, cols), lambda h: (0, before(h)))
    anywhere = pl.BlockSpec(memory_space=pl.ANY)
    return pl.pallas_call(
        fused_kernel,
        grid=(units + 1,),
        in_specs=[
            whole(since.shape), whole(beta_logit.shape), wide, wide, wide, lanes(3, PAD), lanes(3, CONV),
            wide, wide, each(blocks, BLOCK, BLOCK), each(blocks, BLOCK, 2 * BLOCK),
            each(BLOCK, BLOCK), each(BLOCK, BLOCK), wide,
            weight, weight, weight, anywhere,
        ],
        out_specs=[anywhere, anywhere, lanes(3, CONV), whole(beta_logit.shape)],
        out_shape=[
            jax.ShapeDtypeStruct((3, share, width), F32),
            jax.ShapeDtypeStruct((tokens, width), F32),
            jax.ShapeDtypeStruct((3, CONV, width), F32),
            jax.ShapeDtypeStruct(beta_logit.shape, F32),
        ],
        scratch_shapes=[
            pltpu.VMEM((3 * HEADS_STEP, PAD + tokens, BLOCK), F32),
            pltpu.VMEM((2, CONV, PAD + tokens + PAD, BLOCK), F32),
            pltpu.VMEM((4, rows, tokens), BF16),
            pltpu.VMEM((4, rows, tokens), BF16),
            pltpu.VMEM((4, rows, tokens), BF16),
            pltpu.VMEM((RING, 3, tokens, cols), BF16),
            pltpu.VMEM((RING, 3, tokens, cols), BF16),
            pltpu.VMEM((units, 3, PAD, cols), F32),
            pltpu.VMEM((units, 3, PAD, cols), F32),
            pltpu.VMEM((HELD, 4, 3 * rows, cols), BF16),
            pltpu.VMEM((units, 2, 3 * rows, cols), BF16),
            pltpu.VMEM((units, 3 * rows, cols), BF16),
            pltpu.VMEM((units, depth - 1, 3 * share, cols), BF16),
            pltpu.VMEM((tokens, width), F32),
            pltpu.VMEM((3, share, width), F32),
            dma((8,)), dma((4,)), dma((4,)), dma((RING,)), dma((RING,)), dma((units,)), dma((units,)),
            dma((units, 2)), dma((units, 2)), dma((units,)), dma((units,)),
            dma((units, depth - 1, 3)), dma((units, depth - 1, 3)),
        ],
        compiler_params=pltpu.CompilerParams(
            collective_id=5, has_side_effects=True, vmem_limit_bytes=61 * 1024 * 1024
        ),
        name="fused_backward",
    )(
        since, beta_logit, query, key, value, halo, taps, new_add, new_map, inverse, starts, entry, exit_grad, d_core,
        w_query, w_key, w_value, normed,
    )


def ffn_grads_kernel(*refs):
    lefts = [refs[0:HALVES], refs[0:HALVES], refs[HALVES : 2 * HALVES]]
    rights = [refs[(2 + m) * HALVES : (3 + m) * HALVES] for m in range(3)]
    (
        out_ref, left_buf, right_buf, away, landed, total, got2, got3,
        left_sem, right_sem, send1, recv1, send2, recv2, send3, recv3,
    ) = refs[5 * HALVES :]
    dp = lax.axis_index("dp")
    core, x, y = dp % 2, (dp // 2) % 2, dp // 4
    rows = total.shape[2]
    half = rows // 2
    part = left_buf.shape[1] // HALVES
    sib = dp + 1 - 2 * core
    flip_x = dp + 2 * (1 - 2 * x)
    flip_y = dp + 4 * (1 - 2 * y)
    barrier = pltpu.get_barrier_semaphore()
    for target in (sib, flip_x, flip_y):
        pl.semaphore_signal(barrier, inc=1, device_id={"dp": target}, device_id_type=MESH)

    def load_left(m, k, start):
        own = k // 4
        block = (k % 4) * 2 + own * core + (1 - own) * (1 - core)
        lanes = pl.ds(pl.multiple_of(block * rows, rows), rows)
        for at in range(HALVES):
            copy = pltpu.make_async_copy(
                lefts[m][at].at[:, lanes], left_buf.at[k % 2, at * part : (at + 1) * part], left_sem.at[k % 2, at]
            )
            if start:
                copy.start()
            else:
                copy.wait()

    def load_right(m, start):
        for at in range(HALVES):
            copy = pltpu.make_async_copy(
                rights[m][at], right_buf.at[m % 2, at * part : (at + 1) * part], right_sem.at[m % 2, at]
            )
            if start:
                copy.start()
            else:
                copy.wait()

    def send(src, dst, send_sem, recv_sem, target):
        return pltpu.make_async_remote_copy(
            src_ref=src, dst_ref=dst, send_sem=send_sem, recv_sem=recv_sem,
            device_id={"dp": target}, device_id_type=MESH,
        )

    def copy1(m, stripe):
        return send(away.at[m, stripe], landed.at[m, stripe], send1.at[m, stripe], recv1.at[m, stripe], sib)

    def band(h):
        return pl.ds(h * half, half)

    def order(h):
        if h == 0:
            return (lambda j: 2 * j + 1 - x), (lambda j: 2 * j + x), flip_x, flip_y, 1 - y, y
        return (lambda j: 2 * (1 - y) + j), (lambda j: 2 * y + j), flip_y, flip_x, 1 - x, x

    def copy2(m, h, j):
        gone, _, target, _, _, _ = order(h)
        return send(
            total.at[m, gone(j), band(h)], got2.at[m, h, j], send2.at[2 * m + h, j], recv2.at[2 * m + h, j], target
        )

    def copy3(m, h):
        _, kept, _, target, far, _ = order(h)
        return send(total.at[m, kept(far), band(h)], got3.at[m, h], send3.at[m, h], recv3.at[m, h], target)

    def add_to(dst, src):
        step = 32

        def one(at, _):
            at = pl.ds(pl.multiple_of(at * step, step), step)
            dst[at, :] = (dst[at, :].astype(F32) + src[at, :].astype(F32)).astype(dst.dtype)
            return 0

        lax.fori_loop(0, dst.shape[0] // step, one, 0)

    def compute(m):
        load_right(m, False)
        if m + 1 < 3:
            load_right(m + 1, True)

        def one(k, _):
            @pl.when(k < 7)
            def _():
                load_left(m, k + 1, True)

            if m + 1 < 3:
                @pl.when(k == 7)
                def _():
                    load_left(m + 1, 0, True)

            load_left(m, k, False)
            value = lax.dot_general(
                left_buf[k % 2], right_buf[m % 2], (((0,), (0,)), ((), ())), preferred_element_type=F32
            ).astype(BF16)

            @pl.when(k < 4)
            def _():
                away[m, k] = value
                copy1(m, k).start()

            @pl.when(k >= 4)
            def _():
                total[m, k - 4] = value

            return 0

        lax.fori_loop(0, 8, one, 0)

        def join(stripe, _):
            copy1(m, stripe).wait()
            add_to(total.at[m, stripe], landed.at[m, stripe])
            return 0

        lax.fori_loop(0, 4, join, 0)
        for h in range(2):
            for j in range(2):
                copy2(m, h, j).start()

    def second(m):
        for h in range(2):
            _, kept, _, _, far, near = order(h)
            for j in range(2):
                copy2(m, h, j).wait()
            add_to(total.at[m, kept(far), band(h)], got2.at[m, h, far])
            copy3(m, h).start()
            add_to(total.at[m, kept(near), band(h)], got2.at[m, h, near])

    def third(m):
        for h in range(2):
            _, kept, _, _, _, near = order(h)
            copy3(m, h).wait()
            step = 32

            def one(at, _):
                at = at * step
                value = total[m, kept(near), pl.ds(pl.multiple_of(h * half + at, step), step), :].astype(F32)
                value = value + got3[m, h, pl.ds(pl.multiple_of(at, step), step), :].astype(F32)
                out_ref[m, pl.ds(pl.multiple_of(h * half + at, step), step), :] = value
                return 0

            lax.fori_loop(0, half // step, one, 0)

    load_right(0, True)
    load_left(0, 0, True)
    pl.semaphore_wait(barrier, 3)
    compute(0)
    compute(1)
    second(0)
    compute(2)
    third(0)
    second(1)
    third(1)
    second(2)
    third(2)


def ffn_grads(lefts, rights):
    part, height = lefts[0][0].shape
    width = rights[0][0].shape[1]
    rows = height // 8
    half = rows // 2
    dma = pltpu.SemaphoreType.DMA
    operands = [ref for group in (*lefts, *rights) for ref in group]
    return pl.pallas_call(
        ffn_grads_kernel,
        in_specs=[pl.BlockSpec(memory_space=pl.ANY)] * len(operands),
        out_specs=pl.BlockSpec(memory_space=pltpu.VMEM),
        out_shape=jax.ShapeDtypeStruct((3, rows, width), F32),
        scratch_shapes=[
            pltpu.VMEM((2, HALVES * part, rows), BF16),
            pltpu.VMEM((2, HALVES * part, width), BF16),
            pltpu.VMEM((3, 4, rows, width), BF16),
            pltpu.VMEM((3, 4, rows, width), BF16),
            pltpu.VMEM((3, 4, rows, width), BF16),
            pltpu.VMEM((3, 2, 2, half, width), BF16),
            pltpu.VMEM((3, 2, half, width), BF16),
            dma((2, HALVES)), dma((2, HALVES)), dma((3, 4)), dma((3, 4)),
            dma((6, 2)), dma((6, 2)), dma((3, 2)), dma((3, 2)),
        ],
        compiler_params=pltpu.CompilerParams(
            collective_id=4, has_side_effects=True, vmem_limit_bytes=60 * 1024 * 1024
        ),
        name="ffn_grads",
    )(*operands)


def shifted(value, axis, steps):
    count = lax.axis_size(axis)
    first, last = (max(0, -steps), min(count, count - steps))
    return lax.ppermute(value, axis, [(source, source + steps) for source in range(first, last)])


def matmul(left, right):
    return jnp.dot(left, right, preferred_element_type=F32)


def dot_tn(left, right):
    return jnp.einsum("rd,re->de", left, right, preferred_element_type=F32)


def dot_nt(left, right):
    return jnp.einsum("re,de->rd", left, right, preferred_element_type=F32)


def rms_scale(value_in, gain_vec, epsilon):
    return value_in * lax.rsqrt(jnp.mean(value_in * value_in, axis=-1, keepdims=True) + epsilon) * gain_vec


def norm_back(value_in, gain_vec, upstream, epsilon):
    inv_scale = lax.rsqrt(jnp.mean(value_in * value_in, axis=-1, keepdims=True) + epsilon)
    scaled_up = upstream * gain_vec
    gain_term = jnp.sum(upstream * value_in * inv_scale, axis=0)
    cubed = inv_scale * inv_scale * inv_scale
    back_value = inv_scale * scaled_up - value_in * cubed * jnp.mean(
        scaled_up * value_in, axis=-1, keepdims=True
    )
    return (back_value, gain_term)


def since_start(doc_lengths, offset, rows):
    ends = jnp.cumsum(doc_lengths[0])
    position = offset + jnp.arange(rows, dtype=jnp.int32)
    starts = jnp.max(jnp.where(position[:, None] >= ends[None, :], ends[None, :], 0), axis=1)
    return jnp.broadcast_to((position - starts)[:, None], (rows, BLOCK)).astype(jnp.int32)


def scatter_all(value, dim):
    part = lax.psum_scatter(value, "dp", scatter_dimension=dim, tiled=True)
    return lax.psum_scatter(part, "narrow", scatter_dimension=dim, tiled=True)


def local(
    tokens,
    doc_lengths,
    attn_gain,
    w_query,
    w_key,
    w_value,
    w_beta,
    conv_weight,
    out_gain,
    w_out,
    mlp_gain,
    w_gate,
    w_up,
    w_down,
    grad_out,
):
    tok_rows, model_width = tokens.shape
    offset = lax.axis_index("narrow") * tok_rows
    half = tok_rows // HALVES
    parts = [slice(at * half, (at + 1) * half) for at in range(HALVES)]

    def gather(rows):
        return lax.all_gather(rows, "narrow", axis=0, tiled=True)

    def scatter(rows):
        return lax.psum_scatter(rows, "narrow", scatter_dimension=0, tiled=True)

    cot = gather(grad_out)
    since = since_start(doc_lengths, offset, tok_rows)
    inputs = tokens.astype(F32)
    normed = rms_scale(inputs, attn_gain, 1e-06).astype(BF16)
    query, key, value = (matmul(normed, w) for w in (w_query, w_key, w_value))
    beta_logit = matmul(normed, w_beta)
    halo = shifted(
        jnp.stack([part[tok_rows - PAD :].astype(BF16) for part in (query, key, value)]), "narrow", 1
    )
    out_add, out_map, new_add, new_map, inverse, starts, end = mixer_forward(
        since, beta_logit, query, key, value, halo, conv_weight
    )
    transfer = end[:, :, BLOCK:].astype(BF16)
    entry = carry_chain(transfer, end[:, :, :BLOCK], "narrow", True)
    gain_row = out_gain[None, :]
    attn_mixed = mixer_join(out_add, out_map, entry, gain_row)
    hidden = inputs + matmul(attn_mixed, w_out)
    normed_mlp = rms_scale(hidden, mlp_gain, 1e-06).astype(BF16)
    normed_mlp, cot = lax.optimization_barrier((normed_mlp, cot))
    cot = cot.reshape(-1, tok_rows, model_width)
    cot = [cot[:, part].reshape(-1, model_width) for part in parts]
    gathered = [gather(normed_mlp[part]) for part in parts]
    activation, d_gate, d_up, d_normed_parts = [], [], [], []
    for at in range(HALVES):
        gate_proj = matmul(gathered[at], w_gate)
        up_proj = matmul(gathered[at], w_up)
        gate_sigmoid = jax.nn.sigmoid(gate_proj)
        silu_gate = gate_proj * gate_sigmoid
        activation.append((silu_gate * up_proj).astype(BF16))
        d_act = jnp.einsum("rd,fd->rf", cot[at], w_down, preferred_element_type=F32)
        d_gate.append(
            (d_act * up_proj * gate_sigmoid * (1.0 + gate_proj * (1.0 - gate_sigmoid))).astype(BF16)
        )
        d_up.append((d_act * silu_gate).astype(BF16))
        d_normed_parts.append(scatter((dot_nt(d_gate[at], w_gate) + dot_nt(d_up[at], w_up)).astype(BF16)))
    out_parts = [matmul(act, w_down).astype(BF16) for act in activation]
    if lax.axis_size("dp") == 8:
        ffn_sums = ffn_grads((gathered, cot), (d_gate, d_up, activation))
    else:
        ffn_sums = [
            lax.psum_scatter(
                sum(dot_tn(a, c) for a, c in zip(left, right)).astype(BF16), "dp", scatter_dimension=0, tiled=True
            )
            for left, right in ((gathered, d_gate), (gathered, d_up), (cot, activation))
        ]
    d_normed_parts, out_parts, ffn_sums = lax.optimization_barrier((d_normed_parts, out_parts, ffn_sums))
    grad_gate, grad_up, grad_down = ffn_sums[0].astype(F32), ffn_sums[1].astype(F32), ffn_sums[2].astype(F32).T
    d_normed_mlp = jnp.concatenate(d_normed_parts, axis=0).astype(F32)
    d_hidden_norm, mlp_gain_term = norm_back(hidden, mlp_gain, d_normed_mlp, 1e-06)
    d_hidden = grad_out.astype(F32) + d_hidden_norm
    d_branch = d_hidden.astype(BF16)
    w_out_term = dot_tn(d_branch, attn_mixed).astype(BF16)
    d_mixed = dot_nt(d_branch, w_out)
    d_core, start_grad, out_gain_term = mixer_core_back(out_add, out_map, entry, gain_row, d_mixed)
    exit_grad = carry_chain(transfer, start_grad, "narrow", False)
    exit_grad, out_parts = lax.optimization_barrier((exit_grad, out_parts))
    w_out_term = scatter_all(w_out_term, 0)
    ffn_parts = [scatter(part) for part in out_parts]
    mixer_args = (
        since, beta_logit, query, key, value, halo, conv_weight,
        new_add, new_map, inverse, starts, entry, exit_grad, d_core,
    )
    if lax.axis_size("dp") == 8:
        grads, d_normed, conv_term, d_beta = fused_backward(*mixer_args, w_query, w_key, w_value, normed)
    else:
        d_proj, d_halo, conv_term, d_beta = mixer_backward(*mixer_args)
        after = shifted(d_halo.astype(BF16), "narrow", -1)
        d_proj = d_proj.at[:, tok_rows - PAD :].add(after)
        d_normed = sum(dot_nt(part, w) for part, w in zip(d_proj, (w_query, w_key, w_value)))
        grads = jnp.stack([scatter_all(dot_tn(normed, part).astype(BF16), 0).astype(F32) for part in d_proj])
    d_beta_low = d_beta.astype(BF16)
    beta_term = jnp.einsum("rd,rh->dh", normed, d_beta_low, preferred_element_type=F32)
    d_normed = d_normed + jnp.einsum("rh,dh->rd", d_beta_low, w_beta, preferred_element_type=F32)
    d_input_norm, attn_gain_term = norm_back(inputs, attn_gain, d_normed, 1e-06)
    grad_tokens = (d_hidden + d_input_norm).astype(BF16)
    devices = lax.axis_size("dp") * lax.axis_size("narrow")
    heads = w_beta.shape[1]
    taps = 3 * CONV
    gain_share = BLOCK // devices
    gain_column = jnp.pad(
        out_gain_term.reshape(devices, gain_share), ((0, 0), (0, model_width // devices - gain_share))
    ).reshape(model_width, 1)
    small = jnp.concatenate(
        [
            beta_term,
            conv_term.reshape(taps, model_width).T,
            attn_gain_term[:, None],
            mlp_gain_term[:, None],
            gain_column,
        ],
        axis=1,
    )
    small = jnp.pad(small, ((0, 0), (0, BLOCK - small.shape[1])))
    if lax.axis_size("dp") == 8:
        small = reduce_small(small)
    else:
        small = lax.psum_scatter(small, ("dp", "narrow"), scatter_dimension=0, tiled=True)
    grad_beta = small[:, :heads]
    grad_conv = small[:, heads : heads + taps].T.reshape(3, CONV, -1)
    grad_attn_gain = small[:, heads + taps]
    grad_mlp_gain = small[:, heads + taps + 1]
    grad_out_gain = small[:gain_share, heads + taps + 2]
    ffn_parts, w_out_term, grads = lax.optimization_barrier((ffn_parts, w_out_term, grads))
    block_out = (hidden + jnp.concatenate(ffn_parts, axis=0).astype(F32)).astype(BF16)
    grad_query, grad_key, grad_value = grads[0], grads[1], grads[2]
    grad_w_out = w_out_term.astype(F32).T
    return (
        block_out,
        grad_tokens,
        grad_attn_gain,
        grad_query,
        grad_key,
        grad_value,
        grad_beta,
        grad_conv,
        grad_out_gain,
        grad_w_out,
        grad_mlp_gain,
        grad_gate,
        grad_up,
        grad_down,
    )


def solution(mesh):
    placed = (
        P(("dp", "narrow"), None),
        P("dp", None),
        P(),
        P(),
        P(),
        P(),
        P(),
        P(),
        P(),
        P(),
        P(),
        P(None, "narrow"),
        P(None, "narrow"),
        P("narrow", None),
        P(("dp", "narrow"), None),
    )
    return jax.shard_map(
        local,
        mesh=mesh,
        in_specs=placed,
        out_specs=(
            P(("dp", "narrow"), None),
            P(("dp", "narrow"), None),
            P(("dp", "narrow")),
            P(("dp", "narrow"), None),
            P(("dp", "narrow"), None),
            P(("dp", "narrow"), None),
            P(("dp", "narrow"), None),
            P(None, None, ("dp", "narrow")),
            P(("dp", "narrow")),
            P(None, ("dp", "narrow")),
            P(("dp", "narrow")),
            P("dp", "narrow"),
            P("dp", "narrow"),
            P("narrow", "dp"),
        ),
        check_vma=False,
    )
```

```python
import functools

import jax
import jax.numpy as jnp
from jax import lax
from jax.experimental import pallas as pl
from jax.experimental.pallas import tpu as pltpu
from jax.sharding import PartitionSpec as P

CONV = 4
BLOCK = 128
HEADS_STEP = 2
PAD = 8
MESH = pl.DeviceIdType.MESH
F32 = jnp.float32
BF16 = jnp.bfloat16
VMEM_LIMIT = 56 * 1024 * 1024


def mm(left, right, contract=(1, 0)):
    return lax.dot_general(
        left.astype(BF16),
        right.astype(BF16),
        (((contract[0],), (contract[1],)), ((), ())),
        preferred_element_type=F32,
    )


def mm_nt(left, right):
    return mm(left, right, (1, 1))


def mm_tn(left, right):
    return mm(left, right, (0, 0))


def iotas(size):
    row = lax.broadcasted_iota(jnp.int32, (size, size), 0)
    col = lax.broadcasted_iota(jnp.int32, (size, size), 1)
    return row, col


def block_masks(since):
    size = since.shape[0]
    row, col = iotas(size)
    back = row - col
    causal = (back >= 0) & (back <= since)
    strict = (back > 0) & (back <= since)
    keep = (since > row).astype(F32)
    last = since[size - 1 : size, :]
    last_mask = (row >= size - 1 - last).astype(F32)
    keep_last = (last > size - 1).astype(F32)
    return causal, strict, keep, last_mask, keep_last


def unit_lower_inverses(lowers):
    size = lowers[0].shape[0]
    row, col = iotas(size)
    width = 1
    inverses = None
    while width < size:
        join = (row // (2 * width) == col // (2 * width)) & (row // width != col // width)
        pieces = [jnp.where(join, low, 0.0) for low in lowers]
        if inverses is None:
            eye = (row == col).astype(F32)
            inverses = [eye - piece for piece in pieces]
        else:
            halves = [mm(piece, inv) for piece, inv in zip(pieces, inverses)]
            inverses = [inv - mm(inv, half) for inv, half in zip(inverses, halves)]
        width *= 2
    return inverses


def conv_front(ext, proj, halo, taps, since):
    rows = proj.shape[0]
    ext[0:PAD, :] = halo.astype(F32)
    ext[PAD : PAD + rows, :] = proj
    pre = proj * taps[0:1, :]
    for lag in range(1, CONV):
        moved = ext[PAD - lag : PAD - lag + rows, :]
        pre = pre + jnp.where(since >= lag, moved, 0.0) * taps[lag : lag + 1, :]
    gate = 1.0 / (1.0 + jnp.exp(-pre))
    return pre, gate, pre * gate


def unit_rows(value):
    inv = lax.rsqrt(jnp.sum(value * value, axis=-1, keepdims=True) + 1e-06)
    return value * inv, inv


def head_column(array, head):
    lane = lax.broadcasted_iota(jnp.int32, array.shape, 1)
    return jnp.sum(jnp.where(lane == head, array, 0.0), axis=1, keepdims=True)


def forward_kernel(
    since_ref, beta_ref, query_ref, key_ref, value_ref, halo_ref, taps_ref,
    out_add_ref, out_map_ref, new_add_ref, new_map_ref, inverse_ref, starts_ref, end_ref,
    ext,
):
    rows = since_ref.shape[0]
    blocks = rows // BLOCK
    since = since_ref[...]
    jobs = []
    for sub in range(HEADS_STEP):
        head = pl.program_id(0) * HEADS_STEP + sub
        lanes = slice(sub * BLOCK, (sub + 1) * BLOCK)
        mixed = []
        for part, ref in enumerate((query_ref, key_ref, value_ref)):
            _, _, act = conv_front(
                ext.at[sub * 3 + part], ref[:, lanes].astype(F32), halo_ref[part, :, lanes],
                taps_ref[part, :, lanes], since,
            )
            mixed.append(act)
        query = unit_rows(mixed[0])[0] * (BLOCK ** -0.5)
        key = unit_rows(mixed[1])[0]
        beta = 1.0 / (1.0 + jnp.exp(-head_column(beta_ref[...], head)))
        jobs.append((lanes, query, key, mixed[2], beta))
    lowers, scores = [], []
    for lanes, query, key, value, beta in jobs:
        for blk in range(blocks):
            span = slice(blk * BLOCK, (blk + 1) * BLOCK)
            causal, strict, _, _, _ = block_masks(since[span])
            both = mm_nt(jnp.concatenate([key[span], query[span]], axis=0), key[span])
            lowers.append(jnp.where(strict, both[:BLOCK] * beta[span], 0.0))
            scores.append(jnp.where(causal, both[BLOCK:], 0.0).astype(BF16))
    inverses = [inv.astype(BF16) for inv in unit_lower_inverses(lowers)]
    row, col = iotas(BLOCK)
    eye = (row == col).astype(F32)
    states = [jnp.concatenate([jnp.zeros((BLOCK, BLOCK), F32), eye], axis=1) for _ in jobs]
    for blk in range(blocks):
        span = slice(blk * BLOCK, (blk + 1) * BLOCK)
        _, _, keep, last_mask, keep_last = block_masks(since[span])
        for sub, (lanes, query, key, value, beta) in enumerate(jobs):
            at = sub * blocks + blk
            inverse_ref[sub, blk] = inverses[at]
            state = states[sub].astype(BF16)
            starts_ref[sub, blk] = state
            stacked = jnp.concatenate([key[span] * keep, query[span] * keep], axis=0)
            seen = mm(stacked, state)
            rest = jnp.concatenate([value[span], jnp.zeros((BLOCK, BLOCK), F32)], axis=1)
            right = (rest - seen[:BLOCK]) * beta[span]
            new = mm(inverses[at], right).astype(BF16)
            out = seen[BLOCK:] + mm(scores[at], new)
            out_add_ref[span, lanes] = out[:, :BLOCK].astype(BF16)
            out_map_ref[span, lanes] = out[:, BLOCK:].astype(BF16)
            new_add_ref[span, lanes] = new[:, :BLOCK]
            new_map_ref[span, lanes] = new[:, BLOCK:]
            keep_both = jnp.concatenate([keep_last, keep_last], axis=1)
            states[sub] = states[sub] * keep_both + mm_tn(key[span] * last_mask, new)
    for sub in range(len(jobs)):
        end_ref[sub] = states[sub]


def whole_spec(shape):
    return pl.BlockSpec(shape, lambda h: (0,) * len(shape))


def head_spec(rows):
    return pl.BlockSpec((rows, HEADS_STEP * BLOCK), lambda h: (0, h))


def per_head(*tail):
    return pl.BlockSpec((HEADS_STEP,) + tail, lambda h: (h,) + (0,) * len(tail))


def lanes_spec(first, second):
    return pl.BlockSpec((first, second, HEADS_STEP * BLOCK), lambda h: (0, 0, h))


def params():
    return pltpu.CompilerParams(vmem_limit_bytes=VMEM_LIMIT)


def mixer_forward(since, beta_logit, query, key, value, halo, taps):
    rows, width = query.shape
    heads = width // BLOCK
    blocks = rows // BLOCK
    wide = jax.ShapeDtypeStruct((rows, width), BF16)
    return pl.pallas_call(
        forward_kernel,
        grid=(heads // HEADS_STEP,),
        in_specs=[
            whole_spec(since.shape), whole_spec(beta_logit.shape),
            head_spec(rows), head_spec(rows), head_spec(rows),
            lanes_spec(3, PAD), lanes_spec(3, CONV),
        ],
        out_specs=[
            head_spec(rows), head_spec(rows), head_spec(rows), head_spec(rows),
            per_head(blocks, BLOCK, BLOCK), per_head(blocks, BLOCK, 2 * BLOCK),
            per_head(BLOCK, 2 * BLOCK),
        ],
        out_shape=[
            wide, wide, wide, wide,
            jax.ShapeDtypeStruct((heads, blocks, BLOCK, BLOCK), BF16),
            jax.ShapeDtypeStruct((heads, blocks, BLOCK, 2 * BLOCK), BF16),
            jax.ShapeDtypeStruct((heads, BLOCK, 2 * BLOCK), F32),
        ],
        scratch_shapes=[pltpu.VMEM((3 * HEADS_STEP, PAD + rows, BLOCK), F32)],
        compiler_params=params(),
        name="mixer_forward",
    )(since, beta_logit, query, key, value, halo, taps)


def join_kernel(out_add_ref, out_map_ref, entry_ref, gain_ref, mixed_ref):
    for sub in range(HEADS_STEP):
        lanes = slice(sub * BLOCK, (sub + 1) * BLOCK)
        core = out_add_ref[:, lanes].astype(F32) + mm(out_map_ref[:, lanes], entry_ref[sub])
        scale = lax.rsqrt(jnp.mean(core * core, axis=-1, keepdims=True) + 1e-05)
        mixed_ref[:, lanes] = (core * scale * gain_ref[...]).astype(BF16)


def mixer_join(out_add, out_map, entry, gain):
    rows, width = out_add.shape
    heads = width // BLOCK
    return pl.pallas_call(
        join_kernel,
        grid=(heads // HEADS_STEP,),
        in_specs=[head_spec(rows), head_spec(rows), per_head(BLOCK, BLOCK), whole_spec((1, BLOCK))],
        out_specs=head_spec(rows),
        out_shape=jax.ShapeDtypeStruct((rows, width), BF16),
        compiler_params=params(),
        name="mixer_join",
    )(out_add, out_map, entry, gain)


def core_back_kernel(out_add_ref, out_map_ref, entry_ref, gain_ref, up_ref, d_core_ref, start_ref, gain_out_ref):
    @pl.when(pl.program_id(0) == 0)
    def _():
        gain_out_ref[...] = jnp.zeros_like(gain_out_ref)

    for sub in range(HEADS_STEP):
        lanes = slice(sub * BLOCK, (sub + 1) * BLOCK)
        out_map = out_map_ref[:, lanes]
        core = out_add_ref[:, lanes].astype(F32) + mm(out_map, entry_ref[sub])
        scale = lax.rsqrt(jnp.mean(core * core, axis=-1, keepdims=True) + 1e-05)
        unit = core * scale
        up = up_ref[:, lanes].astype(F32)
        gain_out_ref[...] += jnp.sum(up * unit, axis=0, keepdims=True)
        scaled = up * gain_ref[...]
        d_core = scale * (scaled - unit * jnp.mean(scaled * unit, axis=-1, keepdims=True))
        d_core = d_core.astype(BF16)
        d_core_ref[:, lanes] = d_core
        start_ref[sub] = mm_tn(out_map, d_core)


def mixer_core_back(out_add, out_map, entry, gain, up):
    rows, width = out_add.shape
    heads = width // BLOCK
    return pl.pallas_call(
        core_back_kernel,
        grid=(heads // HEADS_STEP,),
        in_specs=[
            head_spec(rows), head_spec(rows), per_head(BLOCK, BLOCK), whole_spec((1, BLOCK)), head_spec(rows),
        ],
        out_specs=[head_spec(rows), per_head(BLOCK, BLOCK), whole_spec((1, BLOCK))],
        out_shape=[
            jax.ShapeDtypeStruct((rows, width), BF16),
            jax.ShapeDtypeStruct((heads, BLOCK, BLOCK), F32),
            jax.ShapeDtypeStruct((1, BLOCK), F32),
        ],
        compiler_params=params(),
        name="mixer_core_back",
    )(out_add, out_map, entry, gain, up)


def backward_heads(
    step, since_ref, beta_ref, query_ref, key_ref, value_ref, halo_ref, taps_ref,
    new_add_ref, new_map_ref, inverse_ref, starts_ref, entry_ref, exit_ref, d_core_ref,
    d_taps_ref, d_beta_ref, ext, back, emit,
):
    rows = since_ref.shape[0]
    blocks = rows // BLOCK
    since = since_ref[...]
    jobs = []
    for sub in range(HEADS_STEP):
        head = step * HEADS_STEP + sub
        lanes = slice(sub * BLOCK, (sub + 1) * BLOCK)
        fronts = []
        for part, ref in enumerate((query_ref, key_ref, value_ref)):
            fronts.append(
                conv_front(
                    ext.at[sub * 3 + part], ref[:, lanes].astype(F32), halo_ref[part, :, lanes],
                    taps_ref[part, :, lanes], since,
                )
            )
        query_unit, query_inv = unit_rows(fronts[0][2])
        key, key_inv = unit_rows(fronts[1][2])
        query = query_unit * (BLOCK ** -0.5)
        beta = 1.0 / (1.0 + jnp.exp(-head_column(beta_ref[...], head)))
        jobs.append((head, lanes, fronts, query, query_unit, query_inv, key, key_inv, beta))

    saved = {}
    for sub, (head, lanes, fronts, query, query_unit, query_inv, key, key_inv, beta) in enumerate(jobs):
        entry = entry_ref[sub].astype(BF16)
        for blk in range(blocks):
            span = slice(blk * BLOCK, (blk + 1) * BLOCK)
            causal, _, keep, last_mask, _ = block_masks(since[span])
            start = starts_ref[sub, blk]
            state = (start[:, :BLOCK].astype(F32) + mm(start[:, BLOCK:], entry)).astype(BF16)
            new = (new_add_ref[span, lanes].astype(F32) + mm(new_map_ref[span, lanes], entry)).astype(BF16)
            scores = jnp.where(causal, mm_nt(query[span], key[span]), 0.0).astype(BF16)
            d_out = d_core_ref[span, lanes]
            d_new = mm_tn(scores, d_out)
            d_state = mm_tn(query[span] * keep, d_out)
            saved[sub, blk] = (state, new, d_out, d_new, d_state)

    carried = [exit_ref[sub].astype(F32) for sub in range(HEADS_STEP)]
    chain = {}
    for blk in reversed(range(blocks)):
        span = slice(blk * BLOCK, (blk + 1) * BLOCK)
        _, _, keep, last_mask, keep_last = block_masks(since[span])
        for sub, (head, lanes, fronts, query, query_unit, query_inv, key, key_inv, beta) in enumerate(jobs):
            state, new, d_out, d_new, d_state = saved[sub, blk]
            after = carried[sub].astype(BF16)
            d_new = d_new + mm(key[span] * last_mask, after)
            d_right = mm_tn(inverse_ref[sub, blk], d_new)
            d_rest = d_right * beta[span]
            carried[sub] = carried[sub] * keep_last + d_state - mm_tn(key[span] * keep, d_rest)
            chain[sub, blk] = (after, d_right, d_rest)

    lane = lax.broadcasted_iota(jnp.int32, (rows, beta_ref.shape[1]), 1)
    d_beta_all = jnp.zeros((rows, beta_ref.shape[1]), F32)
    for sub, (head, lanes, fronts, query, query_unit, query_inv, key, key_inv, beta) in enumerate(jobs):
        d_queries, d_keys, d_values, d_betas = [], [], [], []
        for blk in range(blocks):
            span = slice(blk * BLOCK, (blk + 1) * BLOCK)
            causal, strict, keep, last_mask, _ = block_masks(since[span])
            state, new, d_out, _, _ = saved[sub, blk]
            after, d_right, d_rest = chain[sub, blk]
            both = mm_nt(jnp.concatenate([d_out, d_right.astype(BF16)], axis=0), new)
            d_scores = jnp.where(causal, both[:BLOCK], 0.0).astype(BF16)
            d_gram = (jnp.where(strict, both[BLOCK:], 0.0) * (-beta[span])).astype(BF16)
            key_b = key[span].astype(BF16)
            from_state = mm_nt(jnp.concatenate([d_out, d_rest.astype(BF16)], axis=0), state)
            left = mm(jnp.concatenate([d_scores, d_gram], axis=0), key_b)
            d_queries.append(from_state[:BLOCK] * keep + left[:BLOCK])
            d_key = left[BLOCK:] + mm_tn(
                jnp.concatenate([d_scores, d_gram], axis=0),
                jnp.concatenate([query[span].astype(BF16), key_b], axis=0),
            )
            d_key = d_key + mm_nt(new, after) * last_mask - from_state[BLOCK:] * keep
            d_keys.append(d_key)
            d_values.append(d_rest)
            d_betas.append(
                jnp.sum(d_right * new.astype(F32), axis=1, keepdims=True) * (1.0 - beta[span])
            )
        d_query = jnp.concatenate(d_queries, axis=0) * (BLOCK ** -0.5)
        d_key = jnp.concatenate(d_keys, axis=0)
        d_query = query_inv * (
            d_query - query_unit * jnp.sum(d_query * query_unit, axis=-1, keepdims=True)
        )
        d_key = key_inv * (d_key - key * jnp.sum(d_key * key, axis=-1, keepdims=True))
        d_value = jnp.concatenate(d_values, axis=0)
        d_beta_all = d_beta_all + jnp.where(lane == head, jnp.concatenate(d_betas, axis=0), 0.0)
        for part, d_act in enumerate((d_query, d_key, d_value)):
            pre, gate, _ = fronts[part]
            taps = taps_ref[part, :, lanes]
            source = ext.at[sub * 3 + part]
            d_pre = d_act * gate * (1.0 + pre * (1.0 - gate))
            room = back.at[(sub * 3 + part) % 2]
            total = None
            d_taps = []
            for lag in range(CONV):
                masked = d_pre if lag == 0 else jnp.where(since >= lag, d_pre, 0.0)
                moved = source[PAD - lag : PAD - lag + rows, :]
                d_taps.append(jnp.sum(masked * moved, axis=0, keepdims=True))
                room[lag, 0:PAD, :] = jnp.zeros((PAD, BLOCK), F32)
                room[lag, PAD : PAD + rows, :] = masked * taps[lag : lag + 1, :]
                room[lag, PAD + rows : PAD + rows + PAD, :] = jnp.zeros((PAD, BLOCK), F32)
                term = room[lag, lag : lag + PAD + rows, :]
                total = term if total is None else total + term
            d_taps_ref[part, :, lanes] = jnp.concatenate(d_taps, axis=0)
            emit(part, lanes, total)

    @pl.when(step == 0)
    def _():
        d_beta_ref[...] = d_beta_all

    @pl.when(step > 0)
    def _():
        d_beta_ref[...] += d_beta_all


def backward_kernel(*refs):
    d_proj_ref, d_halo_ref, d_taps_ref, d_beta_ref, ext, back = refs[14:]

    def emit(part, lanes, total):
        d_halo_ref[part, :, lanes] = total[:PAD]
        d_proj_ref[part, :, lanes] = total[PAD:].astype(BF16)

    backward_heads(pl.program_id(0), *refs[:14], d_taps_ref, d_beta_ref, ext, back, emit)


def mixer_backward(
    since, beta_logit, query, key, value, halo, taps, new_add, new_map, inverse, starts, entry, exit_grad, d_core
):
    rows, width = query.shape
    heads = width // BLOCK
    blocks = rows // BLOCK
    return pl.pallas_call(
        backward_kernel,
        grid=(heads // HEADS_STEP,),
        in_specs=[
            whole_spec(since.shape), whole_spec(beta_logit.shape),
            head_spec(rows), head_spec(rows), head_spec(rows),
            lanes_spec(3, PAD), lanes_spec(3, CONV),
            head_spec(rows), head_spec(rows),
            per_head(blocks, BLOCK, BLOCK), per_head(blocks, BLOCK, 2 * BLOCK),
            per_head(BLOCK, BLOCK), per_head(BLOCK, BLOCK), head_spec(rows),
        ],
        out_specs=[
            lanes_spec(3, rows), lanes_spec(3, PAD), lanes_spec(3, CONV), whole_spec(beta_logit.shape),
        ],
        out_shape=[
            jax.ShapeDtypeStruct((3, rows, width), BF16),
            jax.ShapeDtypeStruct((3, PAD, width), F32),
            jax.ShapeDtypeStruct((3, CONV, width), F32),
            jax.ShapeDtypeStruct(beta_logit.shape, F32),
        ],
        scratch_shapes=[
            pltpu.VMEM((3 * HEADS_STEP, PAD + rows, BLOCK), F32),
            pltpu.VMEM((2, CONV, PAD + rows + PAD, BLOCK), F32),
        ],
        compiler_params=params(),
        name="mixer_backward",
    )(
        since, beta_logit, query, key, value, halo, taps, new_add, new_map, inverse, starts, entry, exit_grad, d_core
    )


GROUPS = 4
HALVES = 2


def chain_kernel(axis, forward, map_ref, add_ref, out_ref, sent, landed, send_sem, recv_sem):
    count = lax.axis_size(axis)
    me = lax.axis_index(axis)
    heads = add_ref.shape[0]
    step = heads // GROUPS
    up, down = (me + 1, me - 1) if forward else (me - 1, me + 1)
    first, last = (0, count - 1) if forward else (count - 1, 0)
    barrier = pltpu.get_barrier_semaphore()

    @pl.when(me != first)
    def _():
        pl.semaphore_signal(barrier, inc=1, device_id={axis: down}, device_id_type=MESH)

    @pl.when(me != last)
    def _():
        pl.semaphore_wait(barrier, 1)

    def copy(group, target):
        return pltpu.make_async_remote_copy(
            src_ref=sent.at[group],
            dst_ref=landed.at[group],
            send_sem=send_sem.at[group],
            recv_sem=recv_sem.at[group],
            device_id={axis: target},
            device_id_type=MESH,
        )

    for group in range(GROUPS):
        @pl.when(me != first)
        def _():
            copy(group, up).wait_recv()
            for sub in range(step):
                head = group * step + sub
                out_ref[head] = landed[group, sub].astype(F32)

        @pl.when(me == first)
        def _():
            out_ref[group * step : (group + 1) * step] = jnp.zeros((step,) + out_ref.shape[1:], F32)

        @pl.when(me != last)
        def _():
            for sub in range(step):
                head = group * step + sub
                if forward:
                    moved = mm(map_ref[head], out_ref[head])
                else:
                    moved = mm_tn(map_ref[head], out_ref[head])
                sent[group, sub] = (moved + add_ref[head]).astype(BF16)
            copy(group, up).start()

    @pl.when(me != last)
    def _():
        for group in range(GROUPS):
            copy(group, up).wait_send()


def carry_chain(map_part, add_part, axis, forward):
    heads = add_part.shape[0]
    part = (GROUPS, heads // GROUPS, BLOCK, BLOCK)
    return pl.pallas_call(
        functools.partial(chain_kernel, axis, forward),
        in_specs=[pl.BlockSpec(memory_space=pltpu.VMEM)] * 2,
        out_specs=pl.BlockSpec(memory_space=pltpu.VMEM),
        out_shape=jax.ShapeDtypeStruct(add_part.shape, F32),
        scratch_shapes=[
            pltpu.VMEM(part, BF16),
            pltpu.VMEM(part, BF16),
            pltpu.SemaphoreType.DMA((GROUPS,)),
            pltpu.SemaphoreType.DMA((GROUPS,)),
        ],
        compiler_params=pltpu.CompilerParams(
            collective_id=1 if forward else 2, has_side_effects=True, vmem_limit_bytes=VMEM_LIMIT // 2
        ),
        name="carry_forward" if forward else "carry_backward",
    )(map_part, add_part)


def bits(dp):
    core, x, y = dp % 2, (dp // 2) % 2, dp // 4
    return core, x, y, dp + 1 - 2 * core, dp + 2 * (1 - 2 * x), dp + 4 * (1 - 2 * y)


def remote(src, dst, send_sem, recv_sem, target):
    return pltpu.make_async_remote_copy(
        src_ref=src, dst_ref=dst, send_sem=send_sem, recv_sem=recv_sem, device_id=target, device_id_type=MESH
    )


def meet(dp_targets, narrow_targets):
    barrier = pltpu.get_barrier_semaphore()
    for target in dp_targets:
        pl.semaphore_signal(barrier, inc=1, device_id={"dp": target}, device_id_type=MESH)
    for target in narrow_targets:
        pl.semaphore_signal(barrier, inc=1, device_id={"narrow": target}, device_id_type=MESH)
    pl.semaphore_wait(barrier, len(dp_targets) + len(narrow_targets))


def add_rows(dst, src, step):
    def one(at, _):
        at = pl.ds(pl.multiple_of(at * step, step), step)
        dst[at, :] = (dst[at, :].astype(F32) + src[at, :].astype(F32)).astype(dst.dtype)
        return 0

    lax.fori_loop(0, dst.shape[0] // step, one, 0)


def small_kernel(small_ref, out_ref, landed, total, got2, got3, gotz, send1, recv1, send2, recv2, send3, recv3, sendz, recvz):
    dp, z = lax.axis_index("dp"), lax.axis_index("narrow")
    core, x, y, sib, flip_x, flip_y = bits(dp)
    depth = lax.axis_size("narrow")
    rows = small_ref.shape[0] // 8
    share = rows // depth
    peers = [(z + step) % depth for step in range(1, depth)]
    meet((sib, flip_x, flip_y), peers)

    def stripe_rows(stripe, which):
        return pl.ds(pl.multiple_of((stripe * 2 + which) * rows, rows), rows)

    def share_rows(at):
        return pl.ds(pl.multiple_of(at * share, share), share)

    first = [
        remote(small_ref.at[stripe_rows(k, 1 - core)], landed.at[k], send1.at[k], recv1.at[k], {"dp": sib})
        for k in range(4)
    ]
    for copy in first:
        copy.start()
    for k in range(4):
        first[k].wait()
        total[k] = small_ref[stripe_rows(k, core), :] + landed[k]
    second = [
        remote(total.at[2 * j + 1 - x], got2.at[j], send2.at[j], recv2.at[j], {"dp": flip_x}) for j in range(2)
    ]
    for copy in second:
        copy.start()
    for copy in second:
        copy.wait()
    third = remote(total.at[2 * (1 - y) + x], got3, send3, recv3, {"dp": flip_y})
    total[2 * (1 - y) + x] = total[2 * (1 - y) + x] + got2[1 - y]
    third.start()
    third.wait()
    mine = 2 * y + x
    total[mine] = total[mine] + got2[y] + got3[...]
    last = [
        remote(total.at[mine, share_rows(to)], gotz.at[k], sendz.at[k], recvz.at[k], {"narrow": to})
        for k, to in enumerate(peers)
    ]
    for copy in last:
        copy.start()
    value = total[mine, share_rows(z), :]
    for k, copy in enumerate(last):
        copy.wait()
        value = value + gotz[k]
    out_ref[...] = value


def reduce_small(small):
    height, lanes = small.shape
    depth = lax.axis_size("narrow")
    rows = height // 8
    share = rows // depth
    dma = pltpu.SemaphoreType.DMA
    return pl.pallas_call(
        small_kernel,
        in_specs=[pl.BlockSpec(memory_space=pltpu.VMEM)],
        out_specs=pl.BlockSpec(memory_space=pltpu.VMEM),
        out_shape=jax.ShapeDtypeStruct((share, lanes), F32),
        scratch_shapes=[
            pltpu.VMEM((4, rows, lanes), F32),
            pltpu.VMEM((4, rows, lanes), F32),
            pltpu.VMEM((2, rows, lanes), F32),
            pltpu.VMEM((rows, lanes), F32),
            pltpu.VMEM((depth - 1, share, lanes), F32),
            dma((4,)), dma((4,)), dma((2,)), dma((2,)), dma(()), dma(()), dma((depth - 1,)), dma((depth - 1,)),
        ],
        compiler_params=pltpu.CompilerParams(
            collective_id=3, has_side_effects=True, vmem_limit_bytes=16 * 1024 * 1024
        ),
        name="reduce_small",
    )(small)


RING = 3
HELD = 5


def fused_kernel(*refs):
    heads_in = refs[:14]
    since_ref = refs[0]
    (
        w_query_ref, w_key_ref, w_value_ref, mixed_ref, normed_hbm, branch_hbm,
        grad_hbm, d_normed_hbm, d_taps_ref, d_beta_ref,
        ext, back, left_own, left_sib, d_proj, d_proj_sib, halo_out, halo_in,
        total, got2, got3, gotz, d_normed, grad,
        local_sem, grad_sem, left_send, left_recv, right_send, right_recv, halo_send, halo_recv,
        send2, recv2, send3, recv3, sendz, recvz,
    ) = refs[14:]
    step = pl.program_id(0)
    units = pl.num_programs(0) - 1
    dp, z = lax.axis_index("dp"), lax.axis_index("narrow")
    core, x, y, sib, flip_x, flip_y = bits(dp)
    depth = lax.axis_size("narrow")
    tokens = since_ref.shape[0]
    parts = d_proj_sib.shape[1]
    rows = left_own.shape[2]
    cols = d_proj.shape[3]
    share = rows // depth
    peers = [(z + k) % depth for k in range(1, depth)]

    def stripe_lanes(stripe, which):
        return pl.ds(pl.multiple_of((stripe * 2 + which) * rows, rows), rows)

    def left_copy(k):
        source = (normed_hbm, branch_hbm)[k // 4]
        return remote(
            source.at[:, stripe_lanes(k % 4, 1 - core)], d_proj_sib.at[1 + k // 4, k % 4],
            left_send.at[k], left_recv.at[k], {"dp": sib},
        )

    def right_copies(unit):
        slot = unit % RING
        return [
            remote(
                d_proj.at[slot], d_proj_sib.at[slot, 0 : parts - 1],
                right_send.at[slot, 0], right_recv.at[slot, 0], {"dp": sib},
            ),
            remote(
                mixed_ref, d_proj_sib.at[slot, parts - 1],
                right_send.at[slot, 1], right_recv.at[slot, 1], {"dp": sib},
            ),
        ]

    def halo_copy(unit):
        return remote(
            halo_out.at[unit], halo_in.at[unit], halo_send.at[unit], halo_recv.at[unit], {"narrow": z - 1}
        )

    def order(unit):
        e = unit % 2

        def pick(even, odd):
            return (1 - e) * even + e * odd

        def away(j):
            return pick(2 * j + 1 - x, 2 * (1 - y) + j)

        def kept(j):
            return pick(2 * j + x, 2 * y + j)

        return away, kept, pick(flip_x, flip_y), pick(flip_y, flip_x), pick(1 - y, 1 - x), pick(y, x)

    def copy2(unit, j):
        away, _, target, _, _, _ = order(unit)
        return remote(total.at[unit % HELD, away(j)], got2.at[unit, j], send2.at[unit, j], recv2.at[unit, j], {"dp": target})

    def copy3(unit):
        _, kept, _, target, far, _ = order(unit)
        return remote(total.at[unit % HELD, kept(far)], got3.at[unit], send3.at[unit], recv3.at[unit], {"dp": target})

    def copyz(unit, part, k):
        _, kept, _, _, _, near = order(unit)
        at = pl.ds(pl.multiple_of(part * rows + peers[k] * share, share), share)
        return remote(
            total.at[unit % HELD, kept(near), at], gotz.at[unit, k, part * share : (part + 1) * share],
            sendz.at[unit, k, part], recvz.at[unit, k, part], {"narrow": peers[k]},
        )

    @pl.when(step == 0)
    def _():
        loads = [
            pltpu.make_async_copy(
                (normed_hbm, branch_hbm)[k // 4].at[:, stripe_lanes(k % 4, core)],
                d_proj.at[k // 3, k % 3], local_sem.at[k],
            )
            for k in range(8)
        ]
        for load in loads:
            load.start()
        back[:, :, 0:PAD, :] = jnp.zeros((2, CONV, PAD, BLOCK), F32)
        back[:, :, PAD + tokens :, :] = jnp.zeros((2, CONV, PAD, BLOCK), F32)
        d_normed[...] = jnp.zeros_like(d_normed)
        meet((sib, flip_x, flip_y), peers)
        for k in range(8):
            left_copy(k).start()
        for k in range(8):
            loads[k].wait()
            left_own[k // 4, k % 4] = d_proj[k // 3, k % 3].astype(F32).T.astype(BF16)

    @pl.when(step == 1)
    def _():
        for k in range(8):
            left_copy(k).wait()
            left_sib[k // 4, k % 4] = d_proj_sib[1 + k // 4, k % 4].astype(F32).T.astype(BF16)

    @pl.when(step >= 1)
    def _():
        unit = step - 1

        @pl.when(z < depth - 1)
        def _():
            halo_copy(unit).wait_recv()
            for part in range(3):
                extra = jnp.concatenate([jnp.zeros((PAD, cols), F32), halo_in[unit, part]], axis=0)
                tail = slice(tokens - 2 * PAD, tokens)
                d_proj[unit % RING, part, tail, :] = (
                    d_proj[unit % RING, part, tail, :].astype(F32) + extra
                ).astype(BF16)

        @pl.when(z > 0)
        def _():
            halo_copy(unit).wait_send()

        for copy in right_copies(unit):
            copy.start()

    @pl.when(step < units)
    def _():
        def emit(part, lanes, value):
            halo_out[step, part, :, lanes] = value[:PAD]
            d_proj[step % RING, part, :, lanes] = value[PAD:].astype(BF16)

        backward_heads(step, *heads_in, d_taps_ref, d_beta_ref, ext, back, emit)

        @pl.when(z > 0)
        def _():
            halo_copy(step).start()

    @pl.when(step >= 1)
    def _():
        unit = step - 1
        away, kept, _, _, _, _ = order(unit)
        for copy in right_copies(unit):
            copy.wait()

        def one(k, _):
            j = k % 2
            stripe = (k // 2) * kept(j) + (1 - k // 2) * away(j)
            for part in range(parts):
                which = part // (parts - 1)
                mine = d_proj[unit % RING, part] if which == 0 else mixed_ref[...]
                value = jnp.dot(left_own[which, stripe], mine, preferred_element_type=F32)
                value = value + jnp.dot(
                    left_sib[which, stripe], d_proj_sib[unit % RING, part], preferred_element_type=F32
                )
                total[unit % HELD, stripe, part * rows : (part + 1) * rows, :] = value.astype(BF16)

            @pl.when(k < 2)
            def _():
                copy2(unit, j).start()

            return 0

        lax.fori_loop(0, 4, one, 0)

        def normed_part(at, _):
            at = pl.ds(pl.multiple_of(at * 512, 512), 512)
            value = d_normed[:, at]
            for part, ref in enumerate((w_query_ref, w_key_ref, w_value_ref)):
                value = value + lax.dot_general(
                    d_proj[unit % RING, part], ref[at, :], (((1,), (1,)), ((), ())), preferred_element_type=F32
                )
            d_normed[:, at] = value
            return 0

        lax.fori_loop(0, d_normed.shape[1] // 512, normed_part, 0)

    def second(unit):
        _, kept, _, _, far, near = order(unit)
        for j in range(2):
            copy2(unit, j).wait()
        add_rows(total.at[unit % HELD, kept(far)], got2.at[unit, far], 64)
        copy3(unit).start()
        add_rows(total.at[unit % HELD, kept(near)], got2.at[unit, near], 64)

    def grad_copy(unit):
        at = pl.ds(pl.multiple_of(unit * cols, cols), cols)
        return pltpu.make_async_copy(grad.at[unit % 2], grad_hbm.at[:, :, at], grad_sem.at[unit % 2])

    def third(unit):
        _, kept, _, _, _, near = order(unit)
        copy3(unit).wait()
        add_rows(total.at[unit % HELD, kept(near)], got3.at[unit], 64)
        for k in range(depth - 1):
            for part in range(parts):
                copyz(unit, part, k).start()

    def fourth(unit):
        _, kept, _, _, _, near = order(unit)
        for k in range(depth - 1):
            for part in range(parts):
                copyz(unit, part, k).wait()
        @pl.when(unit >= 2)
        def _():
            grad_copy(unit - 2).wait()

        for part in range(parts):
            at = pl.ds(pl.multiple_of(part * rows + z * share, share), share)
            value = total[unit % HELD, kept(near), at, :].astype(F32)
            for k in range(depth - 1):
                value = value + gotz[unit, k, part * share : (part + 1) * share, :].astype(F32)
            grad[unit % 2, part] = value
        grad_copy(unit).start()

    def stages(at):
        @pl.when((at >= 3) & (at < units + 3))
        def _():
            second(at - 3)

        @pl.when((at >= 4) & (at < units + 4))
        def _():
            third(at - 4)

        @pl.when(at >= 5)
        def _():
            fourth(at - 5)

    stages(step)

    @pl.when(step == units)
    def _():
        save = pltpu.make_async_copy(d_normed, d_normed_hbm, local_sem.at[0])
        save.start()

        def one(at, _):
            stages(at)
            return 0

        lax.fori_loop(units + 1, units + 5, one, 0)
        save.wait()
        grad_copy(units - 2).wait()
        grad_copy(units - 1).wait()


def fused_backward(
    since, beta_logit, query, key, value, halo, taps, new_add, new_map, inverse, starts, entry, exit_grad, d_core,
    w_query, w_key, w_value, mixed, normed, branch,
):
    tokens, width = query.shape
    heads = width // BLOCK
    blocks = tokens // BLOCK
    units = heads // HEADS_STEP
    cols = HEADS_STEP * BLOCK
    depth = lax.axis_size("narrow")
    rows = width // 8
    share = rows // depth
    dma = pltpu.SemaphoreType.DMA

    def now(step):
        return jnp.minimum(step, units - 1)

    def before(step):
        return jnp.maximum(step - 1, 0)

    def whole(shape):
        return pl.BlockSpec(shape, lambda h: (0,) * len(shape))

    wide = pl.BlockSpec((tokens, cols), lambda h: (0, now(h)))

    def lanes(first, second):
        return pl.BlockSpec((first, second, cols), lambda h: (0, 0, now(h)))

    def each(*tail):
        return pl.BlockSpec((HEADS_STEP,) + tail, lambda h: (now(h),) + (0,) * len(tail))

    weight = pl.BlockSpec((width, cols), lambda h: (0, before(h)), pipeline_mode=pl.Buffered(1))
    mixed_spec = pl.BlockSpec((tokens, cols), lambda h: (0, before(h)))
    parts = 4
    anywhere = pl.BlockSpec(memory_space=pl.ANY)
    return pl.pallas_call(
        fused_kernel,
        grid=(units + 1,),
        in_specs=[
            whole(since.shape), whole(beta_logit.shape), wide, wide, wide, lanes(3, PAD), lanes(3, CONV),
            wide, wide, each(blocks, BLOCK, BLOCK), each(blocks, BLOCK, 2 * BLOCK),
            each(BLOCK, BLOCK), each(BLOCK, BLOCK), wide,
            weight, weight, weight, mixed_spec, anywhere, anywhere,
        ],
        out_specs=[anywhere, anywhere, lanes(3, CONV), whole(beta_logit.shape)],
        out_shape=[
            jax.ShapeDtypeStruct((parts, share, width), F32),
            jax.ShapeDtypeStruct((tokens, width), F32),
            jax.ShapeDtypeStruct((3, CONV, width), F32),
            jax.ShapeDtypeStruct(beta_logit.shape, F32),
        ],
        scratch_shapes=[
            pltpu.VMEM((3 * HEADS_STEP, PAD + tokens, BLOCK), F32),
            pltpu.VMEM((2, CONV, PAD + tokens + PAD, BLOCK), F32),
            pltpu.VMEM((2, 4, rows, tokens), BF16),
            pltpu.VMEM((2, 4, rows, tokens), BF16),
            pltpu.VMEM((RING, 3, tokens, cols), BF16),
            pltpu.VMEM((RING, parts, tokens, cols), BF16),
            pltpu.VMEM((units, 3, PAD, cols), F32),
            pltpu.VMEM((units, 3, PAD, cols), F32),
            pltpu.VMEM((HELD, 4, parts * rows, cols), BF16),
            pltpu.VMEM((units, 2, parts * rows, cols), BF16),
            pltpu.VMEM((units, parts * rows, cols), BF16),
            pltpu.VMEM((units, depth - 1, parts * share, cols), BF16),
            pltpu.VMEM((tokens, width), F32),
            pltpu.VMEM((2, parts, share, cols), F32),
            dma((8,)), dma((2,)), dma((8,)), dma((8,)), dma((RING, 2)), dma((RING, 2)), dma((units,)), dma((units,)),
            dma((units, 2)), dma((units, 2)), dma((units,)), dma((units,)),
            dma((units, depth - 1, parts)), dma((units, depth - 1, parts)),
        ],
        compiler_params=pltpu.CompilerParams(
            collective_id=5, has_side_effects=True, vmem_limit_bytes=62 * 1024 * 1024
        ),
        name="fused_backward",
    )(
        since, beta_logit, query, key, value, halo, taps, new_add, new_map, inverse, starts, entry, exit_grad, d_core,
        w_query, w_key, w_value, mixed, normed, branch,
    )


def ffn_grads_kernel(*refs):
    lefts = [refs[0:HALVES], refs[0:HALVES], refs[HALVES : 2 * HALVES]]
    rights = [refs[(2 + m) * HALVES : (3 + m) * HALVES] for m in range(3)]
    (
        out_ref, left_buf, right_buf, away, landed, total, got2, got3,
        left_sem, right_sem, send1, recv1, send2, recv2, send3, recv3,
    ) = refs[5 * HALVES :]
    dp = lax.axis_index("dp")
    core, x, y = dp % 2, (dp // 2) % 2, dp // 4
    rows = total.shape[2]
    half = rows // 2
    part = left_buf.shape[1] // HALVES
    sib = dp + 1 - 2 * core
    flip_x = dp + 2 * (1 - 2 * x)
    flip_y = dp + 4 * (1 - 2 * y)
    barrier = pltpu.get_barrier_semaphore()
    for target in (sib, flip_x, flip_y):
        pl.semaphore_signal(barrier, inc=1, device_id={"dp": target}, device_id_type=MESH)

    def load_left(m, k, start):
        own = k // 4
        block = (k % 4) * 2 + own * core + (1 - own) * (1 - core)
        lanes = pl.ds(pl.multiple_of(block * rows, rows), rows)
        for at in range(HALVES):
            copy = pltpu.make_async_copy(
                lefts[m][at].at[:, lanes], left_buf.at[k % 2, at * part : (at + 1) * part], left_sem.at[k % 2, at]
            )
            if start:
                copy.start()
            else:
                copy.wait()

    def load_right(m, start):
        for at in range(HALVES):
            copy = pltpu.make_async_copy(
                rights[m][at], right_buf.at[m % 2, at * part : (at + 1) * part], right_sem.at[m % 2, at]
            )
            if start:
                copy.start()
            else:
                copy.wait()

    def send(src, dst, send_sem, recv_sem, target):
        return pltpu.make_async_remote_copy(
            src_ref=src, dst_ref=dst, send_sem=send_sem, recv_sem=recv_sem,
            device_id={"dp": target}, device_id_type=MESH,
        )

    def copy1(m, stripe):
        return send(away.at[m, stripe], landed.at[m, stripe], send1.at[m, stripe], recv1.at[m, stripe], sib)

    def band(h):
        return pl.ds(h * half, half)

    def order(h):
        if h == 0:
            return (lambda j: 2 * j + 1 - x), (lambda j: 2 * j + x), flip_x, flip_y, 1 - y, y
        return (lambda j: 2 * (1 - y) + j), (lambda j: 2 * y + j), flip_y, flip_x, 1 - x, x

    def copy2(m, h, j):
        gone, _, target, _, _, _ = order(h)
        return send(
            total.at[m, gone(j), band(h)], got2.at[m, h, j], send2.at[2 * m + h, j], recv2.at[2 * m + h, j], target
        )

    def copy3(m, h):
        _, kept, _, target, far, _ = order(h)
        return send(total.at[m, kept(far), band(h)], got3.at[m, h], send3.at[m, h], recv3.at[m, h], target)

    def add_to(dst, src):
        step = 32

        def one(at, _):
            at = pl.ds(pl.multiple_of(at * step, step), step)
            dst[at, :] = (dst[at, :].astype(F32) + src[at, :].astype(F32)).astype(dst.dtype)
            return 0

        lax.fori_loop(0, dst.shape[0] // step, one, 0)

    def compute(m):
        load_right(m, False)
        if m + 1 < 3:
            load_right(m + 1, True)

        def one(k, _):
            @pl.when(k < 7)
            def _():
                load_left(m, k + 1, True)

            if m + 1 < 3:
                @pl.when(k == 7)
                def _():
                    load_left(m + 1, 0, True)

            load_left(m, k, False)
            value = lax.dot_general(
                left_buf[k % 2], right_buf[m % 2], (((0,), (0,)), ((), ())), preferred_element_type=F32
            ).astype(BF16)

            @pl.when(k < 4)
            def _():
                away[m, k] = value
                copy1(m, k).start()

            @pl.when(k >= 4)
            def _():
                total[m, k - 4] = value

            return 0

        lax.fori_loop(0, 8, one, 0)

        def join(stripe, _):
            copy1(m, stripe).wait()
            add_to(total.at[m, stripe], landed.at[m, stripe])
            return 0

        lax.fori_loop(0, 4, join, 0)
        for h in range(2):
            for j in range(2):
                copy2(m, h, j).start()

    def second(m):
        for h in range(2):
            _, kept, _, _, far, near = order(h)
            for j in range(2):
                copy2(m, h, j).wait()
            add_to(total.at[m, kept(far), band(h)], got2.at[m, h, far])
            copy3(m, h).start()
            add_to(total.at[m, kept(near), band(h)], got2.at[m, h, near])

    def third(m):
        for h in range(2):
            _, kept, _, _, _, near = order(h)
            copy3(m, h).wait()
            step = 32

            def one(at, _):
                at = at * step
                value = total[m, kept(near), pl.ds(pl.multiple_of(h * half + at, step), step), :].astype(F32)
                value = value + got3[m, h, pl.ds(pl.multiple_of(at, step), step), :].astype(F32)
                out_ref[m, pl.ds(pl.multiple_of(h * half + at, step), step), :] = value
                return 0

            lax.fori_loop(0, half // step, one, 0)

    load_right(0, True)
    load_left(0, 0, True)
    pl.semaphore_wait(barrier, 3)
    compute(0)
    compute(1)
    second(0)
    compute(2)
    third(0)
    second(1)
    third(1)
    second(2)
    third(2)


def ffn_grads(lefts, rights):
    part, height = lefts[0][0].shape
    width = rights[0][0].shape[1]
    rows = height // 8
    half = rows // 2
    dma = pltpu.SemaphoreType.DMA
    operands = [ref for group in (*lefts, *rights) for ref in group]
    return pl.pallas_call(
        ffn_grads_kernel,
        in_specs=[pl.BlockSpec(memory_space=pl.ANY)] * len(operands),
        out_specs=pl.BlockSpec(memory_space=pltpu.VMEM),
        out_shape=jax.ShapeDtypeStruct((3, rows, width), F32),
        scratch_shapes=[
            pltpu.VMEM((2, HALVES * part, rows), BF16),
            pltpu.VMEM((2, HALVES * part, width), BF16),
            pltpu.VMEM((3, 4, rows, width), BF16),
            pltpu.VMEM((3, 4, rows, width), BF16),
            pltpu.VMEM((3, 4, rows, width), BF16),
            pltpu.VMEM((3, 2, 2, half, width), BF16),
            pltpu.VMEM((3, 2, half, width), BF16),
            dma((2, HALVES)), dma((2, HALVES)), dma((3, 4)), dma((3, 4)),
            dma((6, 2)), dma((6, 2)), dma((3, 2)), dma((3, 2)),
        ],
        compiler_params=pltpu.CompilerParams(
            collective_id=4, has_side_effects=True, vmem_limit_bytes=60 * 1024 * 1024
        ),
        name="ffn_grads",
    )(*operands)


def shifted(value, axis, steps):
    count = lax.axis_size(axis)
    first, last = (max(0, -steps), min(count, count - steps))
    return lax.ppermute(value, axis, [(source, source + steps) for source in range(first, last)])


def matmul(left, right):
    return jnp.dot(left, right, preferred_element_type=F32)


def dot_tn(left, right):
    return jnp.einsum("rd,re->de", left, right, preferred_element_type=F32)


def dot_nt(left, right):
    return jnp.einsum("re,de->rd", left, right, preferred_element_type=F32)


def rms_scale(value_in, gain_vec, epsilon):
    return value_in * lax.rsqrt(jnp.mean(value_in * value_in, axis=-1, keepdims=True) + epsilon) * gain_vec


def norm_back(value_in, gain_vec, upstream, epsilon):
    inv_scale = lax.rsqrt(jnp.mean(value_in * value_in, axis=-1, keepdims=True) + epsilon)
    scaled_up = upstream * gain_vec
    gain_term = jnp.sum(upstream * value_in * inv_scale, axis=0)
    cubed = inv_scale * inv_scale * inv_scale
    back_value = inv_scale * scaled_up - value_in * cubed * jnp.mean(
        scaled_up * value_in, axis=-1, keepdims=True
    )
    return (back_value, gain_term)


def since_start(doc_lengths, offset, rows):
    ends = jnp.cumsum(doc_lengths[0])
    position = offset + jnp.arange(rows, dtype=jnp.int32)
    starts = jnp.max(jnp.where(position[:, None] >= ends[None, :], ends[None, :], 0), axis=1)
    return jnp.broadcast_to((position - starts)[:, None], (rows, BLOCK)).astype(jnp.int32)


def scatter_all(value, dim):
    part = lax.psum_scatter(value, "dp", scatter_dimension=dim, tiled=True)
    return lax.psum_scatter(part, "narrow", scatter_dimension=dim, tiled=True)


def local(
    tokens,
    doc_lengths,
    attn_gain,
    w_query,
    w_key,
    w_value,
    w_beta,
    conv_weight,
    out_gain,
    w_out,
    mlp_gain,
    w_gate,
    w_up,
    w_down,
    grad_out,
):
    tok_rows, model_width = tokens.shape
    offset = lax.axis_index("narrow") * tok_rows
    half = tok_rows // HALVES
    parts = [slice(at * half, (at + 1) * half) for at in range(HALVES)]

    def gather(rows):
        return lax.all_gather(rows, "narrow", axis=0, tiled=True)

    def scatter(rows):
        return lax.psum_scatter(rows, "narrow", scatter_dimension=0, tiled=True)

    cot = gather(grad_out)
    since = since_start(doc_lengths, offset, tok_rows)
    inputs = tokens.astype(F32)
    normed = rms_scale(inputs, attn_gain, 1e-06).astype(BF16)
    query, key, value = (matmul(normed, w).astype(BF16) for w in (w_query, w_key, w_value))
    beta_logit = matmul(normed, w_beta)
    halo = shifted(
        jnp.stack([part[tok_rows - PAD :] for part in (query, key, value)]), "narrow", 1
    )
    out_add, out_map, new_add, new_map, inverse, starts, end = mixer_forward(
        since, beta_logit, query, key, value, halo, conv_weight
    )
    transfer = end[:, :, BLOCK:].astype(BF16)
    entry = carry_chain(transfer, end[:, :, :BLOCK], "narrow", True)
    gain_row = out_gain[None, :]
    attn_mixed = mixer_join(out_add, out_map, entry, gain_row)
    hidden = inputs + matmul(attn_mixed, w_out)
    normed_mlp = rms_scale(hidden, mlp_gain, 1e-06).astype(BF16)
    normed_mlp, cot = lax.optimization_barrier((normed_mlp, cot))
    cot = cot.reshape(-1, tok_rows, model_width)
    cot = [cot[:, part].reshape(-1, model_width) for part in parts]
    gathered = [gather(normed_mlp[part]) for part in parts]
    activation, d_gate, d_up, d_normed_parts, out_parts = [], [], [], [], []
    for at in range(HALVES):
        gate_proj = matmul(gathered[at], w_gate)
        up_proj = matmul(gathered[at], w_up)
        gate_sigmoid = jax.nn.sigmoid(gate_proj)
        silu_gate = gate_proj * gate_sigmoid
        activation.append((silu_gate * up_proj).astype(BF16))
        d_act = jnp.einsum("rd,fd->rf", cot[at], w_down, preferred_element_type=F32)
        d_gate.append(
            (d_act * up_proj * gate_sigmoid * (1.0 + gate_proj * (1.0 - gate_sigmoid))).astype(BF16)
        )
        d_up.append((d_act * silu_gate).astype(BF16))
        d_part = (dot_nt(d_gate[at], w_gate) + dot_nt(d_up[at], w_up)).astype(BF16)
        out_parts.append(matmul(activation[at], w_down).astype(BF16))
        if at + 1 < HALVES:
            d_part, out_parts[at], gathered[at + 1] = lax.optimization_barrier(
                (d_part, out_parts[at], gathered[at + 1])
            )
        d_normed_parts.append(scatter(d_part))
    if lax.axis_size("dp") == 8:
        ffn_sums = ffn_grads((gathered, cot), (d_gate, d_up, activation))
    else:
        ffn_sums = [
            lax.psum_scatter(
                sum(dot_tn(a, c) for a, c in zip(left, right)).astype(BF16), "dp", scatter_dimension=0, tiled=True
            )
            for left, right in ((gathered, d_gate), (gathered, d_up), (cot, activation))
        ]
    d_normed_parts, out_parts, ffn_sums = lax.optimization_barrier((d_normed_parts, out_parts, ffn_sums))
    grad_gate, grad_up, grad_down = ffn_sums[0].astype(F32), ffn_sums[1].astype(F32), ffn_sums[2].astype(F32).T
    d_normed_mlp = jnp.concatenate(d_normed_parts, axis=0).astype(F32)
    d_hidden_norm, mlp_gain_term = norm_back(hidden, mlp_gain, d_normed_mlp, 1e-06)
    d_hidden = grad_out.astype(F32) + d_hidden_norm
    d_branch = d_hidden.astype(BF16)
    d_mixed = dot_nt(d_branch, w_out)
    d_core, start_grad, out_gain_term = mixer_core_back(out_add, out_map, entry, gain_row, d_mixed)
    exit_grad = carry_chain(transfer, start_grad, "narrow", False)
    exit_grad, out_parts = lax.optimization_barrier((exit_grad, out_parts))
    ffn_parts = [scatter(part) for part in out_parts]
    mixer_args = (
        since, beta_logit, query, key, value, halo, conv_weight,
        new_add, new_map, inverse, starts, entry, exit_grad, d_core,
    )
    if lax.axis_size("dp") == 8:
        grads, d_normed, conv_term, d_beta = fused_backward(
            *mixer_args, w_query, w_key, w_value, attn_mixed, normed, d_branch
        )
    else:
        d_proj, d_halo, conv_term, d_beta = mixer_backward(*mixer_args)
        after = shifted(d_halo.astype(BF16), "narrow", -1)
        d_proj = d_proj.at[:, tok_rows - PAD :].add(after)
        d_normed = sum(dot_nt(part, w) for part, w in zip(d_proj, (w_query, w_key, w_value)))
        pairs = [(normed, part) for part in d_proj] + [(d_branch, attn_mixed)]
        grads = jnp.stack([scatter_all(dot_tn(a, c).astype(BF16), 0).astype(F32) for a, c in pairs])
    d_beta_low = d_beta.astype(BF16)
    beta_term = jnp.einsum("rd,rh->dh", normed, d_beta_low, preferred_element_type=F32)
    d_normed = d_normed + jnp.einsum("rh,dh->rd", d_beta_low, w_beta, preferred_element_type=F32)
    d_input_norm, attn_gain_term = norm_back(inputs, attn_gain, d_normed, 1e-06)
    grad_tokens = (d_hidden + d_input_norm).astype(BF16)
    devices = lax.axis_size("dp") * lax.axis_size("narrow")
    heads = w_beta.shape[1]
    taps = 3 * CONV
    gain_share = BLOCK // devices
    gain_column = jnp.pad(
        out_gain_term.reshape(devices, gain_share), ((0, 0), (0, model_width // devices - gain_share))
    ).reshape(model_width, 1)
    small = jnp.concatenate(
        [
            beta_term,
            conv_term.reshape(taps, model_width).T,
            attn_gain_term[:, None],
            mlp_gain_term[:, None],
            gain_column,
        ],
        axis=1,
    )
    small = jnp.pad(small, ((0, 0), (0, BLOCK - small.shape[1])))
    if lax.axis_size("dp") == 8:
        small = reduce_small(small)
    else:
        small = lax.psum_scatter(small, ("dp", "narrow"), scatter_dimension=0, tiled=True)
    grad_beta = small[:, :heads]
    grad_conv = small[:, heads : heads + taps].T.reshape(3, CONV, -1)
    grad_attn_gain = small[:, heads + taps]
    grad_mlp_gain = small[:, heads + taps + 1]
    grad_out_gain = small[:gain_share, heads + taps + 2]
    ffn_parts, grads = lax.optimization_barrier((ffn_parts, grads))
    block_out = (hidden + jnp.concatenate(ffn_parts, axis=0).astype(F32)).astype(BF16)
    grad_query, grad_key, grad_value = grads[0], grads[1], grads[2]
    grad_w_out = grads[3].T
    return (
        block_out,
        grad_tokens,
        grad_attn_gain,
        grad_query,
        grad_key,
        grad_value,
        grad_beta,
        grad_conv,
        grad_out_gain,
        grad_w_out,
        grad_mlp_gain,
        grad_gate,
        grad_up,
        grad_down,
    )


def solution(mesh):
    placed = (
        P(("dp", "narrow"), None),
        P("dp", None),
        P(),
        P(),
        P(),
        P(),
        P(),
        P(),
        P(),
        P(),
        P(),
        P(None, "narrow"),
        P(None, "narrow"),
        P("narrow", None),
        P(("dp", "narrow"), None),
    )
    return jax.shard_map(
        local,
        mesh=mesh,
        in_specs=placed,
        out_specs=(
            P(("dp", "narrow"), None),
            P(("dp", "narrow"), None),
            P(("dp", "narrow")),
            P(("dp", "narrow"), None),
            P(("dp", "narrow"), None),
            P(("dp", "narrow"), None),
            P(("dp", "narrow"), None),
            P(None, None, ("dp", "narrow")),
            P(("dp", "narrow")),
            P(None, ("dp", "narrow")),
            P(("dp", "narrow")),
            P("dp", "narrow"),
            P("dp", "narrow"),
            P("narrow", "dp"),
        ),
        check_vma=False,
    )
```

```python
import functools

import jax
import jax.numpy as jnp
from jax import lax
from jax.experimental import pallas as pl
from jax.experimental.pallas import tpu as pltpu
from jax.sharding import PartitionSpec as P

CONV = 4
BLOCK = 128
HEADS_STEP = 2
PAD = 8
MESH = pl.DeviceIdType.MESH
F32 = jnp.float32
BF16 = jnp.bfloat16
VMEM_LIMIT = 56 * 1024 * 1024


def mm(left, right, contract=(1, 0)):
    return lax.dot_general(
        left.astype(BF16),
        right.astype(BF16),
        (((contract[0],), (contract[1],)), ((), ())),
        preferred_element_type=F32,
    )


def mm_nt(left, right):
    return mm(left, right, (1, 1))


def mm_tn(left, right):
    return mm(left, right, (0, 0))


def iotas(size):
    row = lax.broadcasted_iota(jnp.int32, (size, size), 0)
    col = lax.broadcasted_iota(jnp.int32, (size, size), 1)
    return row, col


def block_masks(since):
    size = since.shape[0]
    row, col = iotas(size)
    back = row - col
    causal = (back >= 0) & (back <= since)
    strict = (back > 0) & (back <= since)
    keep = (since > row).astype(F32)
    last = since[size - 1 : size, :]
    last_mask = (row >= size - 1 - last).astype(F32)
    keep_last = (last > size - 1).astype(F32)
    return causal, strict, keep, last_mask, keep_last


def unit_lower_inverses(lowers):
    size = lowers[0].shape[0]
    row, col = iotas(size)
    width = 1
    inverses = None
    while width < size:
        join = (row // (2 * width) == col // (2 * width)) & (row // width != col // width)
        pieces = [jnp.where(join, low, 0.0) for low in lowers]
        if inverses is None:
            eye = (row == col).astype(F32)
            inverses = [eye - piece for piece in pieces]
        else:
            halves = [mm(piece, inv) for piece, inv in zip(pieces, inverses)]
            inverses = [inv - mm(inv, half) for inv, half in zip(inverses, halves)]
        width *= 2
    return inverses


def conv_front(ext, proj, halo, taps, since):
    rows = proj.shape[0]
    ext[0:PAD, :] = halo.astype(F32)
    ext[PAD : PAD + rows, :] = proj
    pre = proj * taps[0:1, :]
    for lag in range(1, CONV):
        moved = ext[PAD - lag : PAD - lag + rows, :]
        pre = pre + jnp.where(since >= lag, moved, 0.0) * taps[lag : lag + 1, :]
    gate = 1.0 / (1.0 + jnp.exp(-pre))
    return pre, gate, pre * gate


def unit_rows(value):
    inv = lax.rsqrt(jnp.sum(value * value, axis=-1, keepdims=True) + 1e-06)
    return value * inv, inv


def head_column(array, head):
    lane = lax.broadcasted_iota(jnp.int32, array.shape, 1)
    return jnp.sum(jnp.where(lane == head, array, 0.0), axis=1, keepdims=True)


def forward_kernel(
    since_ref, beta_ref, query_ref, key_ref, value_ref, halo_ref, taps_ref,
    out_add_ref, out_map_ref, new_add_ref, new_map_ref, inverse_ref, starts_ref, end_ref,
    ext,
):
    rows = since_ref.shape[0]
    blocks = rows // BLOCK
    since = since_ref[...]
    jobs = []
    for sub in range(HEADS_STEP):
        head = pl.program_id(0) * HEADS_STEP + sub
        lanes = slice(sub * BLOCK, (sub + 1) * BLOCK)
        mixed = []
        for part, ref in enumerate((query_ref, key_ref, value_ref)):
            _, _, act = conv_front(
                ext.at[sub * 3 + part], ref[:, lanes].astype(F32), halo_ref[part, :, lanes],
                taps_ref[part, :, lanes], since,
            )
            mixed.append(act)
        query = unit_rows(mixed[0])[0] * (BLOCK ** -0.5)
        key = unit_rows(mixed[1])[0]
        beta = 1.0 / (1.0 + jnp.exp(-head_column(beta_ref[...], head)))
        jobs.append((lanes, query, key, mixed[2], beta))
    lowers, scores = [], []
    for lanes, query, key, value, beta in jobs:
        for blk in range(blocks):
            span = slice(blk * BLOCK, (blk + 1) * BLOCK)
            causal, strict, _, _, _ = block_masks(since[span])
            both = mm_nt(jnp.concatenate([key[span], query[span]], axis=0), key[span])
            lowers.append(jnp.where(strict, both[:BLOCK] * beta[span], 0.0))
            scores.append(jnp.where(causal, both[BLOCK:], 0.0).astype(BF16))
    inverses = [inv.astype(BF16) for inv in unit_lower_inverses(lowers)]
    row, col = iotas(BLOCK)
    eye = (row == col).astype(F32)
    states = [jnp.concatenate([jnp.zeros((BLOCK, BLOCK), F32), eye], axis=1) for _ in jobs]
    for blk in range(blocks):
        span = slice(blk * BLOCK, (blk + 1) * BLOCK)
        _, _, keep, last_mask, keep_last = block_masks(since[span])
        for sub, (lanes, query, key, value, beta) in enumerate(jobs):
            at = sub * blocks + blk
            inverse_ref[sub, blk] = inverses[at]
            state = states[sub].astype(BF16)
            starts_ref[sub, blk] = state
            stacked = jnp.concatenate([key[span] * keep, query[span] * keep], axis=0)
            seen = mm(stacked, state)
            rest = jnp.concatenate([value[span], jnp.zeros((BLOCK, BLOCK), F32)], axis=1)
            right = (rest - seen[:BLOCK]) * beta[span]
            new = mm(inverses[at], right).astype(BF16)
            out = seen[BLOCK:] + mm(scores[at], new)
            out_add_ref[span, lanes] = out[:, :BLOCK].astype(BF16)
            out_map_ref[span, lanes] = out[:, BLOCK:].astype(BF16)
            new_add_ref[span, lanes] = new[:, :BLOCK]
            new_map_ref[span, lanes] = new[:, BLOCK:]
            keep_both = jnp.concatenate([keep_last, keep_last], axis=1)
            states[sub] = states[sub] * keep_both + mm_tn(key[span] * last_mask, new)
    for sub in range(len(jobs)):
        end_ref[sub] = states[sub]


def whole_spec(shape):
    return pl.BlockSpec(shape, lambda h: (0,) * len(shape))


def head_spec(rows):
    return pl.BlockSpec((rows, HEADS_STEP * BLOCK), lambda h: (0, h))


def per_head(*tail):
    return pl.BlockSpec((HEADS_STEP,) + tail, lambda h: (h,) + (0,) * len(tail))


def lanes_spec(first, second):
    return pl.BlockSpec((first, second, HEADS_STEP * BLOCK), lambda h: (0, 0, h))


def params():
    return pltpu.CompilerParams(vmem_limit_bytes=VMEM_LIMIT)


def mixer_forward(since, beta_logit, query, key, value, halo, taps):
    rows, width = query.shape
    heads = width // BLOCK
    blocks = rows // BLOCK
    wide = jax.ShapeDtypeStruct((rows, width), BF16)
    return pl.pallas_call(
        forward_kernel,
        grid=(heads // HEADS_STEP,),
        in_specs=[
            whole_spec(since.shape), whole_spec(beta_logit.shape),
            head_spec(rows), head_spec(rows), head_spec(rows),
            lanes_spec(3, PAD), lanes_spec(3, CONV),
        ],
        out_specs=[
            head_spec(rows), head_spec(rows), head_spec(rows), head_spec(rows),
            per_head(blocks, BLOCK, BLOCK), per_head(blocks, BLOCK, 2 * BLOCK),
            per_head(BLOCK, 2 * BLOCK),
        ],
        out_shape=[
            wide, wide, wide, wide,
            jax.ShapeDtypeStruct((heads, blocks, BLOCK, BLOCK), BF16),
            jax.ShapeDtypeStruct((heads, blocks, BLOCK, 2 * BLOCK), BF16),
            jax.ShapeDtypeStruct((heads, BLOCK, 2 * BLOCK), F32),
        ],
        scratch_shapes=[pltpu.VMEM((3 * HEADS_STEP, PAD + rows, BLOCK), F32)],
        compiler_params=params(),
        name="mixer_forward",
    )(since, beta_logit, query, key, value, halo, taps)


def join_kernel(out_add_ref, out_map_ref, entry_ref, gain_ref, mixed_ref):
    for sub in range(HEADS_STEP):
        lanes = slice(sub * BLOCK, (sub + 1) * BLOCK)
        core = out_add_ref[:, lanes].astype(F32) + mm(out_map_ref[:, lanes], entry_ref[sub])
        scale = lax.rsqrt(jnp.mean(core * core, axis=-1, keepdims=True) + 1e-05)
        mixed_ref[:, lanes] = (core * scale * gain_ref[...]).astype(BF16)


def mixer_join(out_add, out_map, entry, gain):
    rows, width = out_add.shape
    heads = width // BLOCK
    return pl.pallas_call(
        join_kernel,
        grid=(heads // HEADS_STEP,),
        in_specs=[head_spec(rows), head_spec(rows), per_head(BLOCK, BLOCK), whole_spec((1, BLOCK))],
        out_specs=head_spec(rows),
        out_shape=jax.ShapeDtypeStruct((rows, width), BF16),
        compiler_params=params(),
        name="mixer_join",
    )(out_add, out_map, entry, gain)


def core_back_kernel(
    out_add_ref, out_map_ref, entry_ref, gain_ref, branch_ref, w_out_ref, d_core_ref, start_ref, gain_out_ref
):
    @pl.when(pl.program_id(0) == 0)
    def _():
        gain_out_ref[...] = jnp.zeros_like(gain_out_ref)

    upstream = mm_nt(branch_ref[...], w_out_ref[...])
    for sub in range(HEADS_STEP):
        lanes = slice(sub * BLOCK, (sub + 1) * BLOCK)
        out_map = out_map_ref[:, lanes]
        core = out_add_ref[:, lanes].astype(F32) + mm(out_map, entry_ref[sub])
        scale = lax.rsqrt(jnp.mean(core * core, axis=-1, keepdims=True) + 1e-05)
        unit = core * scale
        up = upstream[:, lanes]
        gain_out_ref[...] += jnp.sum(up * unit, axis=0, keepdims=True)
        scaled = up * gain_ref[...]
        d_core = scale * (scaled - unit * jnp.mean(scaled * unit, axis=-1, keepdims=True))
        d_core = d_core.astype(BF16)
        d_core_ref[:, lanes] = d_core
        start_ref[sub] = mm_tn(out_map, d_core)


def mixer_core_back(out_add, out_map, entry, gain, branch, w_out):
    rows, width = out_add.shape
    heads = width // BLOCK
    return pl.pallas_call(
        core_back_kernel,
        grid=(heads // HEADS_STEP,),
        in_specs=[
            head_spec(rows), head_spec(rows), per_head(BLOCK, BLOCK), whole_spec((1, BLOCK)),
            whole_spec(branch.shape), pl.BlockSpec((HEADS_STEP * BLOCK, width), lambda h: (h, 0)),
        ],
        out_specs=[head_spec(rows), per_head(BLOCK, BLOCK), whole_spec((1, BLOCK))],
        out_shape=[
            jax.ShapeDtypeStruct((rows, width), BF16),
            jax.ShapeDtypeStruct((heads, BLOCK, BLOCK), F32),
            jax.ShapeDtypeStruct((1, BLOCK), F32),
        ],
        compiler_params=params(),
        name="mixer_core_back",
    )(out_add, out_map, entry, gain, branch, w_out)


def backward_heads(
    step, since_ref, beta_ref, query_ref, key_ref, value_ref, halo_ref, taps_ref,
    new_add_ref, new_map_ref, inverse_ref, starts_ref, entry_ref, exit_ref, d_core_ref,
    d_taps_ref, d_beta_ref, ext, back, emit,
):
    rows = since_ref.shape[0]
    blocks = rows // BLOCK
    since = since_ref[...]
    jobs = []
    for sub in range(HEADS_STEP):
        head = step * HEADS_STEP + sub
        lanes = slice(sub * BLOCK, (sub + 1) * BLOCK)
        fronts = []
        for part, ref in enumerate((query_ref, key_ref, value_ref)):
            fronts.append(
                conv_front(
                    ext.at[sub * 3 + part], ref[:, lanes].astype(F32), halo_ref[part, :, lanes],
                    taps_ref[part, :, lanes], since,
                )
            )
        query_unit, query_inv = unit_rows(fronts[0][2])
        key, key_inv = unit_rows(fronts[1][2])
        query = query_unit * (BLOCK ** -0.5)
        beta = 1.0 / (1.0 + jnp.exp(-head_column(beta_ref[...], head)))
        jobs.append((head, lanes, fronts, query, query_unit, query_inv, key, key_inv, beta))

    saved = {}
    for sub, (head, lanes, fronts, query, query_unit, query_inv, key, key_inv, beta) in enumerate(jobs):
        entry = entry_ref[sub].astype(BF16)
        for blk in range(blocks):
            span = slice(blk * BLOCK, (blk + 1) * BLOCK)
            causal, _, keep, last_mask, _ = block_masks(since[span])
            start = starts_ref[sub, blk]
            state = (start[:, :BLOCK].astype(F32) + mm(start[:, BLOCK:], entry)).astype(BF16)
            new = (new_add_ref[span, lanes].astype(F32) + mm(new_map_ref[span, lanes], entry)).astype(BF16)
            scores = jnp.where(causal, mm_nt(query[span], key[span]), 0.0).astype(BF16)
            d_out = d_core_ref[span, lanes]
            d_new = mm_tn(scores, d_out)
            d_state = mm_tn(query[span] * keep, d_out)
            saved[sub, blk] = (state, new, d_out, d_new, d_state)

    carried = [exit_ref[sub].astype(F32) for sub in range(HEADS_STEP)]
    chain = {}
    for blk in reversed(range(blocks)):
        span = slice(blk * BLOCK, (blk + 1) * BLOCK)
        _, _, keep, last_mask, keep_last = block_masks(since[span])
        for sub, (head, lanes, fronts, query, query_unit, query_inv, key, key_inv, beta) in enumerate(jobs):
            state, new, d_out, d_new, d_state = saved[sub, blk]
            after = carried[sub].astype(BF16)
            d_new = d_new + mm(key[span] * last_mask, after)
            d_right = mm_tn(inverse_ref[sub, blk], d_new)
            d_rest = d_right * beta[span]
            carried[sub] = carried[sub] * keep_last + d_state - mm_tn(key[span] * keep, d_rest)
            chain[sub, blk] = (after, d_right, d_rest)

    lane = lax.broadcasted_iota(jnp.int32, (rows, beta_ref.shape[1]), 1)
    d_beta_all = jnp.zeros((rows, beta_ref.shape[1]), F32)
    for sub, (head, lanes, fronts, query, query_unit, query_inv, key, key_inv, beta) in enumerate(jobs):
        d_queries, d_keys, d_values, d_betas = [], [], [], []
        for blk in range(blocks):
            span = slice(blk * BLOCK, (blk + 1) * BLOCK)
            causal, strict, keep, last_mask, _ = block_masks(since[span])
            state, new, d_out, _, _ = saved[sub, blk]
            after, d_right, d_rest = chain[sub, blk]
            both = mm_nt(jnp.concatenate([d_out, d_right.astype(BF16)], axis=0), new)
            d_scores = jnp.where(causal, both[:BLOCK], 0.0).astype(BF16)
            d_gram = (jnp.where(strict, both[BLOCK:], 0.0) * (-beta[span])).astype(BF16)
            key_b = key[span].astype(BF16)
            from_state = mm_nt(jnp.concatenate([d_out, d_rest.astype(BF16)], axis=0), state)
            left = mm(jnp.concatenate([d_scores, d_gram], axis=0), key_b)
            d_queries.append(from_state[:BLOCK] * keep + left[:BLOCK])
            d_key = left[BLOCK:] + mm_tn(
                jnp.concatenate([d_scores, d_gram], axis=0),
                jnp.concatenate([query[span].astype(BF16), key_b], axis=0),
            )
            d_key = d_key + mm_nt(new, after) * last_mask - from_state[BLOCK:] * keep
            d_keys.append(d_key)
            d_values.append(d_rest)
            d_betas.append(
                jnp.sum(d_right * new.astype(F32), axis=1, keepdims=True) * (1.0 - beta[span])
            )
        d_query = jnp.concatenate(d_queries, axis=0) * (BLOCK ** -0.5)
        d_key = jnp.concatenate(d_keys, axis=0)
        d_query = query_inv * (
            d_query - query_unit * jnp.sum(d_query * query_unit, axis=-1, keepdims=True)
        )
        d_key = key_inv * (d_key - key * jnp.sum(d_key * key, axis=-1, keepdims=True))
        d_value = jnp.concatenate(d_values, axis=0)
        d_beta_all = d_beta_all + jnp.where(lane == head, jnp.concatenate(d_betas, axis=0), 0.0)
        for part, d_act in enumerate((d_query, d_key, d_value)):
            pre, gate, _ = fronts[part]
            taps = taps_ref[part, :, lanes]
            source = ext.at[sub * 3 + part]
            d_pre = d_act * gate * (1.0 + pre * (1.0 - gate))
            room = back.at[(sub * 3 + part) % 2]
            total = None
            d_taps = []
            for lag in range(CONV):
                masked = d_pre if lag == 0 else jnp.where(since >= lag, d_pre, 0.0)
                moved = source[PAD - lag : PAD - lag + rows, :]
                d_taps.append(jnp.sum(masked * moved, axis=0, keepdims=True))
                room[lag, 0:PAD, :] = jnp.zeros((PAD, BLOCK), F32)
                room[lag, PAD : PAD + rows, :] = masked * taps[lag : lag + 1, :]
                room[lag, PAD + rows : PAD + rows + PAD, :] = jnp.zeros((PAD, BLOCK), F32)
                term = room[lag, lag : lag + PAD + rows, :]
                total = term if total is None else total + term
            d_taps_ref[part, :, lanes] = jnp.concatenate(d_taps, axis=0)
            emit(part, lanes, total)

    @pl.when(step == 0)
    def _():
        d_beta_ref[...] = d_beta_all

    @pl.when(step > 0)
    def _():
        d_beta_ref[...] += d_beta_all


def backward_kernel(*refs):
    d_proj_ref, d_halo_ref, d_taps_ref, d_beta_ref, ext, back = refs[14:]

    def emit(part, lanes, total):
        d_halo_ref[part, :, lanes] = total[:PAD]
        d_proj_ref[part, :, lanes] = total[PAD:].astype(BF16)

    backward_heads(pl.program_id(0), *refs[:14], d_taps_ref, d_beta_ref, ext, back, emit)


def mixer_backward(
    since, beta_logit, query, key, value, halo, taps, new_add, new_map, inverse, starts, entry, exit_grad, d_core
):
    rows, width = query.shape
    heads = width // BLOCK
    blocks = rows // BLOCK
    return pl.pallas_call(
        backward_kernel,
        grid=(heads // HEADS_STEP,),
        in_specs=[
            whole_spec(since.shape), whole_spec(beta_logit.shape),
            head_spec(rows), head_spec(rows), head_spec(rows),
            lanes_spec(3, PAD), lanes_spec(3, CONV),
            head_spec(rows), head_spec(rows),
            per_head(blocks, BLOCK, BLOCK), per_head(blocks, BLOCK, 2 * BLOCK),
            per_head(BLOCK, BLOCK), per_head(BLOCK, BLOCK), head_spec(rows),
        ],
        out_specs=[
            lanes_spec(3, rows), lanes_spec(3, PAD), lanes_spec(3, CONV), whole_spec(beta_logit.shape),
        ],
        out_shape=[
            jax.ShapeDtypeStruct((3, rows, width), BF16),
            jax.ShapeDtypeStruct((3, PAD, width), F32),
            jax.ShapeDtypeStruct((3, CONV, width), F32),
            jax.ShapeDtypeStruct(beta_logit.shape, F32),
        ],
        scratch_shapes=[
            pltpu.VMEM((3 * HEADS_STEP, PAD + rows, BLOCK), F32),
            pltpu.VMEM((2, CONV, PAD + rows + PAD, BLOCK), F32),
        ],
        compiler_params=params(),
        name="mixer_backward",
    )(
        since, beta_logit, query, key, value, halo, taps, new_add, new_map, inverse, starts, entry, exit_grad, d_core
    )


GROUPS = 8
HALVES = 2


def chain_kernel(axis, forward, map_ref, add_ref, out_ref, sent, landed, send_sem, recv_sem):
    count = lax.axis_size(axis)
    me = lax.axis_index(axis)
    heads = add_ref.shape[0]
    step = heads // GROUPS
    up, down = (me + 1, me - 1) if forward else (me - 1, me + 1)
    first, last = (0, count - 1) if forward else (count - 1, 0)
    barrier = pltpu.get_barrier_semaphore()

    @pl.when(me != first)
    def _():
        pl.semaphore_signal(barrier, inc=1, device_id={axis: down}, device_id_type=MESH)

    @pl.when(me != last)
    def _():
        pl.semaphore_wait(barrier, 1)

    def copy(group, target):
        return pltpu.make_async_remote_copy(
            src_ref=sent.at[group],
            dst_ref=landed.at[group],
            send_sem=send_sem.at[group],
            recv_sem=recv_sem.at[group],
            device_id={axis: target},
            device_id_type=MESH,
        )

    for group in range(GROUPS):
        @pl.when(me != first)
        def _():
            copy(group, up).wait_recv()
            for sub in range(step):
                head = group * step + sub
                out_ref[head] = landed[group, sub].astype(F32)

        @pl.when(me == first)
        def _():
            out_ref[group * step : (group + 1) * step] = jnp.zeros((step,) + out_ref.shape[1:], F32)

        @pl.when(me != last)
        def _():
            for sub in range(step):
                head = group * step + sub
                if forward:
                    moved = mm(map_ref[head], out_ref[head])
                else:
                    moved = mm_tn(map_ref[head], out_ref[head])
                sent[group, sub] = (moved + add_ref[head]).astype(BF16)
            copy(group, up).start()

    @pl.when(me != last)
    def _():
        for group in range(GROUPS):
            copy(group, up).wait_send()


def carry_chain(map_part, add_part, axis, forward):
    heads = add_part.shape[0]
    part = (GROUPS, heads // GROUPS, BLOCK, BLOCK)
    return pl.pallas_call(
        functools.partial(chain_kernel, axis, forward),
        in_specs=[pl.BlockSpec(memory_space=pltpu.VMEM)] * 2,
        out_specs=pl.BlockSpec(memory_space=pltpu.VMEM),
        out_shape=jax.ShapeDtypeStruct(add_part.shape, F32),
        scratch_shapes=[
            pltpu.VMEM(part, BF16),
            pltpu.VMEM(part, BF16),
            pltpu.SemaphoreType.DMA((GROUPS,)),
            pltpu.SemaphoreType.DMA((GROUPS,)),
        ],
        compiler_params=pltpu.CompilerParams(
            collective_id=1 if forward else 2, has_side_effects=True, vmem_limit_bytes=VMEM_LIMIT // 2
        ),
        name="carry_forward" if forward else "carry_backward",
    )(map_part, add_part)


def bits(dp):
    core, x, y = dp % 2, (dp // 2) % 2, dp // 4
    return core, x, y, dp + 1 - 2 * core, dp + 2 * (1 - 2 * x), dp + 4 * (1 - 2 * y)


def remote(src, dst, send_sem, recv_sem, target):
    return pltpu.make_async_remote_copy(
        src_ref=src, dst_ref=dst, send_sem=send_sem, recv_sem=recv_sem, device_id=target, device_id_type=MESH
    )


def meet(dp_targets, narrow_targets):
    barrier = pltpu.get_barrier_semaphore()
    for target in dp_targets:
        pl.semaphore_signal(barrier, inc=1, device_id={"dp": target}, device_id_type=MESH)
    for target in narrow_targets:
        pl.semaphore_signal(barrier, inc=1, device_id={"narrow": target}, device_id_type=MESH)
    pl.semaphore_wait(barrier, len(dp_targets) + len(narrow_targets))


def add_rows(dst, src, step):
    def one(at, _):
        at = pl.ds(pl.multiple_of(at * step, step), step)
        dst[at, :] = (dst[at, :].astype(F32) + src[at, :].astype(F32)).astype(dst.dtype)
        return 0

    lax.fori_loop(0, dst.shape[0] // step, one, 0)


def small_kernel(small_ref, out_ref, landed, total, got2, got3, gotz, send1, recv1, send2, recv2, send3, recv3, sendz, recvz):
    dp, z = lax.axis_index("dp"), lax.axis_index("narrow")
    core, x, y, sib, flip_x, flip_y = bits(dp)
    depth = lax.axis_size("narrow")
    rows = small_ref.shape[0] // 8
    share = rows // depth
    peers = [(z + step) % depth for step in range(1, depth)]
    meet((sib, flip_x, flip_y), peers)

    def stripe_rows(stripe, which):
        return pl.ds(pl.multiple_of((stripe * 2 + which) * rows, rows), rows)

    def share_rows(at):
        return pl.ds(pl.multiple_of(at * share, share), share)

    first = [
        remote(small_ref.at[stripe_rows(k, 1 - core)], landed.at[k], send1.at[k], recv1.at[k], {"dp": sib})
        for k in range(4)
    ]
    for copy in first:
        copy.start()
    for k in range(4):
        first[k].wait()
        total[k] = small_ref[stripe_rows(k, core), :] + landed[k]
    second = [
        remote(total.at[2 * j + 1 - x], got2.at[j], send2.at[j], recv2.at[j], {"dp": flip_x}) for j in range(2)
    ]
    for copy in second:
        copy.start()
    for copy in second:
        copy.wait()
    third = remote(total.at[2 * (1 - y) + x], got3, send3, recv3, {"dp": flip_y})
    total[2 * (1 - y) + x] = total[2 * (1 - y) + x] + got2[1 - y]
    third.start()
    third.wait()
    mine = 2 * y + x
    total[mine] = total[mine] + got2[y] + got3[...]
    last = [
        remote(total.at[mine, share_rows(to)], gotz.at[k], sendz.at[k], recvz.at[k], {"narrow": to})
        for k, to in enumerate(peers)
    ]
    for copy in last:
        copy.start()
    value = total[mine, share_rows(z), :]
    for k, copy in enumerate(last):
        copy.wait()
        value = value + gotz[k]
    out_ref[...] = value


def reduce_small(small):
    height, lanes = small.shape
    depth = lax.axis_size("narrow")
    rows = height // 8
    share = rows // depth
    dma = pltpu.SemaphoreType.DMA
    return pl.pallas_call(
        small_kernel,
        in_specs=[pl.BlockSpec(memory_space=pltpu.VMEM)],
        out_specs=pl.BlockSpec(memory_space=pltpu.VMEM),
        out_shape=jax.ShapeDtypeStruct((share, lanes), F32),
        scratch_shapes=[
            pltpu.VMEM((4, rows, lanes), F32),
            pltpu.VMEM((4, rows, lanes), F32),
            pltpu.VMEM((2, rows, lanes), F32),
            pltpu.VMEM((rows, lanes), F32),
            pltpu.VMEM((depth - 1, share, lanes), F32),
            dma((4,)), dma((4,)), dma((2,)), dma((2,)), dma(()), dma(()), dma((depth - 1,)), dma((depth - 1,)),
        ],
        compiler_params=pltpu.CompilerParams(
            collective_id=3, has_side_effects=True, vmem_limit_bytes=16 * 1024 * 1024
        ),
        name="reduce_small",
    )(small)


RING = 3
HELD = 5


def fused_kernel(*refs):
    heads_in = refs[:14]
    since_ref = refs[0]
    (
        w_query_ref, w_key_ref, w_value_ref, mixed_ref, normed_hbm, branch_hbm,
        grad_hbm, d_normed_hbm, d_taps_ref, d_beta_ref,
        ext, back, left_own, left_sib, d_proj, d_proj_sib, halo_out, halo_in,
        total, got2, got3, gotz, d_normed, grad,
        local_sem, grad_sem, left_send, left_recv, right_send, right_recv, halo_send, halo_recv,
        send2, recv2, send3, recv3, sendz, recvz,
    ) = refs[14:]
    step = pl.program_id(0)
    units = pl.num_programs(0) - 1
    dp, z = lax.axis_index("dp"), lax.axis_index("narrow")
    core, x, y, sib, flip_x, flip_y = bits(dp)
    depth = lax.axis_size("narrow")
    tokens = since_ref.shape[0]
    parts = d_proj_sib.shape[1]
    rows = left_own.shape[2]
    cols = d_proj.shape[3]
    share = rows // depth
    peers = [(z + k) % depth for k in range(1, depth)]

    def stripe_lanes(stripe, which):
        return pl.ds(pl.multiple_of((stripe * 2 + which) * rows, rows), rows)

    def left_copy(k):
        source = (normed_hbm, branch_hbm)[k // 4]
        return remote(
            source.at[:, stripe_lanes(k % 4, 1 - core)], d_proj_sib.at[1 + k // 4, k % 4],
            left_send.at[k], left_recv.at[k], {"dp": sib},
        )

    def right_copies(unit):
        slot = unit % RING
        return [
            remote(
                d_proj.at[slot], d_proj_sib.at[slot, 0 : parts - 1],
                right_send.at[slot, 0], right_recv.at[slot, 0], {"dp": sib},
            ),
            remote(
                mixed_ref, d_proj_sib.at[slot, parts - 1],
                right_send.at[slot, 1], right_recv.at[slot, 1], {"dp": sib},
            ),
        ]

    def halo_copy(unit):
        return remote(
            halo_out.at[unit], halo_in.at[unit], halo_send.at[unit], halo_recv.at[unit], {"narrow": z - 1}
        )

    def order(unit):
        e = unit % 2

        def pick(even, odd):
            return (1 - e) * even + e * odd

        def away(j):
            return pick(2 * j + 1 - x, 2 * (1 - y) + j)

        def kept(j):
            return pick(2 * j + x, 2 * y + j)

        return away, kept, pick(flip_x, flip_y), pick(flip_y, flip_x), pick(1 - y, 1 - x), pick(y, x)

    def copy2(unit, j):
        away, _, target, _, _, _ = order(unit)
        return remote(total.at[unit % HELD, away(j)], got2.at[unit, j], send2.at[unit, j], recv2.at[unit, j], {"dp": target})

    def copy3(unit):
        _, kept, _, target, far, _ = order(unit)
        return remote(total.at[unit % HELD, kept(far)], got3.at[unit], send3.at[unit], recv3.at[unit], {"dp": target})

    def copyz(unit, part, k):
        _, kept, _, _, _, near = order(unit)
        at = pl.ds(pl.multiple_of(part * rows + peers[k] * share, share), share)
        return remote(
            total.at[unit % HELD, kept(near), at], gotz.at[unit, k, part * share : (part + 1) * share],
            sendz.at[unit, k, part], recvz.at[unit, k, part], {"narrow": peers[k]},
        )

    @pl.when(step == 0)
    def _():
        loads = [
            pltpu.make_async_copy(
                (normed_hbm, branch_hbm)[k // 4].at[:, stripe_lanes(k % 4, core)],
                d_proj.at[k // 3, k % 3], local_sem.at[k],
            )
            for k in range(8)
        ]
        for load in loads:
            load.start()
        back[:, :, 0:PAD, :] = jnp.zeros((2, CONV, PAD, BLOCK), F32)
        back[:, :, PAD + tokens :, :] = jnp.zeros((2, CONV, PAD, BLOCK), F32)
        d_normed[...] = jnp.zeros_like(d_normed)
        meet((sib, flip_x, flip_y), peers)
        for k in range(8):
            left_copy(k).start()
        for k in range(8):
            loads[k].wait()
            left_own[k // 4, k % 4] = d_proj[k // 3, k % 3].astype(F32).T.astype(BF16)

    @pl.when(step == 1)
    def _():
        for k in range(8):
            left_copy(k).wait()
            left_sib[k // 4, k % 4] = d_proj_sib[1 + k // 4, k % 4].astype(F32).T.astype(BF16)

    @pl.when(step >= 1)
    def _():
        unit = step - 1

        @pl.when(z < depth - 1)
        def _():
            halo_copy(unit).wait_recv()
            for part in range(3):
                extra = jnp.concatenate([jnp.zeros((PAD, cols), F32), halo_in[unit, part]], axis=0)
                tail = slice(tokens - 2 * PAD, tokens)
                d_proj[unit % RING, part, tail, :] = (
                    d_proj[unit % RING, part, tail, :].astype(F32) + extra
                ).astype(BF16)

        @pl.when(z > 0)
        def _():
            halo_copy(unit).wait_send()

        for copy in right_copies(unit):
            copy.start()

    @pl.when(step < units)
    def _():
        def emit(part, lanes, value):
            halo_out[step, part, :, lanes] = value[:PAD]
            d_proj[step % RING, part, :, lanes] = value[PAD:].astype(BF16)

        backward_heads(step, *heads_in, d_taps_ref, d_beta_ref, ext, back, emit)

        @pl.when(z > 0)
        def _():
            halo_copy(step).start()

    @pl.when(step >= 1)
    def _():
        unit = step - 1
        away, kept, _, _, _, _ = order(unit)
        for copy in right_copies(unit):
            copy.wait()

        def one(k, _):
            j = k % 2
            stripe = (k // 2) * kept(j) + (1 - k // 2) * away(j)
            for part in range(parts):
                which = part // (parts - 1)
                mine = d_proj[unit % RING, part] if which == 0 else mixed_ref[...]
                value = jnp.dot(left_own[which, stripe], mine, preferred_element_type=F32)
                value = value + jnp.dot(
                    left_sib[which, stripe], d_proj_sib[unit % RING, part], preferred_element_type=F32
                )
                total[unit % HELD, stripe, part * rows : (part + 1) * rows, :] = value.astype(BF16)

            @pl.when(k < 2)
            def _():
                copy2(unit, j).start()

            return 0

        lax.fori_loop(0, 4, one, 0)

        def normed_part(at, _):
            at = pl.ds(pl.multiple_of(at * 512, 512), 512)
            value = d_normed[:, at]
            for part, ref in enumerate((w_query_ref, w_key_ref, w_value_ref)):
                value = value + lax.dot_general(
                    d_proj[unit % RING, part], ref[at, :], (((1,), (1,)), ((), ())), preferred_element_type=F32
                )
            d_normed[:, at] = value
            return 0

        lax.fori_loop(0, d_normed.shape[1] // 512, normed_part, 0)

    def second(unit):
        _, kept, _, _, far, near = order(unit)
        for j in range(2):
            copy2(unit, j).wait()
        add_rows(total.at[unit % HELD, kept(far)], got2.at[unit, far], 64)
        copy3(unit).start()
        add_rows(total.at[unit % HELD, kept(near)], got2.at[unit, near], 64)

    def grad_copy(unit):
        at = pl.ds(pl.multiple_of(unit * cols, cols), cols)
        return pltpu.make_async_copy(grad.at[unit % 2], grad_hbm.at[:, :, at], grad_sem.at[unit % 2])

    def third(unit):
        _, kept, _, _, _, near = order(unit)
        copy3(unit).wait()
        add_rows(total.at[unit % HELD, kept(near)], got3.at[unit], 64)
        for k in range(depth - 1):
            for part in range(parts):
                copyz(unit, part, k).start()

    def fourth(unit):
        _, kept, _, _, _, near = order(unit)
        for k in range(depth - 1):
            for part in range(parts):
                copyz(unit, part, k).wait()
        @pl.when(unit >= 2)
        def _():
            grad_copy(unit - 2).wait()

        for part in range(parts):
            at = pl.ds(pl.multiple_of(part * rows + z * share, share), share)
            value = total[unit % HELD, kept(near), at, :].astype(F32)
            for k in range(depth - 1):
                value = value + gotz[unit, k, part * share : (part + 1) * share, :].astype(F32)
            grad[unit % 2, part] = value
        grad_copy(unit).start()

    def stages(at):
        @pl.when((at >= 3) & (at < units + 3))
        def _():
            second(at - 3)

        @pl.when((at >= 4) & (at < units + 4))
        def _():
            third(at - 4)

        @pl.when(at >= 5)
        def _():
            fourth(at - 5)

    stages(step)

    @pl.when(step == units)
    def _():
        save = pltpu.make_async_copy(d_normed, d_normed_hbm, local_sem.at[0])
        save.start()

        def one(at, _):
            stages(at)
            return 0

        lax.fori_loop(units + 1, units + 5, one, 0)
        save.wait()
        grad_copy(units - 2).wait()
        grad_copy(units - 1).wait()


def fused_backward(
    since, beta_logit, query, key, value, halo, taps, new_add, new_map, inverse, starts, entry, exit_grad, d_core,
    w_query, w_key, w_value, mixed, normed, branch,
):
    tokens, width = query.shape
    heads = width // BLOCK
    blocks = tokens // BLOCK
    units = heads // HEADS_STEP
    cols = HEADS_STEP * BLOCK
    depth = lax.axis_size("narrow")
    rows = width // 8
    share = rows // depth
    dma = pltpu.SemaphoreType.DMA

    def now(step):
        return jnp.minimum(step, units - 1)

    def before(step):
        return jnp.maximum(step - 1, 0)

    def whole(shape):
        return pl.BlockSpec(shape, lambda h: (0,) * len(shape))

    wide = pl.BlockSpec((tokens, cols), lambda h: (0, now(h)))

    def lanes(first, second):
        return pl.BlockSpec((first, second, cols), lambda h: (0, 0, now(h)))

    def each(*tail):
        return pl.BlockSpec((HEADS_STEP,) + tail, lambda h: (now(h),) + (0,) * len(tail))

    weight = pl.BlockSpec((width, cols), lambda h: (0, before(h)), pipeline_mode=pl.Buffered(1))
    mixed_spec = pl.BlockSpec((tokens, cols), lambda h: (0, before(h)))
    parts = 4
    anywhere = pl.BlockSpec(memory_space=pl.ANY)
    return pl.pallas_call(
        fused_kernel,
        grid=(units + 1,),
        in_specs=[
            whole(since.shape), whole(beta_logit.shape), wide, wide, wide, lanes(3, PAD), lanes(3, CONV),
            wide, wide, each(blocks, BLOCK, BLOCK), each(blocks, BLOCK, 2 * BLOCK),
            each(BLOCK, BLOCK), each(BLOCK, BLOCK), wide,
            weight, weight, weight, mixed_spec, anywhere, anywhere,
        ],
        out_specs=[anywhere, anywhere, lanes(3, CONV), whole(beta_logit.shape)],
        out_shape=[
            jax.ShapeDtypeStruct((parts, share, width), F32),
            jax.ShapeDtypeStruct((tokens, width), F32),
            jax.ShapeDtypeStruct((3, CONV, width), F32),
            jax.ShapeDtypeStruct(beta_logit.shape, F32),
        ],
        scratch_shapes=[
            pltpu.VMEM((3 * HEADS_STEP, PAD + tokens, BLOCK), F32),
            pltpu.VMEM((2, CONV, PAD + tokens + PAD, BLOCK), F32),
            pltpu.VMEM((2, 4, rows, tokens), BF16),
            pltpu.VMEM((2, 4, rows, tokens), BF16),
            pltpu.VMEM((RING, 3, tokens, cols), BF16),
            pltpu.VMEM((RING, parts, tokens, cols), BF16),
            pltpu.VMEM((units, 3, PAD, cols), F32),
            pltpu.VMEM((units, 3, PAD, cols), F32),
            pltpu.VMEM((HELD, 4, parts * rows, cols), BF16),
            pltpu.VMEM((units, 2, parts * rows, cols), BF16),
            pltpu.VMEM((units, parts * rows, cols), BF16),
            pltpu.VMEM((units, depth - 1, parts * share, cols), BF16),
            pltpu.VMEM((tokens, width), F32),
            pltpu.VMEM((2, parts, share, cols), F32),
            dma((8,)), dma((2,)), dma((8,)), dma((8,)), dma((RING, 2)), dma((RING, 2)), dma((units,)), dma((units,)),
            dma((units, 2)), dma((units, 2)), dma((units,)), dma((units,)),
            dma((units, depth - 1, parts)), dma((units, depth - 1, parts)),
        ],
        compiler_params=pltpu.CompilerParams(
            collective_id=5, has_side_effects=True, vmem_limit_bytes=62 * 1024 * 1024
        ),
        name="fused_backward",
    )(
        since, beta_logit, query, key, value, halo, taps, new_add, new_map, inverse, starts, entry, exit_grad, d_core,
        w_query, w_key, w_value, mixed, normed, branch,
    )


def ffn_grads_kernel(*refs):
    lefts = [refs[0:HALVES], refs[0:HALVES], refs[HALVES : 2 * HALVES]]
    rights = [refs[(2 + m) * HALVES : (3 + m) * HALVES] for m in range(3)]
    (
        gate_ref, up_ref, down_ref, left_buf, right_buf, away, landed, total, got2, got3,
        left_sem, right_sem, send1, recv1, send2, recv2, send3, recv3,
    ) = refs[5 * HALVES :]
    dp = lax.axis_index("dp")
    core, x, y = dp % 2, (dp // 2) % 2, dp // 4
    rows = total.shape[2]
    half = rows // 2
    part = left_buf.shape[1] // HALVES
    sib = dp + 1 - 2 * core
    flip_x = dp + 2 * (1 - 2 * x)
    flip_y = dp + 4 * (1 - 2 * y)
    barrier = pltpu.get_barrier_semaphore()
    for target in (sib, flip_x, flip_y):
        pl.semaphore_signal(barrier, inc=1, device_id={"dp": target}, device_id_type=MESH)

    def load_left(m, k, start):
        own = k // 4
        block = (k % 4) * 2 + own * core + (1 - own) * (1 - core)
        lanes = pl.ds(pl.multiple_of(block * rows, rows), rows)
        for at in range(HALVES):
            copy = pltpu.make_async_copy(
                lefts[m][at].at[:, lanes], left_buf.at[k % 2, at * part : (at + 1) * part], left_sem.at[k % 2, at]
            )
            if start:
                copy.start()
            else:
                copy.wait()

    def load_right(m, start):
        for at in range(HALVES):
            copy = pltpu.make_async_copy(
                rights[m][at], right_buf.at[m % 2, at * part : (at + 1) * part], right_sem.at[m % 2, at]
            )
            if start:
                copy.start()
            else:
                copy.wait()

    def send(src, dst, send_sem, recv_sem, target):
        return pltpu.make_async_remote_copy(
            src_ref=src, dst_ref=dst, send_sem=send_sem, recv_sem=recv_sem,
            device_id={"dp": target}, device_id_type=MESH,
        )

    def copy1(m, stripe):
        return send(away.at[m, stripe], landed.at[m, stripe], send1.at[m, stripe], recv1.at[m, stripe], sib)

    def band(h):
        return pl.ds(h * half, half)

    def order(h):
        if h == 0:
            return (lambda j: 2 * j + 1 - x), (lambda j: 2 * j + x), flip_x, flip_y, 1 - y, y
        return (lambda j: 2 * (1 - y) + j), (lambda j: 2 * y + j), flip_y, flip_x, 1 - x, x

    def copy2(m, h, j):
        gone, _, target, _, _, _ = order(h)
        return send(
            total.at[m, gone(j), band(h)], got2.at[m, h, j], send2.at[2 * m + h, j], recv2.at[2 * m + h, j], target
        )

    def copy3(m, h):
        _, kept, _, target, far, _ = order(h)
        return send(total.at[m, kept(far), band(h)], got3.at[m, h], send3.at[m, h], recv3.at[m, h], target)

    def add_to(dst, src):
        step = 32

        def one(at, _):
            at = pl.ds(pl.multiple_of(at * step, step), step)
            dst[at, :] = (dst[at, :].astype(F32) + src[at, :].astype(F32)).astype(dst.dtype)
            return 0

        lax.fori_loop(0, dst.shape[0] // step, one, 0)

    def compute(m):
        load_right(m, False)
        if m + 1 < 3:
            load_right(m + 1, True)

        def one(k, _):
            @pl.when(k < 7)
            def _():
                load_left(m, k + 1, True)

            if m + 1 < 3:
                @pl.when(k == 7)
                def _():
                    load_left(m + 1, 0, True)

            load_left(m, k, False)
            value = lax.dot_general(
                left_buf[k % 2], right_buf[m % 2], (((0,), (0,)), ((), ())), preferred_element_type=F32
            ).astype(BF16)

            @pl.when(k < 4)
            def _():
                away[m, k] = value
                copy1(m, k).start()

            @pl.when(k >= 4)
            def _():
                total[m, k - 4] = value

            return 0

        lax.fori_loop(0, 8, one, 0)

        def join(stripe, _):
            copy1(m, stripe).wait()
            add_to(total.at[m, stripe], landed.at[m, stripe])
            return 0

        lax.fori_loop(0, 4, join, 0)
        for h in range(2):
            for j in range(2):
                copy2(m, h, j).start()

    def second(m):
        for h in range(2):
            _, kept, _, _, far, near = order(h)
            for j in range(2):
                copy2(m, h, j).wait()
            add_to(total.at[m, kept(far), band(h)], got2.at[m, h, far])
            copy3(m, h).start()
            add_to(total.at[m, kept(near), band(h)], got2.at[m, h, near])

    def third(m):
        for h in range(2):
            _, kept, _, _, _, near = order(h)
            copy3(m, h).wait()
            if m == 2:
                value = total[m, kept(near), band(h), :].astype(F32) + got3[m, h].astype(F32)
                down_ref[:, band(h)] = value.T
                continue
            step = 32

            def one(at, _):
                at = at * step
                value = total[m, kept(near), pl.ds(pl.multiple_of(h * half + at, step), step), :].astype(F32)
                value = value + got3[m, h, pl.ds(pl.multiple_of(at, step), step), :].astype(F32)
                (gate_ref, up_ref)[m][pl.ds(pl.multiple_of(h * half + at, step), step), :] = value
                return 0

            lax.fori_loop(0, half // step, one, 0)

    load_right(0, True)
    load_left(0, 0, True)
    pl.semaphore_wait(barrier, 3)
    compute(0)
    compute(1)
    second(0)
    compute(2)
    third(0)
    second(1)
    third(1)
    second(2)
    third(2)


def ffn_grads(lefts, rights):
    part, height = lefts[0][0].shape
    width = rights[0][0].shape[1]
    rows = height // 8
    half = rows // 2
    dma = pltpu.SemaphoreType.DMA
    operands = [ref for group in (*lefts, *rights) for ref in group]
    return pl.pallas_call(
        ffn_grads_kernel,
        in_specs=[pl.BlockSpec(memory_space=pl.ANY)] * len(operands),
        out_specs=[pl.BlockSpec(memory_space=pltpu.VMEM)] * 3,
        out_shape=[
            jax.ShapeDtypeStruct((rows, width), F32),
            jax.ShapeDtypeStruct((rows, width), F32),
            jax.ShapeDtypeStruct((width, rows), F32),
        ],
        scratch_shapes=[
            pltpu.VMEM((2, HALVES * part, rows), BF16),
            pltpu.VMEM((2, HALVES * part, width), BF16),
            pltpu.VMEM((3, 4, rows, width), BF16),
            pltpu.VMEM((3, 4, rows, width), BF16),
            pltpu.VMEM((3, 4, rows, width), BF16),
            pltpu.VMEM((3, 2, 2, half, width), BF16),
            pltpu.VMEM((3, 2, half, width), BF16),
            dma((2, HALVES)), dma((2, HALVES)), dma((3, 4)), dma((3, 4)),
            dma((6, 2)), dma((6, 2)), dma((3, 2)), dma((3, 2)),
        ],
        compiler_params=pltpu.CompilerParams(
            collective_id=4, has_side_effects=True, vmem_limit_bytes=60 * 1024 * 1024
        ),
        name="ffn_grads",
    )(*operands)


def shifted(value, axis, steps):
    count = lax.axis_size(axis)
    first, last = (max(0, -steps), min(count, count - steps))
    return lax.ppermute(value, axis, [(source, source + steps) for source in range(first, last)])


def matmul(left, right):
    return jnp.dot(left, right, preferred_element_type=F32)


def dot_tn(left, right):
    return jnp.einsum("rd,re->de", left, right, preferred_element_type=F32)


def dot_nt(left, right):
    return jnp.einsum("re,de->rd", left, right, preferred_element_type=F32)


def rms_scale(value_in, gain_vec, epsilon):
    return value_in * lax.rsqrt(jnp.mean(value_in * value_in, axis=-1, keepdims=True) + epsilon) * gain_vec


def norm_back(value_in, gain_vec, upstream, epsilon):
    inv_scale = lax.rsqrt(jnp.mean(value_in * value_in, axis=-1, keepdims=True) + epsilon)
    scaled_up = upstream * gain_vec
    gain_term = jnp.sum(upstream * value_in * inv_scale, axis=0)
    cubed = inv_scale * inv_scale * inv_scale
    back_value = inv_scale * scaled_up - value_in * cubed * jnp.mean(
        scaled_up * value_in, axis=-1, keepdims=True
    )
    return (back_value, gain_term)


def since_start(doc_lengths, offset, rows):
    ends = jnp.cumsum(doc_lengths[0])
    position = offset + jnp.arange(rows, dtype=jnp.int32)
    starts = jnp.max(jnp.where(position[:, None] >= ends[None, :], ends[None, :], 0), axis=1)
    return jnp.broadcast_to((position - starts)[:, None], (rows, BLOCK)).astype(jnp.int32)


def scatter_all(value, dim):
    part = lax.psum_scatter(value, "dp", scatter_dimension=dim, tiled=True)
    return lax.psum_scatter(part, "narrow", scatter_dimension=dim, tiled=True)


def local(
    tokens,
    doc_lengths,
    attn_gain,
    w_query,
    w_key,
    w_value,
    w_beta,
    conv_weight,
    out_gain,
    w_out,
    mlp_gain,
    w_gate,
    w_up,
    w_down,
    grad_out,
):
    tok_rows, model_width = tokens.shape
    offset = lax.axis_index("narrow") * tok_rows
    half = tok_rows // HALVES
    parts = [slice(at * half, (at + 1) * half) for at in range(HALVES)]

    def gather(rows):
        return lax.all_gather(rows, "narrow", axis=0, tiled=True)

    def scatter(rows):
        return lax.psum_scatter(rows, "narrow", scatter_dimension=0, tiled=True)

    cot = gather(grad_out)
    since = since_start(doc_lengths, offset, tok_rows)
    inputs = tokens.astype(F32)
    normed = rms_scale(inputs, attn_gain, 1e-06).astype(BF16)
    query, key, value = (matmul(normed, w).astype(BF16) for w in (w_query, w_key, w_value))
    beta_logit = matmul(normed, w_beta)
    halo = shifted(
        jnp.stack([part[tok_rows - PAD :] for part in (query, key, value)]), "narrow", 1
    )
    out_add, out_map, new_add, new_map, inverse, starts, end = mixer_forward(
        since, beta_logit, query, key, value, halo, conv_weight
    )
    transfer = end[:, :, BLOCK:].astype(BF16)
    entry = carry_chain(transfer, end[:, :, :BLOCK], "narrow", True)
    gain_row = out_gain[None, :]
    attn_mixed = mixer_join(out_add, out_map, entry, gain_row)
    hidden = inputs + matmul(attn_mixed, w_out)
    normed_mlp = rms_scale(hidden, mlp_gain, 1e-06).astype(BF16)
    normed_mlp, cot = lax.optimization_barrier((normed_mlp, cot))
    cot = cot.reshape(-1, tok_rows, model_width)
    cot = [cot[:, part].reshape(-1, model_width) for part in parts]
    gathered = [gather(normed_mlp[part]) for part in parts]
    activation, d_gate, d_up, d_normed_parts, out_parts = [], [], [], [], []
    for at in range(HALVES):
        gate_proj = matmul(gathered[at], w_gate)
        up_proj = matmul(gathered[at], w_up)
        gate_sigmoid = jax.nn.sigmoid(gate_proj)
        silu_gate = gate_proj * gate_sigmoid
        activation.append((silu_gate * up_proj).astype(BF16))
        d_act = jnp.einsum("rd,fd->rf", cot[at], w_down, preferred_element_type=F32)
        d_gate.append(
            (d_act * up_proj * gate_sigmoid * (1.0 + gate_proj * (1.0 - gate_sigmoid))).astype(BF16)
        )
        d_up.append((d_act * silu_gate).astype(BF16))
        d_part = (dot_nt(d_gate[at], w_gate) + dot_nt(d_up[at], w_up)).astype(BF16)
        out_parts.append(matmul(activation[at], w_down).astype(BF16))
        if at + 1 < HALVES:
            d_part, out_parts[at], gathered[at + 1] = lax.optimization_barrier(
                (d_part, out_parts[at], gathered[at + 1])
            )
        d_normed_parts.append(scatter(d_part))
    if lax.axis_size("dp") == 8:
        ffn_sums = ffn_grads((gathered, cot), (d_gate, d_up, activation))
    else:
        ffn_sums = [
            lax.psum_scatter(
                sum(dot_tn(a, c) for a, c in zip(left, right)).astype(BF16), "dp", scatter_dimension=0, tiled=True
            )
            for left, right in ((gathered, d_gate), (gathered, d_up), (cot, activation))
        ]
        ffn_sums[2] = ffn_sums[2].T
    d_normed_parts, out_parts, ffn_sums = lax.optimization_barrier((d_normed_parts, out_parts, ffn_sums))
    quarters = out_parts[0].reshape(-1, 2, half // 2, model_width)
    out_first, out_second = (quarters[:, at].reshape(-1, model_width) for at in range(2))
    out_rest = [out_second, *out_parts[1:]]
    ffn_parts = [scatter(out_first)]
    grad_gate, grad_up, grad_down = (value.astype(F32) for value in ffn_sums)
    d_normed_mlp = jnp.concatenate(d_normed_parts, axis=0).astype(F32)
    d_hidden_norm, mlp_gain_term = norm_back(hidden, mlp_gain, d_normed_mlp, 1e-06)
    d_hidden = grad_out.astype(F32) + d_hidden_norm
    d_branch = d_hidden.astype(BF16)
    d_core, start_grad, out_gain_term = mixer_core_back(out_add, out_map, entry, gain_row, d_branch, w_out)
    exit_grad = carry_chain(transfer, start_grad, "narrow", False)
    exit_grad, out_rest = lax.optimization_barrier((exit_grad, out_rest))
    ffn_parts += [scatter(part) for part in out_rest]
    mixer_args = (
        since, beta_logit, query, key, value, halo, conv_weight,
        new_add, new_map, inverse, starts, entry, exit_grad, d_core,
    )
    if lax.axis_size("dp") == 8:
        grads, d_normed, conv_term, d_beta = fused_backward(
            *mixer_args, w_query, w_key, w_value, attn_mixed, normed, d_branch
        )
    else:
        d_proj, d_halo, conv_term, d_beta = mixer_backward(*mixer_args)
        after = shifted(d_halo.astype(BF16), "narrow", -1)
        d_proj = d_proj.at[:, tok_rows - PAD :].add(after)
        d_normed = sum(dot_nt(part, w) for part, w in zip(d_proj, (w_query, w_key, w_value)))
        pairs = [(normed, part) for part in d_proj] + [(d_branch, attn_mixed)]
        grads = jnp.stack([scatter_all(dot_tn(a, c).astype(BF16), 0).astype(F32) for a, c in pairs])
    d_beta_low = d_beta.astype(BF16)
    beta_term = jnp.einsum("rd,rh->dh", normed, d_beta_low, preferred_element_type=F32)
    d_normed = d_normed + jnp.einsum("rh,dh->rd", d_beta_low, w_beta, preferred_element_type=F32)
    d_input_norm, attn_gain_term = norm_back(inputs, attn_gain, d_normed, 1e-06)
    grad_tokens = (d_hidden + d_input_norm).astype(BF16)
    devices = lax.axis_size("dp") * lax.axis_size("narrow")
    heads = w_beta.shape[1]
    taps = 3 * CONV
    gain_share = BLOCK // devices
    gain_column = jnp.pad(
        out_gain_term.reshape(devices, gain_share), ((0, 0), (0, model_width // devices - gain_share))
    ).reshape(model_width, 1)
    small = jnp.concatenate(
        [
            beta_term,
            conv_term.reshape(taps, model_width).T,
            attn_gain_term[:, None],
            mlp_gain_term[:, None],
            gain_column,
        ],
        axis=1,
    )
    small = jnp.pad(small, ((0, 0), (0, BLOCK - small.shape[1])))
    if lax.axis_size("dp") == 8:
        small = reduce_small(small)
    else:
        small = lax.psum_scatter(small, ("dp", "narrow"), scatter_dimension=0, tiled=True)
    grad_beta = small[:, :heads]
    grad_conv = small[:, heads : heads + taps].T.reshape(3, CONV, -1)
    grad_attn_gain = small[:, heads + taps]
    grad_mlp_gain = small[:, heads + taps + 1]
    grad_out_gain = small[:gain_share, heads + taps + 2]
    ffn_parts, grads = lax.optimization_barrier((ffn_parts, grads))
    block_out = (hidden + jnp.concatenate(ffn_parts, axis=0).astype(F32)).astype(BF16)
    grad_query, grad_key, grad_value = grads[0], grads[1], grads[2]
    grad_w_out = grads[3].T
    return (
        block_out,
        grad_tokens,
        grad_attn_gain,
        grad_query,
        grad_key,
        grad_value,
        grad_beta,
        grad_conv,
        grad_out_gain,
        grad_w_out,
        grad_mlp_gain,
        grad_gate,
        grad_up,
        grad_down,
    )


def solution(mesh):
    placed = (
        P(("dp", "narrow"), None),
        P("dp", None),
        P(),
        P(),
        P(),
        P(),
        P(),
        P(),
        P(),
        P(),
        P(),
        P(None, "narrow"),
        P(None, "narrow"),
        P("narrow", None),
        P(("dp", "narrow"), None),
    )
    return jax.shard_map(
        local,
        mesh=mesh,
        in_specs=placed,
        out_specs=(
            P(("dp", "narrow"), None),
            P(("dp", "narrow"), None),
            P(("dp", "narrow")),
            P(("dp", "narrow"), None),
            P(("dp", "narrow"), None),
            P(("dp", "narrow"), None),
            P(("dp", "narrow"), None),
            P(None, None, ("dp", "narrow")),
            P(("dp", "narrow")),
            P(None, ("dp", "narrow")),
            P(("dp", "narrow")),
            P("dp", "narrow"),
            P("dp", "narrow"),
            P("narrow", "dp"),
        ),
        check_vma=False,
    )
```

```python
import functools

import jax
import jax.numpy as jnp
from jax import lax
from jax.experimental import pallas as pl
from jax.experimental.pallas import tpu as pltpu
from jax.sharding import PartitionSpec as P

CONV = 4
BLOCK = 128
HEADS_STEP = 2
PAD = 8
MESH = pl.DeviceIdType.MESH
F32 = jnp.float32
BF16 = jnp.bfloat16
VMEM_LIMIT = 56 * 1024 * 1024


def mm(left, right, contract=(1, 0)):
    return lax.dot_general(
        left.astype(BF16),
        right.astype(BF16),
        (((contract[0],), (contract[1],)), ((), ())),
        preferred_element_type=F32,
    )


def mm_nt(left, right):
    return mm(left, right, (1, 1))


def mm_tn(left, right):
    return mm(left, right, (0, 0))


def iotas(size):
    row = lax.broadcasted_iota(jnp.int32, (size, size), 0)
    col = lax.broadcasted_iota(jnp.int32, (size, size), 1)
    return row, col


def block_masks(since):
    size = since.shape[0]
    row, col = iotas(size)
    back = row - col
    causal = (back >= 0) & (back <= since)
    strict = (back > 0) & (back <= since)
    keep = (since > row).astype(F32)
    last = since[size - 1 : size, :]
    last_mask = (row >= size - 1 - last).astype(F32)
    keep_last = (last > size - 1).astype(F32)
    return causal, strict, keep, last_mask, keep_last


def unit_lower_inverses(lowers):
    size = lowers[0].shape[0]
    row, col = iotas(size)
    width = 1
    inverses = None
    while width < size:
        join = (row // (2 * width) == col // (2 * width)) & (row // width != col // width)
        pieces = [jnp.where(join, low, 0.0) for low in lowers]
        if inverses is None:
            eye = (row == col).astype(F32)
            inverses = [eye - piece for piece in pieces]
        else:
            halves = [mm(piece, inv) for piece, inv in zip(pieces, inverses)]
            inverses = [inv - mm(inv, half) for inv, half in zip(inverses, halves)]
        width *= 2
    return inverses


def conv_front(ext, proj, halo, taps, since):
    rows = proj.shape[0]
    ext[0:PAD, :] = halo.astype(F32)
    ext[PAD : PAD + rows, :] = proj
    pre = proj * taps[0:1, :]
    for lag in range(1, CONV):
        moved = ext[PAD - lag : PAD - lag + rows, :]
        pre = pre + jnp.where(since >= lag, moved, 0.0) * taps[lag : lag + 1, :]
    gate = 1.0 / (1.0 + jnp.exp(-pre))
    return pre, gate, pre * gate


def unit_rows(value):
    inv = lax.rsqrt(jnp.sum(value * value, axis=-1, keepdims=True) + 1e-06)
    return value * inv, inv


def head_column(array, head):
    lane = lax.broadcasted_iota(jnp.int32, array.shape, 1)
    return jnp.sum(jnp.where(lane == head, array, 0.0), axis=1, keepdims=True)


def forward_kernel(
    since_ref, beta_ref, query_ref, key_ref, value_ref, halo_ref, taps_ref,
    out_add_ref, out_map_ref, new_add_ref, new_map_ref, inverse_ref, starts_ref, end_ref,
    ext,
):
    rows = since_ref.shape[0]
    blocks = rows // BLOCK
    since = since_ref[...]
    jobs = []
    for sub in range(HEADS_STEP):
        head = pl.program_id(0) * HEADS_STEP + sub
        lanes = slice(sub * BLOCK, (sub + 1) * BLOCK)
        mixed = []
        for part, ref in enumerate((query_ref, key_ref, value_ref)):
            _, _, act = conv_front(
                ext.at[sub * 3 + part], ref[:, lanes].astype(F32), halo_ref[part, :, lanes],
                taps_ref[part, :, lanes], since,
            )
            mixed.append(act)
        query = unit_rows(mixed[0])[0] * (BLOCK ** -0.5)
        key = unit_rows(mixed[1])[0]
        beta = 1.0 / (1.0 + jnp.exp(-head_column(beta_ref[...], head)))
        jobs.append((lanes, query, key, mixed[2], beta))
    lowers, scores = [], []
    for lanes, query, key, value, beta in jobs:
        for blk in range(blocks):
            span = slice(blk * BLOCK, (blk + 1) * BLOCK)
            causal, strict, _, _, _ = block_masks(since[span])
            both = mm_nt(jnp.concatenate([key[span], query[span]], axis=0), key[span])
            lowers.append(jnp.where(strict, both[:BLOCK] * beta[span], 0.0))
            scores.append(jnp.where(causal, both[BLOCK:], 0.0).astype(BF16))
    inverses = [inv.astype(BF16) for inv in unit_lower_inverses(lowers)]
    row, col = iotas(BLOCK)
    eye = (row == col).astype(F32)
    states = [jnp.concatenate([jnp.zeros((BLOCK, BLOCK), F32), eye], axis=1) for _ in jobs]
    for blk in range(blocks):
        span = slice(blk * BLOCK, (blk + 1) * BLOCK)
        _, _, keep, last_mask, keep_last = block_masks(since[span])
        for sub, (lanes, query, key, value, beta) in enumerate(jobs):
            at = sub * blocks + blk
            inverse_ref[sub, blk] = inverses[at]
            state = states[sub].astype(BF16)
            starts_ref[sub, blk] = state
            stacked = jnp.concatenate([key[span] * keep, query[span] * keep], axis=0)
            seen = mm(stacked, state)
            rest = jnp.concatenate([value[span], jnp.zeros((BLOCK, BLOCK), F32)], axis=1)
            right = (rest - seen[:BLOCK]) * beta[span]
            new = mm(inverses[at], right).astype(BF16)
            out = seen[BLOCK:] + mm(scores[at], new)
            out_add_ref[span, lanes] = out[:, :BLOCK].astype(BF16)
            out_map_ref[span, lanes] = out[:, BLOCK:].astype(BF16)
            new_add_ref[span, lanes] = new[:, :BLOCK]
            new_map_ref[span, lanes] = new[:, BLOCK:]
            keep_both = jnp.concatenate([keep_last, keep_last], axis=1)
            states[sub] = states[sub] * keep_both + mm_tn(key[span] * last_mask, new)
    for sub in range(len(jobs)):
        end_ref[sub] = states[sub]


def whole_spec(shape):
    return pl.BlockSpec(shape, lambda h: (0,) * len(shape))


def head_spec(rows):
    return pl.BlockSpec((rows, HEADS_STEP * BLOCK), lambda h: (0, h))


def per_head(*tail):
    return pl.BlockSpec((HEADS_STEP,) + tail, lambda h: (h,) + (0,) * len(tail))


def lanes_spec(first, second):
    return pl.BlockSpec((first, second, HEADS_STEP * BLOCK), lambda h: (0, 0, h))


def params():
    return pltpu.CompilerParams(vmem_limit_bytes=VMEM_LIMIT)


def mixer_forward(since, beta_logit, query, key, value, halo, taps):
    rows, width = query.shape
    heads = width // BLOCK
    blocks = rows // BLOCK
    wide = jax.ShapeDtypeStruct((rows, width), BF16)
    return pl.pallas_call(
        forward_kernel,
        grid=(heads // HEADS_STEP,),
        in_specs=[
            whole_spec(since.shape), whole_spec(beta_logit.shape),
            head_spec(rows), head_spec(rows), head_spec(rows),
            lanes_spec(3, PAD), lanes_spec(3, CONV),
        ],
        out_specs=[
            head_spec(rows), head_spec(rows), head_spec(rows), head_spec(rows),
            per_head(blocks, BLOCK, BLOCK), per_head(blocks, BLOCK, 2 * BLOCK),
            per_head(BLOCK, 2 * BLOCK),
        ],
        out_shape=[
            wide, wide, wide, wide,
            jax.ShapeDtypeStruct((heads, blocks, BLOCK, BLOCK), BF16),
            jax.ShapeDtypeStruct((heads, blocks, BLOCK, 2 * BLOCK), BF16),
            jax.ShapeDtypeStruct((heads, BLOCK, 2 * BLOCK), F32),
        ],
        scratch_shapes=[pltpu.VMEM((3 * HEADS_STEP, PAD + rows, BLOCK), F32)],
        compiler_params=params(),
        name="mixer_forward",
    )(since, beta_logit, query, key, value, halo, taps)


def join_kernel(out_add_ref, out_map_ref, entry_ref, gain_ref, mixed_ref):
    for sub in range(HEADS_STEP):
        lanes = slice(sub * BLOCK, (sub + 1) * BLOCK)
        core = out_add_ref[:, lanes].astype(F32) + mm(out_map_ref[:, lanes], entry_ref[sub])
        scale = lax.rsqrt(jnp.mean(core * core, axis=-1, keepdims=True) + 1e-05)
        mixed_ref[:, lanes] = (core * scale * gain_ref[...]).astype(BF16)


def mixer_join(out_add, out_map, entry, gain):
    rows, width = out_add.shape
    heads = width // BLOCK
    return pl.pallas_call(
        join_kernel,
        grid=(heads // HEADS_STEP,),
        in_specs=[head_spec(rows), head_spec(rows), per_head(BLOCK, BLOCK), whole_spec((1, BLOCK))],
        out_specs=head_spec(rows),
        out_shape=jax.ShapeDtypeStruct((rows, width), BF16),
        compiler_params=params(),
        name="mixer_join",
    )(out_add, out_map, entry, gain)


def core_back_kernel(
    out_add_ref, out_map_ref, entry_ref, gain_ref, branch_ref, w_out_ref, d_core_ref, start_ref, gain_out_ref
):
    @pl.when(pl.program_id(0) == 0)
    def _():
        gain_out_ref[...] = jnp.zeros_like(gain_out_ref)

    upstream = mm_nt(branch_ref[...], w_out_ref[...])
    for sub in range(HEADS_STEP):
        lanes = slice(sub * BLOCK, (sub + 1) * BLOCK)
        out_map = out_map_ref[:, lanes]
        core = out_add_ref[:, lanes].astype(F32) + mm(out_map, entry_ref[sub])
        scale = lax.rsqrt(jnp.mean(core * core, axis=-1, keepdims=True) + 1e-05)
        unit = core * scale
        up = upstream[:, lanes]
        gain_out_ref[...] += jnp.sum(up * unit, axis=0, keepdims=True)
        scaled = up * gain_ref[...]
        d_core = scale * (scaled - unit * jnp.mean(scaled * unit, axis=-1, keepdims=True))
        d_core = d_core.astype(BF16)
        d_core_ref[:, lanes] = d_core
        start_ref[sub] = mm_tn(out_map, d_core)


def mixer_core_back(out_add, out_map, entry, gain, branch, w_out):
    rows, width = out_add.shape
    heads = width // BLOCK
    return pl.pallas_call(
        core_back_kernel,
        grid=(heads // HEADS_STEP,),
        in_specs=[
            head_spec(rows), head_spec(rows), per_head(BLOCK, BLOCK), whole_spec((1, BLOCK)),
            whole_spec(branch.shape), pl.BlockSpec((HEADS_STEP * BLOCK, width), lambda h: (h, 0)),
        ],
        out_specs=[head_spec(rows), per_head(BLOCK, BLOCK), whole_spec((1, BLOCK))],
        out_shape=[
            jax.ShapeDtypeStruct((rows, width), BF16),
            jax.ShapeDtypeStruct((heads, BLOCK, BLOCK), F32),
            jax.ShapeDtypeStruct((1, BLOCK), F32),
        ],
        compiler_params=params(),
        name="mixer_core_back",
    )(out_add, out_map, entry, gain, branch, w_out)


def backward_heads(
    step, since_ref, beta_ref, query_ref, key_ref, value_ref, halo_ref, taps_ref,
    new_add_ref, new_map_ref, inverse_ref, starts_ref, entry_ref, exit_ref, d_core_ref,
    d_taps_ref, d_beta_ref, ext, back, emit,
):
    rows = since_ref.shape[0]
    blocks = rows // BLOCK
    since = since_ref[...]
    jobs = []
    for sub in range(HEADS_STEP):
        head = step * HEADS_STEP + sub
        lanes = slice(sub * BLOCK, (sub + 1) * BLOCK)
        fronts = []
        for part, ref in enumerate((query_ref, key_ref, value_ref)):
            fronts.append(
                conv_front(
                    ext.at[sub * 3 + part], ref[:, lanes].astype(F32), halo_ref[part, :, lanes],
                    taps_ref[part, :, lanes], since,
                )
            )
        query_unit, query_inv = unit_rows(fronts[0][2])
        key, key_inv = unit_rows(fronts[1][2])
        query = query_unit * (BLOCK ** -0.5)
        beta = 1.0 / (1.0 + jnp.exp(-head_column(beta_ref[...], head)))
        jobs.append((head, lanes, fronts, query, query_unit, query_inv, key, key_inv, beta))

    saved = {}
    for sub, (head, lanes, fronts, query, query_unit, query_inv, key, key_inv, beta) in enumerate(jobs):
        entry = entry_ref[sub].astype(BF16)
        for blk in range(blocks):
            span = slice(blk * BLOCK, (blk + 1) * BLOCK)
            causal, _, keep, last_mask, _ = block_masks(since[span])
            start = starts_ref[sub, blk]
            state = (start[:, :BLOCK].astype(F32) + mm(start[:, BLOCK:], entry)).astype(BF16)
            new = (new_add_ref[span, lanes].astype(F32) + mm(new_map_ref[span, lanes], entry)).astype(BF16)
            scores = jnp.where(causal, mm_nt(query[span], key[span]), 0.0).astype(BF16)
            d_out = d_core_ref[span, lanes]
            d_new = mm_tn(scores, d_out)
            d_state = mm_tn(query[span] * keep, d_out)
            saved[sub, blk] = (state, new, d_out, d_new, d_state)

    carried = [exit_ref[sub].astype(F32) for sub in range(HEADS_STEP)]
    chain = {}
    for blk in reversed(range(blocks)):
        span = slice(blk * BLOCK, (blk + 1) * BLOCK)
        _, _, keep, last_mask, keep_last = block_masks(since[span])
        for sub, (head, lanes, fronts, query, query_unit, query_inv, key, key_inv, beta) in enumerate(jobs):
            state, new, d_out, d_new, d_state = saved[sub, blk]
            after = carried[sub].astype(BF16)
            d_new = d_new + mm(key[span] * last_mask, after)
            d_right = mm_tn(inverse_ref[sub, blk], d_new)
            d_rest = d_right * beta[span]
            carried[sub] = carried[sub] * keep_last + d_state - mm_tn(key[span] * keep, d_rest)
            chain[sub, blk] = (after, d_right, d_rest)

    lane = lax.broadcasted_iota(jnp.int32, (rows, beta_ref.shape[1]), 1)
    d_beta_all = jnp.zeros((rows, beta_ref.shape[1]), F32)
    for sub, (head, lanes, fronts, query, query_unit, query_inv, key, key_inv, beta) in enumerate(jobs):
        d_queries, d_keys, d_values, d_betas = [], [], [], []
        for blk in range(blocks):
            span = slice(blk * BLOCK, (blk + 1) * BLOCK)
            causal, strict, keep, last_mask, _ = block_masks(since[span])
            state, new, d_out, _, _ = saved[sub, blk]
            after, d_right, d_rest = chain[sub, blk]
            both = mm_nt(jnp.concatenate([d_out, d_right.astype(BF16)], axis=0), new)
            d_scores = jnp.where(causal, both[:BLOCK], 0.0).astype(BF16)
            d_gram = (jnp.where(strict, both[BLOCK:], 0.0) * (-beta[span])).astype(BF16)
            key_b = key[span].astype(BF16)
            from_state = mm_nt(jnp.concatenate([d_out, d_rest.astype(BF16)], axis=0), state)
            left = mm(jnp.concatenate([d_scores, d_gram], axis=0), key_b)
            d_queries.append(from_state[:BLOCK] * keep + left[:BLOCK])
            d_key = left[BLOCK:] + mm_tn(
                jnp.concatenate([d_scores, d_gram], axis=0),
                jnp.concatenate([query[span].astype(BF16), key_b], axis=0),
            )
            d_key = d_key + mm_nt(new, after) * last_mask - from_state[BLOCK:] * keep
            d_keys.append(d_key)
            d_values.append(d_rest)
            d_betas.append(
                jnp.sum(d_right * new.astype(F32), axis=1, keepdims=True) * (1.0 - beta[span])
            )
        d_query = jnp.concatenate(d_queries, axis=0) * (BLOCK ** -0.5)
        d_key = jnp.concatenate(d_keys, axis=0)
        d_query = query_inv * (
            d_query - query_unit * jnp.sum(d_query * query_unit, axis=-1, keepdims=True)
        )
        d_key = key_inv * (d_key - key * jnp.sum(d_key * key, axis=-1, keepdims=True))
        d_value = jnp.concatenate(d_values, axis=0)
        d_beta_all = d_beta_all + jnp.where(lane == head, jnp.concatenate(d_betas, axis=0), 0.0)
        for part, d_act in enumerate((d_query, d_key, d_value)):
            pre, gate, _ = fronts[part]
            taps = taps_ref[part, :, lanes]
            source = ext.at[sub * 3 + part]
            d_pre = d_act * gate * (1.0 + pre * (1.0 - gate))
            room = back.at[(sub * 3 + part) % 2]
            total = None
            d_taps = []
            for lag in range(CONV):
                masked = d_pre if lag == 0 else jnp.where(since >= lag, d_pre, 0.0)
                moved = source[PAD - lag : PAD - lag + rows, :]
                d_taps.append(jnp.sum(masked * moved, axis=0, keepdims=True))
                room[lag, 0:PAD, :] = jnp.zeros((PAD, BLOCK), F32)
                room[lag, PAD : PAD + rows, :] = masked * taps[lag : lag + 1, :]
                room[lag, PAD + rows : PAD + rows + PAD, :] = jnp.zeros((PAD, BLOCK), F32)
                term = room[lag, lag : lag + PAD + rows, :]
                total = term if total is None else total + term
            d_taps_ref[part, :, lanes] = jnp.concatenate(d_taps, axis=0)
            emit(part, lanes, total)

    @pl.when(step == 0)
    def _():
        d_beta_ref[...] = d_beta_all

    @pl.when(step > 0)
    def _():
        d_beta_ref[...] += d_beta_all


def backward_kernel(*refs):
    d_proj_ref, d_halo_ref, d_taps_ref, d_beta_ref, ext, back = refs[14:]

    def emit(part, lanes, total):
        d_halo_ref[part, :, lanes] = total[:PAD]
        d_proj_ref[part, :, lanes] = total[PAD:].astype(BF16)

    backward_heads(pl.program_id(0), *refs[:14], d_taps_ref, d_beta_ref, ext, back, emit)


def mixer_backward(
    since, beta_logit, query, key, value, halo, taps, new_add, new_map, inverse, starts, entry, exit_grad, d_core
):
    rows, width = query.shape
    heads = width // BLOCK
    blocks = rows // BLOCK
    return pl.pallas_call(
        backward_kernel,
        grid=(heads // HEADS_STEP,),
        in_specs=[
            whole_spec(since.shape), whole_spec(beta_logit.shape),
            head_spec(rows), head_spec(rows), head_spec(rows),
            lanes_spec(3, PAD), lanes_spec(3, CONV),
            head_spec(rows), head_spec(rows),
            per_head(blocks, BLOCK, BLOCK), per_head(blocks, BLOCK, 2 * BLOCK),
            per_head(BLOCK, BLOCK), per_head(BLOCK, BLOCK), head_spec(rows),
        ],
        out_specs=[
            lanes_spec(3, rows), lanes_spec(3, PAD), lanes_spec(3, CONV), whole_spec(beta_logit.shape),
        ],
        out_shape=[
            jax.ShapeDtypeStruct((3, rows, width), BF16),
            jax.ShapeDtypeStruct((3, PAD, width), F32),
            jax.ShapeDtypeStruct((3, CONV, width), F32),
            jax.ShapeDtypeStruct(beta_logit.shape, F32),
        ],
        scratch_shapes=[
            pltpu.VMEM((3 * HEADS_STEP, PAD + rows, BLOCK), F32),
            pltpu.VMEM((2, CONV, PAD + rows + PAD, BLOCK), F32),
        ],
        compiler_params=params(),
        name="mixer_backward",
    )(
        since, beta_logit, query, key, value, halo, taps, new_add, new_map, inverse, starts, entry, exit_grad, d_core
    )


GROUPS = 8
HALVES = 2


def chain_kernel(axis, forward, map_ref, add_ref, out_ref, sent, landed, send_sem, recv_sem):
    count = lax.axis_size(axis)
    me = lax.axis_index(axis)
    heads = add_ref.shape[0]
    step = heads // GROUPS
    up, down = (me + 1, me - 1) if forward else (me - 1, me + 1)
    first, last = (0, count - 1) if forward else (count - 1, 0)
    barrier = pltpu.get_barrier_semaphore()

    @pl.when(me != first)
    def _():
        pl.semaphore_signal(barrier, inc=1, device_id={axis: down}, device_id_type=MESH)

    @pl.when(me != last)
    def _():
        pl.semaphore_wait(barrier, 1)

    def copy(group, target):
        return pltpu.make_async_remote_copy(
            src_ref=sent.at[group],
            dst_ref=landed.at[group],
            send_sem=send_sem.at[group],
            recv_sem=recv_sem.at[group],
            device_id={axis: target},
            device_id_type=MESH,
        )

    for group in range(GROUPS):
        @pl.when(me != first)
        def _():
            copy(group, up).wait_recv()
            for sub in range(step):
                head = group * step + sub
                out_ref[head] = landed[group, sub].astype(F32)

        @pl.when(me == first)
        def _():
            out_ref[group * step : (group + 1) * step] = jnp.zeros((step,) + out_ref.shape[1:], F32)

        @pl.when(me != last)
        def _():
            for sub in range(step):
                head = group * step + sub
                if forward:
                    moved = mm(map_ref[head], out_ref[head])
                else:
                    moved = mm_tn(map_ref[head], out_ref[head])
                sent[group, sub] = (moved + add_ref[head]).astype(BF16)
            copy(group, up).start()

    @pl.when(me != last)
    def _():
        for group in range(GROUPS):
            copy(group, up).wait_send()


def carry_chain(map_part, add_part, axis, forward):
    heads = add_part.shape[0]
    part = (GROUPS, heads // GROUPS, BLOCK, BLOCK)
    return pl.pallas_call(
        functools.partial(chain_kernel, axis, forward),
        in_specs=[pl.BlockSpec(memory_space=pltpu.VMEM)] * 2,
        out_specs=pl.BlockSpec(memory_space=pltpu.VMEM),
        out_shape=jax.ShapeDtypeStruct(add_part.shape, F32),
        scratch_shapes=[
            pltpu.VMEM(part, BF16),
            pltpu.VMEM(part, BF16),
            pltpu.SemaphoreType.DMA((GROUPS,)),
            pltpu.SemaphoreType.DMA((GROUPS,)),
        ],
        compiler_params=pltpu.CompilerParams(
            collective_id=1 if forward else 2, has_side_effects=True, vmem_limit_bytes=VMEM_LIMIT // 2
        ),
        name="carry_forward" if forward else "carry_backward",
    )(map_part, add_part)


def bits(dp):
    core, x, y = dp % 2, (dp // 2) % 2, dp // 4
    return core, x, y, dp + 1 - 2 * core, dp + 2 * (1 - 2 * x), dp + 4 * (1 - 2 * y)


def remote(src, dst, send_sem, recv_sem, target):
    return pltpu.make_async_remote_copy(
        src_ref=src, dst_ref=dst, send_sem=send_sem, recv_sem=recv_sem, device_id=target, device_id_type=MESH
    )


def meet(dp_targets, narrow_targets):
    barrier = pltpu.get_barrier_semaphore()
    for target in dp_targets:
        pl.semaphore_signal(barrier, inc=1, device_id={"dp": target}, device_id_type=MESH)
    for target in narrow_targets:
        pl.semaphore_signal(barrier, inc=1, device_id={"narrow": target}, device_id_type=MESH)
    pl.semaphore_wait(barrier, len(dp_targets) + len(narrow_targets))


def add_rows(dst, src, step):
    def one(at, _):
        at = pl.ds(pl.multiple_of(at * step, step), step)
        dst[at, :] = (dst[at, :].astype(F32) + src[at, :].astype(F32)).astype(dst.dtype)
        return 0

    lax.fori_loop(0, dst.shape[0] // step, one, 0)


def small_kernel(small_ref, out_ref, landed, total, got2, got3, gotz, send1, recv1, send2, recv2, send3, recv3, sendz, recvz):
    dp, z = lax.axis_index("dp"), lax.axis_index("narrow")
    core, x, y, sib, flip_x, flip_y = bits(dp)
    depth = lax.axis_size("narrow")
    rows = small_ref.shape[0] // 8
    share = rows // depth
    peers = [(z + step) % depth for step in range(1, depth)]
    meet((sib, flip_x, flip_y), peers)

    def stripe_rows(stripe, which):
        return pl.ds(pl.multiple_of((stripe * 2 + which) * rows, rows), rows)

    def share_rows(at):
        return pl.ds(pl.multiple_of(at * share, share), share)

    first = [
        remote(small_ref.at[stripe_rows(k, 1 - core)], landed.at[k], send1.at[k], recv1.at[k], {"dp": sib})
        for k in range(4)
    ]
    for copy in first:
        copy.start()
    for k in range(4):
        first[k].wait()
        total[k] = small_ref[stripe_rows(k, core), :] + landed[k]
    second = [
        remote(total.at[2 * j + 1 - x], got2.at[j], send2.at[j], recv2.at[j], {"dp": flip_x}) for j in range(2)
    ]
    for copy in second:
        copy.start()
    for copy in second:
        copy.wait()
    third = remote(total.at[2 * (1 - y) + x], got3, send3, recv3, {"dp": flip_y})
    total[2 * (1 - y) + x] = total[2 * (1 - y) + x] + got2[1 - y]
    third.start()
    third.wait()
    mine = 2 * y + x
    total[mine] = total[mine] + got2[y] + got3[...]
    last = [
        remote(total.at[mine, share_rows(to)], gotz.at[k], sendz.at[k], recvz.at[k], {"narrow": to})
        for k, to in enumerate(peers)
    ]
    for copy in last:
        copy.start()
    value = total[mine, share_rows(z), :]
    for k, copy in enumerate(last):
        copy.wait()
        value = value + gotz[k]
    out_ref[...] = value


def reduce_small(small):
    height, lanes = small.shape
    depth = lax.axis_size("narrow")
    rows = height // 8
    share = rows // depth
    dma = pltpu.SemaphoreType.DMA
    return pl.pallas_call(
        small_kernel,
        in_specs=[pl.BlockSpec(memory_space=pltpu.VMEM)],
        out_specs=pl.BlockSpec(memory_space=pltpu.VMEM),
        out_shape=jax.ShapeDtypeStruct((share, lanes), F32),
        scratch_shapes=[
            pltpu.VMEM((4, rows, lanes), F32),
            pltpu.VMEM((4, rows, lanes), F32),
            pltpu.VMEM((2, rows, lanes), F32),
            pltpu.VMEM((rows, lanes), F32),
            pltpu.VMEM((depth - 1, share, lanes), F32),
            dma((4,)), dma((4,)), dma((2,)), dma((2,)), dma(()), dma(()), dma((depth - 1,)), dma((depth - 1,)),
        ],
        compiler_params=pltpu.CompilerParams(
            collective_id=3, has_side_effects=True, vmem_limit_bytes=16 * 1024 * 1024
        ),
        name="reduce_small",
    )(small)


RING = 3
HELD = 5
LAG = 2


def fused_kernel(*refs):
    heads_in = refs[:14]
    since_ref = refs[0]
    (
        w_query_ref, w_key_ref, w_value_ref, mixed_ref, normed_hbm, branch_hbm,
        grad_hbm, d_normed_hbm, d_taps_ref, d_beta_ref,
        ext, back, left_own, left_sib, d_proj, d_proj_sib, halo_out, halo_in,
        total, got2, got3, gotz, d_normed, grad,
        local_sem, grad_sem, left_send, left_recv, right_send, right_recv, halo_send, halo_recv,
        send2, recv2, send3, recv3, sendz, recvz,
    ) = refs[14:]
    step = pl.program_id(0)
    units = pl.num_programs(0) - 1
    dp, z = lax.axis_index("dp"), lax.axis_index("narrow")
    core, x, y, sib, flip_x, flip_y = bits(dp)
    depth = lax.axis_size("narrow")
    tokens = since_ref.shape[0]
    parts = d_proj_sib.shape[1]
    rows = left_own.shape[2]
    cols = d_proj.shape[3]
    share = rows // depth
    peers = [(z + k) % depth for k in range(1, depth)]

    def stripe_lanes(stripe, which):
        return pl.ds(pl.multiple_of((stripe * 2 + which) * rows, rows), rows)

    def left_copy(k):
        source = (normed_hbm, branch_hbm)[k // 4]
        return remote(
            source.at[:, stripe_lanes(k % 4, 1 - core)], d_proj_sib.at[1 + k // 4, k % 4],
            left_send.at[k], left_recv.at[k], {"dp": sib},
        )

    def right_copies(unit):
        slot = unit % RING
        return [
            remote(
                d_proj.at[slot], d_proj_sib.at[slot, 0 : parts - 1],
                right_send.at[slot, 0], right_recv.at[slot, 0], {"dp": sib},
            ),
            remote(
                mixed_ref, d_proj_sib.at[slot, parts - 1],
                right_send.at[slot, 1], right_recv.at[slot, 1], {"dp": sib},
            ),
        ]

    def halo_copy(unit):
        return remote(
            halo_out.at[unit], halo_in.at[unit], halo_send.at[unit], halo_recv.at[unit], {"narrow": z - 1}
        )

    near = 2 * y + x
    fars = (2 * (1 - y) + x, 2 * y + 1 - x)

    def band(e):
        return pl.ds(2 * e * rows, 2 * rows)

    def copy2(unit, e, j):
        away = (2 * j + 1 - x, 2 * (1 - y) + j)[e]
        return remote(
            total.at[unit % HELD, away, band(e)], got2.at[unit, e, j],
            send2.at[unit, e, j], recv2.at[unit, e, j], {"dp": (flip_x, flip_y)[e]},
        )

    def copy3(unit, e):
        return remote(
            total.at[unit % HELD, fars[e], band(e)], got3.at[unit, e],
            send3.at[unit, e], recv3.at[unit, e], {"dp": (flip_y, flip_x)[e]},
        )

    def copyz(unit, part, k):
        at = pl.ds(pl.multiple_of(part * rows + peers[k] * share, share), share)
        return remote(
            total.at[unit % HELD, near, at], gotz.at[unit, k, part * share : (part + 1) * share],
            sendz.at[unit, k, part], recvz.at[unit, k, part], {"narrow": peers[k]},
        )

    @pl.when(step == 0)
    def _():
        loads = [
            pltpu.make_async_copy(
                (normed_hbm, branch_hbm)[k // 4].at[:, stripe_lanes(k % 4, core)],
                d_proj.at[k // 3, k % 3], local_sem.at[k],
            )
            for k in range(8)
        ]
        for load in loads:
            load.start()
        back[:, :, 0:PAD, :] = jnp.zeros((2, CONV, PAD, BLOCK), F32)
        back[:, :, PAD + tokens :, :] = jnp.zeros((2, CONV, PAD, BLOCK), F32)
        d_normed[...] = jnp.zeros_like(d_normed)
        meet((sib, flip_x, flip_y), peers)
        for k in range(8):
            left_copy(k).start()
        for k in range(8):
            loads[k].wait()
            left_own[k // 4, k % 4] = d_proj[k // 3, k % 3].astype(F32).T.astype(BF16)

    @pl.when(step == 1)
    def _():
        for k in range(8):
            left_copy(k).wait()
            left_sib[k // 4, k % 4] = d_proj_sib[1 + k // 4, k % 4].astype(F32).T.astype(BF16)

    @pl.when(step >= 1)
    def _():
        unit = step - 1

        @pl.when(z < depth - 1)
        def _():
            halo_copy(unit).wait_recv()
            for part in range(3):
                extra = jnp.concatenate([jnp.zeros((PAD, cols), F32), halo_in[unit, part]], axis=0)
                tail = slice(tokens - 2 * PAD, tokens)
                d_proj[unit % RING, part, tail, :] = (
                    d_proj[unit % RING, part, tail, :].astype(F32) + extra
                ).astype(BF16)

        @pl.when(z > 0)
        def _():
            halo_copy(unit).wait_send()

        for copy in right_copies(unit):
            copy.start()

    @pl.when(step < units)
    def _():
        def emit(part, lanes, value):
            halo_out[step, part, :, lanes] = value[:PAD]
            d_proj[step % RING, part, :, lanes] = value[PAD:].astype(BF16)

        backward_heads(step, *heads_in, d_taps_ref, d_beta_ref, ext, back, emit)

        @pl.when(z > 0)
        def _():
            halo_copy(step).start()

    @pl.when(step >= 1)
    def _():
        unit = step - 1
        for copy in right_copies(unit):
            copy.wait()

        def one(k, _):
            to_x, to_y = 1 - k // 2, 1 - k % 2
            stripe = 2 * (to_y * (1 - y) + (1 - to_y) * y) + to_x * (1 - x) + (1 - to_x) * x
            for part in range(parts):
                which = part // (parts - 1)
                mine = d_proj[unit % RING, part] if which == 0 else mixed_ref[...]
                value = jnp.dot(left_own[which, stripe], mine, preferred_element_type=F32)
                value = value + jnp.dot(
                    left_sib[which, stripe], d_proj_sib[unit % RING, part], preferred_element_type=F32
                )
                total[unit % HELD, stripe, part * rows : (part + 1) * rows, :] = value.astype(BF16)

            @pl.when(k == 0)
            def _():
                copy2(unit, 0, 1 - y).start()
                copy2(unit, 1, 1 - x).start()

            @pl.when(k == 1)
            def _():
                copy2(unit, 0, y).start()

            @pl.when(k == 2)
            def _():
                copy2(unit, 1, x).start()

            return 0

        lax.fori_loop(0, 4, one, 0)

        def normed_part(at, _):
            at = pl.ds(pl.multiple_of(at * 512, 512), 512)
            value = d_normed[:, at]
            for part, ref in enumerate((w_query_ref, w_key_ref, w_value_ref)):
                value = value + lax.dot_general(
                    d_proj[unit % RING, part], ref[at, :], (((1,), (1,)), ((), ())), preferred_element_type=F32
                )
            d_normed[:, at] = value
            return 0

        lax.fori_loop(0, d_normed.shape[1] // 512, normed_part, 0)

    def second(unit):
        for e in range(2):
            for j in range(2):
                copy2(unit, e, j).wait()
            add_rows(total.at[unit % HELD, fars[e], band(e)], got2.at[unit, e, (1 - y, 1 - x)[e]], 64)
            copy3(unit, e).start()
        for e in range(2):
            add_rows(total.at[unit % HELD, near, band(e)], got2.at[unit, e, (y, x)[e]], 64)

    def grad_copy(unit):
        at = pl.ds(pl.multiple_of(unit * cols, cols), cols)
        return pltpu.make_async_copy(grad.at[unit % 2], grad_hbm.at[:, :, at], grad_sem.at[unit % 2])

    def third(unit):
        for e in range(2):
            copy3(unit, e).wait()
            add_rows(total.at[unit % HELD, near, band(e)], got3.at[unit, e], 64)
            for k in range(depth - 1):
                for part in (2 * e, 2 * e + 1):
                    copyz(unit, part, k).start()

    def fourth(unit):
        for k in range(depth - 1):
            for part in range(parts):
                copyz(unit, part, k).wait()
        @pl.when(unit >= 2)
        def _():
            grad_copy(unit - 2).wait()

        for part in range(parts):
            at = pl.ds(pl.multiple_of(part * rows + z * share, share), share)
            value = total[unit % HELD, near, at, :].astype(F32)
            for k in range(depth - 1):
                value = value + gotz[unit, k, part * share : (part + 1) * share, :].astype(F32)
            grad[unit % 2, part] = value
        grad_copy(unit).start()

    def stages(at):
        @pl.when((at >= LAG) & (at < units + LAG))
        def _():
            second(at - LAG)

        @pl.when((at >= LAG + 1) & (at < units + LAG + 1))
        def _():
            third(at - LAG - 1)

        @pl.when(at >= LAG + 2)
        def _():
            fourth(at - LAG - 2)

    stages(step)

    @pl.when(step == units)
    def _():
        save = pltpu.make_async_copy(d_normed, d_normed_hbm, local_sem.at[0])
        save.start()

        def one(at, _):
            stages(at)
            return 0

        lax.fori_loop(units + 1, units + LAG + 2, one, 0)
        save.wait()
        grad_copy(units - 2).wait()
        grad_copy(units - 1).wait()


def fused_backward(
    since, beta_logit, query, key, value, halo, taps, new_add, new_map, inverse, starts, entry, exit_grad, d_core,
    w_query, w_key, w_value, mixed, normed, branch,
):
    tokens, width = query.shape
    heads = width // BLOCK
    blocks = tokens // BLOCK
    units = heads // HEADS_STEP
    cols = HEADS_STEP * BLOCK
    depth = lax.axis_size("narrow")
    rows = width // 8
    share = rows // depth
    dma = pltpu.SemaphoreType.DMA

    def now(step):
        return jnp.minimum(step, units - 1)

    def before(step):
        return jnp.maximum(step - 1, 0)

    def whole(shape):
        return pl.BlockSpec(shape, lambda h: (0,) * len(shape))

    wide = pl.BlockSpec((tokens, cols), lambda h: (0, now(h)))

    def lanes(first, second):
        return pl.BlockSpec((first, second, cols), lambda h: (0, 0, now(h)))

    def each(*tail):
        return pl.BlockSpec((HEADS_STEP,) + tail, lambda h: (now(h),) + (0,) * len(tail))

    weight = pl.BlockSpec((width, cols), lambda h: (0, before(h)), pipeline_mode=pl.Buffered(1))
    mixed_spec = pl.BlockSpec((tokens, cols), lambda h: (0, before(h)))
    parts = 4
    anywhere = pl.BlockSpec(memory_space=pl.ANY)
    return pl.pallas_call(
        fused_kernel,
        grid=(units + 1,),
        in_specs=[
            whole(since.shape), whole(beta_logit.shape), wide, wide, wide, lanes(3, PAD), lanes(3, CONV),
            wide, wide, each(blocks, BLOCK, BLOCK), each(blocks, BLOCK, 2 * BLOCK),
            each(BLOCK, BLOCK), each(BLOCK, BLOCK), wide,
            weight, weight, weight, mixed_spec, anywhere, anywhere,
        ],
        out_specs=[anywhere, anywhere, lanes(3, CONV), whole(beta_logit.shape)],
        out_shape=[
            jax.ShapeDtypeStruct((parts, share, width), F32),
            jax.ShapeDtypeStruct((tokens, width), F32),
            jax.ShapeDtypeStruct((3, CONV, width), F32),
            jax.ShapeDtypeStruct(beta_logit.shape, F32),
        ],
        scratch_shapes=[
            pltpu.VMEM((3 * HEADS_STEP, PAD + tokens, BLOCK), F32),
            pltpu.VMEM((2, CONV, PAD + tokens + PAD, BLOCK), F32),
            pltpu.VMEM((2, 4, rows, tokens), BF16),
            pltpu.VMEM((2, 4, rows, tokens), BF16),
            pltpu.VMEM((RING, 3, tokens, cols), BF16),
            pltpu.VMEM((RING, parts, tokens, cols), BF16),
            pltpu.VMEM((units, 3, PAD, cols), F32),
            pltpu.VMEM((units, 3, PAD, cols), F32),
            pltpu.VMEM((HELD, 4, parts * rows, cols), BF16),
            pltpu.VMEM((units, 2, 2, 2 * rows, cols), BF16),
            pltpu.VMEM((units, 2, 2 * rows, cols), BF16),
            pltpu.VMEM((units, depth - 1, parts * share, cols), BF16),
            pltpu.VMEM((tokens, width), F32),
            pltpu.VMEM((2, parts, share, cols), F32),
            dma((8,)), dma((2,)), dma((8,)), dma((8,)), dma((RING, 2)), dma((RING, 2)), dma((units,)), dma((units,)),
            dma((units, 2, 2)), dma((units, 2, 2)), dma((units, 2)), dma((units, 2)),
            dma((units, depth - 1, parts)), dma((units, depth - 1, parts)),
        ],
        compiler_params=pltpu.CompilerParams(
            collective_id=5, has_side_effects=True, vmem_limit_bytes=62 * 1024 * 1024
        ),
        name="fused_backward",
    )(
        since, beta_logit, query, key, value, halo, taps, new_add, new_map, inverse, starts, entry, exit_grad, d_core,
        w_query, w_key, w_value, mixed, normed, branch,
    )


def ffn_grads_kernel(*refs):
    lefts = [refs[0:HALVES], refs[0:HALVES], refs[HALVES : 2 * HALVES]]
    rights = [refs[(2 + m) * HALVES : (3 + m) * HALVES] for m in range(3)]
    (
        gate_ref, up_ref, down_ref, left_buf, right_buf, away, landed, total, got2, got3,
        left_sem, right_sem, send1, recv1, send2, recv2, send3, recv3,
    ) = refs[5 * HALVES :]
    dp = lax.axis_index("dp")
    core, x, y = dp % 2, (dp // 2) % 2, dp // 4
    rows = total.shape[2]
    half = rows // 2
    part = left_buf.shape[1] // HALVES
    sib = dp + 1 - 2 * core
    flip_x = dp + 2 * (1 - 2 * x)
    flip_y = dp + 4 * (1 - 2 * y)
    barrier = pltpu.get_barrier_semaphore()
    for target in (sib, flip_x, flip_y):
        pl.semaphore_signal(barrier, inc=1, device_id={"dp": target}, device_id_type=MESH)

    def load_left(m, k, start):
        own = k // 4
        block = (k % 4) * 2 + own * core + (1 - own) * (1 - core)
        lanes = pl.ds(pl.multiple_of(block * rows, rows), rows)
        for at in range(HALVES):
            copy = pltpu.make_async_copy(
                lefts[m][at].at[:, lanes], left_buf.at[k % 2, at * part : (at + 1) * part], left_sem.at[k % 2, at]
            )
            if start:
                copy.start()
            else:
                copy.wait()

    def load_right(m, start):
        for at in range(HALVES):
            copy = pltpu.make_async_copy(
                rights[m][at], right_buf.at[m % 2, at * part : (at + 1) * part], right_sem.at[m % 2, at]
            )
            if start:
                copy.start()
            else:
                copy.wait()

    def send(src, dst, send_sem, recv_sem, target):
        return pltpu.make_async_remote_copy(
            src_ref=src, dst_ref=dst, send_sem=send_sem, recv_sem=recv_sem,
            device_id={"dp": target}, device_id_type=MESH,
        )

    def copy1(m, stripe):
        return send(away.at[m, stripe], landed.at[m, stripe], send1.at[m, stripe], recv1.at[m, stripe], sib)

    def band(h):
        return pl.ds(h * half, half)

    def order(h):
        if h == 0:
            return (lambda j: 2 * j + 1 - x), (lambda j: 2 * j + x), flip_x, flip_y, 1 - y, y
        return (lambda j: 2 * (1 - y) + j), (lambda j: 2 * y + j), flip_y, flip_x, 1 - x, x

    def copy2(m, h, j):
        gone, _, target, _, _, _ = order(h)
        return send(
            total.at[m, gone(j), band(h)], got2.at[m, h, j], send2.at[2 * m + h, j], recv2.at[2 * m + h, j], target
        )

    def copy3(m, h):
        _, kept, _, target, far, _ = order(h)
        return send(total.at[m, kept(far), band(h)], got3.at[m, h], send3.at[m, h], recv3.at[m, h], target)

    def add_to(dst, src):
        step = 32

        def one(at, _):
            at = pl.ds(pl.multiple_of(at * step, step), step)
            dst[at, :] = (dst[at, :].astype(F32) + src[at, :].astype(F32)).astype(dst.dtype)
            return 0

        lax.fori_loop(0, dst.shape[0] // step, one, 0)

    def compute(m):
        load_right(m, False)
        if m + 1 < 3:
            load_right(m + 1, True)

        def one(k, _):
            @pl.when(k < 7)
            def _():
                load_left(m, k + 1, True)

            if m + 1 < 3:
                @pl.when(k == 7)
                def _():
                    load_left(m + 1, 0, True)

            load_left(m, k, False)
            value = lax.dot_general(
                left_buf[k % 2], right_buf[m % 2], (((0,), (0,)), ((), ())), preferred_element_type=F32
            ).astype(BF16)

            @pl.when(k < 4)
            def _():
                away[m, k] = value
                copy1(m, k).start()

            @pl.when(k >= 4)
            def _():
                total[m, k - 4] = value

            return 0

        lax.fori_loop(0, 8, one, 0)

        def join(stripe, _):
            copy1(m, stripe).wait()
            add_to(total.at[m, stripe], landed.at[m, stripe])
            return 0

        lax.fori_loop(0, 4, join, 0)
        for h in range(2):
            for j in range(2):
                copy2(m, h, j).start()

    def second(m):
        for h in range(2):
            _, kept, _, _, far, near = order(h)
            for j in range(2):
                copy2(m, h, j).wait()
            add_to(total.at[m, kept(far), band(h)], got2.at[m, h, far])
            copy3(m, h).start()
            add_to(total.at[m, kept(near), band(h)], got2.at[m, h, near])

    def third(m):
        for h in range(2):
            _, kept, _, _, _, near = order(h)
            copy3(m, h).wait()
            if m == 2:
                value = total[m, kept(near), band(h), :].astype(F32) + got3[m, h].astype(F32)
                down_ref[:, band(h)] = value.T
                continue
            step = 32

            def one(at, _):
                at = at * step
                value = total[m, kept(near), pl.ds(pl.multiple_of(h * half + at, step), step), :].astype(F32)
                value = value + got3[m, h, pl.ds(pl.multiple_of(at, step), step), :].astype(F32)
                (gate_ref, up_ref)[m][pl.ds(pl.multiple_of(h * half + at, step), step), :] = value
                return 0

            lax.fori_loop(0, half // step, one, 0)

    load_right(0, True)
    load_left(0, 0, True)
    pl.semaphore_wait(barrier, 3)
    compute(0)
    compute(1)
    second(0)
    compute(2)
    third(0)
    second(1)
    third(1)
    second(2)
    third(2)


def ffn_grads(lefts, rights):
    part, height = lefts[0][0].shape
    width = rights[0][0].shape[1]
    rows = height // 8
    half = rows // 2
    dma = pltpu.SemaphoreType.DMA
    operands = [ref for group in (*lefts, *rights) for ref in group]
    return pl.pallas_call(
        ffn_grads_kernel,
        in_specs=[pl.BlockSpec(memory_space=pl.ANY)] * len(operands),
        out_specs=[pl.BlockSpec(memory_space=pltpu.VMEM)] * 3,
        out_shape=[
            jax.ShapeDtypeStruct((rows, width), F32),
            jax.ShapeDtypeStruct((rows, width), F32),
            jax.ShapeDtypeStruct((width, rows), F32),
        ],
        scratch_shapes=[
            pltpu.VMEM((2, HALVES * part, rows), BF16),
            pltpu.VMEM((2, HALVES * part, width), BF16),
            pltpu.VMEM((3, 4, rows, width), BF16),
            pltpu.VMEM((3, 4, rows, width), BF16),
            pltpu.VMEM((3, 4, rows, width), BF16),
            pltpu.VMEM((3, 2, 2, half, width), BF16),
            pltpu.VMEM((3, 2, half, width), BF16),
            dma((2, HALVES)), dma((2, HALVES)), dma((3, 4)), dma((3, 4)),
            dma((6, 2)), dma((6, 2)), dma((3, 2)), dma((3, 2)),
        ],
        compiler_params=pltpu.CompilerParams(
            collective_id=4, has_side_effects=True, vmem_limit_bytes=60 * 1024 * 1024
        ),
        name="ffn_grads",
    )(*operands)


def shifted(value, axis, steps):
    count = lax.axis_size(axis)
    first, last = (max(0, -steps), min(count, count - steps))
    return lax.ppermute(value, axis, [(source, source + steps) for source in range(first, last)])


def matmul(left, right):
    return jnp.dot(left, right, preferred_element_type=F32)


def dot_tn(left, right):
    return jnp.einsum("rd,re->de", left, right, preferred_element_type=F32)


def dot_nt(left, right):
    return jnp.einsum("re,de->rd", left, right, preferred_element_type=F32)


def rms_scale(value_in, gain_vec, epsilon):
    return value_in * lax.rsqrt(jnp.mean(value_in * value_in, axis=-1, keepdims=True) + epsilon) * gain_vec


def norm_back(value_in, gain_vec, upstream, epsilon):
    inv_scale = lax.rsqrt(jnp.mean(value_in * value_in, axis=-1, keepdims=True) + epsilon)
    scaled_up = upstream * gain_vec
    gain_term = jnp.sum(upstream * value_in * inv_scale, axis=0)
    cubed = inv_scale * inv_scale * inv_scale
    back_value = inv_scale * scaled_up - value_in * cubed * jnp.mean(
        scaled_up * value_in, axis=-1, keepdims=True
    )
    return (back_value, gain_term)


def since_start(doc_lengths, offset, rows):
    ends = jnp.cumsum(doc_lengths[0])
    position = offset + jnp.arange(rows, dtype=jnp.int32)
    starts = jnp.max(jnp.where(position[:, None] >= ends[None, :], ends[None, :], 0), axis=1)
    return jnp.broadcast_to((position - starts)[:, None], (rows, BLOCK)).astype(jnp.int32)


def scatter_all(value, dim):
    part = lax.psum_scatter(value, "dp", scatter_dimension=dim, tiled=True)
    return lax.psum_scatter(part, "narrow", scatter_dimension=dim, tiled=True)


def local(
    tokens,
    doc_lengths,
    attn_gain,
    w_query,
    w_key,
    w_value,
    w_beta,
    conv_weight,
    out_gain,
    w_out,
    mlp_gain,
    w_gate,
    w_up,
    w_down,
    grad_out,
):
    tok_rows, model_width = tokens.shape
    offset = lax.axis_index("narrow") * tok_rows
    half = tok_rows // HALVES
    parts = [slice(at * half, (at + 1) * half) for at in range(HALVES)]

    def gather(rows):
        return lax.all_gather(rows, "narrow", axis=0, tiled=True)

    def scatter(rows):
        return lax.psum_scatter(rows, "narrow", scatter_dimension=0, tiled=True)

    cot = gather(grad_out)
    since = since_start(doc_lengths, offset, tok_rows)
    inputs = tokens.astype(F32)
    normed = rms_scale(inputs, attn_gain, 1e-06).astype(BF16)
    query, key, value = (matmul(normed, w).astype(BF16) for w in (w_query, w_key, w_value))
    beta_logit = matmul(normed, w_beta)
    halo = shifted(
        jnp.stack([part[tok_rows - PAD :] for part in (query, key, value)]), "narrow", 1
    )
    out_add, out_map, new_add, new_map, inverse, starts, end = mixer_forward(
        since, beta_logit, query, key, value, halo, conv_weight
    )
    transfer = end[:, :, BLOCK:].astype(BF16)
    entry = carry_chain(transfer, end[:, :, :BLOCK], "narrow", True)
    gain_row = out_gain[None, :]
    attn_mixed = mixer_join(out_add, out_map, entry, gain_row)
    hidden = inputs + matmul(attn_mixed, w_out)
    normed_mlp = rms_scale(hidden, mlp_gain, 1e-06).astype(BF16)
    normed_mlp, cot = lax.optimization_barrier((normed_mlp, cot))
    cot = cot.reshape(-1, tok_rows, model_width)
    cot = [cot[:, part].reshape(-1, model_width) for part in parts]
    gathered = [gather(normed_mlp[part]) for part in parts]
    activation, d_gate, d_up, d_normed_parts, out_parts = [], [], [], [], []
    for at in range(HALVES):
        gate_proj = matmul(gathered[at], w_gate)
        up_proj = matmul(gathered[at], w_up)
        gate_sigmoid = jax.nn.sigmoid(gate_proj)
        silu_gate = gate_proj * gate_sigmoid
        activation.append((silu_gate * up_proj).astype(BF16))
        d_act = jnp.einsum("rd,fd->rf", cot[at], w_down, preferred_element_type=F32)
        d_gate.append(
            (d_act * up_proj * gate_sigmoid * (1.0 + gate_proj * (1.0 - gate_sigmoid))).astype(BF16)
        )
        d_up.append((d_act * silu_gate).astype(BF16))
        d_part = (dot_nt(d_gate[at], w_gate) + dot_nt(d_up[at], w_up)).astype(BF16)
        out_part = matmul(activation[at], w_down).astype(BF16)
        if at + 1 < HALVES:
            quarters = out_part.reshape(-1, 2, half // 2, model_width)
            out_parts += [quarters[:, side].reshape(-1, model_width) for side in range(2)]
            d_part, out_parts, gathered[at + 1] = lax.optimization_barrier((d_part, out_parts, gathered[at + 1]))
        else:
            out_parts.append(out_part)
        d_normed_parts.append(scatter(d_part))
    if lax.axis_size("dp") == 8:
        ffn_sums = ffn_grads((gathered, cot), (d_gate, d_up, activation))
    else:
        ffn_sums = [
            lax.psum_scatter(
                sum(dot_tn(a, c) for a, c in zip(left, right)).astype(BF16), "dp", scatter_dimension=0, tiled=True
            )
            for left, right in ((gathered, d_gate), (gathered, d_up), (cot, activation))
        ]
        ffn_sums[2] = ffn_sums[2].T
    d_normed_parts, out_parts, ffn_sums = lax.optimization_barrier((d_normed_parts, out_parts, ffn_sums))
    out_first, *out_rest = out_parts
    ffn_parts = [scatter(out_first)]
    grad_gate, grad_up, grad_down = (value.astype(F32) for value in ffn_sums)
    d_normed_mlp = jnp.concatenate(d_normed_parts, axis=0).astype(F32)
    d_hidden_norm, mlp_gain_term = norm_back(hidden, mlp_gain, d_normed_mlp, 1e-06)
    d_hidden = grad_out.astype(F32) + d_hidden_norm
    d_branch = d_hidden.astype(BF16)
    d_core, start_grad, out_gain_term = mixer_core_back(out_add, out_map, entry, gain_row, d_branch, w_out)
    exit_grad = carry_chain(transfer, start_grad, "narrow", False)
    exit_grad, out_rest = lax.optimization_barrier((exit_grad, out_rest))
    ffn_parts += [scatter(part) for part in out_rest]
    mixer_args = (
        since, beta_logit, query, key, value, halo, conv_weight,
        new_add, new_map, inverse, starts, entry, exit_grad, d_core,
    )
    if lax.axis_size("dp") == 8:
        grads, d_normed, conv_term, d_beta = fused_backward(
            *mixer_args, w_query, w_key, w_value, attn_mixed, normed, d_branch
        )
    else:
        d_proj, d_halo, conv_term, d_beta = mixer_backward(*mixer_args)
        after = shifted(d_halo.astype(BF16), "narrow", -1)
        d_proj = d_proj.at[:, tok_rows - PAD :].add(after)
        d_normed = sum(dot_nt(part, w) for part, w in zip(d_proj, (w_query, w_key, w_value)))
        pairs = [(normed, part) for part in d_proj] + [(d_branch, attn_mixed)]
        grads = jnp.stack([scatter_all(dot_tn(a, c).astype(BF16), 0).astype(F32) for a, c in pairs])
    d_beta_low = d_beta.astype(BF16)
    beta_term = jnp.einsum("rd,rh->dh", normed, d_beta_low, preferred_element_type=F32)
    d_normed = d_normed + jnp.einsum("rh,dh->rd", d_beta_low, w_beta, preferred_element_type=F32)
    d_input_norm, attn_gain_term = norm_back(inputs, attn_gain, d_normed, 1e-06)
    grad_tokens = (d_hidden + d_input_norm).astype(BF16)
    devices = lax.axis_size("dp") * lax.axis_size("narrow")
    heads = w_beta.shape[1]
    taps = 3 * CONV
    gain_share = BLOCK // devices
    gain_column = jnp.pad(
        out_gain_term.reshape(devices, gain_share), ((0, 0), (0, model_width // devices - gain_share))
    ).reshape(model_width, 1)
    small = jnp.concatenate(
        [
            beta_term,
            conv_term.reshape(taps, model_width).T,
            attn_gain_term[:, None],
            mlp_gain_term[:, None],
            gain_column,
        ],
        axis=1,
    )
    small = jnp.pad(small, ((0, 0), (0, BLOCK - small.shape[1])))
    if lax.axis_size("dp") == 8:
        small = reduce_small(small)
    else:
        small = lax.psum_scatter(small, ("dp", "narrow"), scatter_dimension=0, tiled=True)
    grad_beta = small[:, :heads]
    grad_conv = small[:, heads : heads + taps].T.reshape(3, CONV, -1)
    grad_attn_gain = small[:, heads + taps]
    grad_mlp_gain = small[:, heads + taps + 1]
    grad_out_gain = small[:gain_share, heads + taps + 2]
    ffn_parts, grads = lax.optimization_barrier((ffn_parts, grads))
    block_out = (hidden + jnp.concatenate(ffn_parts, axis=0).astype(F32)).astype(BF16)
    grad_query, grad_key, grad_value = grads[0], grads[1], grads[2]
    grad_w_out = grads[3].T
    return (
        block_out,
        grad_tokens,
        grad_attn_gain,
        grad_query,
        grad_key,
        grad_value,
        grad_beta,
        grad_conv,
        grad_out_gain,
        grad_w_out,
        grad_mlp_gain,
        grad_gate,
        grad_up,
        grad_down,
    )


def solution(mesh):
    placed = (
        P(("dp", "narrow"), None),
        P("dp", None),
        P(),
        P(),
        P(),
        P(),
        P(),
        P(),
        P(),
        P(),
        P(),
        P(None, "narrow"),
        P(None, "narrow"),
        P("narrow", None),
        P(("dp", "narrow"), None),
    )
    return jax.shard_map(
        local,
        mesh=mesh,
        in_specs=placed,
        out_specs=(
            P(("dp", "narrow"), None),
            P(("dp", "narrow"), None),
            P(("dp", "narrow")),
            P(("dp", "narrow"), None),
            P(("dp", "narrow"), None),
            P(("dp", "narrow"), None),
            P(("dp", "narrow"), None),
            P(None, None, ("dp", "narrow")),
            P(("dp", "narrow")),
            P(None, ("dp", "narrow")),
            P(("dp", "narrow")),
            P("dp", "narrow"),
            P("dp", "narrow"),
            P("narrow", "dp"),
        ),
        check_vma=False,
    )
```

```python
import functools

import jax
import jax.numpy as jnp
from jax import lax
from jax.experimental import pallas as pl
from jax.experimental.pallas import tpu as pltpu
from jax.sharding import PartitionSpec as P

CONV = 4
BLOCK = 128
HEADS_STEP = 2
PAD = 8
MESH = pl.DeviceIdType.MESH
F32 = jnp.float32
BF16 = jnp.bfloat16
VMEM_LIMIT = 56 * 1024 * 1024


def mm(left, right, contract=(1, 0)):
    return lax.dot_general(
        left.astype(BF16),
        right.astype(BF16),
        (((contract[0],), (contract[1],)), ((), ())),
        preferred_element_type=F32,
    )


def mm_nt(left, right):
    return mm(left, right, (1, 1))


def mm_tn(left, right):
    return mm(left, right, (0, 0))


def iotas(size):
    row = lax.broadcasted_iota(jnp.int32, (size, size), 0)
    col = lax.broadcasted_iota(jnp.int32, (size, size), 1)
    return row, col


def block_masks(since):
    size = since.shape[0]
    row, col = iotas(size)
    back = row - col
    causal = (back >= 0) & (back <= since)
    strict = (back > 0) & (back <= since)
    keep = (since > row).astype(F32)
    last = since[size - 1 : size, :]
    last_mask = (row >= size - 1 - last).astype(F32)
    keep_last = (last > size - 1).astype(F32)
    return causal, strict, keep, last_mask, keep_last


def unit_lower_inverses(lowers):
    size = lowers[0].shape[0]
    row, col = iotas(size)
    width = 1
    inverses = None
    while width < size:
        join = (row // (2 * width) == col // (2 * width)) & (row // width != col // width)
        pieces = [jnp.where(join, low, 0.0) for low in lowers]
        if inverses is None:
            eye = (row == col).astype(F32)
            inverses = [eye - piece for piece in pieces]
        else:
            halves = [mm(piece, inv) for piece, inv in zip(pieces, inverses)]
            inverses = [inv - mm(inv, half) for inv, half in zip(inverses, halves)]
        width *= 2
    return inverses


def conv_front(ext, proj, halo, taps, since):
    rows = proj.shape[0]
    ext[0:PAD, :] = halo.astype(F32)
    ext[PAD : PAD + rows, :] = proj
    pre = proj * taps[0:1, :]
    for lag in range(1, CONV):
        moved = ext[PAD - lag : PAD - lag + rows, :]
        pre = pre + jnp.where(since >= lag, moved, 0.0) * taps[lag : lag + 1, :]
    gate = 1.0 / (1.0 + jnp.exp(-pre))
    return pre, gate, pre * gate


def unit_rows(value):
    inv = lax.rsqrt(jnp.sum(value * value, axis=-1, keepdims=True) + 1e-06)
    return value * inv, inv


def head_column(array, head):
    lane = lax.broadcasted_iota(jnp.int32, array.shape, 1)
    return jnp.sum(jnp.where(lane == head, array, 0.0), axis=1, keepdims=True)


def forward_kernel(
    since_ref, beta_ref, query_ref, key_ref, value_ref, halo_ref, taps_ref,
    out_add_ref, out_map_ref, new_add_ref, new_map_ref, inverse_ref, starts_ref, end_ref,
    ext,
):
    rows = since_ref.shape[0]
    blocks = rows // BLOCK
    since = since_ref[...]
    jobs = []
    for sub in range(HEADS_STEP):
        head = pl.program_id(0) * HEADS_STEP + sub
        lanes = slice(sub * BLOCK, (sub + 1) * BLOCK)
        mixed = []
        for part, ref in enumerate((query_ref, key_ref, value_ref)):
            _, _, act = conv_front(
                ext.at[sub * 3 + part], ref[:, lanes].astype(F32), halo_ref[part, :, lanes],
                taps_ref[part, :, lanes], since,
            )
            mixed.append(act)
        query = unit_rows(mixed[0])[0] * (BLOCK ** -0.5)
        key = unit_rows(mixed[1])[0]
        beta = 1.0 / (1.0 + jnp.exp(-head_column(beta_ref[...], head)))
        jobs.append((lanes, query, key, mixed[2], beta))
    lowers, scores = [], []
    for lanes, query, key, value, beta in jobs:
        for blk in range(blocks):
            span = slice(blk * BLOCK, (blk + 1) * BLOCK)
            causal, strict, _, _, _ = block_masks(since[span])
            both = mm_nt(jnp.concatenate([key[span], query[span]], axis=0), key[span])
            lowers.append(jnp.where(strict, both[:BLOCK] * beta[span], 0.0))
            scores.append(jnp.where(causal, both[BLOCK:], 0.0).astype(BF16))
    inverses = [inv.astype(BF16) for inv in unit_lower_inverses(lowers)]
    row, col = iotas(BLOCK)
    eye = (row == col).astype(F32)
    states = [jnp.concatenate([jnp.zeros((BLOCK, BLOCK), F32), eye], axis=1) for _ in jobs]
    for blk in range(blocks):
        span = slice(blk * BLOCK, (blk + 1) * BLOCK)
        _, _, keep, last_mask, keep_last = block_masks(since[span])
        for sub, (lanes, query, key, value, beta) in enumerate(jobs):
            at = sub * blocks + blk
            inverse_ref[sub, blk] = inverses[at]
            state = states[sub].astype(BF16)
            starts_ref[sub, blk] = state
            stacked = jnp.concatenate([key[span] * keep, query[span] * keep], axis=0)
            seen = mm(stacked, state)
            rest = jnp.concatenate([value[span], jnp.zeros((BLOCK, BLOCK), F32)], axis=1)
            right = (rest - seen[:BLOCK]) * beta[span]
            new = mm(inverses[at], right).astype(BF16)
            out = seen[BLOCK:] + mm(scores[at], new)
            out_add_ref[span, lanes] = out[:, :BLOCK].astype(BF16)
            out_map_ref[span, lanes] = out[:, BLOCK:].astype(BF16)
            new_add_ref[span, lanes] = new[:, :BLOCK]
            new_map_ref[span, lanes] = new[:, BLOCK:]
            keep_both = jnp.concatenate([keep_last, keep_last], axis=1)
            states[sub] = states[sub] * keep_both + mm_tn(key[span] * last_mask, new)
    for sub in range(len(jobs)):
        end_ref[sub] = states[sub]


def whole_spec(shape):
    return pl.BlockSpec(shape, lambda h: (0,) * len(shape))


def head_spec(rows):
    return pl.BlockSpec((rows, HEADS_STEP * BLOCK), lambda h: (0, h))


def per_head(*tail):
    return pl.BlockSpec((HEADS_STEP,) + tail, lambda h: (h,) + (0,) * len(tail))


def lanes_spec(first, second):
    return pl.BlockSpec((first, second, HEADS_STEP * BLOCK), lambda h: (0, 0, h))


def params():
    return pltpu.CompilerParams(vmem_limit_bytes=VMEM_LIMIT)


def mixer_forward(since, beta_logit, query, key, value, halo, taps):
    rows, width = query.shape
    heads = width // BLOCK
    blocks = rows // BLOCK
    wide = jax.ShapeDtypeStruct((rows, width), BF16)
    return pl.pallas_call(
        forward_kernel,
        grid=(heads // HEADS_STEP,),
        in_specs=[
            whole_spec(since.shape), whole_spec(beta_logit.shape),
            head_spec(rows), head_spec(rows), head_spec(rows),
            lanes_spec(3, PAD), lanes_spec(3, CONV),
        ],
        out_specs=[
            head_spec(rows), head_spec(rows), head_spec(rows), head_spec(rows),
            per_head(blocks, BLOCK, BLOCK), per_head(blocks, BLOCK, 2 * BLOCK),
            per_head(BLOCK, 2 * BLOCK),
        ],
        out_shape=[
            wide, wide, wide, wide,
            jax.ShapeDtypeStruct((heads, blocks, BLOCK, BLOCK), BF16),
            jax.ShapeDtypeStruct((heads, blocks, BLOCK, 2 * BLOCK), BF16),
            jax.ShapeDtypeStruct((heads, BLOCK, 2 * BLOCK), F32),
        ],
        scratch_shapes=[pltpu.VMEM((3 * HEADS_STEP, PAD + rows, BLOCK), F32)],
        compiler_params=params(),
        name="mixer_forward",
    )(since, beta_logit, query, key, value, halo, taps)


def join_kernel(out_add_ref, out_map_ref, entry_ref, gain_ref, mixed_ref):
    for sub in range(HEADS_STEP):
        lanes = slice(sub * BLOCK, (sub + 1) * BLOCK)
        core = out_add_ref[:, lanes].astype(F32) + mm(out_map_ref[:, lanes], entry_ref[sub])
        scale = lax.rsqrt(jnp.mean(core * core, axis=-1, keepdims=True) + 1e-05)
        mixed_ref[:, lanes] = (core * scale * gain_ref[...]).astype(BF16)


def mixer_join(out_add, out_map, entry, gain):
    rows, width = out_add.shape
    heads = width // BLOCK
    return pl.pallas_call(
        join_kernel,
        grid=(heads // HEADS_STEP,),
        in_specs=[head_spec(rows), head_spec(rows), per_head(BLOCK, BLOCK), whole_spec((1, BLOCK))],
        out_specs=head_spec(rows),
        out_shape=jax.ShapeDtypeStruct((rows, width), BF16),
        compiler_params=params(),
        name="mixer_join",
    )(out_add, out_map, entry, gain)


def core_back_kernel(
    out_add_ref, out_map_ref, entry_ref, gain_ref, branch_ref, w_out_ref, d_core_ref, start_ref, gain_out_ref
):
    @pl.when(pl.program_id(0) == 0)
    def _():
        gain_out_ref[...] = jnp.zeros_like(gain_out_ref)

    upstream = mm_nt(branch_ref[...], w_out_ref[...])
    for sub in range(HEADS_STEP):
        lanes = slice(sub * BLOCK, (sub + 1) * BLOCK)
        out_map = out_map_ref[:, lanes]
        core = out_add_ref[:, lanes].astype(F32) + mm(out_map, entry_ref[sub])
        scale = lax.rsqrt(jnp.mean(core * core, axis=-1, keepdims=True) + 1e-05)
        unit = core * scale
        up = upstream[:, lanes]
        gain_out_ref[...] += jnp.sum(up * unit, axis=0, keepdims=True)
        scaled = up * gain_ref[...]
        d_core = scale * (scaled - unit * jnp.mean(scaled * unit, axis=-1, keepdims=True))
        d_core = d_core.astype(BF16)
        d_core_ref[:, lanes] = d_core
        start_ref[sub] = mm_tn(out_map, d_core)


def mixer_core_back(out_add, out_map, entry, gain, branch, w_out):
    rows, width = out_add.shape
    heads = width // BLOCK
    return pl.pallas_call(
        core_back_kernel,
        grid=(heads // HEADS_STEP,),
        in_specs=[
            head_spec(rows), head_spec(rows), per_head(BLOCK, BLOCK), whole_spec((1, BLOCK)),
            whole_spec(branch.shape), pl.BlockSpec((HEADS_STEP * BLOCK, width), lambda h: (h, 0)),
        ],
        out_specs=[head_spec(rows), per_head(BLOCK, BLOCK), whole_spec((1, BLOCK))],
        out_shape=[
            jax.ShapeDtypeStruct((rows, width), BF16),
            jax.ShapeDtypeStruct((heads, BLOCK, BLOCK), F32),
            jax.ShapeDtypeStruct((1, BLOCK), F32),
        ],
        compiler_params=params(),
        name="mixer_core_back",
    )(out_add, out_map, entry, gain, branch, w_out)


def backward_heads(
    step, since_ref, beta_ref, query_ref, key_ref, value_ref, halo_ref, taps_ref,
    new_add_ref, new_map_ref, inverse_ref, starts_ref, entry_ref, exit_ref, d_core_ref,
    d_taps_ref, d_beta_ref, ext, back, emit,
):
    rows = since_ref.shape[0]
    blocks = rows // BLOCK
    since = since_ref[...]
    jobs = []
    for sub in range(HEADS_STEP):
        head = step * HEADS_STEP + sub
        lanes = slice(sub * BLOCK, (sub + 1) * BLOCK)
        fronts = []
        for part, ref in enumerate((query_ref, key_ref, value_ref)):
            fronts.append(
                conv_front(
                    ext.at[sub * 3 + part], ref[:, lanes].astype(F32), halo_ref[part, :, lanes],
                    taps_ref[part, :, lanes], since,
                )
            )
        query_unit, query_inv = unit_rows(fronts[0][2])
        key, key_inv = unit_rows(fronts[1][2])
        query = query_unit * (BLOCK ** -0.5)
        beta = 1.0 / (1.0 + jnp.exp(-head_column(beta_ref[...], head)))
        jobs.append((head, lanes, fronts, query, query_unit, query_inv, key, key_inv, beta))

    saved = {}
    for sub, (head, lanes, fronts, query, query_unit, query_inv, key, key_inv, beta) in enumerate(jobs):
        entry = entry_ref[sub].astype(BF16)
        for blk in range(blocks):
            span = slice(blk * BLOCK, (blk + 1) * BLOCK)
            causal, _, keep, last_mask, _ = block_masks(since[span])
            start = starts_ref[sub, blk]
            state = (start[:, :BLOCK].astype(F32) + mm(start[:, BLOCK:], entry)).astype(BF16)
            new = (new_add_ref[span, lanes].astype(F32) + mm(new_map_ref[span, lanes], entry)).astype(BF16)
            scores = jnp.where(causal, mm_nt(query[span], key[span]), 0.0).astype(BF16)
            d_out = d_core_ref[span, lanes]
            d_new = mm_tn(scores, d_out)
            d_state = mm_tn(query[span] * keep, d_out)
            saved[sub, blk] = (state, new, d_out, d_new, d_state)

    carried = [exit_ref[sub].astype(F32) for sub in range(HEADS_STEP)]
    chain = {}
    for blk in reversed(range(blocks)):
        span = slice(blk * BLOCK, (blk + 1) * BLOCK)
        _, _, keep, last_mask, keep_last = block_masks(since[span])
        for sub, (head, lanes, fronts, query, query_unit, query_inv, key, key_inv, beta) in enumerate(jobs):
            state, new, d_out, d_new, d_state = saved[sub, blk]
            after = carried[sub].astype(BF16)
            d_new = d_new + mm(key[span] * last_mask, after)
            d_right = mm_tn(inverse_ref[sub, blk], d_new)
            d_rest = d_right * beta[span]
            carried[sub] = carried[sub] * keep_last + d_state - mm_tn(key[span] * keep, d_rest)
            chain[sub, blk] = (after, d_right, d_rest)

    lane = lax.broadcasted_iota(jnp.int32, (rows, beta_ref.shape[1]), 1)
    d_beta_all = jnp.zeros((rows, beta_ref.shape[1]), F32)
    for sub, (head, lanes, fronts, query, query_unit, query_inv, key, key_inv, beta) in enumerate(jobs):
        d_queries, d_keys, d_values, d_betas = [], [], [], []
        for blk in range(blocks):
            span = slice(blk * BLOCK, (blk + 1) * BLOCK)
            causal, strict, keep, last_mask, _ = block_masks(since[span])
            state, new, d_out, _, _ = saved[sub, blk]
            after, d_right, d_rest = chain[sub, blk]
            both = mm_nt(jnp.concatenate([d_out, d_right.astype(BF16)], axis=0), new)
            d_scores = jnp.where(causal, both[:BLOCK], 0.0).astype(BF16)
            d_gram = (jnp.where(strict, both[BLOCK:], 0.0) * (-beta[span])).astype(BF16)
            key_b = key[span].astype(BF16)
            from_state = mm_nt(jnp.concatenate([d_out, d_rest.astype(BF16)], axis=0), state)
            left = mm(jnp.concatenate([d_scores, d_gram], axis=0), key_b)
            d_queries.append(from_state[:BLOCK] * keep + left[:BLOCK])
            d_key = left[BLOCK:] + mm_tn(
                jnp.concatenate([d_scores, d_gram], axis=0),
                jnp.concatenate([query[span].astype(BF16), key_b], axis=0),
            )
            d_key = d_key + mm_nt(new, after) * last_mask - from_state[BLOCK:] * keep
            d_keys.append(d_key)
            d_values.append(d_rest)
            d_betas.append(
                jnp.sum(d_right * new.astype(F32), axis=1, keepdims=True) * (1.0 - beta[span])
            )
        d_query = jnp.concatenate(d_queries, axis=0) * (BLOCK ** -0.5)
        d_key = jnp.concatenate(d_keys, axis=0)
        d_query = query_inv * (
            d_query - query_unit * jnp.sum(d_query * query_unit, axis=-1, keepdims=True)
        )
        d_key = key_inv * (d_key - key * jnp.sum(d_key * key, axis=-1, keepdims=True))
        d_value = jnp.concatenate(d_values, axis=0)
        d_beta_all = d_beta_all + jnp.where(lane == head, jnp.concatenate(d_betas, axis=0), 0.0)
        for part, d_act in enumerate((d_query, d_key, d_value)):
            pre, gate, _ = fronts[part]
            taps = taps_ref[part, :, lanes]
            source = ext.at[sub * 3 + part]
            d_pre = d_act * gate * (1.0 + pre * (1.0 - gate))
            room = back.at[(sub * 3 + part) % 2]
            total = None
            d_taps = []
            for lag in range(CONV):
                masked = d_pre if lag == 0 else jnp.where(since >= lag, d_pre, 0.0)
                moved = source[PAD - lag : PAD - lag + rows, :]
                d_taps.append(jnp.sum(masked * moved, axis=0, keepdims=True))
                room[lag, 0:PAD, :] = jnp.zeros((PAD, BLOCK), F32)
                room[lag, PAD : PAD + rows, :] = masked * taps[lag : lag + 1, :]
                room[lag, PAD + rows : PAD + rows + PAD, :] = jnp.zeros((PAD, BLOCK), F32)
                term = room[lag, lag : lag + PAD + rows, :]
                total = term if total is None else total + term
            d_taps_ref[part, :, lanes] = jnp.concatenate(d_taps, axis=0)
            emit(part, lanes, total)

    @pl.when(step == 0)
    def _():
        d_beta_ref[...] = d_beta_all

    @pl.when(step > 0)
    def _():
        d_beta_ref[...] += d_beta_all


def backward_kernel(*refs):
    d_proj_ref, d_halo_ref, d_taps_ref, d_beta_ref, ext, back = refs[14:]

    def emit(part, lanes, total):
        d_halo_ref[part, :, lanes] = total[:PAD]
        d_proj_ref[part, :, lanes] = total[PAD:].astype(BF16)

    backward_heads(pl.program_id(0), *refs[:14], d_taps_ref, d_beta_ref, ext, back, emit)


def mixer_backward(
    since, beta_logit, query, key, value, halo, taps, new_add, new_map, inverse, starts, entry, exit_grad, d_core
):
    rows, width = query.shape
    heads = width // BLOCK
    blocks = rows // BLOCK
    return pl.pallas_call(
        backward_kernel,
        grid=(heads // HEADS_STEP,),
        in_specs=[
            whole_spec(since.shape), whole_spec(beta_logit.shape),
            head_spec(rows), head_spec(rows), head_spec(rows),
            lanes_spec(3, PAD), lanes_spec(3, CONV),
            head_spec(rows), head_spec(rows),
            per_head(blocks, BLOCK, BLOCK), per_head(blocks, BLOCK, 2 * BLOCK),
            per_head(BLOCK, BLOCK), per_head(BLOCK, BLOCK), head_spec(rows),
        ],
        out_specs=[
            lanes_spec(3, rows), lanes_spec(3, PAD), lanes_spec(3, CONV), whole_spec(beta_logit.shape),
        ],
        out_shape=[
            jax.ShapeDtypeStruct((3, rows, width), BF16),
            jax.ShapeDtypeStruct((3, PAD, width), F32),
            jax.ShapeDtypeStruct((3, CONV, width), F32),
            jax.ShapeDtypeStruct(beta_logit.shape, F32),
        ],
        scratch_shapes=[
            pltpu.VMEM((3 * HEADS_STEP, PAD + rows, BLOCK), F32),
            pltpu.VMEM((2, CONV, PAD + rows + PAD, BLOCK), F32),
        ],
        compiler_params=params(),
        name="mixer_backward",
    )(
        since, beta_logit, query, key, value, halo, taps, new_add, new_map, inverse, starts, entry, exit_grad, d_core
    )


GROUPS = 8
HALVES = 2


def chain_kernel(axis, forward, map_ref, add_ref, out_ref, sent, landed, send_sem, recv_sem):
    count = lax.axis_size(axis)
    me = lax.axis_index(axis)
    heads = add_ref.shape[0]
    step = heads // GROUPS
    up, down = (me + 1, me - 1) if forward else (me - 1, me + 1)
    first, last = (0, count - 1) if forward else (count - 1, 0)
    barrier = pltpu.get_barrier_semaphore()

    @pl.when(me != first)
    def _():
        pl.semaphore_signal(barrier, inc=1, device_id={axis: down}, device_id_type=MESH)

    @pl.when(me != last)
    def _():
        pl.semaphore_wait(barrier, 1)

    def copy(group, target):
        return pltpu.make_async_remote_copy(
            src_ref=sent.at[group],
            dst_ref=landed.at[group],
            send_sem=send_sem.at[group],
            recv_sem=recv_sem.at[group],
            device_id={axis: target},
            device_id_type=MESH,
        )

    for group in range(GROUPS):
        @pl.when(me != first)
        def _():
            copy(group, up).wait_recv()
            for sub in range(step):
                head = group * step + sub
                out_ref[head] = landed[group, sub].astype(F32)

        @pl.when(me == first)
        def _():
            out_ref[group * step : (group + 1) * step] = jnp.zeros((step,) + out_ref.shape[1:], F32)

        @pl.when(me != last)
        def _():
            for sub in range(step):
                head = group * step + sub
                if forward:
                    moved = mm(map_ref[head], out_ref[head])
                else:
                    moved = mm_tn(map_ref[head], out_ref[head])
                sent[group, sub] = (moved + add_ref[head]).astype(BF16)
            copy(group, up).start()

    @pl.when(me != last)
    def _():
        for group in range(GROUPS):
            copy(group, up).wait_send()


def carry_chain(map_part, add_part, axis, forward):
    heads = add_part.shape[0]
    part = (GROUPS, heads // GROUPS, BLOCK, BLOCK)
    return pl.pallas_call(
        functools.partial(chain_kernel, axis, forward),
        in_specs=[pl.BlockSpec(memory_space=pltpu.VMEM)] * 2,
        out_specs=pl.BlockSpec(memory_space=pltpu.VMEM),
        out_shape=jax.ShapeDtypeStruct(add_part.shape, F32),
        scratch_shapes=[
            pltpu.VMEM(part, BF16),
            pltpu.VMEM(part, BF16),
            pltpu.SemaphoreType.DMA((GROUPS,)),
            pltpu.SemaphoreType.DMA((GROUPS,)),
        ],
        compiler_params=pltpu.CompilerParams(
            collective_id=1 if forward else 2, has_side_effects=True, vmem_limit_bytes=VMEM_LIMIT // 2
        ),
        name="carry_forward" if forward else "carry_backward",
    )(map_part, add_part)


def bits(dp):
    core, x, y = dp % 2, (dp // 2) % 2, dp // 4
    return core, x, y, dp + 1 - 2 * core, dp + 2 * (1 - 2 * x), dp + 4 * (1 - 2 * y)


def remote(src, dst, send_sem, recv_sem, target):
    return pltpu.make_async_remote_copy(
        src_ref=src, dst_ref=dst, send_sem=send_sem, recv_sem=recv_sem, device_id=target, device_id_type=MESH
    )


def meet(dp_targets, narrow_targets):
    barrier = pltpu.get_barrier_semaphore()
    for target in dp_targets:
        pl.semaphore_signal(barrier, inc=1, device_id={"dp": target}, device_id_type=MESH)
    for target in narrow_targets:
        pl.semaphore_signal(barrier, inc=1, device_id={"narrow": target}, device_id_type=MESH)
    pl.semaphore_wait(barrier, len(dp_targets) + len(narrow_targets))


def add_rows(dst, src, step):
    def one(at, _):
        at = pl.ds(pl.multiple_of(at * step, step), step)
        dst[at, :] = (dst[at, :].astype(F32) + src[at, :].astype(F32)).astype(dst.dtype)
        return 0

    lax.fori_loop(0, dst.shape[0] // step, one, 0)


def small_kernel(small_ref, out_ref, landed, total, got2, got3, gotz, send1, recv1, send2, recv2, send3, recv3, sendz, recvz):
    dp, z = lax.axis_index("dp"), lax.axis_index("narrow")
    core, x, y, sib, flip_x, flip_y = bits(dp)
    depth = lax.axis_size("narrow")
    cols = small_ref.shape[1] // 8
    peers = [(z + step) % depth for step in range(1, depth)]
    meet((sib, flip_x, flip_y), peers)

    def stripe_lanes(stripe, which):
        return pl.ds(pl.multiple_of((stripe * 2 + which) * cols, cols), cols)

    first = [
        remote(small_ref.at[:, stripe_lanes(k, 1 - core)], landed.at[k], send1.at[k], recv1.at[k], {"dp": sib})
        for k in range(4)
    ]
    for copy in first:
        copy.start()
    for k in range(4):
        first[k].wait()
        total[k] = small_ref[:, stripe_lanes(k, core)] + landed[k]
    second = [
        remote(total.at[2 * j + 1 - x], got2.at[j], send2.at[j], recv2.at[j], {"dp": flip_x}) for j in range(2)
    ]
    for copy in second:
        copy.start()
    for copy in second:
        copy.wait()
    third = remote(total.at[2 * (1 - y) + x], got3, send3, recv3, {"dp": flip_y})
    total[2 * (1 - y) + x] = total[2 * (1 - y) + x] + got2[1 - y]
    third.start()
    third.wait()
    mine = 2 * y + x
    total[mine] = total[mine] + got2[y] + got3[...]
    last = [
        remote(total.at[mine], gotz.at[k], sendz.at[k], recvz.at[k], {"narrow": to}) for k, to in enumerate(peers)
    ]
    for copy in last:
        copy.start()
    value = total[mine]
    for k, copy in enumerate(last):
        copy.wait()
        value = value + gotz[k]
    out_ref[...] = value


def reduce_small(small):
    rows, width = small.shape
    depth = lax.axis_size("narrow")
    cols = width // 8
    dma = pltpu.SemaphoreType.DMA
    return pl.pallas_call(
        small_kernel,
        in_specs=[pl.BlockSpec(memory_space=pltpu.VMEM)],
        out_specs=pl.BlockSpec(memory_space=pltpu.VMEM),
        out_shape=jax.ShapeDtypeStruct((rows, cols), F32),
        scratch_shapes=[
            pltpu.VMEM((4, rows, cols), F32),
            pltpu.VMEM((4, rows, cols), F32),
            pltpu.VMEM((2, rows, cols), F32),
            pltpu.VMEM((rows, cols), F32),
            pltpu.VMEM((depth - 1, rows, cols), F32),
            dma((4,)), dma((4,)), dma((2,)), dma((2,)), dma(()), dma(()), dma((depth - 1,)), dma((depth - 1,)),
        ],
        compiler_params=pltpu.CompilerParams(
            collective_id=3, has_side_effects=True, vmem_limit_bytes=16 * 1024 * 1024
        ),
        name="reduce_small",
    )(small)


RING = 3
HELD = 5
LAG = 2


def fused_kernel(*refs):
    heads_in = refs[:14]
    since_ref = refs[0]
    (
        w_query_ref, w_key_ref, w_value_ref, mixed_ref, normed_hbm, branch_hbm,
        grad_hbm, d_normed_hbm, d_taps_ref, d_beta_ref,
        ext, back, left_own, left_sib, d_proj, d_proj_sib, halo_out, halo_in,
        total, got2, got3, gotz, d_normed, grad,
        local_sem, grad_sem, left_send, left_recv, right_send, right_recv, halo_send, halo_recv,
        send2, recv2, send3, recv3, sendz, recvz,
    ) = refs[14:]
    step = pl.program_id(0)
    units = pl.num_programs(0) - 1
    dp, z = lax.axis_index("dp"), lax.axis_index("narrow")
    core, x, y, sib, flip_x, flip_y = bits(dp)
    depth = lax.axis_size("narrow")
    tokens = since_ref.shape[0]
    parts = d_proj_sib.shape[1]
    rows = left_own.shape[2]
    cols = d_proj.shape[3]
    share = rows // depth
    peers = [(z + k) % depth for k in range(1, depth)]

    def stripe_lanes(stripe, which):
        return pl.ds(pl.multiple_of((stripe * 2 + which) * rows, rows), rows)

    def left_copy(k):
        source = (normed_hbm, branch_hbm)[k // 4]
        return remote(
            source.at[:, stripe_lanes(k % 4, 1 - core)], d_proj_sib.at[1 + k // 4, k % 4],
            left_send.at[k], left_recv.at[k], {"dp": sib},
        )

    def right_copies(unit):
        slot = unit % RING
        return [
            remote(
                d_proj.at[slot], d_proj_sib.at[slot, 0 : parts - 1],
                right_send.at[slot, 0], right_recv.at[slot, 0], {"dp": sib},
            ),
            remote(
                mixed_ref, d_proj_sib.at[slot, parts - 1],
                right_send.at[slot, 1], right_recv.at[slot, 1], {"dp": sib},
            ),
        ]

    def halo_copy(unit):
        return remote(
            halo_out.at[unit], halo_in.at[unit], halo_send.at[unit], halo_recv.at[unit], {"narrow": z - 1}
        )

    near = 2 * y + x
    fars = (2 * (1 - y) + x, 2 * y + 1 - x)

    def band(e):
        return pl.ds(2 * e * rows, 2 * rows)

    def copy2(unit, e, j):
        away = (2 * j + 1 - x, 2 * (1 - y) + j)[e]
        return remote(
            total.at[unit % HELD, away, band(e)], got2.at[unit, e, j],
            send2.at[unit, e, j], recv2.at[unit, e, j], {"dp": (flip_x, flip_y)[e]},
        )

    def copy3(unit, e):
        return remote(
            total.at[unit % HELD, fars[e], band(e)], got3.at[unit, e],
            send3.at[unit, e], recv3.at[unit, e], {"dp": (flip_y, flip_x)[e]},
        )

    def copyz(unit, part, k):
        at = pl.ds(pl.multiple_of(part * rows + peers[k] * share, share), share)
        return remote(
            total.at[unit % HELD, near, at], gotz.at[unit, k, part * share : (part + 1) * share],
            sendz.at[unit, k, part], recvz.at[unit, k, part], {"narrow": peers[k]},
        )

    @pl.when(step == 0)
    def _():
        loads = [
            pltpu.make_async_copy(
                (normed_hbm, branch_hbm)[k // 4].at[:, stripe_lanes(k % 4, core)],
                d_proj.at[k // 3, k % 3], local_sem.at[k],
            )
            for k in range(8)
        ]
        for load in loads:
            load.start()
        back[:, :, 0:PAD, :] = jnp.zeros((2, CONV, PAD, BLOCK), F32)
        back[:, :, PAD + tokens :, :] = jnp.zeros((2, CONV, PAD, BLOCK), F32)
        d_normed[...] = jnp.zeros_like(d_normed)
        meet((sib, flip_x, flip_y), peers)
        for k in range(8):
            left_copy(k).start()
        for k in range(8):
            loads[k].wait()
            left_own[k // 4, k % 4] = d_proj[k // 3, k % 3].astype(F32).T.astype(BF16)

    @pl.when(step == 1)
    def _():
        for k in range(8):
            left_copy(k).wait()
            left_sib[k // 4, k % 4] = d_proj_sib[1 + k // 4, k % 4].astype(F32).T.astype(BF16)

    @pl.when(step >= 1)
    def _():
        unit = step - 1

        @pl.when(z < depth - 1)
        def _():
            halo_copy(unit).wait_recv()
            for part in range(3):
                extra = jnp.concatenate([jnp.zeros((PAD, cols), F32), halo_in[unit, part]], axis=0)
                tail = slice(tokens - 2 * PAD, tokens)
                d_proj[unit % RING, part, tail, :] = (
                    d_proj[unit % RING, part, tail, :].astype(F32) + extra
                ).astype(BF16)

        @pl.when(z > 0)
        def _():
            halo_copy(unit).wait_send()

        for copy in right_copies(unit):
            copy.start()

    @pl.when(step < units)
    def _():
        def emit(part, lanes, value):
            halo_out[step, part, :, lanes] = value[:PAD]
            d_proj[step % RING, part, :, lanes] = value[PAD:].astype(BF16)

        backward_heads(step, *heads_in, d_taps_ref, d_beta_ref, ext, back, emit)

        @pl.when(z > 0)
        def _():
            halo_copy(step).start()

    @pl.when(step >= 1)
    def _():
        unit = step - 1
        for copy in right_copies(unit):
            copy.wait()

        def one(k, _):
            to_x, to_y = 1 - k // 2, 1 - k % 2
            stripe = 2 * (to_y * (1 - y) + (1 - to_y) * y) + to_x * (1 - x) + (1 - to_x) * x
            for part in range(parts):
                which = part // (parts - 1)
                mine = d_proj[unit % RING, part] if which == 0 else mixed_ref[...]
                value = jnp.dot(left_own[which, stripe], mine, preferred_element_type=F32)
                value = value + jnp.dot(
                    left_sib[which, stripe], d_proj_sib[unit % RING, part], preferred_element_type=F32
                )
                total[unit % HELD, stripe, part * rows : (part + 1) * rows, :] = value.astype(BF16)

            @pl.when(k == 0)
            def _():
                copy2(unit, 0, 1 - y).start()
                copy2(unit, 1, 1 - x).start()

            @pl.when(k == 1)
            def _():
                copy2(unit, 0, y).start()

            @pl.when(k == 2)
            def _():
                copy2(unit, 1, x).start()

            return 0

        lax.fori_loop(0, 4, one, 0)

        def normed_part(at, _):
            at = pl.ds(pl.multiple_of(at * 512, 512), 512)
            value = d_normed[:, at]
            for part, ref in enumerate((w_query_ref, w_key_ref, w_value_ref)):
                value = value + lax.dot_general(
                    d_proj[unit % RING, part], ref[at, :], (((1,), (1,)), ((), ())), preferred_element_type=F32
                )
            d_normed[:, at] = value
            return 0

        lax.fori_loop(0, d_normed.shape[1] // 512, normed_part, 0)

    def second(unit):
        for e in range(2):
            for j in range(2):
                copy2(unit, e, j).wait()
            add_rows(total.at[unit % HELD, fars[e], band(e)], got2.at[unit, e, (1 - y, 1 - x)[e]], 64)
            copy3(unit, e).start()
        for e in range(2):
            add_rows(total.at[unit % HELD, near, band(e)], got2.at[unit, e, (y, x)[e]], 64)

    def grad_copy(unit):
        at = pl.ds(pl.multiple_of(unit * cols, cols), cols)
        return pltpu.make_async_copy(grad.at[unit % 2], grad_hbm.at[:, :, at], grad_sem.at[unit % 2])

    def third(unit):
        for e in range(2):
            copy3(unit, e).wait()
            add_rows(total.at[unit % HELD, near, band(e)], got3.at[unit, e], 64)
            for k in range(depth - 1):
                for part in (2 * e, 2 * e + 1):
                    copyz(unit, part, k).start()

    def fourth(unit):
        for k in range(depth - 1):
            for part in range(parts):
                copyz(unit, part, k).wait()
        @pl.when(unit >= 2)
        def _():
            grad_copy(unit - 2).wait()

        for part in range(parts):
            at = pl.ds(pl.multiple_of(part * rows + z * share, share), share)
            value = total[unit % HELD, near, at, :].astype(F32)
            for k in range(depth - 1):
                value = value + gotz[unit, k, part * share : (part + 1) * share, :].astype(F32)
            grad[unit % 2, part] = value
        grad_copy(unit).start()

    def stages(at):
        @pl.when((at >= LAG) & (at < units + LAG))
        def _():
            second(at - LAG)

        @pl.when((at >= LAG + 1) & (at < units + LAG + 1))
        def _():
            third(at - LAG - 1)

        @pl.when(at >= LAG + 2)
        def _():
            fourth(at - LAG - 2)

    stages(step)

    @pl.when(step == units)
    def _():
        save = pltpu.make_async_copy(d_normed, d_normed_hbm, local_sem.at[0])
        save.start()

        def one(at, _):
            stages(at)
            return 0

        lax.fori_loop(units + 1, units + LAG + 2, one, 0)
        save.wait()
        grad_copy(units - 2).wait()
        grad_copy(units - 1).wait()


def fused_backward(
    since, beta_logit, query, key, value, halo, taps, new_add, new_map, inverse, starts, entry, exit_grad, d_core,
    w_query, w_key, w_value, mixed, normed, branch,
):
    tokens, width = query.shape
    heads = width // BLOCK
    blocks = tokens // BLOCK
    units = heads // HEADS_STEP
    cols = HEADS_STEP * BLOCK
    depth = lax.axis_size("narrow")
    rows = width // 8
    share = rows // depth
    dma = pltpu.SemaphoreType.DMA

    def now(step):
        return jnp.minimum(step, units - 1)

    def before(step):
        return jnp.maximum(step - 1, 0)

    def whole(shape):
        return pl.BlockSpec(shape, lambda h: (0,) * len(shape))

    wide = pl.BlockSpec((tokens, cols), lambda h: (0, now(h)))

    def lanes(first, second):
        return pl.BlockSpec((first, second, cols), lambda h: (0, 0, now(h)))

    def each(*tail):
        return pl.BlockSpec((HEADS_STEP,) + tail, lambda h: (now(h),) + (0,) * len(tail))

    weight = pl.BlockSpec((width, cols), lambda h: (0, before(h)), pipeline_mode=pl.Buffered(1))
    mixed_spec = pl.BlockSpec((tokens, cols), lambda h: (0, before(h)))
    parts = 4
    anywhere = pl.BlockSpec(memory_space=pl.ANY)
    return pl.pallas_call(
        fused_kernel,
        grid=(units + 1,),
        in_specs=[
            whole(since.shape), whole(beta_logit.shape), wide, wide, wide, lanes(3, PAD), lanes(3, CONV),
            wide, wide, each(blocks, BLOCK, BLOCK), each(blocks, BLOCK, 2 * BLOCK),
            each(BLOCK, BLOCK), each(BLOCK, BLOCK), wide,
            weight, weight, weight, mixed_spec, anywhere, anywhere,
        ],
        out_specs=[anywhere, anywhere, lanes(3, CONV), whole(beta_logit.shape)],
        out_shape=[
            jax.ShapeDtypeStruct((parts, share, width), F32),
            jax.ShapeDtypeStruct((tokens, width), F32),
            jax.ShapeDtypeStruct((3, CONV, width), F32),
            jax.ShapeDtypeStruct(beta_logit.shape, F32),
        ],
        scratch_shapes=[
            pltpu.VMEM((3 * HEADS_STEP, PAD + tokens, BLOCK), F32),
            pltpu.VMEM((2, CONV, PAD + tokens + PAD, BLOCK), F32),
            pltpu.VMEM((2, 4, rows, tokens), BF16),
            pltpu.VMEM((2, 4, rows, tokens), BF16),
            pltpu.VMEM((RING, 3, tokens, cols), BF16),
            pltpu.VMEM((RING, parts, tokens, cols), BF16),
            pltpu.VMEM((units, 3, PAD, cols), F32),
            pltpu.VMEM((units, 3, PAD, cols), F32),
            pltpu.VMEM((HELD, 4, parts * rows, cols), BF16),
            pltpu.VMEM((units, 2, 2, 2 * rows, cols), BF16),
            pltpu.VMEM((units, 2, 2 * rows, cols), BF16),
            pltpu.VMEM((units, depth - 1, parts * share, cols), BF16),
            pltpu.VMEM((tokens, width), F32),
            pltpu.VMEM((2, parts, share, cols), F32),
            dma((8,)), dma((2,)), dma((8,)), dma((8,)), dma((RING, 2)), dma((RING, 2)), dma((units,)), dma((units,)),
            dma((units, 2, 2)), dma((units, 2, 2)), dma((units, 2)), dma((units, 2)),
            dma((units, depth - 1, parts)), dma((units, depth - 1, parts)),
        ],
        compiler_params=pltpu.CompilerParams(
            collective_id=5, has_side_effects=True, vmem_limit_bytes=62 * 1024 * 1024
        ),
        name="fused_backward",
    )(
        since, beta_logit, query, key, value, halo, taps, new_add, new_map, inverse, starts, entry, exit_grad, d_core,
        w_query, w_key, w_value, mixed, normed, branch,
    )


def ffn_grads_kernel(*refs):
    lefts = [refs[0:HALVES], refs[0:HALVES], refs[HALVES : 2 * HALVES]]
    rights = [refs[(2 + m) * HALVES : (3 + m) * HALVES] for m in range(3)]
    (
        gate_ref, up_ref, down_ref, left_buf, right_buf, away, landed, total, got2, got3,
        left_sem, right_sem, send1, recv1, send2, recv2, send3, recv3,
    ) = refs[5 * HALVES :]
    dp = lax.axis_index("dp")
    core, x, y = dp % 2, (dp // 2) % 2, dp // 4
    rows = total.shape[2]
    half = rows // 2
    part = left_buf.shape[1] // HALVES
    sib = dp + 1 - 2 * core
    flip_x = dp + 2 * (1 - 2 * x)
    flip_y = dp + 4 * (1 - 2 * y)
    barrier = pltpu.get_barrier_semaphore()
    for target in (sib, flip_x, flip_y):
        pl.semaphore_signal(barrier, inc=1, device_id={"dp": target}, device_id_type=MESH)

    def load_left(m, k, start):
        own = k // 4
        block = (k % 4) * 2 + own * core + (1 - own) * (1 - core)
        lanes = pl.ds(pl.multiple_of(block * rows, rows), rows)
        for at in range(HALVES):
            copy = pltpu.make_async_copy(
                lefts[m][at].at[:, lanes], left_buf.at[k % 2, at * part : (at + 1) * part], left_sem.at[k % 2, at]
            )
            if start:
                copy.start()
            else:
                copy.wait()

    def load_right(m, start):
        for at in range(HALVES):
            copy = pltpu.make_async_copy(
                rights[m][at], right_buf.at[m % 2, at * part : (at + 1) * part], right_sem.at[m % 2, at]
            )
            if start:
                copy.start()
            else:
                copy.wait()

    def send(src, dst, send_sem, recv_sem, target):
        return pltpu.make_async_remote_copy(
            src_ref=src, dst_ref=dst, send_sem=send_sem, recv_sem=recv_sem,
            device_id={"dp": target}, device_id_type=MESH,
        )

    def copy1(m, stripe):
        return send(away.at[m, stripe], landed.at[m, stripe], send1.at[m, stripe], recv1.at[m, stripe], sib)

    def band(h):
        return pl.ds(h * half, half)

    def order(h):
        if h == 0:
            return (lambda j: 2 * j + 1 - x), (lambda j: 2 * j + x), flip_x, flip_y, 1 - y, y
        return (lambda j: 2 * (1 - y) + j), (lambda j: 2 * y + j), flip_y, flip_x, 1 - x, x

    def copy2(m, h, j):
        gone, _, target, _, _, _ = order(h)
        return send(
            total.at[m, gone(j), band(h)], got2.at[m, h, j], send2.at[2 * m + h, j], recv2.at[2 * m + h, j], target
        )

    def copy3(m, h):
        _, kept, _, target, far, _ = order(h)
        return send(total.at[m, kept(far), band(h)], got3.at[m, h], send3.at[m, h], recv3.at[m, h], target)

    def add_to(dst, src):
        step = 32

        def one(at, _):
            at = pl.ds(pl.multiple_of(at * step, step), step)
            dst[at, :] = (dst[at, :].astype(F32) + src[at, :].astype(F32)).astype(dst.dtype)
            return 0

        lax.fori_loop(0, dst.shape[0] // step, one, 0)

    def compute(m):
        load_right(m, False)
        if m + 1 < 3:
            load_right(m + 1, True)

        def one(k, _):
            @pl.when(k < 7)
            def _():
                load_left(m, k + 1, True)

            if m + 1 < 3:
                @pl.when(k == 7)
                def _():
                    load_left(m + 1, 0, True)

            load_left(m, k, False)
            value = lax.dot_general(
                left_buf[k % 2], right_buf[m % 2], (((0,), (0,)), ((), ())), preferred_element_type=F32
            ).astype(BF16)

            @pl.when(k < 4)
            def _():
                away[m, k] = value
                copy1(m, k).start()

            @pl.when(k >= 4)
            def _():
                total[m, k - 4] = value

            return 0

        lax.fori_loop(0, 8, one, 0)

        def join(stripe, _):
            copy1(m, stripe).wait()
            add_to(total.at[m, stripe], landed.at[m, stripe])
            return 0

        lax.fori_loop(0, 4, join, 0)
        for h in range(2):
            for j in range(2):
                copy2(m, h, j).start()

    def second(m):
        for h in range(2):
            _, kept, _, _, far, near = order(h)
            for j in range(2):
                copy2(m, h, j).wait()
            add_to(total.at[m, kept(far), band(h)], got2.at[m, h, far])
            copy3(m, h).start()
            add_to(total.at[m, kept(near), band(h)], got2.at[m, h, near])

    def third(m):
        for h in range(2):
            _, kept, _, _, _, near = order(h)
            copy3(m, h).wait()
            if m == 2:
                value = total[m, kept(near), band(h), :].astype(F32) + got3[m, h].astype(F32)
                down_ref[:, band(h)] = value.T
                continue
            step = 32

            def one(at, _):
                at = at * step
                value = total[m, kept(near), pl.ds(pl.multiple_of(h * half + at, step), step), :].astype(F32)
                value = value + got3[m, h, pl.ds(pl.multiple_of(at, step), step), :].astype(F32)
                (gate_ref, up_ref)[m][pl.ds(pl.multiple_of(h * half + at, step), step), :] = value
                return 0

            lax.fori_loop(0, half // step, one, 0)

    load_right(0, True)
    load_left(0, 0, True)
    pl.semaphore_wait(barrier, 3)
    compute(0)
    compute(1)
    second(0)
    compute(2)
    third(0)
    second(1)
    third(1)
    second(2)
    third(2)


def ffn_grads(lefts, rights):
    part, height = lefts[0][0].shape
    width = rights[0][0].shape[1]
    rows = height // 8
    half = rows // 2
    dma = pltpu.SemaphoreType.DMA
    operands = [ref for group in (*lefts, *rights) for ref in group]
    return pl.pallas_call(
        ffn_grads_kernel,
        in_specs=[pl.BlockSpec(memory_space=pl.ANY)] * len(operands),
        out_specs=[pl.BlockSpec(memory_space=pltpu.VMEM)] * 3,
        out_shape=[
            jax.ShapeDtypeStruct((rows, width), F32),
            jax.ShapeDtypeStruct((rows, width), F32),
            jax.ShapeDtypeStruct((width, rows), F32),
        ],
        scratch_shapes=[
            pltpu.VMEM((2, HALVES * part, rows), BF16),
            pltpu.VMEM((2, HALVES * part, width), BF16),
            pltpu.VMEM((3, 4, rows, width), BF16),
            pltpu.VMEM((3, 4, rows, width), BF16),
            pltpu.VMEM((3, 4, rows, width), BF16),
            pltpu.VMEM((3, 2, 2, half, width), BF16),
            pltpu.VMEM((3, 2, half, width), BF16),
            dma((2, HALVES)), dma((2, HALVES)), dma((3, 4)), dma((3, 4)),
            dma((6, 2)), dma((6, 2)), dma((3, 2)), dma((3, 2)),
        ],
        compiler_params=pltpu.CompilerParams(
            collective_id=4, has_side_effects=True, vmem_limit_bytes=60 * 1024 * 1024
        ),
        name="ffn_grads",
    )(*operands)


def shifted(value, axis, steps):
    count = lax.axis_size(axis)
    first, last = (max(0, -steps), min(count, count - steps))
    return lax.ppermute(value, axis, [(source, source + steps) for source in range(first, last)])


def matmul(left, right):
    return jnp.dot(left, right, preferred_element_type=F32)


def dot_tn(left, right):
    return jnp.einsum("rd,re->de", left, right, preferred_element_type=F32)


def dot_nt(left, right):
    return jnp.einsum("re,de->rd", left, right, preferred_element_type=F32)


def rms_scale(value_in, gain_vec, epsilon):
    return value_in * lax.rsqrt(jnp.mean(value_in * value_in, axis=-1, keepdims=True) + epsilon) * gain_vec


def norm_back(value_in, gain_vec, upstream, epsilon):
    inv_scale = lax.rsqrt(jnp.mean(value_in * value_in, axis=-1, keepdims=True) + epsilon)
    scaled_up = upstream * gain_vec
    gain_term = jnp.sum(upstream * value_in * inv_scale, axis=0)
    cubed = inv_scale * inv_scale * inv_scale
    back_value = inv_scale * scaled_up - value_in * cubed * jnp.mean(
        scaled_up * value_in, axis=-1, keepdims=True
    )
    return (back_value, gain_term)


def since_start(doc_lengths, offset, rows):
    ends = jnp.cumsum(doc_lengths[0])
    position = offset + jnp.arange(rows, dtype=jnp.int32)
    starts = jnp.max(jnp.where(position[:, None] >= ends[None, :], ends[None, :], 0), axis=1)
    return jnp.broadcast_to((position - starts)[:, None], (rows, BLOCK)).astype(jnp.int32)


def scatter_all(value, dim):
    part = lax.psum_scatter(value, "dp", scatter_dimension=dim, tiled=True)
    return lax.psum_scatter(part, "narrow", scatter_dimension=dim, tiled=True)


def local(
    tokens,
    doc_lengths,
    attn_gain,
    w_query,
    w_key,
    w_value,
    w_beta,
    conv_weight,
    out_gain,
    w_out,
    mlp_gain,
    w_gate,
    w_up,
    w_down,
    grad_out,
):
    tok_rows, model_width = tokens.shape
    offset = lax.axis_index("narrow") * tok_rows
    half = tok_rows // HALVES
    parts = [slice(at * half, (at + 1) * half) for at in range(HALVES)]

    def gather(rows):
        return lax.all_gather(rows, "narrow", axis=0, tiled=True)

    def scatter(rows):
        return lax.psum_scatter(rows, "narrow", scatter_dimension=0, tiled=True)

    cot = gather(grad_out)
    since = since_start(doc_lengths, offset, tok_rows)
    inputs = tokens.astype(F32)
    normed = rms_scale(inputs, attn_gain, 1e-06).astype(BF16)
    query, key, value = (matmul(normed, w).astype(BF16) for w in (w_query, w_key, w_value))
    beta_logit = matmul(normed, w_beta)
    halo = shifted(
        jnp.stack([part[tok_rows - PAD :] for part in (query, key, value)]), "narrow", 1
    )
    out_add, out_map, new_add, new_map, inverse, starts, end = mixer_forward(
        since, beta_logit, query, key, value, halo, conv_weight
    )
    transfer = end[:, :, BLOCK:].astype(BF16)
    entry = carry_chain(transfer, end[:, :, :BLOCK], "narrow", True)
    gain_row = out_gain[None, :]
    attn_mixed = mixer_join(out_add, out_map, entry, gain_row)
    hidden = inputs + matmul(attn_mixed, w_out)
    normed_mlp = rms_scale(hidden, mlp_gain, 1e-06).astype(BF16)
    normed_mlp, cot = lax.optimization_barrier((normed_mlp, cot))
    cot = cot.reshape(-1, tok_rows, model_width)
    cot = [cot[:, part].reshape(-1, model_width) for part in parts]
    gathered = [gather(normed_mlp[part]) for part in parts]
    activation, d_gate, d_up, d_normed_parts, out_parts = [], [], [], [], []
    for at in range(HALVES):
        gate_proj = matmul(gathered[at], w_gate)
        up_proj = matmul(gathered[at], w_up)
        gate_sigmoid = jax.nn.sigmoid(gate_proj)
        silu_gate = gate_proj * gate_sigmoid
        activation.append((silu_gate * up_proj).astype(BF16))
        d_act = jnp.einsum("rd,fd->rf", cot[at], w_down, preferred_element_type=F32)
        d_gate.append(
            (d_act * up_proj * gate_sigmoid * (1.0 + gate_proj * (1.0 - gate_sigmoid))).astype(BF16)
        )
        d_up.append((d_act * silu_gate).astype(BF16))
        d_part = (dot_nt(d_gate[at], w_gate) + dot_nt(d_up[at], w_up)).astype(BF16)
        out_part = matmul(activation[at], w_down).astype(BF16)
        if at + 1 < HALVES:
            quarters = out_part.reshape(-1, 2, half // 2, model_width)
            out_parts += [quarters[:, side].reshape(-1, model_width) for side in range(2)]
            d_part, out_parts, gathered[at + 1] = lax.optimization_barrier((d_part, out_parts, gathered[at + 1]))
        else:
            out_parts.append(out_part)
        d_normed_parts.append(scatter(d_part))
    if lax.axis_size("dp") == 8:
        ffn_sums = ffn_grads((gathered, cot), (d_gate, d_up, activation))
    else:
        ffn_sums = [
            lax.psum_scatter(
                sum(dot_tn(a, c) for a, c in zip(left, right)).astype(BF16), "dp", scatter_dimension=0, tiled=True
            )
            for left, right in ((gathered, d_gate), (gathered, d_up), (cot, activation))
        ]
        ffn_sums[2] = ffn_sums[2].T
    d_normed_parts, out_parts, ffn_sums = lax.optimization_barrier((d_normed_parts, out_parts, ffn_sums))
    out_first, *out_rest = out_parts
    ffn_parts = [scatter(out_first)]
    grad_gate, grad_up, grad_down = (value.astype(F32) for value in ffn_sums)
    d_normed_mlp = jnp.concatenate(d_normed_parts, axis=0).astype(F32)
    d_hidden_norm, mlp_gain_term = norm_back(hidden, mlp_gain, d_normed_mlp, 1e-06)
    d_hidden = grad_out.astype(F32) + d_hidden_norm
    d_branch = d_hidden.astype(BF16)
    d_core, start_grad, out_gain_term = mixer_core_back(out_add, out_map, entry, gain_row, d_branch, w_out)
    exit_grad = carry_chain(transfer, start_grad, "narrow", False)
    exit_grad, out_rest = lax.optimization_barrier((exit_grad, out_rest))
    ffn_parts += [scatter(part) for part in out_rest]
    mixer_args = (
        since, beta_logit, query, key, value, halo, conv_weight,
        new_add, new_map, inverse, starts, entry, exit_grad, d_core,
    )
    if lax.axis_size("dp") == 8:
        grads, d_normed, conv_term, d_beta = fused_backward(
            *mixer_args, w_query, w_key, w_value, attn_mixed, normed, d_branch
        )
    else:
        d_proj, d_halo, conv_term, d_beta = mixer_backward(*mixer_args)
        after = shifted(d_halo.astype(BF16), "narrow", -1)
        d_proj = d_proj.at[:, tok_rows - PAD :].add(after)
        d_normed = sum(dot_nt(part, w) for part, w in zip(d_proj, (w_query, w_key, w_value)))
        pairs = [(normed, part) for part in d_proj] + [(d_branch, attn_mixed)]
        grads = jnp.stack([scatter_all(dot_tn(a, c).astype(BF16), 0).astype(F32) for a, c in pairs])
    d_beta_low = d_beta.astype(BF16)
    beta_term = jnp.einsum("rh,rd->hd", d_beta_low, normed, preferred_element_type=F32)
    d_normed = d_normed + jnp.einsum("rh,dh->rd", d_beta_low, w_beta, preferred_element_type=F32)
    d_input_norm, attn_gain_term = norm_back(inputs, attn_gain, d_normed, 1e-06)
    grad_tokens = (d_hidden + d_input_norm).astype(BF16)
    devices = lax.axis_size("dp") * lax.axis_size("narrow")
    heads = w_beta.shape[1]
    taps = 3 * CONV
    gain_share = BLOCK // devices
    per_device = model_width // devices
    gain_row_term = jnp.pad(
        out_gain_term.reshape(devices, gain_share), ((0, 0), (0, per_device - gain_share))
    ).reshape(1, model_width)
    small = jnp.concatenate(
        [
            beta_term,
            conv_term.reshape(taps, model_width),
            attn_gain_term[None, :],
            mlp_gain_term[None, :],
            gain_row_term,
            jnp.zeros((-(heads + taps + 3) % 8, model_width), F32),
        ],
        axis=0,
    )
    if lax.axis_size("dp") == 8:
        small = lax.dynamic_slice_in_dim(
            reduce_small(small), lax.axis_index("narrow") * per_device, per_device, axis=1
        )
    else:
        small = lax.psum_scatter(small, ("dp", "narrow"), scatter_dimension=1, tiled=True)
    grad_beta = small[:heads].T
    grad_conv = small[heads : heads + taps].reshape(3, CONV, per_device)
    grad_attn_gain = small[heads + taps]
    grad_mlp_gain = small[heads + taps + 1]
    grad_out_gain = small[heads + taps + 2, :gain_share]
    ffn_parts, grads = lax.optimization_barrier((ffn_parts, grads))
    block_out = (hidden + jnp.concatenate(ffn_parts, axis=0).astype(F32)).astype(BF16)
    grad_query, grad_key, grad_value = grads[0], grads[1], grads[2]
    grad_w_out = grads[3].T
    return (
        block_out,
        grad_tokens,
        grad_attn_gain,
        grad_query,
        grad_key,
        grad_value,
        grad_beta,
        grad_conv,
        grad_out_gain,
        grad_w_out,
        grad_mlp_gain,
        grad_gate,
        grad_up,
        grad_down,
    )


def solution(mesh):
    placed = (
        P(("dp", "narrow"), None),
        P("dp", None),
        P(),
        P(),
        P(),
        P(),
        P(),
        P(),
        P(),
        P(),
        P(),
        P(None, "narrow"),
        P(None, "narrow"),
        P("narrow", None),
        P(("dp", "narrow"), None),
    )
    return jax.shard_map(
        local,
        mesh=mesh,
        in_specs=placed,
        out_specs=(
            P(("dp", "narrow"), None),
            P(("dp", "narrow"), None),
            P(("dp", "narrow")),
            P(("dp", "narrow"), None),
            P(("dp", "narrow"), None),
            P(("dp", "narrow"), None),
            P(("dp", "narrow"), None),
            P(None, None, ("dp", "narrow")),
            P(("dp", "narrow")),
            P(None, ("dp", "narrow")),
            P(("dp", "narrow")),
            P("dp", "narrow"),
            P("dp", "narrow"),
            P("narrow", "dp"),
        ),
        check_vma=False,
    )
```

```python
import functools

import jax
import jax.numpy as jnp
from jax import lax
from jax.experimental import pallas as pl
from jax.experimental.pallas import tpu as pltpu
from jax.sharding import PartitionSpec as P

CONV = 4
BLOCK = 128
HEADS_STEP = 2
PAD = 8
MESH = pl.DeviceIdType.MESH
F32 = jnp.float32
BF16 = jnp.bfloat16
VMEM_LIMIT = 56 * 1024 * 1024


def mm(left, right, contract=(1, 0)):
    return lax.dot_general(
        left.astype(BF16),
        right.astype(BF16),
        (((contract[0],), (contract[1],)), ((), ())),
        preferred_element_type=F32,
    )


def mm_nt(left, right):
    return mm(left, right, (1, 1))


def mm_tn(left, right):
    return mm(left, right, (0, 0))


def iotas(size):
    row = lax.broadcasted_iota(jnp.int32, (size, size), 0)
    col = lax.broadcasted_iota(jnp.int32, (size, size), 1)
    return row, col


def block_masks(since):
    size = since.shape[0]
    row, col = iotas(size)
    back = row - col
    causal = (back >= 0) & (back <= since)
    strict = (back > 0) & (back <= since)
    keep = (since > row).astype(F32)
    last = since[size - 1 : size, :]
    last_mask = (row >= size - 1 - last).astype(F32)
    keep_last = (last > size - 1).astype(F32)
    return causal, strict, keep, last_mask, keep_last


def unit_lower_inverses(lowers):
    size = lowers[0].shape[0]
    row, col = iotas(size)
    width = 1
    inverses = None
    while width < size:
        join = (row // (2 * width) == col // (2 * width)) & (row // width != col // width)
        pieces = [jnp.where(join, low, 0.0) for low in lowers]
        if inverses is None:
            eye = (row == col).astype(F32)
            inverses = [eye - piece for piece in pieces]
        else:
            halves = [mm(piece, inv) for piece, inv in zip(pieces, inverses)]
            inverses = [inv - mm(inv, half) for inv, half in zip(inverses, halves)]
        width *= 2
    return inverses


def conv_front(ext, proj, halo, taps, since):
    rows = proj.shape[0]
    ext[0:PAD, :] = halo.astype(F32)
    ext[PAD : PAD + rows, :] = proj
    pre = proj * taps[0:1, :]
    for lag in range(1, CONV):
        moved = ext[PAD - lag : PAD - lag + rows, :]
        pre = pre + jnp.where(since >= lag, moved, 0.0) * taps[lag : lag + 1, :]
    gate = 1.0 / (1.0 + jnp.exp(-pre))
    return pre, gate, pre * gate


def unit_rows(value):
    inv = lax.rsqrt(jnp.sum(value * value, axis=-1, keepdims=True) + 1e-06)
    return value * inv, inv


def head_column(array, head):
    lane = lax.broadcasted_iota(jnp.int32, array.shape, 1)
    return jnp.sum(jnp.where(lane == head, array, 0.0), axis=1, keepdims=True)


def forward_kernel(
    since_ref, beta_ref, query_ref, key_ref, value_ref, halo_ref, taps_ref,
    out_add_ref, out_map_ref, new_add_ref, new_map_ref, inverse_ref, starts_ref, end_ref,
    ext,
):
    rows = since_ref.shape[0]
    blocks = rows // BLOCK
    since = since_ref[...]
    jobs = []
    for sub in range(HEADS_STEP):
        head = pl.program_id(0) * HEADS_STEP + sub
        lanes = slice(sub * BLOCK, (sub + 1) * BLOCK)
        mixed = []
        for part, ref in enumerate((query_ref, key_ref, value_ref)):
            _, _, act = conv_front(
                ext.at[sub * 3 + part], ref[:, lanes].astype(F32), halo_ref[part, :, lanes],
                taps_ref[part, :, lanes], since,
            )
            mixed.append(act)
        query = unit_rows(mixed[0])[0] * (BLOCK ** -0.5)
        key = unit_rows(mixed[1])[0]
        beta = 1.0 / (1.0 + jnp.exp(-head_column(beta_ref[...], head)))
        jobs.append((lanes, query, key, mixed[2], beta))
    lowers, scores = [], []
    for lanes, query, key, value, beta in jobs:
        for blk in range(blocks):
            span = slice(blk * BLOCK, (blk + 1) * BLOCK)
            causal, strict, _, _, _ = block_masks(since[span])
            both = mm_nt(jnp.concatenate([key[span], query[span]], axis=0), key[span])
            lowers.append(jnp.where(strict, both[:BLOCK] * beta[span], 0.0))
            scores.append(jnp.where(causal, both[BLOCK:], 0.0).astype(BF16))
    inverses = [inv.astype(BF16) for inv in unit_lower_inverses(lowers)]
    row, col = iotas(BLOCK)
    eye = (row == col).astype(F32)
    states = [jnp.concatenate([jnp.zeros((BLOCK, BLOCK), F32), eye], axis=1) for _ in jobs]
    for blk in range(blocks):
        span = slice(blk * BLOCK, (blk + 1) * BLOCK)
        _, _, keep, last_mask, keep_last = block_masks(since[span])
        for sub, (lanes, query, key, value, beta) in enumerate(jobs):
            at = sub * blocks + blk
            inverse_ref[sub, blk] = inverses[at]
            state = states[sub].astype(BF16)
            starts_ref[sub, blk] = state
            stacked = jnp.concatenate([key[span] * keep, query[span] * keep], axis=0)
            seen = mm(stacked, state)
            rest = jnp.concatenate([value[span], jnp.zeros((BLOCK, BLOCK), F32)], axis=1)
            right = (rest - seen[:BLOCK]) * beta[span]
            new = mm(inverses[at], right).astype(BF16)
            out = seen[BLOCK:] + mm(scores[at], new)
            out_add_ref[span, lanes] = out[:, :BLOCK].astype(BF16)
            out_map_ref[span, lanes] = out[:, BLOCK:].astype(BF16)
            new_add_ref[span, lanes] = new[:, :BLOCK]
            new_map_ref[span, lanes] = new[:, BLOCK:]
            keep_both = jnp.concatenate([keep_last, keep_last], axis=1)
            states[sub] = states[sub] * keep_both + mm_tn(key[span] * last_mask, new)
    for sub in range(len(jobs)):
        end_ref[sub] = states[sub]


def whole_spec(shape):
    return pl.BlockSpec(shape, lambda h: (0,) * len(shape))


def head_spec(rows):
    return pl.BlockSpec((rows, HEADS_STEP * BLOCK), lambda h: (0, h))


def per_head(*tail):
    return pl.BlockSpec((HEADS_STEP,) + tail, lambda h: (h,) + (0,) * len(tail))


def lanes_spec(first, second):
    return pl.BlockSpec((first, second, HEADS_STEP * BLOCK), lambda h: (0, 0, h))


def params():
    return pltpu.CompilerParams(vmem_limit_bytes=VMEM_LIMIT)


def mixer_forward(since, beta_logit, query, key, value, halo, taps):
    rows, width = query.shape
    heads = width // BLOCK
    blocks = rows // BLOCK
    wide = jax.ShapeDtypeStruct((rows, width), BF16)
    return pl.pallas_call(
        forward_kernel,
        grid=(heads // HEADS_STEP,),
        in_specs=[
            whole_spec(since.shape), whole_spec(beta_logit.shape),
            head_spec(rows), head_spec(rows), head_spec(rows),
            lanes_spec(3, PAD), lanes_spec(3, CONV),
        ],
        out_specs=[
            head_spec(rows), head_spec(rows), head_spec(rows), head_spec(rows),
            per_head(blocks, BLOCK, BLOCK), per_head(blocks, BLOCK, 2 * BLOCK),
            per_head(BLOCK, 2 * BLOCK),
        ],
        out_shape=[
            wide, wide, wide, wide,
            jax.ShapeDtypeStruct((heads, blocks, BLOCK, BLOCK), BF16),
            jax.ShapeDtypeStruct((heads, blocks, BLOCK, 2 * BLOCK), BF16),
            jax.ShapeDtypeStruct((heads, BLOCK, 2 * BLOCK), F32),
        ],
        scratch_shapes=[pltpu.VMEM((3 * HEADS_STEP, PAD + rows, BLOCK), F32)],
        compiler_params=params(),
        name="mixer_forward",
    )(since, beta_logit, query, key, value, halo, taps)


def join_kernel(out_add_ref, out_map_ref, entry_ref, gain_ref, mixed_ref):
    for sub in range(HEADS_STEP):
        lanes = slice(sub * BLOCK, (sub + 1) * BLOCK)
        core = out_add_ref[:, lanes].astype(F32) + mm(out_map_ref[:, lanes], entry_ref[sub])
        scale = lax.rsqrt(jnp.mean(core * core, axis=-1, keepdims=True) + 1e-05)
        mixed_ref[:, lanes] = (core * scale * gain_ref[...]).astype(BF16)


def mixer_join(out_add, out_map, entry, gain):
    rows, width = out_add.shape
    heads = width // BLOCK
    return pl.pallas_call(
        join_kernel,
        grid=(heads // HEADS_STEP,),
        in_specs=[head_spec(rows), head_spec(rows), per_head(BLOCK, BLOCK), whole_spec((1, BLOCK))],
        out_specs=head_spec(rows),
        out_shape=jax.ShapeDtypeStruct((rows, width), BF16),
        compiler_params=params(),
        name="mixer_join",
    )(out_add, out_map, entry, gain)


def core_back_kernel(
    out_add_ref, out_map_ref, entry_ref, gain_ref, branch_ref, w_out_ref, d_core_ref, start_ref, gain_out_ref
):
    @pl.when(pl.program_id(0) == 0)
    def _():
        gain_out_ref[...] = jnp.zeros_like(gain_out_ref)

    upstream = mm_nt(branch_ref[...], w_out_ref[...])
    for sub in range(HEADS_STEP):
        lanes = slice(sub * BLOCK, (sub + 1) * BLOCK)
        out_map = out_map_ref[:, lanes]
        core = out_add_ref[:, lanes].astype(F32) + mm(out_map, entry_ref[sub])
        scale = lax.rsqrt(jnp.mean(core * core, axis=-1, keepdims=True) + 1e-05)
        unit = core * scale
        up = upstream[:, lanes]
        gain_out_ref[...] += jnp.sum(up * unit, axis=0, keepdims=True)
        scaled = up * gain_ref[...]
        d_core = scale * (scaled - unit * jnp.mean(scaled * unit, axis=-1, keepdims=True))
        d_core = d_core.astype(BF16)
        d_core_ref[:, lanes] = d_core
        start_ref[sub] = mm_tn(out_map, d_core)


def mixer_core_back(out_add, out_map, entry, gain, branch, w_out):
    rows, width = out_add.shape
    heads = width // BLOCK
    return pl.pallas_call(
        core_back_kernel,
        grid=(heads // HEADS_STEP,),
        in_specs=[
            head_spec(rows), head_spec(rows), per_head(BLOCK, BLOCK), whole_spec((1, BLOCK)),
            whole_spec(branch.shape), pl.BlockSpec((HEADS_STEP * BLOCK, width), lambda h: (h, 0)),
        ],
        out_specs=[head_spec(rows), per_head(BLOCK, BLOCK), whole_spec((1, BLOCK))],
        out_shape=[
            jax.ShapeDtypeStruct((rows, width), BF16),
            jax.ShapeDtypeStruct((heads, BLOCK, BLOCK), F32),
            jax.ShapeDtypeStruct((1, BLOCK), F32),
        ],
        compiler_params=params(),
        name="mixer_core_back",
    )(out_add, out_map, entry, gain, branch, w_out)


def backward_heads(
    step, since_ref, beta_ref, query_ref, key_ref, value_ref, halo_ref, taps_ref,
    new_add_ref, new_map_ref, inverse_ref, starts_ref, entry_ref, exit_ref, d_core_ref,
    d_taps_ref, d_beta_ref, ext, back, emit,
):
    rows = since_ref.shape[0]
    blocks = rows // BLOCK
    since = since_ref[...]
    jobs = []
    for sub in range(HEADS_STEP):
        head = step * HEADS_STEP + sub
        lanes = slice(sub * BLOCK, (sub + 1) * BLOCK)
        fronts = []
        for part, ref in enumerate((query_ref, key_ref, value_ref)):
            fronts.append(
                conv_front(
                    ext.at[sub * 3 + part], ref[:, lanes].astype(F32), halo_ref[part, :, lanes],
                    taps_ref[part, :, lanes], since,
                )
            )
        query_unit, query_inv = unit_rows(fronts[0][2])
        key, key_inv = unit_rows(fronts[1][2])
        query = query_unit * (BLOCK ** -0.5)
        beta = 1.0 / (1.0 + jnp.exp(-head_column(beta_ref[...], head)))
        jobs.append((head, lanes, fronts, query, query_unit, query_inv, key, key_inv, beta))

    saved = {}
    for sub, (head, lanes, fronts, query, query_unit, query_inv, key, key_inv, beta) in enumerate(jobs):
        entry = entry_ref[sub].astype(BF16)
        for blk in range(blocks):
            span = slice(blk * BLOCK, (blk + 1) * BLOCK)
            causal, _, keep, last_mask, _ = block_masks(since[span])
            start = starts_ref[sub, blk]
            state = (start[:, :BLOCK].astype(F32) + mm(start[:, BLOCK:], entry)).astype(BF16)
            new = (new_add_ref[span, lanes].astype(F32) + mm(new_map_ref[span, lanes], entry)).astype(BF16)
            scores = jnp.where(causal, mm_nt(query[span], key[span]), 0.0).astype(BF16)
            d_out = d_core_ref[span, lanes]
            d_new = mm_tn(scores, d_out)
            d_state = mm_tn(query[span] * keep, d_out)
            saved[sub, blk] = (state, new, d_out, d_new, d_state)

    carried = [exit_ref[sub].astype(F32) for sub in range(HEADS_STEP)]
    chain = {}
    for blk in reversed(range(blocks)):
        span = slice(blk * BLOCK, (blk + 1) * BLOCK)
        _, _, keep, last_mask, keep_last = block_masks(since[span])
        for sub, (head, lanes, fronts, query, query_unit, query_inv, key, key_inv, beta) in enumerate(jobs):
            state, new, d_out, d_new, d_state = saved[sub, blk]
            after = carried[sub].astype(BF16)
            d_new = d_new + mm(key[span] * last_mask, after)
            d_right = mm_tn(inverse_ref[sub, blk], d_new)
            d_rest = d_right * beta[span]
            carried[sub] = carried[sub] * keep_last + d_state - mm_tn(key[span] * keep, d_rest)
            chain[sub, blk] = (after, d_right, d_rest)

    lane = lax.broadcasted_iota(jnp.int32, (rows, beta_ref.shape[1]), 1)
    d_beta_all = jnp.zeros((rows, beta_ref.shape[1]), F32)
    for sub, (head, lanes, fronts, query, query_unit, query_inv, key, key_inv, beta) in enumerate(jobs):
        d_queries, d_keys, d_values, d_betas = [], [], [], []
        for blk in range(blocks):
            span = slice(blk * BLOCK, (blk + 1) * BLOCK)
            causal, strict, keep, last_mask, _ = block_masks(since[span])
            state, new, d_out, _, _ = saved[sub, blk]
            after, d_right, d_rest = chain[sub, blk]
            both = mm_nt(jnp.concatenate([d_out, d_right.astype(BF16)], axis=0), new)
            d_scores = jnp.where(causal, both[:BLOCK], 0.0).astype(BF16)
            d_gram = (jnp.where(strict, both[BLOCK:], 0.0) * (-beta[span])).astype(BF16)
            key_b = key[span].astype(BF16)
            from_state = mm_nt(jnp.concatenate([d_out, d_rest.astype(BF16)], axis=0), state)
            left = mm(jnp.concatenate([d_scores, d_gram], axis=0), key_b)
            d_queries.append(from_state[:BLOCK] * keep + left[:BLOCK])
            d_key = left[BLOCK:] + mm_tn(
                jnp.concatenate([d_scores, d_gram], axis=0),
                jnp.concatenate([query[span].astype(BF16), key_b], axis=0),
            )
            d_key = d_key + mm_nt(new, after) * last_mask - from_state[BLOCK:] * keep
            d_keys.append(d_key)
            d_values.append(d_rest)
            d_betas.append(
                jnp.sum(d_right * new.astype(F32), axis=1, keepdims=True) * (1.0 - beta[span])
            )
        d_query = jnp.concatenate(d_queries, axis=0) * (BLOCK ** -0.5)
        d_key = jnp.concatenate(d_keys, axis=0)
        d_query = query_inv * (
            d_query - query_unit * jnp.sum(d_query * query_unit, axis=-1, keepdims=True)
        )
        d_key = key_inv * (d_key - key * jnp.sum(d_key * key, axis=-1, keepdims=True))
        d_value = jnp.concatenate(d_values, axis=0)
        d_beta_all = d_beta_all + jnp.where(lane == head, jnp.concatenate(d_betas, axis=0), 0.0)
        for part, d_act in enumerate((d_query, d_key, d_value)):
            pre, gate, _ = fronts[part]
            taps = taps_ref[part, :, lanes]
            source = ext.at[sub * 3 + part]
            d_pre = d_act * gate * (1.0 + pre * (1.0 - gate))
            room = back.at[(sub * 3 + part) % 2]
            total = None
            d_taps = []
            for lag in range(CONV):
                masked = d_pre if lag == 0 else jnp.where(since >= lag, d_pre, 0.0)
                moved = source[PAD - lag : PAD - lag + rows, :]
                d_taps.append(jnp.sum(masked * moved, axis=0, keepdims=True))
                room[lag, 0:PAD, :] = jnp.zeros((PAD, BLOCK), F32)
                room[lag, PAD : PAD + rows, :] = masked * taps[lag : lag + 1, :]
                room[lag, PAD + rows : PAD + rows + PAD, :] = jnp.zeros((PAD, BLOCK), F32)
                term = room[lag, lag : lag + PAD + rows, :]
                total = term if total is None else total + term
            d_taps_ref[part, :, lanes] = jnp.concatenate(d_taps, axis=0)
            emit(part, lanes, total)

    @pl.when(step == 0)
    def _():
        d_beta_ref[...] = d_beta_all

    @pl.when(step > 0)
    def _():
        d_beta_ref[...] += d_beta_all


def backward_kernel(*refs):
    d_proj_ref, d_halo_ref, d_taps_ref, d_beta_ref, ext, back = refs[14:]

    def emit(part, lanes, total):
        d_halo_ref[part, :, lanes] = total[:PAD]
        d_proj_ref[part, :, lanes] = total[PAD:].astype(BF16)

    backward_heads(pl.program_id(0), *refs[:14], d_taps_ref, d_beta_ref, ext, back, emit)


def mixer_backward(
    since, beta_logit, query, key, value, halo, taps, new_add, new_map, inverse, starts, entry, exit_grad, d_core
):
    rows, width = query.shape
    heads = width // BLOCK
    blocks = rows // BLOCK
    return pl.pallas_call(
        backward_kernel,
        grid=(heads // HEADS_STEP,),
        in_specs=[
            whole_spec(since.shape), whole_spec(beta_logit.shape),
            head_spec(rows), head_spec(rows), head_spec(rows),
            lanes_spec(3, PAD), lanes_spec(3, CONV),
            head_spec(rows), head_spec(rows),
            per_head(blocks, BLOCK, BLOCK), per_head(blocks, BLOCK, 2 * BLOCK),
            per_head(BLOCK, BLOCK), per_head(BLOCK, BLOCK), head_spec(rows),
        ],
        out_specs=[
            lanes_spec(3, rows), lanes_spec(3, PAD), lanes_spec(3, CONV), whole_spec(beta_logit.shape),
        ],
        out_shape=[
            jax.ShapeDtypeStruct((3, rows, width), BF16),
            jax.ShapeDtypeStruct((3, PAD, width), F32),
            jax.ShapeDtypeStruct((3, CONV, width), F32),
            jax.ShapeDtypeStruct(beta_logit.shape, F32),
        ],
        scratch_shapes=[
            pltpu.VMEM((3 * HEADS_STEP, PAD + rows, BLOCK), F32),
            pltpu.VMEM((2, CONV, PAD + rows + PAD, BLOCK), F32),
        ],
        compiler_params=params(),
        name="mixer_backward",
    )(
        since, beta_logit, query, key, value, halo, taps, new_add, new_map, inverse, starts, entry, exit_grad, d_core
    )


GROUPS = 8
HALVES = 2


def chain_kernel(axis, forward, map_ref, add_ref, out_ref, sent, landed, send_sem, recv_sem):
    count = lax.axis_size(axis)
    me = lax.axis_index(axis)
    heads = add_ref.shape[0]
    step = heads // GROUPS
    up, down = (me + 1, me - 1) if forward else (me - 1, me + 1)
    first, last = (0, count - 1) if forward else (count - 1, 0)
    barrier = pltpu.get_barrier_semaphore()

    @pl.when(me != first)
    def _():
        pl.semaphore_signal(barrier, inc=1, device_id={axis: down}, device_id_type=MESH)

    @pl.when(me != last)
    def _():
        pl.semaphore_wait(barrier, 1)

    def copy(group, target):
        return pltpu.make_async_remote_copy(
            src_ref=sent.at[group],
            dst_ref=landed.at[group],
            send_sem=send_sem.at[group],
            recv_sem=recv_sem.at[group],
            device_id={axis: target},
            device_id_type=MESH,
        )

    for group in range(GROUPS):
        @pl.when(me != first)
        def _():
            copy(group, up).wait_recv()
            for sub in range(step):
                head = group * step + sub
                out_ref[head] = landed[group, sub].astype(F32)

        @pl.when(me == first)
        def _():
            out_ref[group * step : (group + 1) * step] = jnp.zeros((step,) + out_ref.shape[1:], F32)

        @pl.when(me != last)
        def _():
            for sub in range(step):
                head = group * step + sub
                if forward:
                    moved = mm(map_ref[head], out_ref[head])
                else:
                    moved = mm_tn(map_ref[head], out_ref[head])
                sent[group, sub] = (moved + add_ref[head]).astype(BF16)
            copy(group, up).start()

    @pl.when(me != last)
    def _():
        for group in range(GROUPS):
            copy(group, up).wait_send()


def carry_chain(map_part, add_part, axis, forward):
    heads = add_part.shape[0]
    part = (GROUPS, heads // GROUPS, BLOCK, BLOCK)
    return pl.pallas_call(
        functools.partial(chain_kernel, axis, forward),
        in_specs=[pl.BlockSpec(memory_space=pltpu.VMEM)] * 2,
        out_specs=pl.BlockSpec(memory_space=pltpu.VMEM),
        out_shape=jax.ShapeDtypeStruct(add_part.shape, F32),
        scratch_shapes=[
            pltpu.VMEM(part, BF16),
            pltpu.VMEM(part, BF16),
            pltpu.SemaphoreType.DMA((GROUPS,)),
            pltpu.SemaphoreType.DMA((GROUPS,)),
        ],
        compiler_params=pltpu.CompilerParams(
            collective_id=1 if forward else 2, has_side_effects=True, vmem_limit_bytes=VMEM_LIMIT // 2
        ),
        name="carry_forward" if forward else "carry_backward",
    )(map_part, add_part)


def bits(dp):
    core, x, y = dp % 2, (dp // 2) % 2, dp // 4
    return core, x, y, dp + 1 - 2 * core, dp + 2 * (1 - 2 * x), dp + 4 * (1 - 2 * y)


def remote(src, dst, send_sem, recv_sem, target):
    return pltpu.make_async_remote_copy(
        src_ref=src, dst_ref=dst, send_sem=send_sem, recv_sem=recv_sem, device_id=target, device_id_type=MESH
    )


def meet(dp_targets, narrow_targets):
    barrier = pltpu.get_barrier_semaphore()
    for target in dp_targets:
        pl.semaphore_signal(barrier, inc=1, device_id={"dp": target}, device_id_type=MESH)
    for target in narrow_targets:
        pl.semaphore_signal(barrier, inc=1, device_id={"narrow": target}, device_id_type=MESH)
    pl.semaphore_wait(barrier, len(dp_targets) + len(narrow_targets))


def add_rows(dst, src, step):
    def one(at, _):
        at = pl.ds(pl.multiple_of(at * step, step), step)
        dst[at, :] = (dst[at, :].astype(F32) + src[at, :].astype(F32)).astype(dst.dtype)
        return 0

    lax.fori_loop(0, dst.shape[0] // step, one, 0)


def small_kernel(small_ref, out_ref, landed, total, got2, got3, gotz, send1, recv1, send2, recv2, send3, recv3, sendz, recvz):
    dp, z = lax.axis_index("dp"), lax.axis_index("narrow")
    core, x, y, sib, flip_x, flip_y = bits(dp)
    depth = lax.axis_size("narrow")
    cols = small_ref.shape[1] // 8
    peers = [(z + step) % depth for step in range(1, depth)]
    meet((sib, flip_x, flip_y), peers)

    def stripe_lanes(stripe, which):
        return pl.ds(pl.multiple_of((stripe * 2 + which) * cols, cols), cols)

    first = [
        remote(small_ref.at[:, stripe_lanes(k, 1 - core)], landed.at[k], send1.at[k], recv1.at[k], {"dp": sib})
        for k in range(4)
    ]
    for copy in first:
        copy.start()
    for k in range(4):
        first[k].wait()
        total[k] = small_ref[:, stripe_lanes(k, core)] + landed[k]
    second = [
        remote(total.at[2 * j + 1 - x], got2.at[j], send2.at[j], recv2.at[j], {"dp": flip_x}) for j in range(2)
    ]
    for copy in second:
        copy.start()
    for copy in second:
        copy.wait()
    third = remote(total.at[2 * (1 - y) + x], got3, send3, recv3, {"dp": flip_y})
    total[2 * (1 - y) + x] = total[2 * (1 - y) + x] + got2[1 - y]
    third.start()
    third.wait()
    mine = 2 * y + x
    total[mine] = total[mine] + got2[y] + got3[...]
    last = [
        remote(total.at[mine], gotz.at[k], sendz.at[k], recvz.at[k], {"narrow": to}) for k, to in enumerate(peers)
    ]
    for copy in last:
        copy.start()
    value = total[mine]
    for k, copy in enumerate(last):
        copy.wait()
        value = value + gotz[k]
    out_ref[...] = value


def reduce_small(small):
    rows, width = small.shape
    depth = lax.axis_size("narrow")
    cols = width // 8
    dma = pltpu.SemaphoreType.DMA
    return pl.pallas_call(
        small_kernel,
        in_specs=[pl.BlockSpec(memory_space=pltpu.VMEM)],
        out_specs=pl.BlockSpec(memory_space=pltpu.VMEM),
        out_shape=jax.ShapeDtypeStruct((rows, cols), F32),
        scratch_shapes=[
            pltpu.VMEM((4, rows, cols), F32),
            pltpu.VMEM((4, rows, cols), F32),
            pltpu.VMEM((2, rows, cols), F32),
            pltpu.VMEM((rows, cols), F32),
            pltpu.VMEM((depth - 1, rows, cols), F32),
            dma((4,)), dma((4,)), dma((2,)), dma((2,)), dma(()), dma(()), dma((depth - 1,)), dma((depth - 1,)),
        ],
        compiler_params=pltpu.CompilerParams(
            collective_id=3, has_side_effects=True, vmem_limit_bytes=16 * 1024 * 1024
        ),
        name="reduce_small",
    )(small)


RING = 3
HELD = 6
LAG = 2


def fused_kernel(*refs):
    heads_in = refs[:14]
    since_ref = refs[0]
    (
        w_query_ref, w_key_ref, w_value_ref, mixed_ref, normed_hbm, branch_hbm,
        grad_hbm, d_normed_hbm, d_taps_ref, d_beta_ref,
        ext, back, left_own, left_sib, d_proj, d_proj_sib, halo_out, halo_in,
        total, got2, got3, gotz, d_normed, grad,
        local_sem, grad_sem, left_send, left_recv, right_send, right_recv, halo_send, halo_recv,
        send2, recv2, send3, recv3, sendz, recvz,
    ) = refs[14:]
    step = pl.program_id(0)
    units = pl.num_programs(0) - 1
    dp, z = lax.axis_index("dp"), lax.axis_index("narrow")
    core, x, y, sib, flip_x, flip_y = bits(dp)
    depth = lax.axis_size("narrow")
    tokens = since_ref.shape[0]
    parts = d_proj_sib.shape[1]
    rows = left_own.shape[2]
    cols = d_proj.shape[3]
    share = rows // depth
    peers = [(z + k) % depth for k in range(1, depth)]

    def stripe_lanes(stripe, which):
        return pl.ds(pl.multiple_of((stripe * 2 + which) * rows, rows), rows)

    def left_copy(k):
        source = (normed_hbm, branch_hbm)[k // 4]
        return remote(
            source.at[:, stripe_lanes(k % 4, 1 - core)], d_proj_sib.at[1 + k // 4, k % 4],
            left_send.at[k], left_recv.at[k], {"dp": sib},
        )

    def right_copies(unit):
        slot = unit % RING
        return [
            remote(
                d_proj.at[slot], d_proj_sib.at[slot, 0 : parts - 1],
                right_send.at[slot, 0], right_recv.at[slot, 0], {"dp": sib},
            ),
            remote(
                mixed_ref, d_proj_sib.at[slot, parts - 1],
                right_send.at[slot, 1], right_recv.at[slot, 1], {"dp": sib},
            ),
        ]

    def halo_copy(unit):
        return remote(
            halo_out.at[unit], halo_in.at[unit], halo_send.at[unit], halo_recv.at[unit], {"narrow": z - 1}
        )

    near = 2 * y + x
    fars = (2 * (1 - y) + x, 2 * y + 1 - x)

    def band(e):
        return pl.ds(2 * e * rows, 2 * rows)

    def copy2(unit, e, j):
        away = (2 * j + 1 - x, 2 * (1 - y) + j)[e]
        return remote(
            total.at[unit % HELD, away, band(e)], got2.at[unit, e, j],
            send2.at[unit, e, j], recv2.at[unit, e, j], {"dp": (flip_x, flip_y)[e]},
        )

    def copy3(unit, e):
        return remote(
            total.at[unit % HELD, fars[e], band(e)], got3.at[unit, e],
            send3.at[unit, e], recv3.at[unit, e], {"dp": (flip_y, flip_x)[e]},
        )

    def copyz(unit, part, k):
        at = pl.ds(pl.multiple_of(part * rows + peers[k] * share, share), share)
        return remote(
            total.at[unit % HELD, near, at], gotz.at[unit, k, part * share : (part + 1) * share],
            sendz.at[unit, k, part], recvz.at[unit, k, part], {"narrow": peers[k]},
        )

    @pl.when(step == 0)
    def _():
        loads = [
            pltpu.make_async_copy(
                (normed_hbm, branch_hbm)[k // 4].at[:, stripe_lanes(k % 4, core)],
                d_proj.at[k // 3, k % 3], local_sem.at[k],
            )
            for k in range(8)
        ]
        for load in loads:
            load.start()
        back[:, :, 0:PAD, :] = jnp.zeros((2, CONV, PAD, BLOCK), F32)
        back[:, :, PAD + tokens :, :] = jnp.zeros((2, CONV, PAD, BLOCK), F32)
        d_normed[...] = jnp.zeros_like(d_normed)
        meet((sib, flip_x, flip_y), peers)
        for k in range(8):
            left_copy(k).start()
        for k in range(8):
            loads[k].wait()
            left_own[k // 4, k % 4] = d_proj[k // 3, k % 3].astype(F32).T.astype(BF16)

    @pl.when(step == 1)
    def _():
        for k in range(8):
            left_copy(k).wait()
            left_sib[k // 4, k % 4] = d_proj_sib[1 + k // 4, k % 4].astype(F32).T.astype(BF16)

    @pl.when(step >= 1)
    def _():
        unit = step - 1

        @pl.when(z < depth - 1)
        def _():
            halo_copy(unit).wait_recv()
            for part in range(3):
                extra = jnp.concatenate([jnp.zeros((PAD, cols), F32), halo_in[unit, part]], axis=0)
                tail = slice(tokens - 2 * PAD, tokens)
                d_proj[unit % RING, part, tail, :] = (
                    d_proj[unit % RING, part, tail, :].astype(F32) + extra
                ).astype(BF16)

        @pl.when(z > 0)
        def _():
            halo_copy(unit).wait_send()

        for copy in right_copies(unit):
            copy.start()

    @pl.when(step < units)
    def _():
        def emit(part, lanes, value):
            halo_out[step, part, :, lanes] = value[:PAD]
            d_proj[step % RING, part, :, lanes] = value[PAD:].astype(BF16)

        backward_heads(step, *heads_in, d_taps_ref, d_beta_ref, ext, back, emit)

        @pl.when(z > 0)
        def _():
            halo_copy(step).start()

    @pl.when(step >= 1)
    def _():
        unit = step - 1
        for copy in right_copies(unit):
            copy.wait()

        def one(k, _):
            to_x, to_y = 1 - k // 2, 1 - k % 2
            stripe = 2 * (to_y * (1 - y) + (1 - to_y) * y) + to_x * (1 - x) + (1 - to_x) * x
            for part in range(parts):
                which = part // (parts - 1)
                mine = d_proj[unit % RING, part] if which == 0 else mixed_ref[...]
                value = jnp.dot(left_own[which, stripe], mine, preferred_element_type=F32)
                value = value + jnp.dot(
                    left_sib[which, stripe], d_proj_sib[unit % RING, part], preferred_element_type=F32
                )
                total[unit % HELD, stripe, part * rows : (part + 1) * rows, :] = value.astype(BF16)

            @pl.when(k == 0)
            def _():
                copy2(unit, 0, 1 - y).start()
                copy2(unit, 1, 1 - x).start()

            @pl.when(k == 1)
            def _():
                copy2(unit, 0, y).start()

            @pl.when(k == 2)
            def _():
                copy2(unit, 1, x).start()

            return 0

        lax.fori_loop(0, 4, one, 0)

        def normed_part(at, _):
            at = pl.ds(pl.multiple_of(at * 512, 512), 512)
            value = d_normed[:, at]
            for part, ref in enumerate((w_query_ref, w_key_ref, w_value_ref)):
                value = value + lax.dot_general(
                    d_proj[unit % RING, part], ref[at, :], (((1,), (1,)), ((), ())), preferred_element_type=F32
                )
            d_normed[:, at] = value
            return 0

        lax.fori_loop(0, d_normed.shape[1] // 512, normed_part, 0)

    def second(unit):
        for e in range(2):
            for j in range(2):
                copy2(unit, e, j).wait()
            add_rows(total.at[unit % HELD, fars[e], band(e)], got2.at[unit, e, (1 - y, 1 - x)[e]], 64)
            copy3(unit, e).start()
        for e in range(2):
            add_rows(total.at[unit % HELD, near, band(e)], got2.at[unit, e, (y, x)[e]], 64)

    def grad_copy(unit):
        at = pl.ds(pl.multiple_of(unit * cols, cols), cols)
        return pltpu.make_async_copy(grad.at[unit % 2], grad_hbm.at[:, :, at], grad_sem.at[unit % 2])

    def third(unit):
        for e in range(2):
            copy3(unit, e).wait()
            add_rows(total.at[unit % HELD, near, band(e)], got3.at[unit, e], 64)
            for k in range(depth - 1):
                for part in (2 * e, 2 * e + 1):
                    copyz(unit, part, k).start()

    def fourth(unit):
        for k in range(depth - 1):
            for part in range(parts):
                copyz(unit, part, k).wait()
        @pl.when(unit >= 2)
        def _():
            grad_copy(unit - 2).wait()

        for part in range(parts):
            at = pl.ds(pl.multiple_of(part * rows + z * share, share), share)
            value = total[unit % HELD, near, at, :].astype(F32)
            for k in range(depth - 1):
                value = value + gotz[unit, k, part * share : (part + 1) * share, :].astype(F32)
            grad[unit % 2, part] = value
        grad_copy(unit).start()

    def stages(at):
        @pl.when((at >= LAG) & (at < units + LAG))
        def _():
            second(at - LAG)

        @pl.when((at >= LAG + 1) & (at < units + LAG + 1))
        def _():
            third(at - LAG - 1)

        @pl.when(at >= LAG + 3)
        def _():
            fourth(at - LAG - 3)

    stages(step)

    @pl.when(step == units)
    def _():
        save = pltpu.make_async_copy(d_normed, d_normed_hbm, local_sem.at[0])
        save.start()

        def one(at, _):
            stages(at)
            return 0

        lax.fori_loop(units + 1, units + LAG + 3, one, 0)
        save.wait()
        grad_copy(units - 2).wait()
        grad_copy(units - 1).wait()


def fused_backward(
    since, beta_logit, query, key, value, halo, taps, new_add, new_map, inverse, starts, entry, exit_grad, d_core,
    w_query, w_key, w_value, mixed, normed, branch,
):
    tokens, width = query.shape
    heads = width // BLOCK
    blocks = tokens // BLOCK
    units = heads // HEADS_STEP
    cols = HEADS_STEP * BLOCK
    depth = lax.axis_size("narrow")
    rows = width // 8
    share = rows // depth
    dma = pltpu.SemaphoreType.DMA

    def now(step):
        return jnp.minimum(step, units - 1)

    def before(step):
        return jnp.maximum(step - 1, 0)

    def whole(shape):
        return pl.BlockSpec(shape, lambda h: (0,) * len(shape), pipeline_mode=pl.Buffered(1))

    wide = pl.BlockSpec((tokens, cols), lambda h: (0, now(h)))
    wide_once = pl.BlockSpec((tokens, cols), lambda h: (0, now(h)), pipeline_mode=pl.Buffered(1))

    def lanes(first, second):
        return pl.BlockSpec((first, second, cols), lambda h: (0, 0, now(h)))

    def each(*tail):
        return pl.BlockSpec((HEADS_STEP,) + tail, lambda h: (now(h),) + (0,) * len(tail))

    weight = pl.BlockSpec((width, cols), lambda h: (0, before(h)), pipeline_mode=pl.Buffered(1))
    mixed_spec = pl.BlockSpec((tokens, cols), lambda h: (0, before(h)), pipeline_mode=pl.Buffered(1))
    parts = 4
    anywhere = pl.BlockSpec(memory_space=pl.ANY)
    return pl.pallas_call(
        fused_kernel,
        grid=(units + 1,),
        in_specs=[
            whole(since.shape), whole(beta_logit.shape), wide_once, wide_once, wide_once, lanes(3, PAD), lanes(3, CONV),
            wide, wide, each(blocks, BLOCK, BLOCK), each(blocks, BLOCK, 2 * BLOCK),
            each(BLOCK, BLOCK), each(BLOCK, BLOCK), wide,
            weight, weight, weight, mixed_spec, anywhere, anywhere,
        ],
        out_specs=[
            anywhere, anywhere, lanes(3, CONV), pl.BlockSpec(beta_logit.shape, lambda h: (0, 0)),
        ],
        out_shape=[
            jax.ShapeDtypeStruct((parts, share, width), F32),
            jax.ShapeDtypeStruct((tokens, width), F32),
            jax.ShapeDtypeStruct((3, CONV, width), F32),
            jax.ShapeDtypeStruct(beta_logit.shape, F32),
        ],
        scratch_shapes=[
            pltpu.VMEM((3 * HEADS_STEP, PAD + tokens, BLOCK), F32),
            pltpu.VMEM((2, CONV, PAD + tokens + PAD, BLOCK), F32),
            pltpu.VMEM((2, 4, rows, tokens), BF16),
            pltpu.VMEM((2, 4, rows, tokens), BF16),
            pltpu.VMEM((RING, 3, tokens, cols), BF16),
            pltpu.VMEM((RING, parts, tokens, cols), BF16),
            pltpu.VMEM((units, 3, PAD, cols), F32),
            pltpu.VMEM((units, 3, PAD, cols), F32),
            pltpu.VMEM((HELD, 4, parts * rows, cols), BF16),
            pltpu.VMEM((units, 2, 2, 2 * rows, cols), BF16),
            pltpu.VMEM((units, 2, 2 * rows, cols), BF16),
            pltpu.VMEM((units, depth - 1, parts * share, cols), BF16),
            pltpu.VMEM((tokens, width), F32),
            pltpu.VMEM((2, parts, share, cols), F32),
            dma((8,)), dma((2,)), dma((8,)), dma((8,)), dma((RING, 2)), dma((RING, 2)), dma((units,)), dma((units,)),
            dma((units, 2, 2)), dma((units, 2, 2)), dma((units, 2)), dma((units, 2)),
            dma((units, depth - 1, parts)), dma((units, depth - 1, parts)),
        ],
        compiler_params=pltpu.CompilerParams(
            collective_id=5, has_side_effects=True, vmem_limit_bytes=125 * 512 * 1024
        ),
        name="fused_backward",
    )(
        since, beta_logit, query, key, value, halo, taps, new_add, new_map, inverse, starts, entry, exit_grad, d_core,
        w_query, w_key, w_value, mixed, normed, branch,
    )


def ffn_grads_kernel(*refs):
    lefts = [refs[0:HALVES], refs[0:HALVES], refs[HALVES : 2 * HALVES]]
    rights = [refs[(2 + m) * HALVES : (3 + m) * HALVES] for m in range(3)]
    (
        gate_ref, up_ref, down_ref, left_buf, right_buf, away, landed, total, got2, got3,
        left_sem, right_sem, send1, recv1, send2, recv2, send3, recv3,
    ) = refs[5 * HALVES :]
    dp = lax.axis_index("dp")
    core, x, y = dp % 2, (dp // 2) % 2, dp // 4
    rows = total.shape[2]
    half = rows // 2
    part = left_buf.shape[1] // HALVES
    sib = dp + 1 - 2 * core
    flip_x = dp + 2 * (1 - 2 * x)
    flip_y = dp + 4 * (1 - 2 * y)
    barrier = pltpu.get_barrier_semaphore()
    for target in (sib, flip_x, flip_y):
        pl.semaphore_signal(barrier, inc=1, device_id={"dp": target}, device_id_type=MESH)

    def load_left(m, k, start):
        own = k // 4
        block = (k % 4) * 2 + own * core + (1 - own) * (1 - core)
        lanes = pl.ds(pl.multiple_of(block * rows, rows), rows)
        for at in range(HALVES):
            copy = pltpu.make_async_copy(
                lefts[m][at].at[:, lanes], left_buf.at[k % 2, at * part : (at + 1) * part], left_sem.at[k % 2, at]
            )
            if start:
                copy.start()
            else:
                copy.wait()

    def load_right(m, start):
        for at in range(HALVES):
            copy = pltpu.make_async_copy(
                rights[m][at], right_buf.at[m % 2, at * part : (at + 1) * part], right_sem.at[m % 2, at]
            )
            if start:
                copy.start()
            else:
                copy.wait()

    def send(src, dst, send_sem, recv_sem, target):
        return pltpu.make_async_remote_copy(
            src_ref=src, dst_ref=dst, send_sem=send_sem, recv_sem=recv_sem,
            device_id={"dp": target}, device_id_type=MESH,
        )

    def copy1(m, stripe):
        return send(away.at[m, stripe], landed.at[m, stripe], send1.at[m, stripe], recv1.at[m, stripe], sib)

    def band(h):
        return pl.ds(h * half, half)

    def order(h):
        if h == 0:
            return (lambda j: 2 * j + 1 - x), (lambda j: 2 * j + x), flip_x, flip_y, 1 - y, y
        return (lambda j: 2 * (1 - y) + j), (lambda j: 2 * y + j), flip_y, flip_x, 1 - x, x

    def copy2(m, h, j):
        gone, _, target, _, _, _ = order(h)
        return send(
            total.at[m, gone(j), band(h)], got2.at[m, h, j], send2.at[2 * m + h, j], recv2.at[2 * m + h, j], target
        )

    def copy3(m, h):
        _, kept, _, target, far, _ = order(h)
        return send(total.at[m, kept(far), band(h)], got3.at[m, h], send3.at[m, h], recv3.at[m, h], target)

    def add_to(dst, src):
        step = 32

        def one(at, _):
            at = pl.ds(pl.multiple_of(at * step, step), step)
            dst[at, :] = (dst[at, :].astype(F32) + src[at, :].astype(F32)).astype(dst.dtype)
            return 0

        lax.fori_loop(0, dst.shape[0] // step, one, 0)

    def compute(m):
        load_right(m, False)
        if m + 1 < 3:
            load_right(m + 1, True)

        def one(k, _):
            @pl.when(k < 7)
            def _():
                load_left(m, k + 1, True)

            if m + 1 < 3:
                @pl.when(k == 7)
                def _():
                    load_left(m + 1, 0, True)

            load_left(m, k, False)
            value = lax.dot_general(
                left_buf[k % 2], right_buf[m % 2], (((0,), (0,)), ((), ())), preferred_element_type=F32
            ).astype(BF16)

            @pl.when(k < 4)
            def _():
                away[m, k] = value
                copy1(m, k).start()

            @pl.when(k >= 4)
            def _():
                total[m, k - 4] = value

            return 0

        lax.fori_loop(0, 8, one, 0)

        def join(stripe, _):
            copy1(m, stripe).wait()
            add_to(total.at[m, stripe], landed.at[m, stripe])
            return 0

        lax.fori_loop(0, 4, join, 0)
        for h in range(2):
            for j in range(2):
                copy2(m, h, j).start()

    def second(m):
        for h in range(2):
            _, kept, _, _, far, near = order(h)
            for j in range(2):
                copy2(m, h, j).wait()
            add_to(total.at[m, kept(far), band(h)], got2.at[m, h, far])
            copy3(m, h).start()
            add_to(total.at[m, kept(near), band(h)], got2.at[m, h, near])

    def third(m):
        for h in range(2):
            _, kept, _, _, _, near = order(h)
            copy3(m, h).wait()
            if m == 2:
                value = total[m, kept(near), band(h), :].astype(F32) + got3[m, h].astype(F32)
                down_ref[:, band(h)] = value.T
                continue
            step = 32

            def one(at, _):
                at = at * step
                value = total[m, kept(near), pl.ds(pl.multiple_of(h * half + at, step), step), :].astype(F32)
                value = value + got3[m, h, pl.ds(pl.multiple_of(at, step), step), :].astype(F32)
                (gate_ref, up_ref)[m][pl.ds(pl.multiple_of(h * half + at, step), step), :] = value
                return 0

            lax.fori_loop(0, half // step, one, 0)

    load_right(0, True)
    load_left(0, 0, True)
    pl.semaphore_wait(barrier, 3)
    compute(0)
    compute(1)
    second(0)
    compute(2)
    third(0)
    second(1)
    third(1)
    second(2)
    third(2)


def ffn_grads(lefts, rights):
    part, height = lefts[0][0].shape
    width = rights[0][0].shape[1]
    rows = height // 8
    half = rows // 2
    dma = pltpu.SemaphoreType.DMA
    operands = [ref for group in (*lefts, *rights) for ref in group]
    return pl.pallas_call(
        ffn_grads_kernel,
        in_specs=[pl.BlockSpec(memory_space=pl.ANY)] * len(operands),
        out_specs=[pl.BlockSpec(memory_space=pltpu.VMEM)] * 3,
        out_shape=[
            jax.ShapeDtypeStruct((rows, width), F32),
            jax.ShapeDtypeStruct((rows, width), F32),
            jax.ShapeDtypeStruct((width, rows), F32),
        ],
        scratch_shapes=[
            pltpu.VMEM((2, HALVES * part, rows), BF16),
            pltpu.VMEM((2, HALVES * part, width), BF16),
            pltpu.VMEM((3, 4, rows, width), BF16),
            pltpu.VMEM((3, 4, rows, width), BF16),
            pltpu.VMEM((3, 4, rows, width), BF16),
            pltpu.VMEM((3, 2, 2, half, width), BF16),
            pltpu.VMEM((3, 2, half, width), BF16),
            dma((2, HALVES)), dma((2, HALVES)), dma((3, 4)), dma((3, 4)),
            dma((6, 2)), dma((6, 2)), dma((3, 2)), dma((3, 2)),
        ],
        compiler_params=pltpu.CompilerParams(
            collective_id=4, has_side_effects=True, vmem_limit_bytes=60 * 1024 * 1024
        ),
        name="ffn_grads",
    )(*operands)


def shifted(value, axis, steps):
    count = lax.axis_size(axis)
    first, last = (max(0, -steps), min(count, count - steps))
    return lax.ppermute(value, axis, [(source, source + steps) for source in range(first, last)])


def matmul(left, right):
    return jnp.dot(left, right, preferred_element_type=F32)


def dot_tn(left, right):
    return jnp.einsum("rd,re->de", left, right, preferred_element_type=F32)


def dot_nt(left, right):
    return jnp.einsum("re,de->rd", left, right, preferred_element_type=F32)


def rms_scale(value_in, gain_vec, epsilon):
    return value_in * lax.rsqrt(jnp.mean(value_in * value_in, axis=-1, keepdims=True) + epsilon) * gain_vec


def norm_back(value_in, gain_vec, upstream, epsilon):
    inv_scale = lax.rsqrt(jnp.mean(value_in * value_in, axis=-1, keepdims=True) + epsilon)
    scaled_up = upstream * gain_vec
    gain_term = jnp.sum(upstream * value_in * inv_scale, axis=0)
    cubed = inv_scale * inv_scale * inv_scale
    back_value = inv_scale * scaled_up - value_in * cubed * jnp.mean(
        scaled_up * value_in, axis=-1, keepdims=True
    )
    return (back_value, gain_term)


def since_start(doc_lengths, offset, rows):
    ends = jnp.cumsum(doc_lengths[0])
    position = offset + jnp.arange(rows, dtype=jnp.int32)
    starts = jnp.max(jnp.where(position[:, None] >= ends[None, :], ends[None, :], 0), axis=1)
    return jnp.broadcast_to((position - starts)[:, None], (rows, BLOCK)).astype(jnp.int32)


def scatter_all(value, dim):
    part = lax.psum_scatter(value, "dp", scatter_dimension=dim, tiled=True)
    return lax.psum_scatter(part, "narrow", scatter_dimension=dim, tiled=True)


def local(
    tokens,
    doc_lengths,
    attn_gain,
    w_query,
    w_key,
    w_value,
    w_beta,
    conv_weight,
    out_gain,
    w_out,
    mlp_gain,
    w_gate,
    w_up,
    w_down,
    grad_out,
):
    tok_rows, model_width = tokens.shape
    offset = lax.axis_index("narrow") * tok_rows
    half = tok_rows // HALVES
    parts = [slice(at * half, (at + 1) * half) for at in range(HALVES)]

    def gather(rows):
        return lax.all_gather(rows, "narrow", axis=0, tiled=True)

    def scatter(rows):
        return lax.psum_scatter(rows, "narrow", scatter_dimension=0, tiled=True)

    cot = gather(grad_out)
    since = since_start(doc_lengths, offset, tok_rows)
    inputs = tokens.astype(F32)
    normed = rms_scale(inputs, attn_gain, 1e-06).astype(BF16)
    query, key, value = (matmul(normed, w).astype(BF16) for w in (w_query, w_key, w_value))
    beta_logit = matmul(normed, w_beta)
    halo = shifted(
        jnp.stack([part[tok_rows - PAD :] for part in (query, key, value)]), "narrow", 1
    )
    out_add, out_map, new_add, new_map, inverse, starts, end = mixer_forward(
        since, beta_logit, query, key, value, halo, conv_weight
    )
    transfer = end[:, :, BLOCK:].astype(BF16)
    entry = carry_chain(transfer, end[:, :, :BLOCK], "narrow", True)
    gain_row = out_gain[None, :]
    attn_mixed = mixer_join(out_add, out_map, entry, gain_row)
    hidden = inputs + matmul(attn_mixed, w_out)
    normed_mlp = rms_scale(hidden, mlp_gain, 1e-06).astype(BF16)
    normed_mlp, cot = lax.optimization_barrier((normed_mlp, cot))
    cot = cot.reshape(-1, tok_rows, model_width)
    cot = [cot[:, part].reshape(-1, model_width) for part in parts]
    gathered = [gather(normed_mlp[part]) for part in parts]
    activation, d_gate, d_up, d_normed_parts, out_parts = [], [], [], [], []
    for at in range(HALVES):
        gate_proj = matmul(gathered[at], w_gate)
        up_proj = matmul(gathered[at], w_up)
        gate_sigmoid = jax.nn.sigmoid(gate_proj)
        silu_gate = gate_proj * gate_sigmoid
        activation.append((silu_gate * up_proj).astype(BF16))
        d_act = jnp.einsum("rd,fd->rf", cot[at], w_down, preferred_element_type=F32)
        d_gate.append(
            (d_act * up_proj * gate_sigmoid * (1.0 + gate_proj * (1.0 - gate_sigmoid))).astype(BF16)
        )
        d_up.append((d_act * silu_gate).astype(BF16))
        d_part = (dot_nt(d_gate[at], w_gate) + dot_nt(d_up[at], w_up)).astype(BF16)
        out_part = matmul(activation[at], w_down).astype(BF16)
        if at + 1 < HALVES:
            quarters = out_part.reshape(-1, 2, half // 2, model_width)
            out_parts += [quarters[:, side].reshape(-1, model_width) for side in range(2)]
            d_part, out_parts, gathered[at + 1] = lax.optimization_barrier((d_part, out_parts, gathered[at + 1]))
        else:
            out_parts.append(out_part)
        d_normed_parts.append(scatter(d_part))
    if lax.axis_size("dp") == 8:
        ffn_sums = ffn_grads((gathered, cot), (d_gate, d_up, activation))
    else:
        ffn_sums = [
            lax.psum_scatter(
                sum(dot_tn(a, c) for a, c in zip(left, right)).astype(BF16), "dp", scatter_dimension=0, tiled=True
            )
            for left, right in ((gathered, d_gate), (gathered, d_up), (cot, activation))
        ]
        ffn_sums[2] = ffn_sums[2].T
    d_normed_parts, out_parts, ffn_sums = lax.optimization_barrier((d_normed_parts, out_parts, ffn_sums))
    out_first, *out_rest = out_parts
    ffn_parts = [scatter(out_first)]
    grad_gate, grad_up, grad_down = (value.astype(F32) for value in ffn_sums)
    d_normed_mlp = jnp.concatenate(d_normed_parts, axis=0).astype(F32)
    d_hidden_norm, mlp_gain_term = norm_back(hidden, mlp_gain, d_normed_mlp, 1e-06)
    d_hidden = grad_out.astype(F32) + d_hidden_norm
    d_branch = d_hidden.astype(BF16)
    d_core, start_grad, out_gain_term = mixer_core_back(out_add, out_map, entry, gain_row, d_branch, w_out)
    exit_grad = carry_chain(transfer, start_grad, "narrow", False)
    exit_grad, out_rest = lax.optimization_barrier((exit_grad, out_rest))
    ffn_parts += [scatter(part) for part in out_rest]
    mixer_args = (
        since, beta_logit, query, key, value, halo, conv_weight,
        new_add, new_map, inverse, starts, entry, exit_grad, d_core,
    )
    if lax.axis_size("dp") == 8:
        grads, d_normed, conv_term, d_beta = fused_backward(
            *mixer_args, w_query, w_key, w_value, attn_mixed, normed, d_branch
        )
    else:
        d_proj, d_halo, conv_term, d_beta = mixer_backward(*mixer_args)
        after = shifted(d_halo.astype(BF16), "narrow", -1)
        d_proj = d_proj.at[:, tok_rows - PAD :].add(after)
        d_normed = sum(dot_nt(part, w) for part, w in zip(d_proj, (w_query, w_key, w_value)))
        pairs = [(normed, part) for part in d_proj] + [(d_branch, attn_mixed)]
        grads = jnp.stack([scatter_all(dot_tn(a, c).astype(BF16), 0).astype(F32) for a, c in pairs])
    d_beta_low = d_beta.astype(BF16)
    beta_term = jnp.einsum("rh,rd->hd", d_beta_low, normed, preferred_element_type=F32)
    d_normed = d_normed + jnp.einsum("rh,dh->rd", d_beta_low, w_beta, preferred_element_type=F32)
    d_input_norm, attn_gain_term = norm_back(inputs, attn_gain, d_normed, 1e-06)
    grad_tokens = (d_hidden + d_input_norm).astype(BF16)
    devices = lax.axis_size("dp") * lax.axis_size("narrow")
    heads = w_beta.shape[1]
    taps = 3 * CONV
    gain_share = BLOCK // devices
    per_device = model_width // devices
    gain_row_term = jnp.pad(
        out_gain_term.reshape(devices, gain_share), ((0, 0), (0, per_device - gain_share))
    ).reshape(1, model_width)
    small = jnp.concatenate(
        [
            beta_term,
            conv_term.reshape(taps, model_width),
            attn_gain_term[None, :],
            mlp_gain_term[None, :],
            gain_row_term,
            jnp.zeros((-(heads + taps + 3) % 8, model_width), F32),
        ],
        axis=0,
    )
    if lax.axis_size("dp") == 8:
        small = lax.dynamic_slice_in_dim(
            reduce_small(small), lax.axis_index("narrow") * per_device, per_device, axis=1
        )
    else:
        small = lax.psum_scatter(small, ("dp", "narrow"), scatter_dimension=1, tiled=True)
    grad_beta = small[:heads].T
    grad_conv = small[heads : heads + taps].reshape(3, CONV, per_device)
    grad_attn_gain = small[heads + taps]
    grad_mlp_gain = small[heads + taps + 1]
    grad_out_gain = small[heads + taps + 2, :gain_share]
    ffn_parts, grads = lax.optimization_barrier((ffn_parts, grads))
    block_out = (hidden + jnp.concatenate(ffn_parts, axis=0).astype(F32)).astype(BF16)
    grad_query, grad_key, grad_value = grads[0], grads[1], grads[2]
    grad_w_out = grads[3].T
    return (
        block_out,
        grad_tokens,
        grad_attn_gain,
        grad_query,
        grad_key,
        grad_value,
        grad_beta,
        grad_conv,
        grad_out_gain,
        grad_w_out,
        grad_mlp_gain,
        grad_gate,
        grad_up,
        grad_down,
    )


def solution(mesh):
    placed = (
        P(("dp", "narrow"), None),
        P("dp", None),
        P(),
        P(),
        P(),
        P(),
        P(),
        P(),
        P(),
        P(),
        P(),
        P(None, "narrow"),
        P(None, "narrow"),
        P("narrow", None),
        P(("dp", "narrow"), None),
    )
    return jax.shard_map(
        local,
        mesh=mesh,
        in_specs=placed,
        out_specs=(
            P(("dp", "narrow"), None),
            P(("dp", "narrow"), None),
            P(("dp", "narrow")),
            P(("dp", "narrow"), None),
            P(("dp", "narrow"), None),
            P(("dp", "narrow"), None),
            P(("dp", "narrow"), None),
            P(None, None, ("dp", "narrow")),
            P(("dp", "narrow")),
            P(None, ("dp", "narrow")),
            P(("dp", "narrow")),
            P("dp", "narrow"),
            P("dp", "narrow"),
            P("narrow", "dp"),
        ),
        check_vma=False,
    )
```
